32 devices in a mesh: expert: 8 (over z, y), tensor: 4 (over x, core).
Axes of the slice: x: 2, y: 2, z: 4, core: 2. Of those that a mesh axis runs over, the one named last changes fastest.
Arguments:
- tokens: bfloat16 [7880, 512], P('expert'), may hold values from -6 to 6
- routes: int32 [2, 7880, 2], P(None, 'expert'), may hold values from 0 to 7, all different within a row
- ln_gain: float32 [2, 2, 512], replicated, may hold values from 0.5 to 1.5
- ln_bias: float32 [2, 2, 512], replicated, may hold values from -1.5 to 1.5
- w_qkv: bfloat16 [2, 3, 512, 512], P(None, None, None, 'tensor'), may hold values from -0.25 to 0.25
- w_out: bfloat16 [2, 512, 512], P(None, 'tensor'), may hold values from -1 to 1
- w_router: bfloat16 [2, 512, 8], replicated, may hold values from -0.1875 to 0.1875
- w_up: bfloat16 [2, 8, 512, 2048], P(None, 'expert', None, 'tensor'), may hold values from -0.25 to 0.25
- w_down: bfloat16 [2, 8, 2048, 512], P(None, 'expert', 'tensor'), may hold values from -0.1875 to 0.1875
- cotangent: bfloat16 [7880, 512], P('expert'), may hold values from -6 to 6
Outputs:
- result: bfloat16 [7880, 512], P('expert')
- grad_tokens: float32 [7880, 512], P('expert')
- grad_gain: float32 [2, 2, 512], replicated
- grad_bias_one: float32 [2, 512], replicated
- grad_bias_two: float32 [2, 512], replicated
- grad_qkv: float32 [2, 3, 512, 512], P(None, None, None, 'tensor')
- grad_out: float32 [2, 512, 512], P(None, 'tensor')
- grad_router: float32 [2, 512, 8], replicated
- grad_up: float32 [2, 8, 512, 2048], P(None, 'expert', None, 'tensor')
- grad_down: float32 [2, 8, 2048, 512], P(None, 'expert', 'tensor')
The draws below stay inside these ranges and needn't reach their ends.
Inputs may be any that keep to these rules, and one draw needn't show every extreme that they name: `routes`: each token names 2 different experts in each block; every expert is named by some token.
All inputs are finite; a program needn't handle non-finite values.
Results may differ from the reference program's by a relative error of at most 0.034.
Values may be sent and summed in bfloat16 or wider, within the bound.
A program may use at most 128 MiB of HBM per device.

```python
import jax
import jax.numpy as jnp
from jax import lax

D = 512
HEADS = 8
HEAD_DIM = 64
FF = 2048
SEQ = 197
TOP = 2
LAYERS = 2
IMG_DEV = 5
TOK_DEV = 985
TOKENS = 7880
EXPERTS = 8
CAPS = 304
N_EXPERT = 8


def steps_of(rng, extent, pieces, smallest, high):
    def one(position, parts):
        heights = jax.random.uniform(jax.random.fold_in(jax.random.fold_in(rng, 6), position), (parts,), jnp.float32, smallest / len(pieces), high / len(pieces))
        return jnp.repeat(jnp.exp(heights), extent[position] // parts).reshape((-1,) + (1,) * (len(extent) - position - 1))

    gain = one(*pieces[0])
    for cut in pieces[1:]:
        gain = gain * one(*cut)
    return gain


def picks_of(key, rows, amount, top, lift):
    sequence = jax.random.permutation(jax.random.fold_in(key, 1), amount)
    boost = sequence
    for power in range(3):
        boost = boost * boost // amount
    boost = boost * lift // amount
    chance = jax.random.randint(jax.random.fold_in(key, 2), (rows, amount), 0, 4096) + boost
    holders = jax.random.permutation(jax.random.fold_in(key, 3), rows)[jnp.arange(amount) % rows]
    chance = jnp.where(jnp.arange(rows)[:, None] == holders[None, :], 1 << 14, chance)
    score = chance * amount + jnp.arange(amount)
    return lax.top_k(score.astype(jnp.int32), top)[1].astype(jnp.int32)


def scatter_about(rng, shape, deviation, bound, cuts=(), kind=jnp.bfloat16):
    factor_of = steps_of(rng, shape, cuts, -0.22, 0.18) if cuts else 1.0
    values = jax.random.normal(rng, shape, jnp.float32) * deviation * factor_of
    return jnp.minimum(jnp.maximum(values, -bound), bound).astype(kind)


def setup_inputs(seed: int = 0) -> dict:
    splits = jax.random.split(jax.random.key(seed), 11)
    return {
        "tokens": scatter_about(splits[0], (TOKENS, D), 1.0, 6.0, ((0, 8),)),
        "routes": picks_of(splits[1], LAYERS * TOKENS, EXPERTS, TOP, 2048).reshape((LAYERS, TOKENS, TOP)),
        "ln_gain": jnp.clip(1.0 + 0.1 * jax.random.normal(splits[2], (LAYERS, 2, D), jnp.float32), 0.5, 1.5),
        "ln_bias": scatter_about(splits[3], (LAYERS, 2, D), 0.3, 1.5, (), jnp.float32),
        "w_qkv": scatter_about(splits[4], (LAYERS, 3, D, D), D ** -0.5, 0.25, ((3, 4),)),
        "w_out": scatter_about(splits[5], (LAYERS, D, D), (D // 16) ** -0.5, 1.0, ((1, 4),)),
        "w_router": scatter_about(splits[6], (LAYERS, D, EXPERTS), (2 * D) ** -0.5, 0.1875),
        "w_up": scatter_about(splits[7], (LAYERS, EXPERTS, D, FF), D ** -0.5, 0.25, ((1, 8), (3, 4))),
        "w_down": scatter_about(splits[8], (LAYERS, EXPERTS, FF, D), (FF // 2) ** -0.5, 0.1875, ((1, 8), (2, 4))),
        "cotangent": scatter_about(splits[9], (TOKENS, D), 1.0, 6.0, ((0, 8),)),
    }


HIGH = lax.Precision.HIGHEST

@jax.custom_vjp
def low(v):
    return lax.optimization_barrier(v.astype(jnp.bfloat16)).astype(jnp.float32)

@jax.custom_vjp
def low_back(v):
    return v

def low_keep(v):
    return (low(v), None)

def low_pass(kept, grad):
    return (grad,)

def back_keep(v):
    return (v, None)

def back_low(kept, grad):
    return (low(grad),)
low.defvjp(low_keep, low_pass)
low_back.defvjp(back_keep, back_low)

def matmul(left_side, right_side):
    return jnp.dot(left_side, right_side, precision=HIGH, preferred_element_type=jnp.float32)

def norm_apply(stream, gain_row, bias_row):
    centered = stream - lax.optimization_barrier(jnp.mean(stream, -1, keepdims=True))
    return centered * lax.rsqrt(lax.optimization_barrier(jnp.mean(centered * centered, -1, keepdims=True)) + 1e-06) * gain_row + bias_row

def attend_group(tensors):
    query, keyed, valued = tensors
    scores = low_back(jnp.einsum('bqhe,bkhe->bhqk', query, keyed, precision=HIGH) * HEAD_DIM ** (-0.5))
    expd = jnp.exp(scores - lax.optimization_barrier(jnp.max(scores, -1, keepdims=True)))
    attn_prob = expd / lax.optimization_barrier(jnp.sum(expd, -1, keepdims=True))
    mixed = jnp.einsum('bhqk,bkhe->bqhe', low(attn_prob), valued, precision=HIGH)
    return low(low_back(mixed))

def expert_apply(tensors):
    rows_in, up_mat, down_mat = tensors
    pre_act = low_back(matmul(rows_in, up_mat))
    hidden = low(jax.nn.gelu(pre_act))
    return low(low_back(matmul(hidden, down_mat)))

def layer_apply(stream, route_pair, gain_pair, bias_pair, w_qkv, w_out, w_router, w_up, w_down):
    hidden_in = low(norm_apply(stream, gain_pair[0], bias_pair[0]))
    proj = tuple((low(low_back(matmul(hidden_in, w_qkv[part]))).reshape(N_EXPERT, IMG_DEV, SEQ, HEADS, HEAD_DIM) for part in range(3)))
    mixed = lax.map(jax.checkpoint(attend_group), proj).reshape(TOKENS, D)
    after_attn = stream + low_back(matmul(mixed, w_out))
    hidden_two = low(norm_apply(after_attn, gain_pair[1], bias_pair[1]))
    logits = low_back(matmul(hidden_two, w_router))
    chosen = jnp.take_along_axis(logits, route_pair, 1)
    shifted = jnp.exp(chosen - lax.optimization_barrier(jnp.max(chosen, -1, keepdims=True)))
    gate_share = shifted / lax.optimization_barrier(jnp.sum(shifted, -1, keepdims=True))
    flat_route = route_pair.reshape(N_EXPERT, TOP * TOK_DEV).astype(jnp.int32)
    onehot = (flat_route[..., None] == jnp.arange(EXPERTS, dtype=jnp.int32)).astype(jnp.int32)
    place_in = lax.optimization_barrier(jnp.sum((jnp.cumsum(onehot, 1) - onehot) * onehot, -1))
    kept_mask = place_in < CAPS
    slot_place = jnp.minimum(place_in, CAPS - 1).astype(jnp.int32)
    source = jnp.broadcast_to(jnp.arange(N_EXPERT, dtype=jnp.int32)[:, None], flat_route.shape)
    paired = jnp.repeat(hidden_two.reshape(N_EXPERT, TOK_DEV, D), TOP, axis=1) * kept_mask[..., None].astype(jnp.float32)
    buffer = jnp.zeros((EXPERTS, N_EXPERT, CAPS, D), jnp.float32).at[flat_route, source, slot_place].add(paired)
    recv_rows = low_back(buffer).reshape(EXPERTS, N_EXPERT * CAPS, D)
    outputs = lax.map(jax.checkpoint(expert_apply), (recv_rows, w_up, w_down)).reshape(EXPERTS, N_EXPERT, CAPS, D)
    picked = outputs[flat_route, source, slot_place] * kept_mask[..., None].astype(jnp.float32)
    picked = picked.reshape(TOKENS, TOP, D)
    return after_attn + lax.optimization_barrier(jnp.sum(gate_share[..., None] * picked, 1))

def forward(stream, gains, biases, w_qkv, w_out, w_router, w_up, w_down, routes):
    for layer_index in range(LAYERS):
        stream = layer_apply(stream, routes[layer_index], gains[layer_index], biases[layer_index], w_qkv[layer_index], w_out[layer_index], w_router[layer_index], w_up[layer_index], w_down[layer_index])
    return stream

def reference(tokens, routes, ln_gain, ln_bias, w_qkv, w_out, w_router, w_up, w_down, cotangent):
    floats = tuple((item.astype(jnp.float32) for item in (tokens, ln_gain, ln_bias, w_qkv, w_out, w_router, w_up, w_down)))

    def apply_all(*values):
        return forward(*values, routes)
    result, pullback = jax.vjp(apply_all, *floats)
    grads = pullback(cotangent.astype(jnp.float32))
    return (result.astype(jnp.bfloat16), grads[0], grads[1], grads[2][:, 0], grads[2][:, 1], grads[3], grads[4], grads[5], grads[6], grads[7])
```

```python
import functools

import jax
import jax.numpy as jnp
from jax import lax
from jax.experimental import pallas as pl
from jax.experimental.pallas import tpu as pltpu
from jax.sharding import PartitionSpec as P

HEAD_DIM = 64
SEQ = 197
PAD = 208
LAYERS = 2
EPS = 1e-06
MESH = pl.DeviceIdType.MESH
F32 = jnp.float32
BF16 = jnp.bfloat16
SCALE = HEAD_DIM ** (-0.5)
MIB = 1 << 20


def up_to(count, multiple):
    return -(-count // multiple) * multiple


def dot(left, right):
    return lax.dot_general(left, right, (((1,), (0,)), ((), ())), preferred_element_type=F32)


def dot_nt(left, right):
    return lax.dot_general(left, right, (((1,), (1,)), ((), ())), preferred_element_type=F32)


def dot_tn(left, right):
    return lax.dot_general(left, right, (((0,), (0,)), ((), ())), preferred_element_type=F32)


def norm_parts(rows):
    centered = rows - jnp.mean(rows, -1, keepdims=True)
    scaled = lax.rsqrt(jnp.mean(centered * centered, -1, keepdims=True) + EPS)
    return centered * scaled, scaled


def norm_pull(grad_in, normed, scaled, gain_row):
    grad_normed = grad_in * gain_row
    inner = (
        grad_normed
        - jnp.mean(grad_normed, -1, keepdims=True)
        - normed * jnp.mean(grad_normed * normed, -1, keepdims=True)
    )
    return inner * scaled


def tensor_place():
    place = lax.axis_index("tensor")
    core = lax.rem(place, 2)
    core_peer = place + 1 - 2 * core
    chip_peer = lax.rem(place + 2, 4)
    return place, core, core_peer, chip_peer


def greet_tensor(core_peer, chip_peer):
    barrier = pltpu.get_barrier_semaphore()
    for peer in (core_peer, chip_peer):
        pl.semaphore_signal(barrier, inc=1, device_id={"tensor": peer}, device_id_type=MESH)


def greet_expert(size):
    me = lax.axis_index("expert")
    barrier = pltpu.get_barrier_semaphore()

    def one(step, carry):
        peer = lax.rem(me + step, size)
        pl.semaphore_signal(barrier, inc=1, device_id={"expert": peer}, device_id_type=MESH)
        return carry

    lax.fori_loop(1, size, one, 0)


class TensorSum:
    def __init__(self, part, near, chip_sum, far, final, send, recv):
        self.part, self.near, self.chip_sum, self.far, self.final = part, near, chip_sum, far, final
        self.send, self.recv = send, recv
        _, self.core, self.core_peer, self.chip_peer = tensor_place()

    @staticmethod
    def scratch(images):
        rows = images * PAD
        half = (rows, 256)
        return [
            pltpu.VMEM((2,) + half, BF16),
            pltpu.VMEM(half, BF16),
            pltpu.VMEM(half, BF16),
            pltpu.VMEM(half, BF16),
            pltpu.VMEM((2,) + half, BF16),
            pltpu.SemaphoreType.DMA((3, images)),
            pltpu.SemaphoreType.DMA((3, images)),
        ]

    def rows(self, image):
        return pl.ds(pl.multiple_of(image * PAD, PAD), PAD)

    def first(self, image):
        rows = self.rows(image)
        return pltpu.make_async_remote_copy(
            src_ref=self.part.at[1 - self.core, rows],
            dst_ref=self.near.at[rows],
            send_sem=self.send.at[0, image],
            recv_sem=self.recv.at[0, image],
            device_id={"tensor": self.core_peer},
            device_id_type=MESH,
        )

    def second(self, image):
        rows = self.rows(image)
        return pltpu.make_async_remote_copy(
            src_ref=self.chip_sum.at[rows],
            dst_ref=self.far.at[rows],
            send_sem=self.send.at[1, image],
            recv_sem=self.recv.at[1, image],
            device_id={"tensor": self.chip_peer},
            device_id_type=MESH,
        )

    def third(self, image):
        rows = self.rows(image)
        return pltpu.make_async_remote_copy(
            src_ref=self.final.at[self.core, rows],
            dst_ref=self.final.at[self.core, rows],
            send_sem=self.send.at[2, image],
            recv_sem=self.recv.at[2, image],
            device_id={"tensor": self.core_peer},
            device_id_type=MESH,
        )

    def put(self, image, value):
        rows = self.rows(image)
        self.part[0, rows, :] = value[:, :256].astype(BF16)
        self.part[1, rows, :] = value[:, 256:].astype(BF16)

    def step_near(self, image):
        rows = self.rows(image)
        self.first(image).wait()
        self.chip_sum[rows, :] = (
            self.part[self.core, rows, :].astype(F32) + self.near[rows, :].astype(F32)
        ).astype(BF16)
        self.second(image).start()

    def step_far(self, image):
        rows = self.rows(image)
        self.second(image).wait()
        self.final[self.core, rows, :] = (
            self.chip_sum[rows, :].astype(F32) + self.far[rows, :].astype(F32)
        ).astype(BF16)
        self.third(image).start()

    def step_end(self, image):
        self.third(image).wait()

    def get(self, image):
        rows = self.rows(image)
        return jnp.concatenate(
            [self.final[0, rows, :].astype(F32), self.final[1, rows, :].astype(F32)], axis=1
        )


def finish_sum(total, images, use):
    def far(image, carry):
        total.step_far(image)
        return carry

    def body(image, carry):
        total.step_far(image)
        total.step_end(image - 1)
        use(image - 1, total.get(image - 1))
        return carry

    total.step_far(0)
    lax.fori_loop(1, images, body, 0)
    total.step_end(images - 1)
    use(images - 1, total.get(images - 1))


class Exchange:
    def __init__(self, size, block, src, dst, send, recv, local):
        self.size, self.block, self.src, self.dst = size, block, src, dst
        self.send, self.recv, self.local = send, recv, local
        self.me = lax.axis_index("expert")

    @staticmethod
    def scratch(size):
        return [
            pltpu.SemaphoreType.DMA((size,)),
            pltpu.SemaphoreType.DMA((size,)),
            pltpu.SemaphoreType.DMA,
        ]

    def rows(self, index):
        return pl.ds(pl.multiple_of(index * self.block, self.block), self.block)

    def own(self):
        return pltpu.make_async_copy(
            self.src.at[self.rows(self.me)], self.dst.at[self.rows(self.me)], self.local
        )

    def copy(self, step):
        target = lax.rem(self.me + step, self.size)
        return pltpu.make_async_remote_copy(
            src_ref=self.src.at[self.rows(target)],
            dst_ref=self.dst.at[self.rows(self.me)],
            send_sem=self.send.at[step],
            recv_sem=self.recv.at[step],
            device_id={"expert": target},
            device_id_type=MESH,
        )

    def start(self):
        def one(step, carry):
            self.copy(step).start()
            return carry

        lax.fori_loop(1, self.size, one, 0)
        self.own().start()

    def wait(self):
        def one(step, carry):
            self.copy(step).wait()
            return carry

        self.own().wait()
        lax.fori_loop(1, self.size, one, 0)


def attend_forward(images, refs):
    (
        x_ref, gain_ref, bias_ref, wqkv_ref, wout_ref,
        y_ref, h_ref, qkv_ref, prob_ref, mixed_ref,
    ) = refs[:10]
    total = TensorSum(*refs[10:])
    greet_tensor(total.core_peer, total.chip_peer)
    joint = jnp.concatenate([wqkv_ref[0], wqkv_ref[1], wqkv_ref[2]], axis=1)
    w_out = wout_ref[...]
    first_head = lax.broadcasted_iota(jnp.int32, (PAD, 2 * HEAD_DIM), 1) < HEAD_DIM
    key_real = lax.broadcasted_iota(jnp.int32, (2 * PAD, PAD), 1) < SEQ
    nothing = jnp.zeros((PAD, 2 * HEAD_DIM), BF16)

    def compute(image):
        rows = total.rows(image)
        normed, _ = norm_parts(x_ref[rows, :])
        hidden = (normed * gain_ref[0:1, :] + bias_ref[0:1, :]).astype(BF16)
        h_ref[rows, :] = hidden
        proj = dot(hidden, joint).astype(BF16)
        qkv_ref[rows, :] = proj
        query, keyed, valued = proj[:, :128], proj[:, 128:256], proj[:, 256:]
        both = jnp.concatenate(
            [jnp.where(first_head, query, nothing), jnp.where(first_head, nothing, query)], axis=0
        )
        scores = jnp.where(key_real, dot_nt(both, keyed) * SCALE, -1e30)
        expd = jnp.exp(scores - jnp.max(scores, -1, keepdims=True))
        prob = (expd / jnp.sum(expd, -1, keepdims=True)).astype(BF16)
        prob_ref[image] = prob
        out = dot(prob, valued)
        mixed = jnp.where(first_head, out[:PAD], out[PAD:]).astype(BF16)
        mixed_ref[rows, :] = mixed
        total.put(image, dot(mixed, w_out))

    def body(image, carry):
        compute(image)
        total.first(image).start()
        total.step_near(image - 1)
        return carry

    compute(0)
    pl.semaphore_wait(pltpu.get_barrier_semaphore(), 2)
    total.first(0).start()
    lax.fori_loop(1, images, body, 0)
    total.step_near(images - 1)

    def use(image, value):
        rows = total.rows(image)
        y_ref[rows, :] = x_ref[rows, :] + value

    finish_sum(total, images, use)


def attention_forward(x, gain, bias, w_qkv, w_out, collective_id):
    rows = x.shape[0]
    images = rows // PAD

    def kernel(*refs):
        attend_forward(images, refs)

    return pl.pallas_call(
        kernel,
        name="attention_forward",
        out_shape=(
            jax.ShapeDtypeStruct((rows, 512), F32),
            jax.ShapeDtypeStruct((rows, 512), BF16),
            jax.ShapeDtypeStruct((rows, 384), BF16),
            jax.ShapeDtypeStruct((images, 2 * PAD, PAD), BF16),
            jax.ShapeDtypeStruct((rows, 128), BF16),
        ),
        scratch_shapes=TensorSum.scratch(images),
        compiler_params=pltpu.CompilerParams(
            collective_id=collective_id, has_side_effects=True, vmem_limit_bytes=40 * MIB
        ),
    )(x, gain, bias, w_qkv, w_out)


def attend_backward(images, refs):
    (
        g_ref, x_ref, h_ref, qkv_ref, prob_ref, mixed_ref, gain_ref, wqkv_ref, wout_ref,
        gin_ref, gqkv_ref, gout_ref, gvec_ref, low_ref, dproj_ref,
    ) = refs[:15]
    total = TensorSum(*refs[15:])
    greet_tensor(total.core_peer, total.chip_peer)
    joint = jnp.concatenate([wqkv_ref[0], wqkv_ref[1], wqkv_ref[2]], axis=1)
    w_out = wout_ref[...]
    first_head = lax.broadcasted_iota(jnp.int32, (PAD, 2 * HEAD_DIM), 1) < HEAD_DIM
    nothing = jnp.zeros((PAD, 2 * HEAD_DIM), BF16)

    def split(value):
        return jnp.concatenate(
            [jnp.where(first_head, value, nothing), jnp.where(first_head, nothing, value)], axis=0
        )

    def compute(image):
        rows = total.rows(image)
        out_low = g_ref[rows, :].astype(BF16)
        low_ref[rows, :] = out_low
        proj = qkv_ref[rows, :]
        query, keyed, valued = proj[:, :128], proj[:, 128:256], proj[:, 256:]
        mixed_grad = split(dot_nt(out_low, w_out).astype(BF16))
        prob_low = prob_ref[image]
        prob = prob_low.astype(F32)
        prob_grad = dot_nt(mixed_grad, valued)
        score_grad = (
            prob * (prob_grad - jnp.sum(prob_grad * prob, -1, keepdims=True))
        ).astype(BF16)
        query_both = dot(score_grad, keyed)
        query_grad = jnp.where(first_head, query_both[:PAD], query_both[PAD:]) * SCALE
        key_grad = dot_tn(score_grad, split(query)) * SCALE
        value_grad = dot_tn(prob_low, mixed_grad)
        proj_grad = jnp.concatenate([query_grad, key_grad, value_grad], axis=1).astype(BF16)
        dproj_ref[rows, :] = proj_grad
        total.put(image, dot_nt(proj_grad, joint))

    def body(image, carry):
        compute(image)
        total.first(image).start()
        total.step_near(image - 1)
        return carry

    compute(0)
    pl.semaphore_wait(pltpu.get_barrier_semaphore(), 2)
    total.first(0).start()
    lax.fori_loop(1, images, body, 0)
    total.step_near(images - 1)
    gout_ref[...] = dot_tn(mixed_ref[...], low_ref[...])
    gqkv_ref[...] = dot_tn(h_ref[...], dproj_ref[...])
    gvec_ref[...] = jnp.zeros_like(gvec_ref)

    def use(image, value):
        rows = total.rows(image)
        normed, scaled = norm_parts(x_ref[rows, :])
        gin_ref[rows, :] = g_ref[rows, :] + norm_pull(value, normed, scaled, gain_ref[0:1, :])
        gvec_ref[0:1, :] += jnp.sum(value * normed, 0, keepdims=True)
        gvec_ref[1:2, :] += jnp.sum(value, 0, keepdims=True)

    finish_sum(total, images, use)


def attention_backward(grad, x, saved, gain, w_qkv, w_out, collective_id):
    rows = x.shape[0]
    images = rows // PAD
    hidden, qkv, prob, mixed = saved

    def kernel(*refs):
        attend_backward(images, refs)

    return pl.pallas_call(
        kernel,
        name="attention_backward",
        out_shape=(
            jax.ShapeDtypeStruct((rows, 512), F32),
            jax.ShapeDtypeStruct((512, 384), F32),
            jax.ShapeDtypeStruct((128, 512), F32),
            jax.ShapeDtypeStruct((8, 512), F32),
        ),
        scratch_shapes=[pltpu.VMEM((rows, 512), BF16), pltpu.VMEM((rows, 384), BF16)]
        + TensorSum.scratch(images),
        compiler_params=pltpu.CompilerParams(
            collective_id=collective_id, has_side_effects=True, vmem_limit_bytes=48 * MIB
        ),
    )(grad, x, hidden, qkv, prob, mixed, gain, w_qkv, w_out)


class Plan:
    def __init__(self, tok_rows, experts):
        self.images = tok_rows // SEQ
        self.rows = self.images * PAD
        self.lanes = up_to(self.rows, 128)
        self.experts = experts
        self.per_rank = max(1, 10 * tok_rows // (4 * experts * 4))
        self.capacity = 4 * self.per_rank
        self.block = up_to(self.per_rank, 16)
        self.slots = experts * self.block
        self.extra = up_to(experts, 16)


def gelu(pre):
    inner = 0.7978845608028654 * (pre + 0.044715 * (pre * pre * pre))
    return 0.5 * pre * (1.0 + jnp.tanh(inner))


def gelu_both(pre):
    square = pre * pre
    inner = pre * (0.7978845608028654 + 0.035677408136300125 * square)
    bent = jnp.tanh(inner)
    half = 0.5 * (1.0 + bent)
    slope = half + 0.5 * pre * (1.0 - bent * bent) * (
        0.7978845608028654 + 0.10703222440890037 * square
    )
    return half * pre, slope


def build_members(plan, place_ref, gate_ref, member_ref, slot_gate_ref):
    slot = lax.broadcasted_iota(jnp.int32, (plan.block, plan.lanes), 0).astype(F32)

    def one(expert, carry):
        rows = pl.ds(pl.multiple_of(expert * plan.block, plan.block), plan.block)
        hit = place_ref[pl.ds(expert, 1), :] == slot
        member_ref[rows, :] = jnp.where(hit, 1.0, 0.0).astype(BF16)
        slot_gate_ref[rows, :] = jnp.sum(
            jnp.where(hit, gate_ref[pl.ds(expert, 1), :], 0.0), -1, keepdims=True
        )
        return carry

    lax.fori_loop(0, plan.experts, one, 0)


def run_moe_forward(plan, refs):
    (
        y_ref, route_ref, gain_ref, bias_ref, router_ref, up_ref, down_ref,
        next_ref, h2_ref, recv_ref, back_ref, place_ref, gate_ref,
        member_ref, slot_gate_ref, send_ref, ret_ref,
    ) = refs[:17]
    out_move = Exchange(plan.experts, plan.block, send_ref, recv_ref, *refs[17:20])
    back_move = Exchange(plan.experts, plan.block, ret_ref, back_ref, *refs[20:23])
    total = TensorSum(*refs[23:])
    greet_tensor(total.core_peer, total.chip_peer)
    greet_expert(plan.experts)
    rank = lax.axis_index("tensor")

    def norm_body(image, carry):
        rows = total.rows(image)
        normed, _ = norm_parts(y_ref[rows, :])
        h2_ref[rows, :] = (normed * gain_ref[1:2, :] + bias_ref[1:2, :]).astype(BF16)
        return carry

    lax.fori_loop(0, plan.images, norm_body, 0)
    if plan.lanes > plan.rows:
        h2_ref[plan.rows :, :] = jnp.zeros((plan.lanes - plan.rows, 512), BF16)
    hidden = h2_ref[...]
    logits = dot_nt(router_ref[...], hidden)
    shape = (plan.experts, plan.lanes)
    expert_id = lax.broadcasted_iota(jnp.int32, shape, 0)
    named = (expert_id == route_ref[0:1, :]) | (expert_id == route_ref[1:2, :])
    shifted = jnp.where(named, logits, -1e30)
    top = jnp.max(shifted, 0, keepdims=True)
    expd = jnp.where(named, jnp.exp(shifted - top), 0.0)
    share = expd / jnp.maximum(jnp.sum(expd, 0, keepdims=True), 1e-30)
    gate_ref[...] = share
    count = jnp.where(named, 1.0, 0.0)
    lane = lax.broadcasted_iota(jnp.int32, shape, 1)
    running = count
    step = 1
    while step < plan.lanes:
        running = running + jnp.where(lane >= step, pltpu.roll(running, step, 1), 0.0)
        step *= 2
    before = running - count
    mine = before - (rank * plan.per_rank).astype(F32)
    valid = named & (mine >= 0.0) & (mine < float(plan.per_rank))
    place_ref[...] = jnp.where(valid, mine, -1.0)
    build_members(plan, place_ref, gate_ref, member_ref, slot_gate_ref)
    send_ref[...] = dot(member_ref[...], hidden).astype(BF16)
    pl.semaphore_wait(pltpu.get_barrier_semaphore(), 2 + plan.experts - 1)
    out_move.start()
    out_move.wait()
    recv = recv_ref[...]
    result = jnp.zeros((plan.slots, 512), F32)
    for part in range(4):
        hidden_part = gelu(dot(recv, up_ref[part])).astype(BF16)
        result = result + dot(hidden_part, down_ref[part])
    ret_ref[...] = result.astype(BF16)
    back_move.start()
    back_move.wait()
    gated = (back_ref[...].astype(F32) * slot_gate_ref[...]).astype(BF16)
    mixed = dot_tn(member_ref[...], gated)
    for image in range(plan.images):
        total.put(image, mixed[image * PAD : (image + 1) * PAD])

    def go(image, carry):
        total.first(image).start()
        return carry

    def near(image, carry):
        total.step_near(image)
        return carry

    lax.fori_loop(0, plan.images, go, 0)
    lax.fori_loop(0, plan.images, near, 0)

    def use(image, value):
        rows = total.rows(image)
        next_ref[rows, :] = y_ref[rows, :] + value

    finish_sum(total, plan.images, use)


def moe_forward(plan, y, route, gain, bias, router, w_up, w_down, collective_id):
    def kernel(*refs):
        run_moe_forward(plan, refs)

    return pl.pallas_call(
        kernel,
        name="moe_forward",
        out_shape=(
            jax.ShapeDtypeStruct((plan.rows, 512), F32),
            jax.ShapeDtypeStruct((plan.lanes, 512), BF16),
            jax.ShapeDtypeStruct((plan.slots, 512), BF16),
            jax.ShapeDtypeStruct((plan.slots, 512), BF16),
            jax.ShapeDtypeStruct((plan.experts, plan.lanes), F32),
            jax.ShapeDtypeStruct((plan.experts, plan.lanes), F32),
        ),
        scratch_shapes=[
            pltpu.VMEM((plan.slots, plan.lanes), BF16),
            pltpu.VMEM((plan.slots, 1), F32),
            pltpu.VMEM((plan.slots, 512), BF16),
            pltpu.VMEM((plan.slots, 512), BF16),
        ]
        + Exchange.scratch(plan.experts)
        + Exchange.scratch(plan.experts)
        + TensorSum.scratch(plan.images),
        compiler_params=pltpu.CompilerParams(
            collective_id=collective_id, has_side_effects=True, vmem_limit_bytes=56 * MIB
        ),
    )(y, route, gain, bias, router, w_up, w_down)


def run_moe_backward(plan, refs):
    (
        g_ref, y_ref, h2_ref, recv_ref, back_ref, place_ref, gate_ref, gain_ref, router_ref,
        up_ref, down_ref,
        gy_ref, gup_ref, gdown_ref, grouter_ref, gvec_ref,
        member_ref, slot_gate_ref, low_ref, send_ref, drecv_ref, ret_ref, dback_ref,
        act_ref, slope_ref, dpre_ref,
    ) = refs[:26]
    out_move = Exchange(plan.experts, plan.block, send_ref, drecv_ref, *refs[26:29])
    back_move = Exchange(
        plan.experts, plan.block, ret_ref, dback_ref.at[pl.ds(0, plan.slots)], *refs[29:32]
    )
    total = TensorSum(*refs[32:])
    greet_tensor(total.core_peer, total.chip_peer)
    greet_expert(plan.experts)
    low_ref[: plan.rows, :] = g_ref[...].astype(BF16)
    if plan.lanes > plan.rows:
        low_ref[plan.rows :, :] = jnp.zeros((plan.lanes - plan.rows, 512), BF16)
    build_members(plan, place_ref, gate_ref, member_ref, slot_gate_ref)
    members = member_ref.at[pl.ds(0, plan.slots)]
    slot_grad = dot(members[...], low_ref[...])
    send_ref[...] = (slot_grad * slot_gate_ref[...]).astype(BF16)
    pl.semaphore_wait(pltpu.get_barrier_semaphore(), 2 + plan.experts - 1)
    out_move.start()

    product = (slot_grad * back_ref[...].astype(F32)).astype(BF16)
    gate_row = dot_nt(jnp.ones((plan.experts, 512), BF16), product)
    shape = (plan.experts, plan.slots)
    own = lax.broadcasted_iota(jnp.int32, shape, 0) == (
        lax.broadcasted_iota(jnp.int32, shape, 1) // plan.block
    )
    spread = jnp.where(own, gate_row, 0.0)
    spread_high = spread.astype(BF16)
    spread_low = (spread - spread_high.astype(F32)).astype(BF16)
    gate_grad = dot(spread_high, members[...]) + dot(spread_low, members[...])
    share = gate_ref[...]
    logit_grad = share * (gate_grad - jnp.sum(share * gate_grad, 0, keepdims=True))
    logit_low = logit_grad.astype(BF16)
    grouter_ref[...] = dot(logit_low, h2_ref[...])
    member_ref[plan.slots :, :] = jnp.zeros((plan.extra, plan.lanes), BF16)
    member_ref[plan.slots : plan.slots + plan.experts, :] = logit_low
    dback_ref[plan.slots :, :] = jnp.zeros((plan.extra, 512), BF16)
    dback_ref[plan.slots : plan.slots + plan.experts, :] = router_ref[...]
    recv = recv_ref[...]
    for part in range(4):
        act, slope = gelu_both(dot(recv, up_ref[part]))
        act_ref[part] = act.astype(BF16)
        slope_ref[part] = slope.astype(BF16)
    out_move.wait()

    drecv = drecv_ref[...]
    result = jnp.zeros((plan.slots, 512), F32)
    for part in range(4):
        pre_grad = (dot_nt(drecv, down_ref[part]) * slope_ref[part].astype(F32)).astype(BF16)
        dpre_ref[part] = pre_grad
        result = result + dot_nt(pre_grad, up_ref[part])
    ret_ref[...] = result.astype(BF16)
    back_move.start()
    for part in range(4):
        gdown_ref[part] = dot_tn(act_ref[part], drecv).astype(BF16)
        gup_ref[part] = dot_tn(recv, dpre_ref[part]).astype(BF16)
    back_move.wait()

    mixed = dot_tn(member_ref[...], dback_ref[...])
    for image in range(plan.images):
        total.put(image, mixed[image * PAD : (image + 1) * PAD])

    def go(image, carry):
        total.first(image).start()
        return carry

    def near(image, carry):
        total.step_near(image)
        return carry

    lax.fori_loop(0, plan.images, go, 0)
    lax.fori_loop(0, plan.images, near, 0)
    gvec_ref[...] = jnp.zeros_like(gvec_ref)

    def use(image, value):
        rows = total.rows(image)
        normed, scaled = norm_parts(y_ref[rows, :])
        gy_ref[rows, :] = g_ref[rows, :] + norm_pull(value, normed, scaled, gain_ref[1:2, :])
        gvec_ref[0:1, :] += jnp.sum(value * normed, 0, keepdims=True)
        gvec_ref[1:2, :] += jnp.sum(value, 0, keepdims=True)

    finish_sum(total, plan.images, use)


def moe_backward(plan, grad, y, saved, gain, router, w_up, w_down, collective_id):
    h2, recv, back, place, gate = saved

    def kernel(*refs):
        run_moe_backward(plan, refs)

    return pl.pallas_call(
        kernel,
        name="moe_backward",
        out_shape=(
            jax.ShapeDtypeStruct((plan.rows, 512), F32),
            jax.ShapeDtypeStruct((4, 512, 512), BF16),
            jax.ShapeDtypeStruct((4, 512, 512), BF16),
            jax.ShapeDtypeStruct((plan.experts, 512), F32),
            jax.ShapeDtypeStruct((8, 512), F32),
        ),
        scratch_shapes=[
            pltpu.VMEM((plan.slots + plan.extra, plan.lanes), BF16),
            pltpu.VMEM((plan.slots, 1), F32),
            pltpu.VMEM((plan.lanes, 512), BF16),
            pltpu.VMEM((plan.slots, 512), BF16),
            pltpu.VMEM((plan.slots, 512), BF16),
            pltpu.VMEM((plan.slots, 512), BF16),
            pltpu.VMEM((plan.slots + plan.extra, 512), BF16),
            pltpu.VMEM((4, plan.slots, 512), BF16),
            pltpu.VMEM((4, plan.slots, 512), BF16),
            pltpu.VMEM((4, plan.slots, 512), BF16),
        ]
        + Exchange.scratch(plan.experts)
        + Exchange.scratch(plan.experts)
        + TensorSum.scratch(plan.images),
        compiler_params=pltpu.CompilerParams(
            collective_id=collective_id, has_side_effects=True, vmem_limit_bytes=60 * MIB
        ),
    )(grad, y, h2, recv, back, place, gate, gain, router, w_up, w_down)


def body(tokens, routes, ln_gain, ln_bias, w_qkv, w_out, w_router, w_up, w_down, cotangent):
    tok_rows = tokens.shape[0]
    experts = w_router.shape[2]
    plan = Plan(tok_rows, experts)

    def pad_rows(value):
        value = value.astype(F32).reshape(plan.images, SEQ, -1)
        return jnp.pad(value, ((0, 0), (0, PAD - SEQ), (0, 0))).reshape(plan.rows, -1)

    def cut_rows(value):
        return value.reshape(plan.images, PAD, -1)[:, :SEQ].reshape(tok_rows, -1)

    up_all = [lax.all_gather(w_up[layer, 0], "tensor") for layer in range(LAYERS)]
    down_all = [lax.all_gather(w_down[layer, 0], "tensor") for layer in range(LAYERS)]
    route_rows = routes.reshape(LAYERS, plan.images, SEQ, 2)
    route_rows = jnp.pad(
        route_rows, ((0, 0), (0, 0), (0, PAD - SEQ), (0, 0)), constant_values=-1
    ).reshape(LAYERS, plan.rows, 2)
    route_rows = jnp.pad(
        route_rows, ((0, 0), (0, plan.lanes - plan.rows), (0, 0)), constant_values=-1
    ).transpose(0, 2, 1)
    router_rows = w_router.transpose(0, 2, 1)

    stream = pad_rows(tokens)
    kept = []
    for layer in range(LAYERS):
        after, *saved_one = attention_forward(
            stream, ln_gain[layer], ln_bias[layer], w_qkv[layer], w_out[layer], 4 * layer
        )
        following, *saved_two = moe_forward(
            plan, after, route_rows[layer], ln_gain[layer], ln_bias[layer], router_rows[layer],
            up_all[layer], down_all[layer], 4 * layer + 1,
        )
        kept.append((stream, after, saved_one, saved_two))
        stream = following
    result = cut_rows(stream).astype(BF16)
    grad = pad_rows(cotangent)
    per_layer = [None] * LAYERS
    for layer in reversed(range(LAYERS)):
        stream, after, saved_one, saved_two = kept[layer]
        grad, gup, gdown, grouter, gvec_two = moe_backward(
            plan, grad, after, saved_two, ln_gain[layer], router_rows[layer],
            up_all[layer], down_all[layer], 4 * layer + 2,
        )
        gup = lax.psum_scatter(gup, "tensor", scatter_dimension=0, tiled=False)
        gdown = lax.psum_scatter(gdown, "tensor", scatter_dimension=0, tiled=False)
        grad, gqkv, gout, gvec_one = attention_backward(
            grad, stream, saved_one, ln_gain[layer], w_qkv[layer], w_out[layer], 4 * layer + 3
        )
        grouter = lax.psum(grouter, ("expert", "tensor"))
        gqkv, gout, gvec = lax.psum(
            (gqkv, gout, jnp.stack([gvec_one[:2], gvec_two[:2]])), "expert"
        )
        gqkv = gqkv.reshape(512, 3, 128).transpose(1, 0, 2)
        per_layer[layer] = (
            gvec[:, 0], gvec[0, 1], gvec[1, 1], gqkv, gout, grouter.T,
            gup.astype(F32)[None], gdown.astype(F32)[None],
        )
    stacked = [jnp.stack([entry[member] for entry in per_layer]) for member in range(8)]
    return (result, cut_rows(grad), *stacked)


def solution(mesh):
    in_specs = (
        P("expert", None),
        P(None, "expert", None),
        P(),
        P(),
        P(None, None, None, "tensor"),
        P(None, "tensor", None),
        P(),
        P(None, "expert", None, "tensor"),
        P(None, "expert", "tensor", None),
        P("expert", None),
    )
    out_specs = (
        P("expert", None),
        P("expert", None),
        P(),
        P(),
        P(),
        P(None, None, None, "tensor"),
        P(None, "tensor", None),
        P(),
        P(None, "expert", None, "tensor"),
        P(None, "expert", "tensor", None),
    )
    return jax.shard_map(body, mesh=mesh, in_specs=in_specs, out_specs=out_specs, check_vma=False)
```

```python
import types

import jax
import jax.numpy as jnp
from jax import lax
from jax.experimental import pallas as pl
from jax.experimental.pallas import tpu as pltpu
from jax.sharding import PartitionSpec as P

HEAD_DIM = 64
SEQ = 197
PAD = 208
EPS = 1e-06
MESH = pl.DeviceIdType.MESH
F32 = jnp.float32
BF16 = jnp.bfloat16
SCALE = HEAD_DIM ** (-0.5)
MIB = 1 << 20
VMEM = pltpu.VMEM
DMA = pltpu.SemaphoreType.DMA


def up_to(count, multiple):
    return -(-count // multiple) * multiple


def dot(left, right):
    return lax.dot_general(left, right, (((1,), (0,)), ((), ())), preferred_element_type=F32)


def dot_nt(left, right):
    return lax.dot_general(left, right, (((1,), (1,)), ((), ())), preferred_element_type=F32)


def dot_tn(left, right):
    return lax.dot_general(left, right, (((0,), (0,)), ((), ())), preferred_element_type=F32)


def norm_parts(rows):
    centered = rows - jnp.mean(rows, -1, keepdims=True)
    scaled = lax.rsqrt(jnp.mean(centered * centered, -1, keepdims=True) + EPS)
    return centered * scaled, scaled


def norm_pull(grad_in, normed, scaled, gain_row):
    grad_normed = grad_in * gain_row
    inner = (
        grad_normed
        - jnp.mean(grad_normed, -1, keepdims=True)
        - normed * jnp.mean(grad_normed * normed, -1, keepdims=True)
    )
    return inner * scaled


def gelu(pre):
    inner = pre * (0.7978845608028654 + 0.035677408136300125 * (pre * pre))
    return 0.5 * pre * (1.0 + jnp.tanh(inner))


def gelu_both(pre):
    square = pre * pre
    inner = pre * (0.7978845608028654 + 0.035677408136300125 * square)
    bent = jnp.tanh(inner)
    half = 0.5 + 0.5 * bent
    slope = half + half * (1.0 - bent) * pre * (
        0.7978845608028654 + 0.10703222440890037 * square
    )
    return half * pre, slope


class Plan:
    def __init__(self, tok_rows, experts):
        self.images = tok_rows // SEQ
        self.rows = self.images * PAD
        self.lanes = up_to(self.rows, 128)
        self.experts = experts
        self.per_rank = max(1, 10 * tok_rows // (4 * experts * 4))
        self.capacity = 4 * self.per_rank
        self.block = up_to(self.per_rank + 2, 16)
        self.slots = experts * self.block
        self.group = max(
            size for size in range(1, experts)
            if experts % size == 0 and (size == 1 or size * self.block <= 320)
        )
        self.stored = 4 * self.slots <= 2560
        self.small = up_to(4 * (4 + experts), 16)
        self.chunk = up_to(-(-(2048 + self.small) // experts), 16)
        self.packed = experts * self.chunk


def image_rows(image):
    return pl.ds(pl.multiple_of(image * PAD, PAD), PAD)


def each(low, high, use):
    def one(index, carry):
        use(index)
        return carry

    lax.fori_loop(low, high, one, 0)


class Place:
    def __init__(self, experts):
        self.tensor = lax.axis_index("tensor")
        self.core = lax.rem(self.tensor, 2)
        self.core_peer = self.tensor + 1 - 2 * self.core
        self.chip_peer = lax.rem(self.tensor + 2, 4)
        self.experts = experts
        self.expert = lax.axis_index("expert")

    def ahead(self, step):
        return lax.rem(self.expert + step, self.experts)

    def behind(self, step):
        return lax.rem(self.expert + self.experts - step, self.experts)

    def greet(self):
        barrier = pltpu.get_barrier_semaphore()
        for peer in (self.core_peer, self.chip_peer):
            pl.semaphore_signal(barrier, inc=1, device_id={"tensor": peer}, device_id_type=MESH)

        def one(step):
            pl.semaphore_signal(
                barrier, inc=1, device_id={"expert": self.ahead(step)}, device_id_type=MESH
            )

        each(1, self.experts, one)

    def met(self):
        pl.semaphore_wait(pltpu.get_barrier_semaphore(), 2 + self.experts - 1)

    def to_core(self, src, dst, send, recv):
        return pltpu.make_async_remote_copy(
            src_ref=src, dst_ref=dst, send_sem=send, recv_sem=recv,
            device_id={"tensor": self.core_peer}, device_id_type=MESH,
        )

    def to_chip(self, src, dst, send, recv):
        return pltpu.make_async_remote_copy(
            src_ref=src, dst_ref=dst, send_sem=send, recv_sem=recv,
            device_id={"tensor": self.chip_peer}, device_id_type=MESH,
        )

    def to_expert(self, expert, src, dst, send, recv):
        return pltpu.make_async_remote_copy(
            src_ref=src, dst_ref=dst, send_sem=send, recv_sem=recv,
            device_id={"expert": expert}, device_id_type=MESH,
        )


class TensorSum:
    def __init__(self, place, refs):
        self.place, self.core = place, place.core
        self.part, self.near, self.far, self.final, self.send, self.recv = refs

    @staticmethod
    def scratch(images):
        half = (images * PAD, 256)
        return [
            VMEM((2,) + half, BF16), VMEM(half, BF16), VMEM(half, BF16),
            VMEM((2,) + half, BF16), DMA((3, images)), DMA((3, images)),
        ]

    def first(self, image):
        rows = image_rows(image)
        return self.place.to_core(
            self.part.at[1 - self.core, rows], self.near.at[rows],
            self.send.at[0, image], self.recv.at[0, image],
        )

    def second(self, image):
        rows = image_rows(image)
        return self.place.to_chip(
            self.part.at[self.core, rows], self.far.at[rows],
            self.send.at[1, image], self.recv.at[1, image],
        )

    def third(self, image):
        rows = image_rows(image)
        half = self.final.at[self.core, rows]
        return self.place.to_core(half, half, self.send.at[2, image], self.recv.at[2, image])

    def put(self, image, value):
        rows = image_rows(image)
        self.part[0, rows, :] = value[:, :256].astype(BF16)
        self.part[1, rows, :] = value[:, 256:].astype(BF16)
        self.first(image).start()

    def step_near(self, image):
        rows = image_rows(image)
        self.first(image).wait()
        self.part[self.core, rows, :] = (
            self.part[self.core, rows, :].astype(F32) + self.near[rows, :].astype(F32)
        ).astype(BF16)
        self.second(image).start()

    def step_far(self, image):
        rows = image_rows(image)
        self.second(image).wait()
        self.final[self.core, rows, :] = (
            self.part[self.core, rows, :].astype(F32) + self.far[rows, :].astype(F32)
        ).astype(BF16)
        self.third(image).start()

    def get(self, image):
        rows = image_rows(image)
        self.third(image).wait()
        return jnp.concatenate(
            [self.final[0, rows, :].astype(F32), self.final[1, rows, :].astype(F32)], axis=1
        )

    def finish(self, images, use):
        def one(image):
            self.step_far(image)
            use(image - 1, self.get(image - 1))

        self.step_far(0)
        each(1, images, one)
        use(images - 1, self.get(images - 1))


class Exchange:
    def __init__(self, place, block, src, dst, refs):
        self.place, self.block, self.src, self.dst = place, block, src, dst
        self.send, self.recv, self.local = refs

    @staticmethod
    def scratch(experts):
        return [DMA((experts,)), DMA((experts,)), DMA]

    def rows(self, step):
        return pl.ds(pl.multiple_of(step * self.block, self.block), self.block)

    def own(self):
        rows = pl.ds(0, self.block)
        return pltpu.make_async_copy(self.src.at[rows], self.dst.at[rows], self.local)

    def copy(self, step):
        rows = self.rows(step)
        return self.place.to_expert(
            self.place.ahead(step), self.src.at[rows], self.dst.at[rows],
            self.send.at[step], self.recv.at[step],
        )

    def start_all(self):
        self.own().start()
        each(1, self.place.experts, lambda step: self.copy(step).start())

    def wait(self, low, high):
        if low == 0:
            self.own().wait()
        each(max(1, low), high, lambda step: self.copy(step).wait())


class Return:
    def __init__(self, place, block, slots, src, dst, refs):
        self.place, self.block, self.slots, self.src, self.dst = place, block, slots, src, dst
        self.send, self.recv, self.local = refs

    @staticmethod
    def scratch(experts):
        return [DMA((4, experts)), DMA((4, experts)), DMA]

    def rows(self, quarter, step):
        return pl.ds(
            pl.multiple_of(quarter * self.slots + step * self.block, self.block), self.block
        )

    def own(self):
        return pltpu.make_async_copy(
            self.src.at[pl.ds(0, self.block)],
            self.dst.at[self.rows(self.place.tensor, 0)], self.local,
        )

    def home(self, step):
        rows = pl.ds(pl.multiple_of(step * self.block, self.block), self.block)
        return self.place.to_expert(
            self.place.behind(step), self.src.at[rows],
            self.dst.at[self.rows(self.place.tensor, step)],
            self.send.at[0, step], self.recv.at[0, step],
        )

    def to_chip(self, step):
        block = self.dst.at[self.rows(self.place.tensor, step)]
        return self.place.to_chip(block, block, self.send.at[1, step], self.recv.at[1, step])

    def to_core(self, step):
        block = self.dst.at[self.rows(self.place.tensor, step)]
        return self.place.to_core(block, block, self.send.at[2, step], self.recv.at[2, step])

    def on_to_core(self, step):
        block = self.dst.at[self.rows(self.place.chip_peer, step)]
        return self.place.to_core(block, block, self.send.at[3, step], self.recv.at[3, step])

    def start(self, low, high):
        if low == 0:
            self.own().start()
        each(max(1, low), high, lambda step: self.home(step).start())

    def pass_on(self):
        self.own().wait()
        self.to_chip(0).start()
        self.to_core(0).start()

        def one(step):
            self.home(step).wait()
            self.to_chip(step).start()
            self.to_core(step).start()
            self.to_chip(step - 1).wait()
            self.on_to_core(step - 1).start()

        each(1, self.place.experts, one)
        last = self.place.experts - 1
        self.to_chip(last).wait()
        self.on_to_core(last).start()

    def finish(self):
        def one(step):
            self.to_core(step).wait()
            self.on_to_core(step).wait()

        each(0, self.place.experts, one)


class WeightGather:
    def __init__(self, place, shards, wholes, refs):
        self.place, self.shards, self.wholes = place, shards, wholes
        self.send, self.recv, self.local = refs

    @staticmethod
    def scratch():
        return [DMA((2, 3)), DMA((2, 3)), DMA((2,))]

    def own(self, which):
        return pltpu.make_async_copy(
            self.shards[which], self.wholes[which].at[self.place.tensor], self.local.at[which]
        )

    def to_chip(self, which):
        return self.place.to_chip(
            self.shards[which], self.wholes[which].at[self.place.tensor],
            self.send.at[which, 0], self.recv.at[which, 0],
        )

    def to_core(self, which):
        return self.place.to_core(
            self.shards[which], self.wholes[which].at[self.place.tensor],
            self.send.at[which, 1], self.recv.at[which, 1],
        )

    def on_to_core(self, which):
        part = self.wholes[which].at[self.place.chip_peer]
        return self.place.to_core(
            part, part, self.send.at[which, 2], self.recv.at[which, 2]
        )

    def start(self):
        for which in range(2):
            self.own(which).start()
            self.to_chip(which).start()
            self.to_core(which).start()

    def pass_on(self):
        for which in range(2):
            self.to_chip(which).wait()
            self.on_to_core(which).start()

    def finish(self):
        for which in range(2):
            self.own(which).wait()
            self.to_core(which).wait()
            self.on_to_core(which).wait()


class ExpertSum:
    def __init__(self, place, chunk, src, total, refs):
        self.place, self.chunk, self.src, self.total = place, chunk, src, total
        self.inbox, self.send, self.recv = refs

    @staticmethod
    def scratch(plan):
        return [
            VMEM((plan.packed, 128), BF16),
            DMA((2, plan.experts)), DMA((2, plan.experts)),
        ]

    def rows(self, index):
        return pl.ds(pl.multiple_of(index * self.chunk, self.chunk), self.chunk)

    def scatter(self, step):
        peer = self.place.ahead(step)
        return self.place.to_expert(
            peer, self.src.at[self.rows(peer)], self.inbox.at[self.rows(step)],
            self.send.at[0, step], self.recv.at[0, step],
        )

    def share(self, step):
        mine = self.total.at[self.rows(self.place.expert)]
        return self.place.to_expert(
            self.place.ahead(step), mine, mine, self.send.at[1, step], self.recv.at[1, step]
        )

    def start(self):
        each(1, self.place.experts, lambda step: self.scatter(step).start())

    def add(self):
        each(1, self.place.experts, lambda step: self.scatter(step).wait())
        mine = self.rows(self.place.expert)

        def one(step, total):
            return total + self.inbox[self.rows(step), :].astype(F32)

        total = lax.fori_loop(1, self.place.experts, one, self.src[mine, :].astype(F32))
        self.total[mine, :] = total.astype(BF16)
        each(1, self.place.experts, lambda step: self.share(step).start())

    def finish(self):
        each(1, self.place.experts, lambda step: self.share(step).wait())


class PairSum:
    @staticmethod
    def scratch_near():
        return [VMEM((2, 2, 512, 512), BF16), DMA((2, 2)), DMA((2, 2))]

    @staticmethod
    def scratch_far():
        return [VMEM((2, 512, 512), BF16), DMA((2,)), DMA((2,))]

    @staticmethod
    def near(place, part, refs, which, chip):
        inbox, send, recv = refs
        quarter = 2 * chip + 1 - place.core
        return place.to_core(
            part.at[which, quarter], inbox.at[which, chip],
            send.at[which, chip], recv.at[which, chip],
        )

    @staticmethod
    def far(place, out, refs, which):
        inbox, send, recv = refs
        return place.to_chip(out, inbox.at[which], send.at[which], recv.at[which])


def route_places(plan, place, r):
    shape = (plan.experts, plan.lanes)
    expert_id = lax.broadcasted_iota(jnp.int32, shape, 0)
    lane = lax.broadcasted_iota(jnp.int32, shape, 1)
    first, second = r.route[0:1, :], r.route[1:2, :]
    is_first, is_second = expert_id == first, expert_id == second
    named = is_first | is_second
    count = jnp.where(named, 1.0, 0.0)
    running = count
    step = 1
    while step < plan.lanes:
        running = running + jnp.where(lane >= step, pltpu.roll(running, step, 1), 0.0)
        step *= 2
    before = running - count
    mine = before - (place.tensor * plan.per_rank).astype(F32)
    valid = named & (mine >= 0.0) & (mine < float(plan.per_rank))
    r.place[...] = jnp.where(valid, mine, -1.0)
    quarter = jnp.zeros(shape, F32)
    for bound in range(1, 4):
        quarter = quarter + jnp.where(before >= float(bound * plan.per_rank), 1.0, 0.0)
    step_of = expert_id - place.expert
    step_of = jnp.where(step_of < 0, step_of + plan.experts, step_of).astype(F32)
    code = (
        quarter * float(plan.slots - plan.per_rank) + step_of * float(plan.block) + before
    )
    kept = before < float(plan.capacity)
    nowhere = -1.0
    code_first = jnp.max(jnp.where(is_first & kept, code, nowhere), 0, keepdims=True)
    code_second = jnp.max(jnp.where(is_second & kept, code, nowhere), 0, keepdims=True)
    table = jnp.concatenate(
        [code_first, code_second, first.astype(F32), second.astype(F32),
         jnp.zeros((4, plan.lanes), F32)], axis=0,
    )
    r.codes[...] = table.T


def build_members(plan, place, r):
    slot = lax.broadcasted_iota(jnp.int32, (plan.block, plan.lanes), 0).astype(F32)

    def one(step):
        rows = pl.ds(pl.multiple_of(step * plan.block, plan.block), plan.block)
        hit = r.place[pl.ds(place.ahead(step), 1), :] == slot
        r.member[rows, :] = jnp.where(hit, 1.0, 0.0).astype(BF16)

    each(0, plan.experts, one)


def picks_part(plan, r, image, quarter):
    slot = (
        lax.broadcasted_iota(jnp.int32, (PAD, plan.slots), 1) + quarter * plan.slots
    ).astype(F32)
    rows = image_rows(image)
    hit = (r.codes[rows, 0:1] == slot) | (r.codes[rows, 1:2] == slot)
    return jnp.where(hit, 1.0, 0.0).astype(BF16)


def build_picks(plan, r):
    if not plan.stored:
        return
    for quarter in range(4):

        def one(image):
            r.picks[image_rows(image), quarter * plan.slots : (quarter + 1) * plan.slots] = (
                picks_part(plan, r, image, quarter)
            )

        each(0, plan.images, one)


def picks_of(plan, r, image):
    if plan.stored:
        return r.picks[image_rows(image), :]
    return jnp.concatenate([picks_part(plan, r, image, quarter) for quarter in range(4)], axis=1)


def picks_scratch(plan):
    return VMEM((plan.rows, 4 * plan.slots) if plan.stored else (16, 128), BF16)


def diagonal(plan):
    shape = (plan.block, 128)
    return lax.broadcasted_iota(jnp.int32, shape, 0) == lax.broadcasted_iota(jnp.int32, shape, 1)


def tail_rows(plan, base):
    return pl.ds(pl.multiple_of(base + plan.block - 16, 16), 16)


def write_spare(plan, ref, base, column):
    row = jnp.sum(jnp.where(diagonal(plan), column, 0.0), 0, keepdims=True)
    high = row.astype(BF16).astype(F32)
    rest = jnp.zeros((1, 512 - 128), F32)
    high_row = jnp.concatenate([high, rest], axis=1)
    low_row = jnp.concatenate([row - high, rest], axis=1)
    rows = tail_rows(plan, base)
    index = lax.broadcasted_iota(jnp.int32, (16, 512), 0)
    old = ref[rows, :].astype(F32)
    ref[rows, :] = jnp.where(index == 14, high_row, jnp.where(index == 15, low_row, old)).astype(
        BF16
    )


def read_spare(plan, ref, base):
    index = lax.broadcasted_iota(jnp.int32, (16, 128), 0)
    tail = ref[tail_rows(plan, base), 0:128].astype(F32)
    row = jnp.sum(jnp.where(index >= 14, tail, 0.0), 0, keepdims=True)
    return jnp.sum(jnp.where(diagonal(plan), row, 0.0), 1, keepdims=True)


def joint_weights(r):
    return jnp.concatenate([r.wqkv[0], r.wqkv[1], r.wqkv[2]], axis=1)


def attend_forward(r, total, image, joint):
    first_head = lax.broadcasted_iota(jnp.int32, (PAD, 2 * HEAD_DIM), 1) < HEAD_DIM
    key_real = lax.broadcasted_iota(jnp.int32, (2 * PAD, PAD), 1) < SEQ
    nothing = jnp.zeros((PAD, 2 * HEAD_DIM), BF16)
    rows = image_rows(image)
    normed, _ = norm_parts(r.x[rows, :])
    hidden = (normed * r.gain[0:1, :] + r.bias[0:1, :]).astype(BF16)
    r.h[rows, :] = hidden
    proj = dot(hidden, joint).astype(BF16)
    r.qkv[rows, :] = proj
    query, keyed, valued = proj[:, :128], proj[:, 128:256], proj[:, 256:]
    both = jnp.concatenate(
        [jnp.where(first_head, query, nothing), jnp.where(first_head, nothing, query)], axis=0
    )
    scores = jnp.where(key_real, dot_nt(both, keyed) * SCALE, -1e30)
    expd = jnp.exp(scores - jnp.max(scores, -1, keepdims=True))
    prob = (expd / jnp.sum(expd, -1, keepdims=True)).astype(BF16)
    r.prob[image] = prob
    out = dot(prob, valued)
    mixed = jnp.where(first_head, out[:PAD], out[PAD:]).astype(BF16)
    r.mixed[rows, :] = mixed
    total.put(image, dot(mixed, r.wout[...]))


def attend_backward(r, total, image, joint, grad):
    first_head = lax.broadcasted_iota(jnp.int32, (PAD, 2 * HEAD_DIM), 1) < HEAD_DIM
    nothing = jnp.zeros((PAD, 2 * HEAD_DIM), BF16)

    def split(value):
        return jnp.concatenate(
            [jnp.where(first_head, value, nothing), jnp.where(first_head, nothing, value)], axis=0
        )

    rows = image_rows(image)
    out_low = grad.astype(BF16)
    proj = r.qkv[rows, :]
    query, keyed, valued = proj[:, :128], proj[:, 128:256], proj[:, 256:]
    mixed_grad = split(dot_nt(out_low, r.wout[...]).astype(BF16))
    prob_low = r.prob[image]
    prob = prob_low.astype(F32)
    prob_grad = dot_nt(mixed_grad, valued)
    score_grad = (
        prob * (prob_grad - jnp.sum(prob_grad * prob, -1, keepdims=True))
    ).astype(BF16)
    query_both = dot(score_grad, keyed)
    query_grad = jnp.where(first_head, query_both[:PAD], query_both[PAD:]) * SCALE
    key_grad = dot_tn(score_grad, split(query)) * SCALE
    value_grad = dot_tn(prob_low, mixed_grad)
    proj_grad = jnp.concatenate([query_grad, key_grad, value_grad], axis=1).astype(BF16)
    r.dproj[rows, :] = proj_grad
    total.put(image, dot_nt(proj_grad, joint))


def pack_gradients(plan, r):
    hidden, out_low = r.h[...], r.gin[...].astype(BF16)
    for part in range(3):
        r.packed[part * 512 : (part + 1) * 512, :] = dot_tn(
            hidden, r.dproj[:, part * 128 : (part + 1) * 128]
        ).astype(BF16)
    r.packed[3 * 512 : 4 * 512, :] = dot_tn(out_low, r.mixed[...]).astype(BF16)


def pack_small(plan, r, vectors):
    router = dot_tn(r.dz[...], r.h2[: plan.rows, :])[: plan.experts]
    rows = jnp.concatenate([vectors, router], axis=0)
    rows = jnp.concatenate([rows[:, part * 128 : (part + 1) * 128] for part in range(4)], axis=0)
    spare = plan.packed - 2048 - rows.shape[0]
    r.packed[2048:, :] = jnp.concatenate([rows, jnp.zeros((spare, 128), F32)], axis=0).astype(BF16)


def second_norm(plan, r, total):
    def use(image, value):
        rows = image_rows(image)
        after = r.x[rows, :] + value
        r.y[rows, :] = after
        normed, _ = norm_parts(after)
        r.h2[rows, :] = (normed * r.gain[1:2, :] + r.bias[1:2, :]).astype(BF16)

    if plan.lanes > plan.rows:
        r.h2[plan.rows :, :] = jnp.zeros((plan.lanes - plan.rows, 512), BF16)
    total.finish(plan.images, use)
    logits = dot_nt(r.router[: plan.experts, :], r.h2[...])
    expert_id = lax.broadcasted_iota(jnp.int32, (plan.experts, plan.lanes), 0)
    is_first, is_second = expert_id == r.route[0:1, :], expert_id == r.route[1:2, :]
    named = is_first | is_second
    shifted = jnp.where(named, logits, -1e30)
    top = jnp.max(shifted, 0, keepdims=True)
    expd = jnp.where(named, jnp.exp(shifted - top), 0.0)
    share = expd / jnp.maximum(jnp.sum(expd, 0, keepdims=True), 1e-30)
    r.gate[...] = share
    gate_first = jnp.sum(jnp.where(is_first, share, 0.0), 0, keepdims=True)
    gate_second = jnp.sum(jnp.where(is_second, share, 0.0), 0, keepdims=True)
    r.gates[...] = jnp.concatenate(
        [gate_first, gate_second, jnp.zeros((6, plan.lanes), F32)], axis=0
    ).T


def send_slots(plan, place, r, move):
    r.send[...] = dot(r.member[...], r.h2[...]).astype(BF16)
    slot = lax.broadcasted_iota(jnp.int32, (plan.block, plan.lanes), 0).astype(F32)

    def one(step):
        expert = place.ahead(step)
        hit = r.place[pl.ds(expert, 1), :] == slot
        column = jnp.sum(jnp.where(hit, r.gate[pl.ds(expert, 1), :], 0.0), 1, keepdims=True)
        write_spare(plan, r.send, step * plan.block, column)

    each(0, plan.experts, one)
    move.start_all()


def read_gates(plan, r, low, high):
    def one(step):
        base = step * plan.block
        rows = pl.ds(pl.multiple_of(base, plan.block), plan.block)
        r.slot_gate[rows, :] = read_spare(plan, r.recv, base)

    each(low, high, one)


def groups(plan):
    return [(low, low + plan.group) for low in range(0, plan.experts, plan.group)]


def return_gradient(plan, r, low, high, value, column):
    r.gret[low * plan.block : high * plan.block, :] = value.astype(BF16)
    r.column[low * plan.block : high * plan.block, :] = column

    def one(step):
        base = step * plan.block
        rows = pl.ds(pl.multiple_of(base, plan.block), plan.block)
        write_spare(plan, r.gret, base, r.column[rows, :])

    each(low, high, one)


def expert_grads(plan, place, r, near):
    drecv, recv = r.dr[...], r.recv[...]
    for part in range(4):
        r.gpart[0, part] = dot_tn(recv, r.dpre[part]).astype(BF16)
        r.gpart[1, part] = dot_tn(r.act[part], drecv).astype(BF16)
    for which in range(2):
        for chip in range(2):
            PairSum.near(place, r.gpart, near, which, chip).start()


def near_sums(place, r, near):
    chip = place.tensor // 2
    inbox = near[0]
    for which in range(2):
        for side in range(2):
            PairSum.near(place, r.gpart, near, which, side).wait()
        for quarter, side in ((place.chip_peer, 1 - chip), (place.tensor, chip)):
            r.gpart[which, quarter] = (
                r.gpart[which, quarter].astype(F32) + inbox[which, side].astype(F32)
            ).astype(BF16)


def near_outs(place, r):
    return [
        pltpu.make_async_copy(r.gpart.at[which, quarter], out.at[which], r.out_sems.at[which, side])
        for which in range(2)
        for side, (quarter, out) in enumerate(((place.chip_peer, r.gfar), (place.tensor, r.gown)))
    ]


def back_through(plan, place, r, total, joint):
    experts = plan.experts

    def spread(index):
        base = index * plan.block
        rows = pl.ds(pl.multiple_of(base, plan.block), plan.block)
        expert = place.ahead(lax.rem(index, experts))
        lane = lax.broadcasted_iota(jnp.int32, (plan.block, 128), 1)
        r.gdg[rows, :] = jnp.where(lane == expert, read_spare(plan, r.gback, base), 0.0).astype(BF16)

    each(0, 4 * experts, spread)
    r.vec[...] = jnp.zeros_like(r.vec)

    def one(image):
        rows = image_rows(image)
        picks = picks_of(plan, r, image)
        lane = lax.broadcasted_iota(jnp.int32, (PAD, 128), 1).astype(F32)
        share = jnp.where(
            lane == r.codes[rows, 2:3], r.gates[rows, 0:1],
            jnp.where(lane == r.codes[rows, 3:4], r.gates[rows, 1:2], 0.0),
        )
        gated = dot(picks, r.gdg[...])
        logit_grad = (gated - share * jnp.sum(gated, -1, keepdims=True)).astype(BF16)
        r.dz[rows, :] = logit_grad
        value = dot(picks, r.gback[...]) + dot(logit_grad, r.router[...])
        normed, scaled = norm_parts(r.y[rows, :])
        grad = r.g[rows, :].astype(F32) + norm_pull(value, normed, scaled, r.gain[1:2, :])
        r.gin[rows, :] = grad
        r.vec[1:2, :] += jnp.sum(value * normed, 0, keepdims=True)
        r.vec[3:4, :] += jnp.sum(value, 0, keepdims=True)
        attend_backward(r, total, image, joint, grad)

    def next_one(image):
        one(image)
        total.step_near(image - 1)

    one(0)
    each(1, plan.images, next_one)
    total.step_near(plan.images - 1)


def first_norm_back(plan, r, total):
    def use(image, value):
        rows = image_rows(image)
        normed, scaled = norm_parts(r.x[rows, :])
        r.gin[rows, :] += norm_pull(value, normed, scaled, r.gain[0:1, :])
        r.vec[0:1, :] += jnp.sum(value * normed, 0, keepdims=True)
        r.vec[2:3, :] += jnp.sum(value, 0, keepdims=True)

    total.finish(plan.images, use)


def run_kernel(name, body, inputs, outputs, scratch, collective_id, vmem, in_hbm=()):
    flat, layout = [], []
    for key, value in scratch.items():
        group = value if isinstance(value, list) else [value]
        layout.append((key, len(group), isinstance(value, list)))
        flat.extend(group)
    plain = list(inputs) + list(outputs)

    def kernel(*refs):
        named = dict(zip(plain, refs))
        at = len(plain)
        for key, size, grouped in layout:
            named[key] = refs[at : at + size] if grouped else refs[at]
            at += size
        body(types.SimpleNamespace(**named))

    results = pl.pallas_call(
        kernel,
        name=name,
        in_specs=[
            pl.BlockSpec(memory_space=pl.ANY if key in in_hbm else VMEM) for key in inputs
        ],
        out_specs=tuple(
            pl.BlockSpec(memory_space=pl.ANY if key in in_hbm else VMEM) for key in outputs
        ),
        out_shape=tuple(jax.ShapeDtypeStruct(*value) for value in outputs.values()),
        scratch_shapes=flat,
        compiler_params=pltpu.CompilerParams(
            collective_id=collective_id, has_side_effects=True, vmem_limit_bytes=vmem * MIB
        ),
    )(*inputs.values())
    return types.SimpleNamespace(**dict(zip(outputs, results)))


def forward_shapes(plan):
    rows, lanes, slots = plan.rows, plan.lanes, plan.slots
    return {
        "y": ((rows, 512), F32),
        "h": ((rows, 512), BF16),
        "qkv": ((rows, 384), BF16),
        "prob": ((plan.images, 2 * PAD, PAD), BF16),
        "mixed": ((rows, 128), BF16),
        "h2": ((lanes, 512), BF16),
        "place": ((plan.experts, lanes), F32),
        "codes": ((lanes, 8), F32),
        "gates": ((lanes, 8), F32),
        "recv": ((slots, 512), BF16),
        "ret": ((slots, 512), BF16),
        "slot_gate": ((slots, 1), F32),
        "up": ((4, 512, 512), BF16),
        "down": ((4, 512, 512), BF16),
    }


def as_scratch(shapes):
    return {key: VMEM(*value) for key, value in shapes.items()}


def first_forward(plan, inputs):
    def body(r):
        place = Place(plan.experts)
        place.greet()
        total = TensorSum(place, r.total)
        weights = WeightGather(place, (r.up_own, r.down_own), (r.up, r.down), r.weights)
        move = Exchange(place, plan.block, r.send, r.recv, r.move)
        back = Return(place, plan.block, plan.slots, r.ret, r.back, r.back_sems)
        joint = joint_weights(r)
        route_places(plan, place, r)
        build_members(plan, place, r)
        place.met()
        attend_forward(r, total, 0, joint)
        weights.start()

        def next_one(image):
            attend_forward(r, total, image, joint)
            total.step_near(image - 1)

        each(1, plan.images, next_one)
        total.step_near(plan.images - 1)
        second_norm(plan, r, total)
        send_slots(plan, place, r, move)
        build_picks(plan, r)
        weights.pass_on()
        weights.finish()
        for low, high in groups(plan):
            move.wait(low, high)
            read_gates(plan, r, low, high)
            rows = slice(low * plan.block, high * plan.block)
            rows_in = r.recv[rows, :]
            result = jnp.zeros((rows.stop - rows.start, 512), F32)
            for part in range(4):
                act = gelu(dot(rows_in, r.up[part])).astype(BF16)
                result = result + dot(act, r.down[part])
            r.ret[rows, :] = (result * r.slot_gate[rows, :]).astype(BF16)
            back.start(low, high)
        back.pass_on()
        back.finish()

        def combine(image):
            rows = image_rows(image)
            r.next[rows, :] = r.y[rows, :] + dot(picks_of(plan, r, image), r.back[...])

        each(0, plan.images, combine)

    outputs = dict(forward_shapes(plan), next=((plan.rows, 512), F32))
    scratch = {
        "member": VMEM((plan.slots, plan.lanes), BF16),
        "gate": VMEM((plan.experts, plan.lanes), F32),
        "picks": picks_scratch(plan),
        "send": VMEM((plan.slots, 512), BF16),
        "back": VMEM((4 * plan.slots, 512), BF16),
        "total": TensorSum.scratch(plan.images),
        "weights": WeightGather.scratch(),
        "move": Exchange.scratch(plan.experts),
        "back_sems": Return.scratch(plan.experts),
    }
    return run_kernel(
        "first_forward", body, inputs, outputs, scratch, 0, 60, ("up_own", "down_own")
    )


def second_whole(plan, inputs):
    def body(r):
        place = Place(plan.experts)
        place.greet()
        r.gret, r.ret, r.dr = r.send, r.gsend, r.grecv
        total = TensorSum(place, r.total)
        total_back = TensorSum(place, r.total)
        weights = WeightGather(place, (r.up_own, r.down_own), (r.up, r.down), r.weights)
        move = Exchange(place, plan.block, r.send, r.recv, r.move)
        gmove = Exchange(place, plan.block, r.gsend, r.grecv, r.gmove)
        back = Return(place, plan.block, plan.slots, r.ret, r.back, r.back_sems)
        gback = Return(place, plan.block, plan.slots, r.gret, r.gback, r.gback_sems)
        joint = joint_weights(r)
        place.met()
        attend_forward(r, total, 0, joint)
        weights.start()

        def next_one(image):
            attend_forward(r, total, image, joint)
            total.step_near(image - 1)

        each(1, plan.images, next_one)
        total.step_near(plan.images - 1)
        route_places(plan, place, r)
        build_members(plan, place, r)
        r.gsend[...] = dot(r.member[:, : plan.rows], r.g[...]).astype(BF16)
        gmove.start_all()
        second_norm(plan, r, total)
        send_slots(plan, place, r, move)
        build_picks(plan, r)
        weights.pass_on()
        weights.finish()
        gmove.wait(0, plan.experts)
        for low, high in groups(plan):
            move.wait(low, high)
            read_gates(plan, r, low, high)
            rows = slice(low * plan.block, high * plan.block)
            rows_in = r.recv[rows, :]
            gate = r.slot_gate[rows, :]
            raw = r.grecv[rows, :].astype(F32)
            scaled = (raw * gate).astype(BF16)
            r.dr[rows, :] = scaled
            result = jnp.zeros((rows.stop - rows.start, 512), F32)
            slots_grad = jnp.zeros((rows.stop - rows.start, 512), F32)
            for part in range(4):
                act, slope = gelu_both(dot(rows_in, r.up[part]))
                act = act.astype(BF16)
                r.act[part, rows, :] = act
                result = result + dot(act, r.down[part])
                pre_grad = (dot_nt(scaled, r.down[part]) * slope).astype(BF16)
                r.dpre[part, rows, :] = pre_grad
                slots_grad = slots_grad + dot_nt(pre_grad, r.up[part])
            result = result * gate
            r.ret[rows, :] = result.astype(BF16)
            column = jnp.sum(result * raw, -1, keepdims=True)
            return_gradient(plan, r, low, high, slots_grad, column)
            gback.start(low, high)
        back.start(0, plan.experts)
        expert_grads(plan, place, r, r.near)
        gback.pass_on()
        near_sums(place, r, r.near)
        outs = near_outs(place, r)
        for copy in outs:
            copy.start()
        gback.finish()
        back_through(plan, place, r, total_back, joint)
        back.pass_on()
        pack_gradients(plan, r)
        first_norm_back(plan, r, total_back)
        pack_small(plan, r, r.vec[0:4, :])
        back.finish()

        def combine(image):
            rows = image_rows(image)
            r.result[rows, :] = (
                r.y[rows, :] + dot(picks_of(plan, r, image), r.back[...])
            ).astype(BF16)

        each(0, plan.images, combine)
        for copy in outs:
            copy.wait()

    outputs = {
        "result": ((plan.rows, 512), BF16),
        "gin": ((plan.rows, 512), F32),
        "packed": ((plan.packed, 128), BF16),
        "gfar": ((2, 512, 512), BF16),
        "gown": ((2, 512, 512), BF16),
    }
    scratch = dict(
        as_scratch({k: v for k, v in forward_shapes(plan).items() if k != "ret"}),
        member=VMEM((plan.slots, plan.lanes), BF16),
        gate=VMEM((plan.experts, plan.lanes), F32),
        picks=picks_scratch(plan),
        send=VMEM((plan.slots, 512), BF16),
        back=VMEM((4 * plan.slots, 512), BF16),
        total=TensorSum.scratch(plan.images),
        weights=WeightGather.scratch(),
        move=Exchange.scratch(plan.experts),
        back_sems=Return.scratch(plan.experts),
        gmove=Exchange.scratch(plan.experts),
        gback_sems=Return.scratch(plan.experts),
        gsend=VMEM((plan.slots, 512), BF16),
        grecv=VMEM((plan.slots, 512), BF16),
        out_sems=DMA((2, 2)),
        **backward_scratch(plan),
    )
    return run_kernel(
        "second_whole", body, inputs, outputs, scratch, 1, 63, ("up_own", "down_own", "gfar", "gown")
    )


def backward_scratch(plan):
    return {
        "gback": VMEM((4 * plan.slots, 512), BF16),
        "act": VMEM((4, plan.slots, 512), BF16),
        "dpre": VMEM((4, plan.slots, 512), BF16),
        "gpart": VMEM((2, 4, 512, 512), BF16),
        "gdg": VMEM((4 * plan.slots, 128), BF16),
        "column": VMEM((plan.slots, 1), F32),
        "dz": VMEM((plan.rows, 128), BF16),
        "dproj": VMEM((plan.rows, 384), BF16),
        "vec": VMEM((8, 512), F32),
        "near": PairSum.scratch_near(),
    }


def first_backward(plan, inputs):
    def body(r):
        place = Place(plan.experts)
        place.greet()
        r.gret, r.dr = r.gsend, r.grecv
        total = TensorSum(place, r.total)
        gmove = Exchange(place, plan.block, r.gsend, r.grecv, r.gmove)
        gback = Return(place, plan.block, plan.slots, r.gret, r.gback, r.gback_sems)
        later = ExpertSum(place, plan.chunk, r.packed_later, r.sum_later, r.later_sum)
        sooner = ExpertSum(place, plan.chunk, r.packed, r.sum_first, r.sooner_sum)
        joint = joint_weights(r)
        build_members(plan, place, r)
        r.gsend[...] = dot(r.member[:, : plan.rows], r.g[...].astype(BF16)).astype(BF16)
        place.met()
        gmove.start_all()
        for which in range(2):
            PairSum.far(place, r.gfar_later.at[which], r.far_later, which).start()
        own_copy = pltpu.make_async_copy(r.gown_later, r.glater, r.own_sem)
        own_copy.start()
        for low, high in groups(plan):
            rows = slice(low * plan.block, high * plan.block)
            for part in range(4):
                act, slope = gelu_both(dot(r.recv[rows, :], r.up[part]))
                r.act[part, rows, :] = act.astype(BF16)
                r.dpre[part, rows, :] = slope.astype(BF16)
        build_picks(plan, r)
        for low, high in groups(plan):
            gmove.wait(low, high)
            rows = slice(low * plan.block, high * plan.block)
            raw = r.grecv[rows, :].astype(F32)
            scaled = (raw * r.slot_gate[rows, :]).astype(BF16)
            r.dr[rows, :] = scaled
            slots_grad = jnp.zeros((rows.stop - rows.start, 512), F32)
            for part in range(4):
                pre_grad = (
                    dot_nt(scaled, r.down[part]) * r.dpre[part, rows, :].astype(F32)
                ).astype(BF16)
                r.dpre[part, rows, :] = pre_grad
                slots_grad = slots_grad + dot_nt(pre_grad, r.up[part])
            column = jnp.sum(r.ret[rows, :].astype(F32) * raw, -1, keepdims=True)
            return_gradient(plan, r, low, high, slots_grad, column)
            gback.start(low, high)
        expert_grads(plan, place, r, r.near)
        gback.pass_on()
        own_copy.wait()
        for which in range(2):
            PairSum.far(place, r.gfar_later.at[which], r.far_later, which).wait()
            r.glater[which] = (
                r.glater[which].astype(F32) + r.far_later[0][which].astype(F32)
            ).astype(BF16)
        near_sums(place, r, r.near)
        for which in range(2):
            PairSum.far(place, r.gpart.at[which, place.chip_peer], r.far, which).start()
        gback.finish()
        later.start()
        back_through(plan, place, r, total, joint)
        later.add()
        pack_gradients(plan, r)
        first_norm_back(plan, r, total)
        pack_small(plan, r, r.vec[0:4, :])
        sooner.start()
        later.finish()
        for which in range(2):
            PairSum.far(place, r.gpart.at[which, place.chip_peer], r.far, which).wait()
            r.gfirst[which] = (
                r.gpart[which, place.tensor].astype(F32) + r.far[0][which].astype(F32)
            ).astype(BF16)
        sooner.add()
        sooner.finish()

    outputs = {
        "gin": ((plan.rows, 512), F32),
        "gfirst": ((2, 512, 512), BF16),
        "glater": ((2, 512, 512), BF16),
        "sum_first": ((plan.packed, 128), BF16),
        "sum_later": ((plan.packed, 128), BF16),
    }
    scratch = dict(
        member=VMEM((plan.slots, plan.lanes), BF16),
        picks=picks_scratch(plan),
        total=TensorSum.scratch(plan.images),
        gmove=Exchange.scratch(plan.experts),
        gback_sems=Return.scratch(plan.experts),
        gsend=VMEM((plan.slots, 512), BF16),
        grecv=VMEM((plan.slots, 512), BF16),
        packed=VMEM((plan.packed, 128), BF16),
        own_sem=DMA,
        far=PairSum.scratch_far(),
        far_later=PairSum.scratch_far(),
        later_sum=ExpertSum.scratch(plan),
        sooner_sum=ExpertSum.scratch(plan),
        **backward_scratch(plan),
    )
    return run_kernel("first_backward", body, inputs, outputs, scratch, 2, 63, ("gfar_later", "gown_later"))


def body(tokens, routes, ln_gain, ln_bias, w_qkv, w_out, w_router, w_up, w_down, cotangent):
    tok_rows = tokens.shape[0]
    experts = w_router.shape[2]
    plan = Plan(tok_rows, experts)

    def pad_rows(value, kind):
        value = value.reshape(plan.images, SEQ, -1)
        value = jnp.pad(value, ((0, 0), (0, PAD - SEQ), (0, 0)))
        return value.reshape(plan.rows, -1).astype(kind)

    def cut_rows(value):
        return value.reshape(plan.images, PAD, -1)[:, :SEQ].reshape(tok_rows, -1)

    route_rows = routes.reshape(2, plan.images, SEQ, 2)
    route_rows = jnp.pad(
        route_rows, ((0, 0), (0, 0), (0, PAD - SEQ), (0, 0)), constant_values=-1
    ).reshape(2, plan.rows, 2)
    route_rows = jnp.pad(
        route_rows, ((0, 0), (0, plan.lanes - plan.rows), (0, 0)), constant_values=-1
    ).transpose(0, 2, 1)
    router_rows = jnp.pad(w_router.transpose(0, 2, 1), ((0, 0), (0, 128 - experts), (0, 0)))

    def layer_inputs(layer):
        return {
            "route": route_rows[layer], "gain": ln_gain[layer], "bias": ln_bias[layer],
            "wqkv": w_qkv[layer], "wout": w_out[layer], "router": router_rows[layer],
            "up_own": w_up[layer, 0], "down_own": w_down[layer, 0],
        }

    start = pad_rows(tokens, F32)
    one = first_forward(plan, dict(x=start, **layer_inputs(0)))
    two = second_whole(
        plan, dict(x=one.next, g=pad_rows(cotangent, BF16), **layer_inputs(1))
    )
    shared = {
        key: getattr(one, key)
        for key in (
            "y", "h", "qkv", "prob", "mixed", "h2", "place", "codes", "gates", "recv", "ret",
            "slot_gate", "up", "down",
        )
    }
    kept = {key: layer_inputs(0)[key] for key in ("gain", "wqkv", "wout", "router")}
    three = first_backward(
        plan,
        dict(
            g=two.gin, x=start, gfar_later=two.gfar, gown_later=two.gown,
            packed_later=two.packed, **shared, **kept,
        ),
    )
    packs = [pack.astype(F32) for pack in (three.sum_first, three.sum_later)]
    grad_qkv = jnp.stack([pack[:1536].reshape(3, 512, 128) for pack in packs])
    grad_out = jnp.stack([pack[1536:2048].T for pack in packs])
    small = [
        pack[2048 : 2048 + 4 * (4 + experts)].reshape(4, 4 + experts, 128).transpose(1, 0, 2)
        .reshape(4 + experts, 512)
        for pack in packs
    ]
    grad_gain = jnp.stack([entry[0:2] for entry in small])
    grad_bias = jnp.stack([entry[2:4] for entry in small])
    grad_router = jnp.stack([entry[4:].T for entry in small])
    experts_first, experts_later = three.gfirst, three.glater
    grad_up = jnp.stack([experts_first[0], experts_later[0]])[:, None].astype(F32)
    grad_down = jnp.stack([experts_first[1], experts_later[1]])[:, None].astype(F32)
    return (
        cut_rows(two.result),
        cut_rows(three.gin),
        grad_gain,
        grad_bias[:, 0],
        grad_bias[:, 1],
        grad_qkv,
        grad_out,
        grad_router,
        grad_up,
        grad_down,
    )


def solution(mesh):
    in_specs = (
        P("expert", None),
        P(None, "expert", None),
        P(),
        P(),
        P(None, None, None, "tensor"),
        P(None, "tensor", None),
        P(),
        P(None, "expert", None, "tensor"),
        P(None, "expert", "tensor", None),
        P("expert", None),
    )
    out_specs = (
        P("expert", None),
        P("expert", None),
        P(),
        P(),
        P(),
        P(None, None, None, "tensor"),
        P(None, "tensor", None),
        P(),
        P(None, "expert", None, "tensor"),
        P(None, "expert", "tensor", None),
    )
    return jax.shard_map(body, mesh=mesh, in_specs=in_specs, out_specs=out_specs, check_vma=False)
```

```python
import types

import jax
import jax.numpy as jnp
from jax import lax
from jax.experimental import pallas as pl
from jax.experimental.pallas import tpu as pltpu
from jax.sharding import PartitionSpec as P

HEAD_DIM = 64
SEQ = 197
PAD = 208
EPS = 1e-06
MESH = pl.DeviceIdType.MESH
F32 = jnp.float32
BF16 = jnp.bfloat16
SCALE = HEAD_DIM ** (-0.5)
MIB = 1 << 20
VMEM = pltpu.VMEM
DMA = pltpu.SemaphoreType.DMA


def up_to(count, multiple):
    return -(-count // multiple) * multiple


def dot(left, right):
    return lax.dot_general(left, right, (((1,), (0,)), ((), ())), preferred_element_type=F32)


def dot_nt(left, right):
    return lax.dot_general(left, right, (((1,), (1,)), ((), ())), preferred_element_type=F32)


def dot_tn(left, right):
    return lax.dot_general(left, right, (((0,), (0,)), ((), ())), preferred_element_type=F32)


def norm_parts(rows):
    centered = rows - jnp.mean(rows, -1, keepdims=True)
    scaled = lax.rsqrt(jnp.mean(centered * centered, -1, keepdims=True) + EPS)
    return centered * scaled, scaled


def norm_pull(grad_in, normed, scaled, gain_row):
    grad_normed = grad_in * gain_row
    inner = (
        grad_normed
        - jnp.mean(grad_normed, -1, keepdims=True)
        - normed * jnp.mean(grad_normed * normed, -1, keepdims=True)
    )
    return inner * scaled


def gelu(pre):
    inner = pre * (0.7978845608028654 + 0.035677408136300125 * (pre * pre))
    return 0.5 * pre * (1.0 + jnp.tanh(inner))


def gelu_both(pre):
    square = pre * pre
    inner = pre * (0.7978845608028654 + 0.035677408136300125 * square)
    bent = jnp.tanh(inner)
    half = 0.5 + 0.5 * bent
    slope = half + half * (1.0 - bent) * pre * (
        0.7978845608028654 + 0.10703222440890037 * square
    )
    return half * pre, slope


class Plan:
    def __init__(self, tok_rows, experts):
        self.images = tok_rows // SEQ
        self.rows = self.images * PAD
        self.lanes = up_to(self.rows, 128)
        self.experts = experts
        self.per_rank = max(1, 10 * tok_rows // (4 * experts * 4))
        self.capacity = 4 * self.per_rank
        self.block = up_to(self.per_rank + 2, 16)
        self.slots = experts * self.block
        self.group = max(
            size for size in range(1, experts)
            if experts % size == 0 and (size == 1 or size * self.block <= 320)
        )
        self.stored = 4 * self.slots <= 2560
        main = up_to(512, 16 * experts)
        small = up_to(4 * (4 + experts), 16 * experts)
        self.panels = [(start, main) for start in range(0, 2048, main)] + [(2048, small)]
        self.packed = 2048 + small


def image_rows(image):
    return pl.ds(pl.multiple_of(image * PAD, PAD), PAD)


def each(low, high, use):
    def one(index, carry):
        use(index)
        return carry

    lax.fori_loop(low, high, one, 0)


class Place:
    def __init__(self, experts):
        self.tensor = lax.axis_index("tensor")
        self.core = lax.rem(self.tensor, 2)
        self.chip = lax.div(self.tensor, 2)
        self.core_peer = self.tensor + 1 - 2 * self.core
        self.chip_peer = lax.rem(self.tensor + 2, 4)
        self.experts = experts
        self.expert = lax.axis_index("expert")

    def ahead(self, step):
        return lax.rem(self.expert + step, self.experts)

    def behind(self, step):
        return lax.rem(self.expert + self.experts - step, self.experts)

    def greet(self):
        barrier = pltpu.get_barrier_semaphore()
        for peer in (self.core_peer, self.chip_peer):
            pl.semaphore_signal(barrier, inc=1, device_id={"tensor": peer}, device_id_type=MESH)

        def one(step):
            pl.semaphore_signal(
                barrier, inc=1, device_id={"expert": self.ahead(step)}, device_id_type=MESH
            )

        each(1, self.experts, one)

    def met(self):
        pl.semaphore_wait(pltpu.get_barrier_semaphore(), 2 + self.experts - 1)

    def to_core(self, src, dst, send, recv):
        return pltpu.make_async_remote_copy(
            src_ref=src, dst_ref=dst, send_sem=send, recv_sem=recv,
            device_id={"tensor": self.core_peer}, device_id_type=MESH,
        )

    def to_chip(self, src, dst, send, recv):
        return pltpu.make_async_remote_copy(
            src_ref=src, dst_ref=dst, send_sem=send, recv_sem=recv,
            device_id={"tensor": self.chip_peer}, device_id_type=MESH,
        )

    def to_expert(self, expert, src, dst, send, recv):
        return pltpu.make_async_remote_copy(
            src_ref=src, dst_ref=dst, send_sem=send, recv_sem=recv,
            device_id={"expert": expert}, device_id_type=MESH,
        )


class CoreSum:
    def __init__(self, place, refs):
        self.place = place
        self.part, self.near, self.send, self.recv = refs

    @staticmethod
    def scratch(images):
        rows = (images * PAD, 512)
        return [VMEM(rows, BF16), VMEM(rows, BF16), DMA((images,)), DMA((images,))]

    def copy(self, image):
        rows = image_rows(image)
        return self.place.to_core(
            self.part.at[rows], self.near.at[rows], self.send.at[image], self.recv.at[image]
        )

    def put(self, image, value):
        self.part[image_rows(image), :] = value.astype(BF16)
        self.copy(image).start()

    def get(self, image):
        rows = image_rows(image)
        self.copy(image).wait()
        return self.part[rows, :].astype(F32) + self.near[rows, :].astype(F32)


class HeadSwap:
    def __init__(self, place, qkv, out, joint, out_all, refs):
        self.place, self.qkv, self.out = place, qkv, out
        self.joint, self.out_all = joint, out_all
        self.send, self.recv, self.local = refs

    @staticmethod
    def scratch():
        return [DMA((4,)), DMA((4,)), DMA((4,))]

    def ends(self, part):
        if part == 3:
            rows = pl.ds(pl.multiple_of(self.place.chip * 128, 128), 128)
            return self.out, self.out_all.at[rows]
        columns = pl.ds(part * 128, 128)
        return self.qkv.at[part], self.joint.at[self.place.chip, :, columns]

    def own(self, part):
        return pltpu.make_async_copy(*self.ends(part), self.local.at[part])

    def swap(self, part):
        return self.place.to_chip(*self.ends(part), self.send.at[part], self.recv.at[part])

    def start_own(self):
        for part in range(4):
            self.own(part).start()

    def start_swap(self):
        for part in range(4):
            self.swap(part).start()

    def wait_own(self):
        for part in range(4):
            self.own(part).wait()

    def wait_swap(self):
        for part in range(4):
            self.swap(part).wait()


class Exchange:
    def __init__(self, place, block, src, dst, refs):
        self.place, self.block, self.src, self.dst = place, block, src, dst
        self.send, self.recv, self.local = refs

    @staticmethod
    def scratch(experts):
        return [DMA((2, experts)), DMA((2, experts)), DMA((2,))]

    def part(self, step, tail):
        base = pl.multiple_of(step * self.block, self.block)
        if tail is None:
            return pl.ds(base, self.block)
        if tail:
            return pl.ds(pl.multiple_of(base + self.block - 16, 16), 16)
        return pl.ds(base, self.block - 16)

    def own(self, tail=None):
        rows = self.part(0, tail)
        return pltpu.make_async_copy(
            self.src.at[rows], self.dst.at[rows], self.local.at[int(bool(tail))]
        )

    def copy(self, step, tail=None):
        rows, which = self.part(step, tail), int(bool(tail))
        return self.place.to_expert(
            self.place.ahead(step), self.src.at[rows], self.dst.at[rows],
            self.send.at[which, step], self.recv.at[which, step],
        )

    def start_all(self, tail=None):
        self.own(tail).start()
        each(1, self.place.experts, lambda step: self.copy(step, tail).start())

    def wait(self, low, high, tail=None):
        if low == 0:
            self.own(tail).wait()
        each(max(1, low), high, lambda step: self.copy(step, tail).wait())


class Return:
    def __init__(self, place, block, slots, src, dst, refs):
        self.place, self.block, self.slots, self.src, self.dst = place, block, slots, src, dst
        self.send, self.recv, self.local = refs

    @staticmethod
    def scratch(experts):
        return [DMA((4, experts)), DMA((4, experts)), DMA]

    def rows(self, quarter, step):
        return pl.ds(
            pl.multiple_of(quarter * self.slots + step * self.block, self.block), self.block
        )

    def own(self):
        return pltpu.make_async_copy(
            self.src.at[pl.ds(0, self.block)],
            self.dst.at[self.rows(self.place.tensor, 0)], self.local,
        )

    def home(self, step):
        rows = pl.ds(pl.multiple_of(step * self.block, self.block), self.block)
        return self.place.to_expert(
            self.place.behind(step), self.src.at[rows],
            self.dst.at[self.rows(self.place.tensor, step)],
            self.send.at[0, step], self.recv.at[0, step],
        )

    def to_chip(self, step):
        block = self.dst.at[self.rows(self.place.tensor, step)]
        return self.place.to_chip(block, block, self.send.at[1, step], self.recv.at[1, step])

    def to_core(self, step):
        block = self.dst.at[self.rows(self.place.tensor, step)]
        return self.place.to_core(block, block, self.send.at[2, step], self.recv.at[2, step])

    def on_to_core(self, step):
        block = self.dst.at[self.rows(self.place.chip_peer, step)]
        return self.place.to_core(block, block, self.send.at[3, step], self.recv.at[3, step])

    def start(self, low, high):
        if low == 0:
            self.own().start()
        each(max(1, low), high, lambda step: self.home(step).start())

    def pass_on(self):
        self.own().wait()
        self.to_chip(0).start()
        self.to_core(0).start()

        def one(step):
            self.home(step).wait()
            self.to_chip(step).start()
            self.to_core(step).start()
            self.to_chip(step - 1).wait()
            self.on_to_core(step - 1).start()

        each(1, self.place.experts, one)
        last = self.place.experts - 1
        self.to_chip(last).wait()
        self.on_to_core(last).start()

    def finish(self):
        def one(step):
            self.to_core(step).wait()
            self.on_to_core(step).wait()

        each(0, self.place.experts, one)


class WeightGather:
    def __init__(self, place, shards, wholes, refs):
        self.place, self.shards, self.wholes = place, shards, wholes
        self.send, self.recv, self.local = refs

    @staticmethod
    def scratch():
        return [DMA((2, 3)), DMA((2, 3)), DMA((2,))]

    def own(self, which):
        return pltpu.make_async_copy(
            self.shards[which], self.wholes[which].at[self.place.tensor], self.local.at[which]
        )

    def to_chip(self, which):
        return self.place.to_chip(
            self.shards[which], self.wholes[which].at[self.place.tensor],
            self.send.at[which, 0], self.recv.at[which, 0],
        )

    def to_core(self, which):
        return self.place.to_core(
            self.shards[which], self.wholes[which].at[self.place.tensor],
            self.send.at[which, 1], self.recv.at[which, 1],
        )

    def on_to_core(self, which):
        part = self.wholes[which].at[self.place.chip_peer]
        return self.place.to_core(
            part, part, self.send.at[which, 2], self.recv.at[which, 2]
        )

    def start(self):
        for which in range(2):
            self.own(which).start()
            self.to_chip(which).start()
            self.to_core(which).start()

    def pass_on(self):
        for which in range(2):
            self.to_chip(which).wait()
            self.on_to_core(which).start()

    def finish(self):
        for which in range(2):
            self.own(which).wait()
            self.to_core(which).wait()
            self.on_to_core(which).wait()


class ExpertSum:
    def __init__(self, place, panels, src, total, refs):
        self.place, self.panels, self.src, self.total = place, panels, src, total
        self.inbox, self.chunks, self.send, self.recv = refs
        self.side = lax.rem(place.expert, 2)
        self.pair = place.expert + 1 - 2 * self.side
        self.group = place.experts // 2
        self.index = lax.div(place.expert, 2)

    @staticmethod
    def scratch(plan):
        panels = len(plan.panels)
        half = plan.packed // 2
        return [
            VMEM((half, 128), BF16), VMEM((half, 128), BF16),
            DMA((2, panels, max(2, plan.experts // 2))), DMA((2, panels, max(2, plan.experts // 2))),
        ]

    def half(self, panel, side):
        start, rows = self.panels[panel]
        return pl.ds(pl.multiple_of(start + side * (rows // 2), 16), rows // 2)

    def local(self, panel):
        start, rows = self.panels[panel]
        return pl.ds(start // 2, rows // 2)

    def chunk(self, panel, index):
        start, rows = self.panels[panel]
        size = rows // self.place.experts
        return pl.ds(pl.multiple_of(start // 2 + index * size, 16), size)

    def chunk_whole(self, panel, index):
        start, rows = self.panels[panel]
        size = rows // self.place.experts
        return pl.ds(pl.multiple_of(start + self.side * (rows // 2) + index * size, 16), size)

    def member(self, step):
        return lax.rem(self.place.expert + 2 * step, self.place.experts)

    def pair_in(self, panel):
        return self.place.to_expert(
            self.pair, self.src.at[self.half(panel, 1 - self.side)],
            self.inbox.at[self.local(panel)],
            self.send.at[0, panel, 0], self.recv.at[0, panel, 0],
        )

    def scatter(self, panel, step):
        peer = lax.rem(self.index + step, self.group)
        return self.place.to_expert(
            self.member(step), self.src.at[self.chunk_whole(panel, peer)],
            self.chunks.at[self.chunk(panel, step)],
            self.send.at[0, panel, step], self.recv.at[0, panel, step],
        )

    def share(self, panel, step):
        mine = self.total.at[self.chunk_whole(panel, self.index)]
        return self.place.to_expert(
            self.member(step), mine, mine,
            self.send.at[1, panel, step], self.recv.at[1, panel, step],
        )

    def pair_out(self, panel):
        half = self.total.at[self.half(panel, self.side)]
        return self.place.to_expert(
            self.pair, half, half, self.send.at[1, panel, 0], self.recv.at[1, panel, 0]
        )

    def step_pair(self, panel):
        self.pair_in(panel).start()

    def step_scatter(self, panel):
        self.pair_in(panel).wait()
        mine = self.half(panel, self.side)
        self.src[mine, :] = (
            self.src[mine, :].astype(F32) + self.inbox[self.local(panel), :].astype(F32)
        ).astype(BF16)
        each(1, self.group, lambda step: self.scatter(panel, step).start())

    def step_share(self, panel):
        mine = self.chunk_whole(panel, self.index)

        def one(step, total):
            self.scatter(panel, step).wait()
            return total + self.chunks[self.chunk(panel, step), :].astype(F32)

        total = lax.fori_loop(1, self.group, one, self.src[mine, :].astype(F32))
        self.total[mine, :] = total.astype(BF16)
        each(1, self.group, lambda step: self.share(panel, step).start())

    def step_out(self, panel):
        each(1, self.group, lambda step: self.share(panel, step).wait())
        self.pair_out(panel).start()

    def step_end(self, panel):
        self.pair_out(panel).wait()

    def every(self, step):
        for panel in range(len(self.panels)):
            step(panel)


class PairSum:
    @staticmethod
    def scratch_near():
        return [VMEM((2, 2, 512, 512), BF16), DMA((2, 2)), DMA((2, 2))]

    @staticmethod
    def scratch_far():
        return [VMEM((2, 512, 512), BF16), DMA((2,)), DMA((2,))]

    @staticmethod
    def near(place, part, refs, which, chip):
        inbox, send, recv = refs
        quarter = 2 * chip + 1 - place.core
        return place.to_core(
            part.at[which, quarter], inbox.at[which, chip],
            send.at[which, chip], recv.at[which, chip],
        )

    @staticmethod
    def far(place, out, refs, which):
        inbox, send, recv = refs
        return place.to_chip(out, inbox.at[which], send.at[which], recv.at[which])


def route_places(plan, place, r):
    shape = (plan.experts, plan.lanes)
    expert_id = lax.broadcasted_iota(jnp.int32, shape, 0)
    lane = lax.broadcasted_iota(jnp.int32, shape, 1)
    first, second = r.route[0:1, :], r.route[1:2, :]
    is_first, is_second = expert_id == first, expert_id == second
    named = is_first | is_second
    count = jnp.where(named, 1.0, 0.0)
    running = count
    step = 1
    while step < plan.lanes:
        running = running + jnp.where(lane >= step, pltpu.roll(running, step, 1), 0.0)
        step *= 2
    before = running - count
    mine = before - (place.tensor * plan.per_rank).astype(F32)
    valid = named & (mine >= 0.0) & (mine < float(plan.per_rank))
    r.place[...] = jnp.where(valid, mine, -1.0)
    quarter = jnp.zeros(shape, F32)
    for bound in range(1, 4):
        quarter = quarter + jnp.where(before >= float(bound * plan.per_rank), 1.0, 0.0)
    step_of = expert_id - place.expert
    step_of = jnp.where(step_of < 0, step_of + plan.experts, step_of).astype(F32)
    code = (
        quarter * float(plan.slots - plan.per_rank) + step_of * float(plan.block) + before
    )
    kept = before < float(plan.capacity)
    nowhere = -1.0
    code_first = jnp.max(jnp.where(is_first & kept, code, nowhere), 0, keepdims=True)
    code_second = jnp.max(jnp.where(is_second & kept, code, nowhere), 0, keepdims=True)
    r.codes[...] = jnp.concatenate(
        [code_first, code_second, first.astype(F32), second.astype(F32)], axis=0
    )


def build_members(plan, place, r):
    slot = lax.broadcasted_iota(jnp.int32, (plan.block, plan.lanes), 0).astype(F32)

    def one(step):
        rows = pl.ds(pl.multiple_of(step * plan.block, plan.block), plan.block)
        hit = r.place[pl.ds(place.ahead(step), 1), :] == slot
        r.member[rows, :] = jnp.where(hit, 1.0, 0.0).astype(BF16)

    each(0, plan.experts, one)


def picks_part(plan, r, image, quarter):
    slot = (
        lax.broadcasted_iota(jnp.int32, (PAD, plan.slots), 1) + quarter * plan.slots
    ).astype(F32)
    rows = image_rows(image)
    hit = (r.table[rows, 0:1] == slot) | (r.table[rows, 1:2] == slot)
    return jnp.where(hit, 1.0, 0.0).astype(BF16)


def build_picks(plan, r):
    if not plan.stored:
        return
    for quarter in range(4):

        def one(image):
            r.picks[image_rows(image), quarter * plan.slots : (quarter + 1) * plan.slots] = (
                picks_part(plan, r, image, quarter)
            )

        each(0, plan.images, one)


def picks_of(plan, r, image):
    if plan.stored:
        return r.picks[image_rows(image), :]
    return jnp.concatenate([picks_part(plan, r, image, quarter) for quarter in range(4)], axis=1)


def picks_scratch(plan):
    return VMEM((plan.rows, 4 * plan.slots) if plan.stored else (16, 128), BF16)


def diagonal(plan):
    shape = (plan.block, 128)
    return lax.broadcasted_iota(jnp.int32, shape, 0) == lax.broadcasted_iota(jnp.int32, shape, 1)


def tail_rows(plan, base):
    return pl.ds(pl.multiple_of(base + plan.block - 16, 16), 16)


def write_spare(plan, ref, base, column):
    row = jnp.sum(jnp.where(diagonal(plan), column, 0.0), 0, keepdims=True)
    high = row.astype(BF16).astype(F32)
    rest = jnp.zeros((1, 512 - 128), F32)
    high_row = jnp.concatenate([high, rest], axis=1)
    low_row = jnp.concatenate([row - high, rest], axis=1)
    rows = tail_rows(plan, base)
    index = lax.broadcasted_iota(jnp.int32, (16, 512), 0)
    old = ref[rows, :].astype(F32)
    ref[rows, :] = jnp.where(index == 14, high_row, jnp.where(index == 15, low_row, old)).astype(
        BF16
    )


def read_spare(plan, ref, base):
    index = lax.broadcasted_iota(jnp.int32, (16, 128), 0)
    tail = ref[tail_rows(plan, base), 0:128].astype(F32)
    row = jnp.sum(jnp.where(index >= 14, tail, 0.0), 0, keepdims=True)
    return jnp.sum(jnp.where(diagonal(plan), row, 0.0), 1, keepdims=True)


def head_split(value):
    first_head = lax.broadcasted_iota(jnp.int32, value.shape, 1) < HEAD_DIM
    nothing = jnp.zeros(value.shape, value.dtype)
    return jnp.concatenate(
        [jnp.where(first_head, value, nothing), jnp.where(first_head, nothing, value)], axis=0
    )


def head_join(value):
    rows = value.shape[0] // 2
    first_head = lax.broadcasted_iota(jnp.int32, (rows, 128), 1) < HEAD_DIM
    return jnp.where(first_head, value[:rows], value[rows:])


def first_norm(r, image):
    rows = image_rows(image)
    normed, _ = norm_parts(r.x[rows, :])
    r.h[rows, :] = (normed * r.gain[0:1, :] + r.bias[0:1, :]).astype(BF16)


def attend_forward(r, image, side):
    key_real = lax.broadcasted_iota(jnp.int32, (2 * PAD, PAD), 1) < SEQ
    rows = image_rows(image)
    proj = dot(r.h[rows, :], r.joint[side]).astype(BF16)
    r.qkv[side, rows, :] = proj
    query, keyed, valued = proj[:, :128], proj[:, 128:256], proj[:, 256:]
    scores = jnp.where(key_real, dot_nt(head_split(query * SCALE), keyed), -1e30)
    expd = jnp.exp(scores - jnp.max(scores, -1, keepdims=True))
    prob = (expd * (1.0 / jnp.sum(expd, -1, keepdims=True))).astype(BF16)
    r.prob[side, image] = prob
    r.mixed[side, rows, :] = head_join(dot(prob, valued)).astype(BF16)


def attend_out(r, total, image):
    rows = image_rows(image)
    mixed = jnp.concatenate([r.mixed[0, rows, :], r.mixed[1, rows, :]], axis=1)
    total.put(image, dot(mixed, r.out_all[...]))


def attend_backward(r, total, image):
    rows = image_rows(image)
    mixed_grads = dot_nt(r.gin[rows, :].astype(BF16), r.out_all[...])
    back = jnp.zeros((PAD, 512), F32)
    for side in range(2):
        proj = r.qkv[side, rows, :]
        query, keyed, valued = proj[:, :128], proj[:, 128:256], proj[:, 256:]
        grad = mixed_grads[:, side * 128 : (side + 1) * 128]
        mixed_grad = head_split(grad.astype(BF16))
        inner = jnp.sum(head_split(grad * r.mixed[side, rows, :].astype(F32)), -1, keepdims=True)
        prob = r.prob[side, image]
        prob_grad = dot_nt(mixed_grad, valued)
        score_grad = (prob.astype(F32) * (prob_grad - inner)).astype(BF16)
        query_grad = head_join(dot(score_grad, keyed)) * SCALE
        key_grad = dot_tn(score_grad, head_split(query * SCALE))
        value_grad = dot_tn(prob, mixed_grad)
        proj_grad = jnp.concatenate([query_grad, key_grad, value_grad], axis=1).astype(BF16)
        r.dproj[side, rows, :] = proj_grad
        back = back + dot_nt(proj_grad, r.joint[side])
    total.put(image, back)


def pack_out(plan, place, r):
    r.packed[0:512, :] = dot_tn(r.gin[...].astype(BF16), r.mixed[place.chip]).astype(BF16)


def pack_qkv(plan, place, r):
    grads = dot_tn(r.h[...], r.dproj[place.chip]).astype(BF16)
    for part in range(3):
        r.packed[(part + 1) * 512 : (part + 2) * 512, :] = grads[:, part * 128 : (part + 1) * 128]


def pack_small(plan, r):
    router = dot_tn(r.dz[...], r.h2[: plan.rows, :])[: plan.experts]
    rows = jnp.concatenate([r.vec[0:4, :], router], axis=0)
    rows = jnp.concatenate([rows[:, part * 128 : (part + 1) * 128] for part in range(4)], axis=0)
    spare = plan.packed - 2048 - rows.shape[0]
    r.packed[2048:, :] = jnp.concatenate([rows, jnp.zeros((spare, 128), F32)], axis=0).astype(BF16)


def second_norm(plan, r, total):
    def one(image):
        rows = image_rows(image)
        after = r.x[rows, :] + total.get(image)
        r.y[rows, :] = after
        normed, _ = norm_parts(after)
        r.h2[rows, :] = (normed * r.gain[1:2, :] + r.bias[1:2, :]).astype(BF16)

    if plan.lanes > plan.rows:
        r.h2[plan.rows :, :] = jnp.zeros((plan.lanes - plan.rows, 512), BF16)
    each(0, plan.images, one)


def send_slots(plan, place, r, move):
    r.send[...] = dot(r.member[...], r.h2[...]).astype(BF16)
    move.start_all(False)
    logits = dot_nt(r.router[: plan.experts, :], r.h2[...])
    expert_id = lax.broadcasted_iota(jnp.int32, (plan.experts, plan.lanes), 0)
    is_first, is_second = expert_id == r.route[0:1, :], expert_id == r.route[1:2, :]
    named = is_first | is_second
    shifted = jnp.where(named, logits, -1e30)
    top = jnp.max(shifted, 0, keepdims=True)
    expd = jnp.where(named, jnp.exp(shifted - top), 0.0)
    share = expd / jnp.maximum(jnp.sum(expd, 0, keepdims=True), 1e-30)
    r.gate[...] = share
    gate_first = jnp.sum(jnp.where(is_first, share, 0.0), 0, keepdims=True)
    gate_second = jnp.sum(jnp.where(is_second, share, 0.0), 0, keepdims=True)
    r.table[...] = jnp.concatenate(
        [r.codes[...], gate_first, gate_second, jnp.zeros((2, plan.lanes), F32)], axis=0
    ).T
    slot = lax.broadcasted_iota(jnp.int32, (plan.block, plan.lanes), 0).astype(F32)

    def one(step):
        expert = place.ahead(step)
        hit = r.place[pl.ds(expert, 1), :] == slot
        column = jnp.sum(jnp.where(hit, r.gate[pl.ds(expert, 1), :], 0.0), 1, keepdims=True)
        write_spare(plan, r.send, step * plan.block, column)

    each(0, plan.experts, one)
    move.start_all(True)


def read_gates(plan, r, low, high):
    def one(step):
        base = step * plan.block
        rows = pl.ds(pl.multiple_of(base, plan.block), plan.block)
        r.slot_gate[rows, :] = read_spare(plan, r.recv, base)

    each(low, high, one)


def groups(plan):
    return [(low, low + plan.group) for low in range(0, plan.experts, plan.group)]


def return_gradient(plan, r, low, high, value, column):
    r.gret[low * plan.block : high * plan.block, :] = value.astype(BF16)
    r.column[low * plan.block : high * plan.block, :] = column

    def one(step):
        base = step * plan.block
        rows = pl.ds(pl.multiple_of(base, plan.block), plan.block)
        write_spare(plan, r.gret, base, r.column[rows, :])

    each(low, high, one)


def expert_grads(plan, place, r, near):
    drecv, recv = r.dr[...], r.recv[...]
    for part in range(4):
        r.gpart[0, part] = dot_tn(recv, r.dpre[part]).astype(BF16)
        r.gpart[1, part] = dot_tn(r.act[part], drecv).astype(BF16)
    for which in range(2):
        for chip in range(2):
            PairSum.near(place, r.gpart, near, which, chip).start()


def near_sums(place, r, near):
    chip = place.tensor // 2
    inbox = near[0]
    for which in range(2):
        for side in range(2):
            PairSum.near(place, r.gpart, near, which, side).wait()
        for quarter, side in ((place.chip_peer, 1 - chip), (place.tensor, chip)):
            r.gpart[which, quarter] = (
                r.gpart[which, quarter].astype(F32) + inbox[which, side].astype(F32)
            ).astype(BF16)


def near_outs(place, r):
    return [
        pltpu.make_async_copy(r.gpart.at[which, quarter], out.at[which], r.out_sems.at[which, side])
        for which in range(2)
        for side, (quarter, out) in enumerate(((place.chip_peer, r.gfar), (place.tensor, r.gown)))
    ]


def combined(plan, r, rows_in, out):
    if plan.stored:
        out[...] = dot(r.picks[...], rows_in[...])
        return

    def one(image):
        out[image_rows(image), :] = dot(picks_of(plan, r, image), rows_in[...])

    each(0, plan.images, one)


def back_to_attention(plan, place, r):
    experts = plan.experts

    def spread(index):
        base = index * plan.block
        rows = pl.ds(pl.multiple_of(base, plan.block), plan.block)
        expert = place.ahead(lax.rem(index, experts))
        lane = lax.broadcasted_iota(jnp.int32, (plan.block, 128), 1)
        r.gdg[rows, :] = jnp.where(lane == expert, read_spare(plan, r.gback, base), 0.0).astype(BF16)

    each(0, 4 * experts, spread)
    combined(plan, r, r.gdg, r.gated)
    combined(plan, r, r.gback, r.gin)
    r.vec[...] = jnp.zeros_like(r.vec)

    def one(image):
        rows = image_rows(image)
        lane = lax.broadcasted_iota(jnp.int32, (PAD, 128), 1).astype(F32)
        share = jnp.where(
            lane == r.table[rows, 2:3], r.table[rows, 4:5],
            jnp.where(lane == r.table[rows, 3:4], r.table[rows, 5:6], 0.0),
        )
        gated = r.gated[rows, :]
        logit_grad = (gated - share * jnp.sum(gated, -1, keepdims=True)).astype(BF16)
        r.dz[rows, :] = logit_grad
        value = r.gin[rows, :] + dot(logit_grad, r.router[...])
        normed, scaled = norm_parts(r.y[rows, :])
        r.gin[rows, :] = r.g[rows, :].astype(F32) + norm_pull(
            value, normed, scaled, r.gain[1:2, :]
        )
        r.vec[1:2, :] += jnp.sum(value * normed, 0, keepdims=True)
        r.vec[3:4, :] += jnp.sum(value, 0, keepdims=True)

    each(0, plan.images, one)


def first_norm_back(plan, r, total, image):
    rows = image_rows(image)
    value = total.get(image)
    normed, scaled = norm_parts(r.x[rows, :])
    r.vec[0:1, :] += jnp.sum(value * normed, 0, keepdims=True)
    r.vec[2:3, :] += jnp.sum(value, 0, keepdims=True)
    return r.gin[rows, :] + norm_pull(value, normed, scaled, r.gain[0:1, :])


class Copies:
    def __init__(self, pairs, sems):
        self.copies = {
            key: pltpu.make_async_copy(src, dst, sems.at[index])
            for index, (key, (src, dst)) in enumerate(pairs.items())
        }

    def start(self, *keys):
        for key in keys:
            self.copies[key].start()

    def wait(self, *keys):
        for key in keys:
            self.copies[key].wait()


def run_kernel(name, body, inputs, outputs, scratch, collective_id, vmem, in_vmem=()):
    flat, layout = [], []
    for key, value in scratch.items():
        group = value if isinstance(value, list) else [value]
        layout.append((key, len(group), isinstance(value, list)))
        flat.extend(group)
    plain = list(inputs) + list(outputs)

    def kernel(*refs):
        named = dict(zip(plain, refs))
        at = len(plain)
        for key, size, grouped in layout:
            named[key] = refs[at : at + size] if grouped else refs[at]
            at += size
        body(types.SimpleNamespace(**named))

    def spec(key):
        return pl.BlockSpec(memory_space=VMEM if key in in_vmem else pl.ANY)

    results = pl.pallas_call(
        kernel,
        name=name,
        in_specs=[spec(key) for key in inputs],
        out_specs=tuple(spec(key) for key in outputs),
        out_shape=tuple(jax.ShapeDtypeStruct(*value) for value in outputs.values()),
        scratch_shapes=flat,
        compiler_params=pltpu.CompilerParams(
            collective_id=collective_id, has_side_effects=True, vmem_limit_bytes=vmem * MIB
        ),
    )(*inputs.values())
    return types.SimpleNamespace(**dict(zip(outputs, results)))


SMALL = ("route_all", "gain_all", "bias_all", "router_all")


def layer_views(r, layer):
    r.gain, r.bias = r.gain_all.at[layer], r.bias_all.at[layer]
    r.router = r.router_all.at[layer]
    if hasattr(r, "route_all"):
        r.route = r.route_all.at[layer]


def forward_shapes(plan):
    rows, lanes, slots = plan.rows, plan.lanes, plan.slots
    return {
        "joint": ((2, 512, 384), BF16),
        "out_all": ((256, 512), BF16),
        "x": ((rows, 512), F32),
        "y": ((rows, 512), F32),
        "h": ((rows, 512), BF16),
        "qkv": ((2, rows, 384), BF16),
        "prob": ((2, plan.images, 2 * PAD, PAD), BF16),
        "mixed": ((2, rows, 128), BF16),
        "h2": ((lanes, 512), BF16),
        "place": ((plan.experts, lanes), F32),
        "table": ((lanes, 8), F32),
        "recv": ((slots, 512), BF16),
        "ret": ((slots, 512), BF16),
        "slot_gate": ((slots, 1), F32),
        "up": ((4, 512, 512), BF16),
        "down": ((4, 512, 512), BF16),
    }


def as_scratch(shapes):
    return {key: VMEM(*value) for key, value in shapes.items()}


def as_saved(shapes):
    return {"out_" + key: value for key, value in shapes.items()}


def pad_images(plan, source, target, staging):
    tokens = plan.images * SEQ
    staging[0:tokens, :] = source[...].astype(F32)
    target[...] = jnp.zeros_like(target)
    for image in range(plan.images):
        target[image * PAD : image * PAD + SEQ, :] = staging[
            image * SEQ : (image + 1) * SEQ, :
        ].astype(target.dtype)


def first_forward(plan, inputs, tokens):
    saved = forward_shapes(plan)

    def body(r):
        place = Place(plan.experts)
        place.greet()
        layer_views(r, 0)
        swap = HeadSwap(
            place, r.w_qkv.at[0], r.w_out.at[0], r.joint, r.out_all, r.swap
        )
        later = HeadSwap(
            place, r.w_qkv.at[1], r.w_out.at[1], r.joint_later, r.out_later, r.swap_later
        )
        saves = Copies({k: (getattr(r, k), getattr(r, "out_" + k)) for k in saved}, r.saves)
        total = CoreSum(place, r.total)
        weights = WeightGather(
            place, (r.w_up.at[0, 0], r.w_down.at[0, 0]), (r.up, r.down), r.weights
        )
        move = Exchange(place, plan.block, r.send, r.recv, r.move)
        back = Return(place, plan.block, plan.slots, r.ret, r.back, r.back_sems)
        swap.start_own()
        pad_images(plan, r.tokens, r.x, r.y)
        saves.start("x")
        place.met()
        swap.start_swap()
        weights.start()
        later.start_own()
        later.start_swap()
        route_places(plan, place, r)
        build_members(plan, place, r)
        swap.wait_own()

        def own_heads(image):
            first_norm(r, image)
            attend_forward(r, image, place.chip)

        def other_heads(image):
            attend_forward(r, image, 1 - place.chip)
            attend_out(r, total, image)

        each(0, plan.images, own_heads)
        swap.wait_swap()
        each(0, plan.images, other_heads)
        saves.start("joint", "out_all", "h", "qkv", "prob", "mixed", "place")
        second_norm(plan, r, total)
        send_slots(plan, place, r, move)
        saves.start("y", "h2", "table")
        build_picks(plan, r)
        weights.pass_on()
        weights.finish()
        saves.start("up", "down")
        for low, high in groups(plan):
            move.wait(low, high, False)
            move.wait(low, high, True)
            read_gates(plan, r, low, high)
            rows = slice(low * plan.block, high * plan.block)
            rows_in = r.recv[rows, :]
            result = jnp.zeros((rows.stop - rows.start, 512), F32)
            for part in range(4):
                act = gelu(dot(rows_in, r.up[part])).astype(BF16)
                result = result + dot(act, r.down[part])
            r.ret[rows, :] = (result * r.slot_gate[rows, :]).astype(BF16)
            back.start(low, high)
        saves.start("recv", "ret", "slot_gate")
        back.pass_on()
        back.finish()
        saves.wait("x")
        combined(plan, r, r.back, r.x)
        r.x[...] += r.y[...]
        out = pltpu.make_async_copy(r.x, r.next, r.out_sem)
        out.start()
        saves.wait(*(k for k in saved if k != "x"))
        later.wait_own()
        later.wait_swap()
        out.wait()

    outputs = dict(
        as_saved(saved),
        next=((plan.rows, 512), F32),
        joint_later=saved["joint"],
        out_later=saved["out_all"],
    )
    scratch = dict(
        as_scratch(saved),
        codes=VMEM((4, plan.lanes), F32),
        member=VMEM((plan.slots, plan.lanes), BF16),
        gate=VMEM((plan.experts, plan.lanes), F32),
        picks=picks_scratch(plan),
        send=VMEM((plan.slots, 512), BF16),
        back=VMEM((4 * plan.slots, 512), BF16),
        total=CoreSum.scratch(plan.images),
        weights=WeightGather.scratch(),
        swap=HeadSwap.scratch(),
        swap_later=HeadSwap.scratch(),
        move=Exchange.scratch(plan.experts),
        back_sems=Return.scratch(plan.experts),
        saves=DMA((len(saved),)),
        out_sem=DMA,
    )
    return run_kernel(
        "first_forward", body, dict(inputs, tokens=tokens), outputs, scratch, 0, 62,
        SMALL + ("tokens",),
    )


def second_whole(plan, inputs, cotangent, start, joint, out_all):
    def body(r):
        place = Place(plan.experts)
        place.greet()
        layer_views(r, 1)
        r.gret, r.ret, r.dr, r.column = r.send, r.gsend, r.grecv, r.slot_gate
        loads = Copies(
            {k: (getattr(r, "in_" + k), getattr(r, k)) for k in ("x", "joint", "out_all")}, r.loads
        )
        total = CoreSum(place, r.total)
        total_back = CoreSum(place, r.total)
        weights = WeightGather(
            place, (r.w_up.at[1, 0], r.w_down.at[1, 0]), (r.up, r.down), r.weights
        )
        move = Exchange(place, plan.block, r.send, r.recv, r.move)
        gmove = Exchange(place, plan.block, r.gsend, r.grecv, r.gmove)
        back = Return(place, plan.block, plan.slots, r.ret, r.back, r.back_sems)
        gback = Return(place, plan.block, plan.slots, r.gret, r.gback, r.gback_sems)
        loads.start("x", "joint", "out_all")
        pad_images(plan, r.cotangent, r.g, r.y)
        route_places(plan, place, r)
        build_members(plan, place, r)
        r.gsend[...] = dot(r.member[:, : plan.rows], r.g[...]).astype(BF16)
        place.met()
        weights.start()
        gmove.start_all()
        loads.wait("x", "joint", "out_all")

        def heads(image):
            first_norm(r, image)
            for side in range(2):
                attend_forward(r, image, side)
            attend_out(r, total, image)

        each(0, plan.images, heads)
        second_norm(plan, r, total)
        send_slots(plan, place, r, move)
        build_picks(plan, r)
        weights.pass_on()
        weights.finish()
        gmove.wait(0, plan.experts)
        for low, high in groups(plan):
            move.wait(low, high, False)
            move.wait(low, high, True)
            read_gates(plan, r, low, high)
            rows = slice(low * plan.block, high * plan.block)
            rows_in = r.recv[rows, :]
            gate = r.slot_gate[rows, :]
            raw = r.grecv[rows, :].astype(F32)
            scaled = (raw * gate).astype(BF16)
            r.dr[rows, :] = scaled
            result = jnp.zeros((rows.stop - rows.start, 512), F32)
            slots_grad = jnp.zeros((rows.stop - rows.start, 512), F32)
            for part in range(4):
                act, slope = gelu_both(dot(rows_in, r.up[part]))
                act = act.astype(BF16)
                r.act[part, rows, :] = act
                result = result + dot(act, r.down[part])
                pre_grad = (dot_nt(scaled, r.down[part]) * slope).astype(BF16)
                r.dpre[part, rows, :] = pre_grad
                slots_grad = slots_grad + dot_nt(pre_grad, r.up[part])
            result = result * gate
            r.ret[rows, :] = result.astype(BF16)
            column = jnp.sum(result * raw, -1, keepdims=True)
            return_gradient(plan, r, low, high, slots_grad, column)
            gback.start(low, high)
        back.start(0, plan.experts)
        expert_grads(plan, place, r, r.near)
        gback.pass_on()
        near_sums(place, r, r.near)
        outs = near_outs(place, r)
        for copy in outs:
            copy.start()
        gback.finish()
        back_to_attention(plan, place, r)
        half = plan.images // 2
        each(0, half, lambda image: attend_backward(r, total_back, image))
        back.pass_on()
        each(half, plan.images, lambda image: attend_backward(r, total_back, image))
        pack_out(plan, place, r)
        pack_qkv(plan, place, r)

        def input_grad(image):
            rows = image_rows(image)
            r.gin[rows, :] = first_norm_back(plan, r, total_back, image)

        each(0, plan.images, input_grad)
        out = pltpu.make_async_copy(r.gin, r.grad, r.late_sems.at[0])
        out.start()
        pack_small(plan, r)
        out_packed = pltpu.make_async_copy(r.packed, r.out_packed, r.late_sems.at[1])
        out_packed.start()
        back.finish()
        combined(plan, r, r.back, r.x)
        for image in range(plan.images):
            rows = slice(image * PAD, image * PAD + SEQ)
            r.y[image * SEQ : (image + 1) * SEQ, :] = r.y[rows, :] + r.x[rows, :]
        r.result[...] = r.y[0 : plan.images * SEQ, :].astype(BF16)
        for copy in outs + [out, out_packed]:
            copy.wait()

    outputs = {
        "result": (cotangent.shape, BF16),
        "grad": ((plan.rows, 512), F32),
        "out_packed": ((plan.packed, 128), BF16),
        "gfar": ((2, 512, 512), BF16),
        "gown": ((2, 512, 512), BF16),
    }
    scratch = dict(
        as_scratch({k: v for k, v in forward_shapes(plan).items() if k != "ret"}),
        codes=VMEM((4, plan.lanes), F32),
        member=VMEM((plan.slots, plan.lanes), BF16),
        gate=VMEM((plan.experts, plan.lanes), F32),
        picks=picks_scratch(plan),
        send=VMEM((plan.slots, 512), BF16),
        back=VMEM((4 * plan.slots, 512), BF16),
        total=CoreSum.scratch(plan.images),
        weights=WeightGather.scratch(),
        move=Exchange.scratch(plan.experts),
        back_sems=Return.scratch(plan.experts),
        gmove=Exchange.scratch(plan.experts),
        gback_sems=Return.scratch(plan.experts),
        gsend=VMEM((plan.slots, 512), BF16),
        grecv=VMEM((plan.slots, 512), BF16),
        g=VMEM((plan.rows, 512), BF16),
        out_sems=DMA((2, 2)),
        late_sems=DMA((2,)),
        loads=DMA((3,)),
        **backward_scratch(plan),
    )
    return run_kernel(
        "second_whole", body,
        dict(inputs, cotangent=cotangent, in_x=start, in_joint=joint, in_out_all=out_all),
        outputs, scratch, 1, 63, SMALL + ("cotangent", "result"),
    )


def backward_scratch(plan):
    return {
        "gback": VMEM((4 * plan.slots, 512), BF16),
        "act": VMEM((4, plan.slots, 512), BF16),
        "dpre": VMEM((4, plan.slots, 512), BF16),
        "gpart": VMEM((2, 4, 512, 512), BF16),
        "gdg": VMEM((4 * plan.slots, 128), BF16),
        "gated": VMEM((plan.rows, 128), F32),
        "dz": VMEM((plan.rows, 128), BF16),
        "gin": VMEM((plan.rows, 512), F32),
        "dproj": VMEM((2, plan.rows, 384), BF16),
        "packed": VMEM((plan.packed, 128), BF16),
        "vec": VMEM((8, 512), F32),
        "near": PairSum.scratch_near(),
    }


def first_backward(plan, inputs, saved, grad, gfar, gown, packed, out_shape):
    def body(r):
        place = Place(plan.experts)
        place.greet()
        layer_views(r, 0)
        r.gret, r.dr, r.column = r.gsend, r.grecv, r.slot_gate
        r.x = r.g
        loads = Copies(
            {k: (getattr(r, "in_" + k), getattr(r, k)) for k in list(saved) + ["g", "later"]},
            r.loads,
        )
        total = CoreSum(place, r.total)
        gmove = Exchange(place, plan.block, r.gsend, r.grecv, r.gmove)
        gback = Return(place, plan.block, plan.slots, r.gret, r.gback, r.gback_sems)
        later = ExpertSum(place, plan.panels, r.later, r.sum_later, r.later_sum)
        sooner = ExpertSum(place, plan.panels, r.packed, r.sum_first, r.sooner_sum)
        first_loads = ("g", "place", "recv", "up", "down", "ret", "slot_gate", "table")
        loads.start(*first_loads)
        loads.start(*(k for k in loads.copies if k not in first_loads + ("x",)))
        loads.wait("place")
        build_members(plan, place, r)
        loads.wait("g")
        r.gsend[...] = dot(r.member[:, : plan.rows], r.g[...].astype(BF16)).astype(BF16)
        place.met()
        gmove.start_all()
        for which in range(2):
            PairSum.far(place, r.gfar_later.at[which], r.far_later, which).start()
        own_copy = pltpu.make_async_copy(r.gown_later, r.glater, r.own_sem)
        own_copy.start()
        loads.wait("recv", "up", "down")
        for low, high in groups(plan):
            rows = slice(low * plan.block, high * plan.block)
            for part in range(4):
                act, slope = gelu_both(dot(r.recv[rows, :], r.up[part]))
                r.act[part, rows, :] = act.astype(BF16)
                r.dpre[part, rows, :] = slope.astype(BF16)
        loads.wait("table")
        build_picks(plan, r)
        loads.wait("ret", "slot_gate", "later")
        for low, high in groups(plan):
            gmove.wait(low, high)
            rows = slice(low * plan.block, high * plan.block)
            raw = r.grecv[rows, :].astype(F32)
            scaled = (raw * r.slot_gate[rows, :]).astype(BF16)
            r.dr[rows, :] = scaled
            slots_grad = jnp.zeros((rows.stop - rows.start, 512), F32)
            for part in range(4):
                pre_grad = (
                    dot_nt(scaled, r.down[part]) * r.dpre[part, rows, :].astype(F32)
                ).astype(BF16)
                r.dpre[part, rows, :] = pre_grad
                slots_grad = slots_grad + dot_nt(pre_grad, r.up[part])
            column = jnp.sum(r.ret[rows, :].astype(F32) * raw, -1, keepdims=True)
            return_gradient(plan, r, low, high, slots_grad, column)
            gback.start(low, high)
        expert_grads(plan, place, r, r.near)
        gback.pass_on()
        later.every(later.step_pair)
        near_sums(place, r, r.near)
        for which in range(2):
            PairSum.far(place, r.gpart.at[which, place.chip_peer], r.far, which).start()
        loads.wait(*(k for k in loads.copies if k not in first_loads + ("later", "x")))
        gback.finish()
        back_to_attention(plan, place, r)
        loads.start("x")
        later.every(later.step_scatter)
        pack_out(plan, place, r)
        sooner.step_pair(0)
        half = plan.images // 2
        each(0, half, lambda image: attend_backward(r, total, image))
        later.every(later.step_share)
        sooner.step_scatter(0)
        each(half, plan.images, lambda image: attend_backward(r, total, image))
        pack_qkv(plan, place, r)
        panels = len(plan.panels)
        for panel in range(1, panels - 1):
            sooner.step_pair(panel)
        loads.wait("x")
        for image in range(plan.images):
            out = first_norm_back(plan, r, total, image)
            r.grad[image * SEQ : (image + 1) * SEQ, :] = out[:SEQ]
        pack_small(plan, r)
        sooner.step_pair(panels - 1)
        for panel in range(1, panels):
            sooner.step_scatter(panel)
        later.every(later.step_out)
        own_copy.wait()
        for which in range(2):
            PairSum.far(place, r.gfar_later.at[which], r.far_later, which).wait()
            r.glater[which] = (
                r.glater[which].astype(F32) + r.far_later[0][which].astype(F32)
            ).astype(BF16)
        sooner.every(sooner.step_share)
        later.every(later.step_end)
        for which in range(2):
            PairSum.far(place, r.gpart.at[which, place.chip_peer], r.far, which).wait()
            r.gfirst[which] = (
                r.gpart[which, place.tensor].astype(F32) + r.far[0][which].astype(F32)
            ).astype(BF16)
        sooner.every(sooner.step_out)
        sooner.every(sooner.step_end)

    outputs = {
        "grad": (out_shape, F32),
        "gfirst": ((2, 512, 512), BF16),
        "glater": ((2, 512, 512), BF16),
        "sum_first": ((plan.packed, 128), BF16),
        "sum_later": ((plan.packed, 128), BF16),
    }
    scratch = dict(
        as_scratch({k: v for k, v in forward_shapes(plan).items() if k != "x"}),
        member=VMEM((plan.slots, plan.lanes), BF16),
        picks=picks_scratch(plan),
        total=CoreSum.scratch(plan.images),
        gmove=Exchange.scratch(plan.experts),
        gback_sems=Return.scratch(plan.experts),
        gsend=VMEM((plan.slots, 512), BF16),
        grecv=VMEM((plan.slots, 512), BF16),
        g=VMEM((plan.rows, 512), F32),
        later=VMEM((plan.packed, 128), BF16),
        own_sem=DMA,
        far=PairSum.scratch_far(),
        far_later=PairSum.scratch_far(),
        later_sum=ExpertSum.scratch(plan),
        sooner_sum=ExpertSum.scratch(plan),
        loads=DMA((len(saved) + 2,)),
        **backward_scratch(plan),
    )
    arrays = dict({"in_" + k: v for k, v in saved.items()}, in_g=grad, in_later=packed)
    return run_kernel(
        "first_backward", body,
        dict(inputs, gfar_later=gfar, gown_later=gown, **arrays),
        outputs, scratch, 2, 63, SMALL + tuple(outputs),
    )


def body(tokens, routes, ln_gain, ln_bias, w_qkv, w_out, w_router, w_up, w_down, cotangent):
    tok_rows = tokens.shape[0]
    experts = w_router.shape[2]
    plan = Plan(tok_rows, experts)
    route_rows = routes.reshape(2, plan.images, SEQ, 2)
    route_rows = jnp.pad(
        route_rows, ((0, 0), (0, 0), (0, PAD - SEQ), (0, 0)), constant_values=-1
    ).reshape(2, plan.rows, 2)
    route_rows = jnp.pad(
        route_rows, ((0, 0), (0, plan.lanes - plan.rows), (0, 0)), constant_values=-1
    ).transpose(0, 2, 1)
    router_rows = jnp.pad(w_router.transpose(0, 2, 1), ((0, 0), (0, 128 - experts), (0, 0)))
    small = {"gain_all": ln_gain, "bias_all": ln_bias, "router_all": router_rows}
    weights = {"w_up": w_up, "w_down": w_down}
    one = first_forward(
        plan, dict(small, route_all=route_rows, w_qkv=w_qkv, w_out=w_out, **weights), tokens
    )
    two = second_whole(
        plan, dict(small, route_all=route_rows, **weights), cotangent,
        one.next, one.joint_later, one.out_later,
    )
    saved = {key: getattr(one, "out_" + key) for key in forward_shapes(plan)}
    three = first_backward(
        plan, small, saved, two.grad, two.gfar, two.gown, two.out_packed, tokens.shape
    )
    packs = [pack.astype(F32) for pack in (three.sum_first, three.sum_later)]
    grad_out = jnp.stack([pack[:512].T for pack in packs])
    grad_qkv = jnp.stack([pack[512:2048].reshape(3, 512, 128) for pack in packs])
    vectors = [
        pack[2048 : 2048 + 4 * (4 + experts)].reshape(4, 4 + experts, 128).transpose(1, 0, 2)
        .reshape(4 + experts, 512)
        for pack in packs
    ]
    grad_gain = jnp.stack([entry[0:2] for entry in vectors])
    grad_bias = jnp.stack([entry[2:4] for entry in vectors])
    grad_router = jnp.stack([entry[4:].T for entry in vectors])
    grad_up = jnp.stack([three.gfirst[0], three.glater[0]])[:, None].astype(F32)
    grad_down = jnp.stack([three.gfirst[1], three.glater[1]])[:, None].astype(F32)
    return (
        two.result, three.grad, grad_gain, grad_bias[:, 0], grad_bias[:, 1],
        grad_qkv, grad_out, grad_router, grad_up, grad_down,
    )


def solution(mesh):
    in_specs = (
        P("expert", None),
        P(None, "expert", None),
        P(),
        P(),
        P(None, None, None, "tensor"),
        P(None, "tensor", None),
        P(),
        P(None, "expert", None, "tensor"),
        P(None, "expert", "tensor", None),
        P("expert", None),
    )
    out_specs = (
        P("expert", None),
        P("expert", None),
        P(),
        P(),
        P(),
        P(None, None, None, "tensor"),
        P(None, "tensor", None),
        P(),
        P(None, "expert", None, "tensor"),
        P(None, "expert", "tensor", None),
    )
    return jax.shard_map(body, mesh=mesh, in_specs=in_specs, out_specs=out_specs, check_vma=False)
```

```python
import types

import jax
import jax.numpy as jnp
from jax import lax
from jax.experimental import pallas as pl
from jax.experimental.pallas import tpu as pltpu
from jax.sharding import PartitionSpec as P

HEAD_DIM = 64
SEQ = 197
PAD = 208
EPS = 1e-06
MESH = pl.DeviceIdType.MESH
F32 = jnp.float32
BF16 = jnp.bfloat16
SCALE = HEAD_DIM ** (-0.5)
MIB = 1 << 20
VMEM = pltpu.VMEM
DMA = pltpu.SemaphoreType.DMA


def up_to(count, multiple):
    return -(-count // multiple) * multiple


def dot(left, right):
    return lax.dot_general(left, right, (((1,), (0,)), ((), ())), preferred_element_type=F32)


def dot_nt(left, right):
    return lax.dot_general(left, right, (((1,), (1,)), ((), ())), preferred_element_type=F32)


def dot_tn(left, right):
    return lax.dot_general(left, right, (((0,), (0,)), ((), ())), preferred_element_type=F32)


def norm_parts(rows):
    centered = rows - jnp.mean(rows, -1, keepdims=True)
    scaled = lax.rsqrt(jnp.mean(centered * centered, -1, keepdims=True) + EPS)
    return centered * scaled, scaled


def norm_pull(grad_in, normed, scaled, gain_row):
    grad_normed = grad_in * gain_row
    inner = (
        grad_normed
        - jnp.mean(grad_normed, -1, keepdims=True)
        - normed * jnp.mean(grad_normed * normed, -1, keepdims=True)
    )
    return inner * scaled


def gelu(pre):
    inner = pre * (0.7978845608028654 + 0.035677408136300125 * (pre * pre))
    return 0.5 * pre * (1.0 + jnp.tanh(inner))


def gelu_both(pre):
    square = pre * pre
    inner = pre * (0.7978845608028654 + 0.035677408136300125 * square)
    bent = jnp.tanh(inner)
    half = 0.5 + 0.5 * bent
    slope = half + half * (1.0 - bent) * pre * (
        0.7978845608028654 + 0.10703222440890037 * square
    )
    return half * pre, slope


class Plan:
    def __init__(self, tok_rows, experts):
        self.images = tok_rows // SEQ
        self.rows = self.images * PAD
        self.lanes = up_to(self.rows, 128)
        self.experts = experts
        self.per_rank = max(1, 10 * tok_rows // (4 * experts * 4))
        self.capacity = 4 * self.per_rank
        self.block = up_to(self.per_rank + 2, 16)
        self.slots = experts * self.block
        self.group = max(
            size for size in range(1, experts)
            if experts % size == 0 and (size == 1 or size * self.block <= 320)
        )
        self.stored = 4 * self.slots <= 2560
        main = up_to(512, 16 * experts)
        small = up_to(4 * (4 + experts), 16 * experts)
        self.panels = [(start, main) for start in range(0, 2048, main)] + [(2048, small)]
        self.packed = 2048 + small


def image_rows(image):
    return pl.ds(pl.multiple_of(image * PAD, PAD), PAD)


def each(low, high, use):
    def one(index, carry):
        use(index)
        return carry

    lax.fori_loop(low, high, one, 0)


class Place:
    def __init__(self, experts):
        self.tensor = lax.axis_index("tensor")
        self.core = lax.rem(self.tensor, 2)
        self.chip = lax.div(self.tensor, 2)
        self.core_peer = self.tensor + 1 - 2 * self.core
        self.chip_peer = lax.rem(self.tensor + 2, 4)
        self.experts = experts
        self.expert = lax.axis_index("expert")

    def ahead(self, step):
        return lax.rem(self.expert + step, self.experts)

    def behind(self, step):
        return lax.rem(self.expert + self.experts - step, self.experts)

    def greet(self):
        barrier = pltpu.get_barrier_semaphore()
        for peer in (self.core_peer, self.chip_peer):
            pl.semaphore_signal(barrier, inc=1, device_id={"tensor": peer}, device_id_type=MESH)

        def one(step):
            pl.semaphore_signal(
                barrier, inc=1, device_id={"expert": self.ahead(step)}, device_id_type=MESH
            )

        each(1, self.experts, one)

    def met(self):
        pl.semaphore_wait(pltpu.get_barrier_semaphore(), 2 + self.experts - 1)

    def to_core(self, src, dst, send, recv):
        return pltpu.make_async_remote_copy(
            src_ref=src, dst_ref=dst, send_sem=send, recv_sem=recv,
            device_id={"tensor": self.core_peer}, device_id_type=MESH,
        )

    def to_chip(self, src, dst, send, recv):
        return pltpu.make_async_remote_copy(
            src_ref=src, dst_ref=dst, send_sem=send, recv_sem=recv,
            device_id={"tensor": self.chip_peer}, device_id_type=MESH,
        )

    def to_expert(self, expert, src, dst, send, recv):
        return pltpu.make_async_remote_copy(
            src_ref=src, dst_ref=dst, send_sem=send, recv_sem=recv,
            device_id={"expert": expert}, device_id_type=MESH,
        )


class CoreSum:
    def __init__(self, place, refs):
        self.place = place
        self.part, self.near, self.send, self.recv = refs

    @staticmethod
    def scratch(images):
        rows = (images * PAD, 512)
        return [VMEM(rows, BF16), VMEM(rows, BF16), DMA((images,)), DMA((images,))]

    def copy(self, image):
        rows = image_rows(image)
        return self.place.to_core(
            self.part.at[rows], self.near.at[rows], self.send.at[image], self.recv.at[image]
        )

    def put(self, image, value):
        self.part[image_rows(image), :] = value.astype(BF16)
        self.copy(image).start()

    def get(self, image):
        rows = image_rows(image)
        self.copy(image).wait()
        return self.part[rows, :].astype(F32) + self.near[rows, :].astype(F32)


class HeadSwap:
    def __init__(self, place, qkv, out, joint, out_all, refs):
        self.place, self.qkv, self.out = place, qkv, out
        self.joint, self.out_all = joint, out_all
        self.send, self.recv, self.local = refs

    @staticmethod
    def scratch():
        return [DMA((4,)), DMA((4,)), DMA((4,))]

    def ends(self, part):
        if part == 3:
            rows = pl.ds(pl.multiple_of(self.place.chip * 128, 128), 128)
            return self.out, self.out_all.at[rows]
        columns = pl.ds(part * 128, 128)
        return self.qkv.at[part], self.joint.at[self.place.chip, :, columns]

    def own(self, part):
        return pltpu.make_async_copy(*self.ends(part), self.local.at[part])

    def swap(self, part):
        return self.place.to_chip(*self.ends(part), self.send.at[part], self.recv.at[part])

    def start_own(self):
        for part in range(4):
            self.own(part).start()

    def start_swap(self):
        for part in range(4):
            self.swap(part).start()

    def wait_own(self):
        for part in range(4):
            self.own(part).wait()

    def wait_swap(self, parts=range(4)):
        for part in parts:
            self.swap(part).wait()


class Exchange:
    def __init__(self, place, block, src, dst, refs):
        self.place, self.block, self.src, self.dst = place, block, src, dst
        self.send, self.recv, self.local = refs

    @staticmethod
    def scratch(experts):
        return [DMA((2, experts)), DMA((2, experts)), DMA((2,))]

    def part(self, step, tail):
        base = pl.multiple_of(step * self.block, self.block)
        if tail is None:
            return pl.ds(base, self.block)
        if tail:
            return pl.ds(pl.multiple_of(base + self.block - 16, 16), 16)
        return pl.ds(base, self.block - 16)

    def own(self, tail=None):
        rows = self.part(0, tail)
        return pltpu.make_async_copy(
            self.src.at[rows], self.dst.at[rows], self.local.at[int(bool(tail))]
        )

    def copy(self, step, tail=None):
        rows, which = self.part(step, tail), int(bool(tail))
        return self.place.to_expert(
            self.place.ahead(step), self.src.at[rows], self.dst.at[rows],
            self.send.at[which, step], self.recv.at[which, step],
        )

    def start_all(self, tail=None):
        self.own(tail).start()
        each(1, self.place.experts, lambda step: self.copy(step, tail).start())

    def wait(self, low, high, tail=None):
        if low == 0:
            self.own(tail).wait()
        each(max(1, low), high, lambda step: self.copy(step, tail).wait())


class Return:
    def __init__(self, place, block, slots, src, dst, refs):
        self.place, self.block, self.slots, self.src, self.dst = place, block, slots, src, dst
        self.send, self.recv, self.local = refs

    @staticmethod
    def scratch(experts):
        return [DMA((4, experts)), DMA((4, experts)), DMA]

    def rows(self, quarter, step):
        return pl.ds(
            pl.multiple_of(quarter * self.slots + step * self.block, self.block), self.block
        )

    def own(self):
        return pltpu.make_async_copy(
            self.src.at[pl.ds(0, self.block)],
            self.dst.at[self.rows(self.place.tensor, 0)], self.local,
        )

    def home(self, step):
        rows = pl.ds(pl.multiple_of(step * self.block, self.block), self.block)
        return self.place.to_expert(
            self.place.behind(step), self.src.at[rows],
            self.dst.at[self.rows(self.place.tensor, step)],
            self.send.at[0, step], self.recv.at[0, step],
        )

    def to_chip(self, step):
        block = self.dst.at[self.rows(self.place.tensor, step)]
        return self.place.to_chip(block, block, self.send.at[1, step], self.recv.at[1, step])

    def to_core(self, step):
        block = self.dst.at[self.rows(self.place.tensor, step)]
        return self.place.to_core(block, block, self.send.at[2, step], self.recv.at[2, step])

    def on_to_core(self, step):
        block = self.dst.at[self.rows(self.place.chip_peer, step)]
        return self.place.to_core(block, block, self.send.at[3, step], self.recv.at[3, step])

    def start(self, low, high):
        if low == 0:
            self.own().start()
        each(max(1, low), high, lambda step: self.home(step).start())

    def pass_on(self, arrived=lambda quarter, step: None):
        place, last = self.place, self.place.experts

        def give(step):
            self.to_chip(step).start()
            self.to_core(step).start()
            arrived(place.tensor, step)

        def one(step):
            self.home(step).wait_recv()
            give(step)

        def two(step):
            one(step)
            self.on(step - self.LAG, arrived)

        self.own().wait()
        give(0)
        each(1, self.LAG, one)
        each(self.LAG, last, two)

    LAG = 4

    def on(self, step, arrived):
        self.to_chip(step).wait_recv()
        self.on_to_core(step).start()
        arrived(self.place.chip_peer, step)

    def near(self, arrived=lambda quarter, step: None):
        def one(step):
            self.to_core(step).wait_recv()
            arrived(self.place.core_peer, step)

        each(0, self.place.experts, one)

    def far(self, arrived=lambda quarter, step: None):
        place, last = self.place, self.place.experts
        each(last - self.LAG, last, lambda step: self.on(step, arrived))

        def one(step):
            self.on_to_core(step).wait_recv()
            arrived(3 - place.tensor, step)

        each(0, last, one)

    def finish(self):
        def one(step):
            self.to_chip(step).wait_send()
            self.to_core(step).wait_send()
            self.on_to_core(step).wait_send()

        each(0, self.place.experts, one)
        each(1, self.place.experts, lambda step: self.home(step).wait_send())


class WeightGather:
    def __init__(self, place, shards, wholes, refs):
        self.place, self.shards, self.wholes = place, shards, wholes
        self.send, self.recv, self.local = refs

    @staticmethod
    def scratch():
        return [DMA((2, 3)), DMA((2, 3)), DMA((2,))]

    def own(self, which):
        return pltpu.make_async_copy(
            self.shards[which], self.wholes[which].at[self.place.tensor], self.local.at[which]
        )

    def to_chip(self, which):
        return self.place.to_chip(
            self.shards[which], self.wholes[which].at[self.place.tensor],
            self.send.at[which, 0], self.recv.at[which, 0],
        )

    def to_core(self, which):
        return self.place.to_core(
            self.shards[which], self.wholes[which].at[self.place.tensor],
            self.send.at[which, 1], self.recv.at[which, 1],
        )

    def on_to_core(self, which):
        part = self.wholes[which].at[self.place.chip_peer]
        return self.place.to_core(
            part, part, self.send.at[which, 2], self.recv.at[which, 2]
        )

    def start(self):
        for which in range(2):
            self.own(which).start()
            self.to_chip(which).start()
            self.to_core(which).start()

    def pass_on(self):
        for which in range(2):
            self.to_chip(which).wait()
            self.on_to_core(which).start()

    def finish(self):
        for which in range(2):
            self.own(which).wait()
            self.to_core(which).wait()
            self.on_to_core(which).wait()


class ExpertSum:
    def __init__(self, place, panels, src, total, refs):
        self.place, self.panels, self.src, self.total = place, panels, src, total
        self.inbox, self.chunks, self.send, self.recv = refs
        self.side = lax.rem(place.expert, 2)
        self.pair = place.expert + 1 - 2 * self.side
        self.group = place.experts // 2
        self.index = lax.div(place.expert, 2)

    @staticmethod
    def scratch(plan):
        panels = len(plan.panels)
        half = plan.packed // 2
        return [
            VMEM((half, 128), BF16), VMEM((half, 128), BF16),
            DMA((2, panels, max(2, plan.experts // 2))), DMA((2, panels, max(2, plan.experts // 2))),
        ]

    def half(self, panel, side):
        start, rows = self.panels[panel]
        return pl.ds(pl.multiple_of(start + side * (rows // 2), 16), rows // 2)

    def local(self, panel):
        start, rows = self.panels[panel]
        return pl.ds(start // 2, rows // 2)

    def chunk(self, panel, index):
        start, rows = self.panels[panel]
        size = rows // self.place.experts
        return pl.ds(pl.multiple_of(start // 2 + index * size, 16), size)

    def chunk_whole(self, panel, index):
        start, rows = self.panels[panel]
        size = rows // self.place.experts
        return pl.ds(pl.multiple_of(start + self.side * (rows // 2) + index * size, 16), size)

    def member(self, step):
        return lax.rem(self.place.expert + 2 * step, self.place.experts)

    def pair_in(self, panel):
        return self.place.to_expert(
            self.pair, self.src.at[self.half(panel, 1 - self.side)],
            self.inbox.at[self.local(panel)],
            self.send.at[0, panel, 0], self.recv.at[0, panel, 0],
        )

    def scatter(self, panel, step):
        peer = lax.rem(self.index + step, self.group)
        return self.place.to_expert(
            self.member(step), self.src.at[self.chunk_whole(panel, peer)],
            self.chunks.at[self.chunk(panel, step)],
            self.send.at[0, panel, step], self.recv.at[0, panel, step],
        )

    def share(self, panel, step):
        mine = self.total.at[self.chunk_whole(panel, self.index)]
        return self.place.to_expert(
            self.member(step), mine, mine,
            self.send.at[1, panel, step], self.recv.at[1, panel, step],
        )

    def pair_out(self, panel):
        half = self.total.at[self.half(panel, self.side)]
        return self.place.to_expert(
            self.pair, half, half, self.send.at[1, panel, 0], self.recv.at[1, panel, 0]
        )

    def step_pair(self, panel):
        self.pair_in(panel).start()

    def step_scatter(self, panel):
        self.pair_in(panel).wait()
        mine = self.half(panel, self.side)
        self.src[mine, :] = (
            self.src[mine, :].astype(F32) + self.inbox[self.local(panel), :].astype(F32)
        ).astype(BF16)
        each(1, self.group, lambda step: self.scatter(panel, step).start())

    def step_share(self, panel):
        mine = self.chunk_whole(panel, self.index)

        def one(step, total):
            self.scatter(panel, step).wait()
            return total + self.chunks[self.chunk(panel, step), :].astype(F32)

        total = lax.fori_loop(1, self.group, one, self.src[mine, :].astype(F32))
        self.total[mine, :] = total.astype(BF16)
        each(1, self.group, lambda step: self.share(panel, step).start())

    def step_out(self, panel):
        each(1, self.group, lambda step: self.share(panel, step).wait())
        self.pair_out(panel).start()

    def step_end(self, panel):
        self.pair_out(panel).wait()

    def every(self, step):
        for panel in range(len(self.panels)):
            step(panel)


class PairSum:
    @staticmethod
    def scratch_near():
        return [VMEM((2, 2, 512, 512), BF16), DMA((2, 2)), DMA((2, 2))]

    @staticmethod
    def scratch_far():
        return [VMEM((2, 512, 512), BF16), DMA((2,)), DMA((2,))]

    @staticmethod
    def near(place, part, refs, which, chip):
        inbox, send, recv = refs
        quarter = 2 * chip + 1 - place.core
        return place.to_core(
            part.at[which, quarter], inbox.at[which, chip],
            send.at[which, chip], recv.at[which, chip],
        )

    @staticmethod
    def far(place, out, refs, which):
        inbox, send, recv = refs
        return place.to_chip(out, inbox.at[which], send.at[which], recv.at[which])


def route_places(plan, place, r):
    shape = (plan.experts, plan.lanes)
    expert_id = lax.broadcasted_iota(jnp.int32, shape, 0)
    lane = lax.broadcasted_iota(jnp.int32, shape, 1)
    first, second = r.route[0:1, :], r.route[1:2, :]
    is_first, is_second = expert_id == first, expert_id == second
    named = is_first | is_second
    count = jnp.where(named, 1.0, 0.0)
    running = count
    step = 1
    while step < plan.lanes:
        running = running + jnp.where(lane >= step, pltpu.roll(running, step, 1), 0.0)
        step *= 2
    before = running - count
    mine = before - (place.tensor * plan.per_rank).astype(F32)
    valid = named & (mine >= 0.0) & (mine < float(plan.per_rank))
    r.place[...] = jnp.where(valid, mine, -1.0)
    quarter = jnp.zeros(shape, F32)
    for bound in range(1, 4):
        quarter = quarter + jnp.where(before >= float(bound * plan.per_rank), 1.0, 0.0)
    step_of = expert_id - place.expert
    step_of = jnp.where(step_of < 0, step_of + plan.experts, step_of).astype(F32)
    code = (
        quarter * float(plan.slots - plan.per_rank) + step_of * float(plan.block) + before
    )
    kept = before < float(plan.capacity)
    nowhere = -1.0
    code_first = jnp.max(jnp.where(is_first & kept, code, nowhere), 0, keepdims=True)
    code_second = jnp.max(jnp.where(is_second & kept, code, nowhere), 0, keepdims=True)
    r.codes[...] = jnp.concatenate(
        [code_first, code_second, first.astype(F32), second.astype(F32)], axis=0
    )


def build_members(plan, place, r):
    slot = lax.broadcasted_iota(jnp.int32, (plan.block, plan.lanes), 0).astype(F32)

    def one(step):
        rows = pl.ds(pl.multiple_of(step * plan.block, plan.block), plan.block)
        hit = r.place[pl.ds(place.ahead(step), 1), :] == slot
        r.member[rows, :] = jnp.where(hit, 1.0, 0.0).astype(BF16)

    each(0, plan.experts, one)


def picks_part(plan, r, image, quarter):
    slot = lax.broadcasted_iota(jnp.int32, (PAD, plan.slots), 1) + quarter * plan.slots
    slot = slot.astype(F32)
    rows = image_rows(image)
    hit = (r.table[rows, 0:1] == slot) | (r.table[rows, 1:2] == slot)
    return jnp.where(hit, 1.0, 0.0).astype(BF16)


def build_picks(plan, r):
    if not plan.stored:
        return
    for quarter in range(4):
        columns = slice(quarter % 2 * plan.slots, (quarter % 2 + 1) * plan.slots)

        def one(image):
            r.picks[quarter // 2, image_rows(image), columns] = picks_part(
                plan, r, image, quarter
            )

        each(0, plan.images, one)


def picks_scratch(plan):
    return VMEM((2, plan.rows, 2 * plan.slots) if plan.stored else (2, 16, 128), BF16)


def diagonal(plan):
    shape = (plan.block, 128)
    return lax.broadcasted_iota(jnp.int32, shape, 0) == lax.broadcasted_iota(jnp.int32, shape, 1)


def tail_rows(plan, base):
    return pl.ds(pl.multiple_of(base + plan.block - 16, 16), 16)


def write_spare(plan, ref, base, column):
    row = jnp.sum(jnp.where(diagonal(plan), column, 0.0), 0, keepdims=True)
    high = row.astype(BF16).astype(F32)
    rest = jnp.zeros((1, 512 - 128), F32)
    high_row = jnp.concatenate([high, rest], axis=1)
    low_row = jnp.concatenate([row - high, rest], axis=1)
    rows = tail_rows(plan, base)
    index = lax.broadcasted_iota(jnp.int32, (16, 512), 0)
    old = ref[rows, :].astype(F32)
    ref[rows, :] = jnp.where(index == 14, high_row, jnp.where(index == 15, low_row, old)).astype(
        BF16
    )


def read_spare(plan, ref, base):
    index = lax.broadcasted_iota(jnp.int32, (16, 128), 0)
    tail = ref[tail_rows(plan, base), 0:128].astype(F32)
    row = jnp.sum(jnp.where(index >= 14, tail, 0.0), 0, keepdims=True)
    return jnp.sum(jnp.where(diagonal(plan), row, 0.0), 1, keepdims=True)


def head_split(value):
    first_head = lax.broadcasted_iota(jnp.int32, value.shape, 1) < HEAD_DIM
    nothing = jnp.zeros(value.shape, value.dtype)
    return jnp.concatenate(
        [jnp.where(first_head, value, nothing), jnp.where(first_head, nothing, value)], axis=0
    )


def head_join(value):
    rows = value.shape[0] // 2
    first_head = lax.broadcasted_iota(jnp.int32, (rows, 128), 1) < HEAD_DIM
    return jnp.where(first_head, value[:rows], value[rows:])


def first_norm(r, image):
    rows = image_rows(image)
    normed, _ = norm_parts(r.x[rows, :])
    r.h[rows, :] = (normed * r.gain[0:1, :] + r.bias[0:1, :]).astype(BF16)


def attend_forward(r, image, side):
    key_real = lax.broadcasted_iota(jnp.int32, (2 * PAD, PAD), 1) < SEQ
    rows = image_rows(image)
    proj = dot(r.h[rows, :], r.joint[side]).astype(BF16)
    r.qkv[side, rows, :] = proj
    query, keyed, valued = proj[:, :128], proj[:, 128:256], proj[:, 256:]
    scores = jnp.where(key_real, dot_nt(head_split(query * SCALE), keyed), -1e30)
    expd = jnp.exp(scores - jnp.max(scores, -1, keepdims=True))
    prob = (expd * (1.0 / jnp.sum(expd, -1, keepdims=True))).astype(BF16)
    r.prob[side, image] = prob
    r.mixed[side, rows, :] = head_join(dot(prob, valued)).astype(BF16)


def attend_out(r, total, image):
    rows = image_rows(image)
    mixed = jnp.concatenate([r.mixed[0, rows, :], r.mixed[1, rows, :]], axis=1)
    total.put(image, dot(mixed, r.out_all[...]))


def attend_backward(r, total, image):
    rows = image_rows(image)
    mixed_grads = dot_nt(r.gin[rows, :].astype(BF16), r.out_all[...])
    back = jnp.zeros((PAD, 512), F32)
    for side in range(2):
        proj = r.qkv[side, rows, :]
        query, keyed, valued = proj[:, :128], proj[:, 128:256], proj[:, 256:]
        grad = mixed_grads[:, side * 128 : (side + 1) * 128]
        mixed_grad = head_split(grad.astype(BF16))
        inner = jnp.sum(head_split(grad * r.mixed[side, rows, :].astype(F32)), -1, keepdims=True)
        prob = r.prob[side, image]
        prob_grad = dot_nt(mixed_grad, valued)
        score_grad = (prob.astype(F32) * (prob_grad - inner)).astype(BF16)
        query_grad = head_join(dot(score_grad, keyed)) * SCALE
        key_grad = dot_tn(score_grad, head_split(query * SCALE))
        value_grad = dot_tn(prob, mixed_grad)
        proj_grad = jnp.concatenate([query_grad, key_grad, value_grad], axis=1).astype(BF16)
        r.dproj[side, rows, :] = proj_grad
        back = back + dot_nt(proj_grad, r.joint[side])
    total.put(image, back)


def pack_out(plan, place, r):
    r.packed[0:512, :] = dot_tn(r.gin[...].astype(BF16), r.mixed[place.chip]).astype(BF16)


def pack_qkv(plan, place, r):
    grads = dot_tn(r.h[...], r.dproj[place.chip]).astype(BF16)
    for part in range(3):
        r.packed[(part + 1) * 512 : (part + 2) * 512, :] = grads[:, part * 128 : (part + 1) * 128]


def pack_small(plan, r):
    router = dot_tn(r.dz[...], r.h2[: plan.rows, :])[: plan.experts]
    rows = jnp.concatenate([r.vec[0:4, :], router], axis=0)
    rows = jnp.concatenate([rows[:, part * 128 : (part + 1) * 128] for part in range(4)], axis=0)
    spare = plan.packed - 2048 - rows.shape[0]
    r.packed[2048:, :] = jnp.concatenate([rows, jnp.zeros((spare, 128), F32)], axis=0).astype(BF16)


def second_norm(plan, r, total):
    def one(image):
        rows = image_rows(image)
        after = r.x[rows, :] + total.get(image)
        r.y[rows, :] = after
        normed, _ = norm_parts(after)
        r.h2[rows, :] = (normed * r.gain[1:2, :] + r.bias[1:2, :]).astype(BF16)

    if plan.lanes > plan.rows:
        r.h2[plan.rows :, :] = jnp.zeros((plan.lanes - plan.rows, 512), BF16)
    each(0, plan.images, one)


def send_slots(plan, place, r, move):
    r.send[...] = dot(r.member[...], r.h2[...]).astype(BF16)
    move.start_all(False)
    logits = dot_nt(r.router[: plan.experts, :], r.h2[...])
    expert_id = lax.broadcasted_iota(jnp.int32, (plan.experts, plan.lanes), 0)
    is_first, is_second = expert_id == r.route[0:1, :], expert_id == r.route[1:2, :]
    named = is_first | is_second
    shifted = jnp.where(named, logits, -1e30)
    top = jnp.max(shifted, 0, keepdims=True)
    expd = jnp.where(named, jnp.exp(shifted - top), 0.0)
    share = expd / jnp.maximum(jnp.sum(expd, 0, keepdims=True), 1e-30)
    r.gate[...] = share
    gate_first = jnp.sum(jnp.where(is_first, share, 0.0), 0, keepdims=True)
    gate_second = jnp.sum(jnp.where(is_second, share, 0.0), 0, keepdims=True)
    r.table[...] = jnp.concatenate(
        [r.codes[...], gate_first, gate_second, jnp.zeros((10, plan.lanes), F32)], axis=0
    ).T
    slot = lax.broadcasted_iota(jnp.int32, (plan.block, plan.lanes), 0).astype(F32)

    def one(step):
        expert = place.ahead(step)
        hit = r.place[pl.ds(expert, 1), :] == slot
        column = jnp.sum(jnp.where(hit, r.gate[pl.ds(expert, 1), :], 0.0), 1, keepdims=True)
        write_spare(plan, r.send, step * plan.block, column)

    each(0, plan.experts, one)
    move.start_all(True)


def read_gates(plan, r, low, high):
    def one(step):
        base = step * plan.block
        rows = pl.ds(pl.multiple_of(base, plan.block), plan.block)
        r.slot_gate[rows, :] = read_spare(plan, r.recv, base)

    each(low, high, one)


def groups(plan):
    return [(low, low + plan.group) for low in range(0, plan.experts, plan.group)]


def return_gradient(plan, r, low, high, value, column):
    r.gret[low * plan.block : high * plan.block, :] = value.astype(BF16)
    r.column[low * plan.block : high * plan.block, :] = column

    def one(step):
        base = step * plan.block
        rows = pl.ds(pl.multiple_of(base, plan.block), plan.block)
        write_spare(plan, r.gret, base, r.column[rows, :])

    each(low, high, one)


def expert_grads(plan, place, r, near):
    drecv, recv = r.dr[...], r.recv[...]
    for part in range(4):
        r.gpart[0, part] = dot_tn(recv, r.dpre[part]).astype(BF16)
        r.gpart[1, part] = dot_tn(r.act[part], drecv).astype(BF16)
    for which in range(2):
        for chip in range(2):
            PairSum.near(place, r.gpart, near, which, chip).start()


def near_sums(place, r, near):
    chip = place.tensor // 2
    inbox = near[0]
    for which in range(2):
        for side in range(2):
            PairSum.near(place, r.gpart, near, which, side).wait()
        for quarter, side in ((place.chip_peer, 1 - chip), (place.tensor, chip)):
            r.gpart[which, quarter] = (
                r.gpart[which, quarter].astype(F32) + inbox[which, side].astype(F32)
            ).astype(BF16)


def near_outs(place, r):
    return [
        pltpu.make_async_copy(r.gpart.at[which, quarter], out.at[which], r.out_sems.at[which, side])
        for which in range(2)
        for side, (quarter, out) in enumerate(((place.chip_peer, r.gfar), (place.tensor, r.gown)))
    ]


def combined(plan, r, chip, rows_in, out, add):
    rows = pl.ds(pl.multiple_of(chip * 2 * plan.slots, plan.slots), 2 * plan.slots)
    if plan.stored:
        value = dot(r.picks[chip], rows_in[rows, :])
        out[...] = out[...] + value if add else value
        return

    def one(image):
        picks = [picks_part(plan, r, image, 2 * chip + quarter) for quarter in range(2)]
        value = dot(jnp.concatenate(picks, axis=1), rows_in[rows, :])
        tokens = image_rows(image)
        out[tokens, :] = out[tokens, :] + value if add else value

    each(0, plan.images, one)


def norm_table(plan, r):
    def one(image):
        rows = image_rows(image)
        for source, column in ((r.y, 6), (r.x, 8)):
            value = source[rows, :]
            mean = jnp.mean(value, -1, keepdims=True)
            centered = value - mean
            r.table[rows, column : column + 1] = mean
            r.table[rows, column + 1 : column + 2] = lax.rsqrt(
                jnp.mean(centered * centered, -1, keepdims=True) + EPS
            )

    each(0, plan.images, one)


def norm_again(r, source, rows, column):
    scaled = r.table[rows, column + 1 : column + 2]
    return (source[rows, :] - r.table[rows, column : column + 1]) * scaled, scaled


def spread_gates(plan, place, r):
    def arrived(quarter, step):
        base = quarter * plan.slots + step * plan.block
        rows = pl.ds(pl.multiple_of(base, plan.block), plan.block)
        expert = place.ahead(step)
        lane = lax.broadcasted_iota(jnp.int32, (plan.block, 128), 1)
        r.gdg[rows, :] = jnp.where(lane == expert, read_spare(plan, r.gback, base), 0.0).astype(BF16)

    return arrived


def back_to_attention(plan, place, r, gback, between):
    arrived = spread_gates(plan, place, r)
    gback.pass_on(arrived)
    gback.near(arrived)
    combined(plan, r, place.chip, r.gdg, r.gated, False)
    combined(plan, r, place.chip, r.gback, r.gin, False)
    between()
    gback.far(arrived)
    combined(plan, r, 1 - place.chip, r.gdg, r.gated, True)
    combined(plan, r, 1 - place.chip, r.gback, r.gin, True)
    r.vec[...] = jnp.zeros_like(r.vec)

    def one(image):
        rows = image_rows(image)
        lane = lax.broadcasted_iota(jnp.int32, (PAD, 128), 1).astype(F32)
        share = jnp.where(
            lane == r.table[rows, 2:3], r.table[rows, 4:5],
            jnp.where(lane == r.table[rows, 3:4], r.table[rows, 5:6], 0.0),
        )
        gated = r.gated[rows, :]
        logit_grad = (gated - share * jnp.sum(gated, -1, keepdims=True)).astype(BF16)
        r.dz[rows, :] = logit_grad
        value = r.gin[rows, :] + dot(logit_grad, r.router[...])
        normed, scaled = norm_again(r, r.y, rows, 6)
        r.gin[rows, :] = r.g[rows, :].astype(F32) + norm_pull(
            value, normed, scaled, r.gain[1:2, :]
        )
        r.vec[1:2, :] += jnp.sum(value * normed, 0, keepdims=True)
        r.vec[3:4, :] += jnp.sum(value, 0, keepdims=True)

    each(0, plan.images, one)


def first_norm_back(plan, r, total, image):
    rows = image_rows(image)
    value = total.get(image)
    normed, scaled = norm_again(r, r.x, rows, 8)
    r.vec[0:1, :] += jnp.sum(value * normed, 0, keepdims=True)
    r.vec[2:3, :] += jnp.sum(value, 0, keepdims=True)
    return r.gin[rows, :] + norm_pull(value, normed, scaled, r.gain[0:1, :])


class Copies:
    def __init__(self, pairs, sems):
        self.copies = {
            key: pltpu.make_async_copy(src, dst, sems.at[index])
            for index, (key, (src, dst)) in enumerate(pairs.items())
        }

    def start(self, *keys):
        for key in keys:
            self.copies[key].start()

    def wait(self, *keys):
        for key in keys:
            self.copies[key].wait()


def run_kernel(name, body, inputs, outputs, scratch, collective_id, vmem, in_vmem=()):
    flat, layout = [], []
    for key, value in scratch.items():
        group = value if isinstance(value, list) else [value]
        layout.append((key, len(group), isinstance(value, list)))
        flat.extend(group)
    plain = list(inputs) + list(outputs)

    def kernel(*refs):
        named = dict(zip(plain, refs))
        at = len(plain)
        for key, size, grouped in layout:
            named[key] = refs[at : at + size] if grouped else refs[at]
            at += size
        body(types.SimpleNamespace(**named))

    def spec(key):
        return pl.BlockSpec(memory_space=VMEM if key in in_vmem else pl.ANY)

    results = pl.pallas_call(
        kernel,
        name=name,
        in_specs=[spec(key) for key in inputs],
        out_specs=tuple(spec(key) for key in outputs),
        out_shape=tuple(jax.ShapeDtypeStruct(*value) for value in outputs.values()),
        scratch_shapes=flat,
        compiler_params=pltpu.CompilerParams(
            collective_id=collective_id, has_side_effects=True, vmem_limit_bytes=vmem * MIB
        ),
    )(*inputs.values())
    return types.SimpleNamespace(**dict(zip(outputs, results)))


SMALL = ("route_all", "gain_all", "bias_all", "router_all")


def layer_views(r, layer):
    r.gain, r.bias = r.gain_all.at[layer], r.bias_all.at[layer]
    r.router = r.router_all.at[layer]
    if hasattr(r, "route_all"):
        r.route = r.route_all.at[layer]


def forward_shapes(plan):
    rows, lanes, slots = plan.rows, plan.lanes, plan.slots
    return {
        "joint": ((2, 512, 384), BF16),
        "out_all": ((256, 512), BF16),
        "x": ((rows, 512), F32),
        "y": ((rows, 512), F32),
        "h": ((rows, 512), BF16),
        "qkv": ((2, rows, 384), BF16),
        "prob": ((2, plan.images, 2 * PAD, PAD), BF16),
        "mixed": ((2, rows, 128), BF16),
        "h2": ((lanes, 512), BF16),
        "place": ((plan.experts, lanes), F32),
        "table": ((lanes, 16), F32),
        "recv": ((slots, 512), BF16),
        "ret": ((slots, 512), BF16),
        "slot_gate": ((slots, 1), F32),
        "up": ((4, 512, 512), BF16),
        "down": ((4, 512, 512), BF16),
    }


def as_scratch(shapes):
    return {key: VMEM(*value) for key, value in shapes.items()}


def as_saved(shapes):
    return {"out_" + key: value for key, value in shapes.items()}


def pad_images(plan, source, target, staging):
    tokens = plan.images * SEQ
    staging[0:tokens, :] = source[...].astype(F32)
    target[...] = jnp.zeros_like(target)
    for image in range(plan.images):
        target[image * PAD : image * PAD + SEQ, :] = staging[
            image * SEQ : (image + 1) * SEQ, :
        ].astype(target.dtype)


def first_forward(plan, inputs, tokens):
    saved = forward_shapes(plan)

    def body(r):
        place = Place(plan.experts)
        place.greet()
        layer_views(r, 0)
        swap = HeadSwap(
            place, r.w_qkv.at[0], r.w_out.at[0], r.joint, r.out_all, r.swap
        )
        later = HeadSwap(
            place, r.w_qkv.at[1], r.w_out.at[1], r.joint_later, r.out_later, r.swap_later
        )
        saves = Copies({k: (getattr(r, k), getattr(r, "out_" + k)) for k in saved}, r.saves)
        total = CoreSum(place, r.total)
        weights = WeightGather(
            place, (r.w_up.at[0, 0], r.w_down.at[0, 0]), (r.up, r.down), r.weights
        )
        move = Exchange(place, plan.block, r.send, r.recv, r.move)
        back = Return(place, plan.block, plan.slots, r.ret, r.back, r.back_sems)
        swap.start_own()
        pad_images(plan, r.tokens, r.x, r.y)
        saves.start("x")
        place.met()
        swap.start_swap()
        weights.start()
        later.start_own()
        later.start_swap()
        swap.wait_own()

        def own_heads(image):
            first_norm(r, image)
            attend_forward(r, image, place.chip)

        each(0, plan.images, own_heads)
        route_places(plan, place, r)
        build_members(plan, place, r)
        swap.wait_swap(range(3))
        each(0, plan.images, lambda image: attend_forward(r, image, 1 - place.chip))
        swap.wait_swap((3,))
        each(0, plan.images, lambda image: attend_out(r, total, image))
        saves.start("joint", "out_all", "h", "qkv", "prob", "mixed", "place")
        second_norm(plan, r, total)
        send_slots(plan, place, r, move)
        saves.start("y", "h2")
        norm_table(plan, r)
        saves.start("table")
        build_picks(plan, r)
        weights.pass_on()
        weights.finish()
        saves.start("up", "down")
        for low, high in groups(plan):
            move.wait(low, high, False)
            move.wait(low, high, True)
            read_gates(plan, r, low, high)
            rows = slice(low * plan.block, high * plan.block)
            rows_in = r.recv[rows, :]
            result = jnp.zeros((rows.stop - rows.start, 512), F32)
            for part in range(4):
                act = gelu(dot(rows_in, r.up[part])).astype(BF16)
                result = result + dot(act, r.down[part])
            r.ret[rows, :] = (result * r.slot_gate[rows, :]).astype(BF16)
            back.start(low, high)
        saves.start("recv", "ret", "slot_gate")
        saves.wait("x")
        back.pass_on()
        back.near()
        combined(plan, r, place.chip, r.back, r.x, False)
        back.far()
        combined(plan, r, 1 - place.chip, r.back, r.x, True)
        r.x[...] += r.y[...]
        back.finish()
        out = pltpu.make_async_copy(r.x, r.next, r.out_sem)
        out.start()
        saves.wait(*(k for k in saved if k != "x"))
        later.wait_own()
        later.wait_swap()
        out.wait()

    outputs = dict(
        as_saved(saved),
        next=((plan.rows, 512), F32),
        joint_later=saved["joint"],
        out_later=saved["out_all"],
    )
    scratch = dict(
        as_scratch(saved),
        codes=VMEM((4, plan.lanes), F32),
        member=VMEM((plan.slots, plan.lanes), BF16),
        gate=VMEM((plan.experts, plan.lanes), F32),
        picks=picks_scratch(plan),
        send=VMEM((plan.slots, 512), BF16),
        back=VMEM((4 * plan.slots, 512), BF16),
        total=CoreSum.scratch(plan.images),
        weights=WeightGather.scratch(),
        swap=HeadSwap.scratch(),
        swap_later=HeadSwap.scratch(),
        move=Exchange.scratch(plan.experts),
        back_sems=Return.scratch(plan.experts),
        saves=DMA((len(saved),)),
        out_sem=DMA,
    )
    return run_kernel(
        "first_forward", body, dict(inputs, tokens=tokens), outputs, scratch, 0, 62,
        SMALL + ("tokens",),
    )


def second_whole(plan, inputs, cotangent, start, joint, out_all):
    def body(r):
        place = Place(plan.experts)
        place.greet()
        layer_views(r, 1)
        r.gret, r.ret, r.dr, r.column = r.send, r.gsend, r.grecv, r.slot_gate
        loads = Copies(
            {k: (getattr(r, "in_" + k), getattr(r, k)) for k in ("x", "joint", "out_all")}, r.loads
        )
        total = CoreSum(place, r.total)
        total_back = CoreSum(place, r.total)
        weights = WeightGather(
            place, (r.w_up.at[1, 0], r.w_down.at[1, 0]), (r.up, r.down), r.weights
        )
        move = Exchange(place, plan.block, r.send, r.recv, r.move)
        gmove = Exchange(place, plan.block, r.gsend, r.grecv, r.gmove)
        back = Return(place, plan.block, plan.slots, r.ret, r.back, r.back_sems)
        gback = Return(place, plan.block, plan.slots, r.gret, r.gback, r.gback_sems)
        loads.start("x", "joint", "out_all")
        pad_images(plan, r.cotangent, r.g, r.y)
        route_places(plan, place, r)
        build_members(plan, place, r)
        r.gsend[...] = dot(r.member[:, : plan.rows], r.g[...]).astype(BF16)
        place.met()
        weights.start()
        gmove.start_all()
        loads.wait("x", "joint", "out_all")

        def heads(image):
            first_norm(r, image)
            for side in range(2):
                attend_forward(r, image, side)
            attend_out(r, total, image)

        each(0, plan.images, heads)
        second_norm(plan, r, total)
        send_slots(plan, place, r, move)
        norm_table(plan, r)
        build_picks(plan, r)
        weights.pass_on()
        weights.finish()
        gmove.wait(0, plan.experts)
        for low, high in groups(plan):
            move.wait(low, high, False)
            move.wait(low, high, True)
            read_gates(plan, r, low, high)
            rows = slice(low * plan.block, high * plan.block)
            rows_in = r.recv[rows, :]
            gate = r.slot_gate[rows, :]
            raw = r.grecv[rows, :].astype(F32)
            scaled = (raw * gate).astype(BF16)
            r.dr[rows, :] = scaled
            result = jnp.zeros((rows.stop - rows.start, 512), F32)
            slots_grad = jnp.zeros((rows.stop - rows.start, 512), F32)
            for part in range(4):
                act, slope = gelu_both(dot(rows_in, r.up[part]))
                act = act.astype(BF16)
                r.act[part, rows, :] = act
                result = result + dot(act, r.down[part])
                pre_grad = (dot_nt(scaled, r.down[part]) * slope).astype(BF16)
                r.dpre[part, rows, :] = pre_grad
                slots_grad = slots_grad + dot_nt(pre_grad, r.up[part])
            result = result * gate
            r.ret[rows, :] = result.astype(BF16)
            column = jnp.sum(result * raw, -1, keepdims=True)
            return_gradient(plan, r, low, high, slots_grad, column)
            gback.start(low, high)
        back.start(0, plan.experts)
        expert_grads(plan, place, r, r.near)
        outs = near_outs(place, r)

        def between():
            near_sums(place, r, r.near)
            for copy in outs:
                copy.start()

        back_to_attention(plan, place, r, gback, between)
        back.pass_on()
        each(0, plan.images, lambda image: attend_backward(r, total_back, image))
        pack_out(plan, place, r)
        pack_qkv(plan, place, r)

        def input_grad(image):
            rows = image_rows(image)
            r.gin[rows, :] = first_norm_back(plan, r, total_back, image)

        each(0, plan.images, input_grad)
        out = pltpu.make_async_copy(r.gin, r.grad, r.late_sems.at[0])
        out.start()
        pack_small(plan, r)
        out_packed = pltpu.make_async_copy(r.packed, r.out_packed, r.late_sems.at[1])
        out_packed.start()
        back.near()
        combined(plan, r, place.chip, r.back, r.x, False)
        back.far()
        combined(plan, r, 1 - place.chip, r.back, r.x, True)
        for image in range(plan.images):
            rows = slice(image * PAD, image * PAD + SEQ)
            r.y[image * SEQ : (image + 1) * SEQ, :] = r.y[rows, :] + r.x[rows, :]
        r.result[...] = r.y[0 : plan.images * SEQ, :].astype(BF16)
        back.finish()
        gback.finish()
        for copy in outs + [out, out_packed]:
            copy.wait()

    outputs = {
        "result": (cotangent.shape, BF16),
        "grad": ((plan.rows, 512), F32),
        "out_packed": ((plan.packed, 128), BF16),
        "gfar": ((2, 512, 512), BF16),
        "gown": ((2, 512, 512), BF16),
    }
    scratch = dict(
        as_scratch({k: v for k, v in forward_shapes(plan).items() if k != "ret"}),
        codes=VMEM((4, plan.lanes), F32),
        member=VMEM((plan.slots, plan.lanes), BF16),
        gate=VMEM((plan.experts, plan.lanes), F32),
        picks=picks_scratch(plan),
        send=VMEM((plan.slots, 512), BF16),
        back=VMEM((4 * plan.slots, 512), BF16),
        total=CoreSum.scratch(plan.images),
        weights=WeightGather.scratch(),
        move=Exchange.scratch(plan.experts),
        back_sems=Return.scratch(plan.experts),
        gmove=Exchange.scratch(plan.experts),
        gback_sems=Return.scratch(plan.experts),
        gsend=VMEM((plan.slots, 512), BF16),
        grecv=VMEM((plan.slots, 512), BF16),
        g=VMEM((plan.rows, 512), BF16),
        out_sems=DMA((2, 2)),
        late_sems=DMA((2,)),
        loads=DMA((3,)),
        **backward_scratch(plan),
    )
    return run_kernel(
        "second_whole", body,
        dict(inputs, cotangent=cotangent, in_x=start, in_joint=joint, in_out_all=out_all),
        outputs, scratch, 1, 63, SMALL + ("cotangent", "result"),
    )


def backward_scratch(plan):
    return {
        "gback": VMEM((4 * plan.slots, 512), BF16),
        "act": VMEM((4, plan.slots, 512), BF16),
        "dpre": VMEM((4, plan.slots, 512), BF16),
        "gpart": VMEM((2, 4, 512, 512), BF16),
        "gdg": VMEM((4 * plan.slots, 128), BF16),
        "gated": VMEM((plan.rows, 128), F32),
        "dz": VMEM((plan.rows, 128), BF16),
        "gin": VMEM((plan.rows, 512), F32),
        "dproj": VMEM((2, plan.rows, 384), BF16),
        "packed": VMEM((plan.packed, 128), BF16),
        "vec": VMEM((8, 512), F32),
        "near": PairSum.scratch_near(),
    }


def expert_out(place, r, layer, which):
    out = (r.grad_up, r.grad_down)[which]
    return pltpu.make_async_copy(
        r.y.at[pl.ds(which * 512, 512)], out.at[layer], r.expert_sems.at[layer, which]
    )


class Finals:
    def __init__(self, plan, r):
        self.plan, self.r = plan, r

    def write(self, layer, total):
        r, experts = self.r, self.plan.experts
        r.grad_out[layer] = total[0:512, :].astype(F32).T
        for part in range(3):
            r.grad_qkv[layer, part] = total[(part + 1) * 512 : (part + 2) * 512, :].astype(F32)
        count = 4 + experts
        small = total[2048 : 2048 + up_to(4 * count, 16), :].astype(F32)
        rows = jnp.concatenate(
            [small[part * count : (part + 1) * count] for part in range(4)], axis=1
        )
        r.grad_gain[layer] = rows[0:2]
        r.grad_bias[layer] = rows[2:4]
        r.grad_router[layer] = rows[4:]


def first_backward(plan, inputs, saved, grad, gfar, gown, packed, out_shape):
    def body(r):
        place = Place(plan.experts)
        place.greet()
        layer_views(r, 0)
        r.gret, r.dr, r.column = r.gsend, r.grecv, r.slot_gate
        r.x = r.g
        loads = Copies(
            {k: (getattr(r, "in_" + k), getattr(r, k)) for k in list(saved) + ["g", "later"]},
            r.loads,
        )
        total = CoreSum(place, r.total)
        gmove = Exchange(place, plan.block, r.gsend, r.grecv, r.gmove)
        gback = Return(place, plan.block, plan.slots, r.gret, r.gback, r.gback_sems)
        later = ExpertSum(place, plan.panels, r.later, r.sum_later, r.later_sum)
        sooner = ExpertSum(place, plan.panels, r.packed, r.sum_first, r.sooner_sum)
        first_loads = ("g", "place", "recv", "up", "down", "ret", "slot_gate", "table")
        loads.start(*first_loads)
        loads.start(*(k for k in loads.copies if k not in first_loads + ("x",)))
        loads.wait("place")
        build_members(plan, place, r)
        loads.wait("g")
        r.gsend[...] = dot(r.member[:, : plan.rows], r.g[...].astype(BF16)).astype(BF16)
        place.met()
        gmove.start_all()
        for which in range(2):
            PairSum.far(place, r.gfar_later.at[which], r.far_later, which).start()
        own_copy = pltpu.make_async_copy(r.gown_later, r.own_later, r.own_sem)
        own_copy.start()
        loads.wait("recv", "up", "down")
        for low, high in groups(plan):
            rows = slice(low * plan.block, high * plan.block)
            for part in range(4):
                act, slope = gelu_both(dot(r.recv[rows, :], r.up[part]))
                r.act[part, rows, :] = act.astype(BF16)
                r.dpre[part, rows, :] = slope.astype(BF16)
        loads.wait("table")
        build_picks(plan, r)
        loads.wait("ret", "slot_gate", "later")
        for low, high in groups(plan):
            gmove.wait(low, high)
            rows = slice(low * plan.block, high * plan.block)
            raw = r.grecv[rows, :].astype(F32)
            scaled = (raw * r.slot_gate[rows, :]).astype(BF16)
            r.dr[rows, :] = scaled
            slots_grad = jnp.zeros((rows.stop - rows.start, 512), F32)
            for part in range(4):
                pre_grad = (
                    dot_nt(scaled, r.down[part]) * r.dpre[part, rows, :].astype(F32)
                ).astype(BF16)
                r.dpre[part, rows, :] = pre_grad
                slots_grad = slots_grad + dot_nt(pre_grad, r.up[part])
            column = jnp.sum(r.ret[rows, :].astype(F32) * raw, -1, keepdims=True)
            return_gradient(plan, r, low, high, slots_grad, column)
            gback.start(low, high)
        expert_grads(plan, place, r, r.near)

        def between():
            later.every(later.step_pair)
            near_sums(place, r, r.near)
            for which in range(2):
                PairSum.far(place, r.gpart.at[which, place.chip_peer], r.far, which).start()

        loads.wait(*(k for k in loads.copies if k not in first_loads + ("later", "x")))
        back_to_attention(plan, place, r, gback, between)
        loads.start("x")
        later.every(later.step_scatter)
        pack_out(plan, place, r)
        sooner.step_pair(0)
        own_copy.wait()
        outs = [expert_out(place, r, layer, which) for layer in range(2) for which in range(2)]
        for which in range(2):
            PairSum.far(place, r.gfar_later.at[which], r.far_later, which).wait()
            r.y[which * 512 : (which + 1) * 512, :] = (
                r.own_later[which].astype(F32) + r.far_later[0][which].astype(F32)
            )
            outs[2 + which].start()
        half = plan.images // 2
        each(0, half, lambda image: attend_backward(r, total, image))
        later.every(later.step_share)
        sooner.step_scatter(0)
        each(half, plan.images, lambda image: attend_backward(r, total, image))
        pack_qkv(plan, place, r)
        panels = len(plan.panels)
        for panel in range(1, panels - 1):
            sooner.step_pair(panel)
        later.every(later.step_out)
        loads.wait("x")
        for image in range(plan.images):
            out = first_norm_back(plan, r, total, image)
            r.grad[image * SEQ : (image + 1) * SEQ, :] = out[:SEQ]
        pack_small(plan, r)
        sooner.step_pair(panels - 1)
        for panel in range(1, panels):
            sooner.step_scatter(panel)
        later.every(later.step_end)
        finals = Finals(plan, r)
        finals.write(1, r.sum_later)
        sooner.every(sooner.step_share)
        for which in range(2):
            outs[2 + which].wait()
            PairSum.far(place, r.gpart.at[which, place.chip_peer], r.far, which).wait()
            r.y[which * 512 : (which + 1) * 512, :] = (
                r.gpart[which, place.tensor].astype(F32) + r.far[0][which].astype(F32)
            )
            outs[which].start()
        gback.finish()
        sooner.every(sooner.step_out)
        sooner.every(sooner.step_end)
        finals.write(0, r.sum_first)
        for which in range(2):
            outs[which].wait()

    outputs = {
        "grad": (out_shape, F32),
        "grad_up": ((2, 512, 512), F32),
        "grad_down": ((2, 512, 512), F32),
        "grad_qkv": ((2, 3, 512, 128), F32),
        "grad_out": ((2, 128, 512), F32),
        "grad_gain": ((2, 2, 512), F32),
        "grad_bias": ((2, 2, 512), F32),
        "grad_router": ((2, plan.experts, 512), F32),
    }
    scratch = dict(
        as_scratch({k: v for k, v in forward_shapes(plan).items() if k != "x"}),
        member=VMEM((plan.slots, plan.lanes), BF16),
        picks=picks_scratch(plan),
        total=CoreSum.scratch(plan.images),
        gmove=Exchange.scratch(plan.experts),
        gback_sems=Return.scratch(plan.experts),
        gsend=VMEM((plan.slots, 512), BF16),
        grecv=VMEM((plan.slots, 512), BF16),
        g=VMEM((plan.rows, 512), F32),
        later=VMEM((plan.packed, 128), BF16),
        own_later=VMEM((2, 512, 512), BF16),
        sum_first=VMEM((plan.packed, 128), BF16),
        sum_later=VMEM((plan.packed, 128), BF16),
        expert_sems=DMA((2, 2)),
        own_sem=DMA,
        far=PairSum.scratch_far(),
        far_later=PairSum.scratch_far(),
        later_sum=ExpertSum.scratch(plan),
        sooner_sum=ExpertSum.scratch(plan),
        loads=DMA((len(saved) + 2,)),
        **backward_scratch(plan),
    )
    arrays = dict({"in_" + k: v for k, v in saved.items()}, in_g=grad, in_later=packed)
    return run_kernel(
        "first_backward", body,
        dict(inputs, gfar_later=gfar, gown_later=gown, **arrays),
        outputs, scratch, 2, 63,
        SMALL + tuple(k for k in outputs if k not in ("grad_up", "grad_down")),
    )


def body(tokens, routes, ln_gain, ln_bias, w_qkv, w_out, w_router, w_up, w_down, cotangent):
    tok_rows = tokens.shape[0]
    experts = w_router.shape[2]
    plan = Plan(tok_rows, experts)
    route_rows = routes.reshape(2, plan.images, SEQ, 2)
    route_rows = jnp.pad(
        route_rows, ((0, 0), (0, 0), (0, PAD - SEQ), (0, 0)), constant_values=-1
    ).reshape(2, plan.rows, 2)
    route_rows = jnp.pad(
        route_rows, ((0, 0), (0, plan.lanes - plan.rows), (0, 0)), constant_values=-1
    ).transpose(0, 2, 1)
    router_rows = jnp.pad(w_router.transpose(0, 2, 1), ((0, 0), (0, 128 - experts), (0, 0)))
    small = {"gain_all": ln_gain, "bias_all": ln_bias, "router_all": router_rows}
    weights = {"w_up": w_up, "w_down": w_down}
    one = first_forward(
        plan, dict(small, route_all=route_rows, w_qkv=w_qkv, w_out=w_out, **weights), tokens
    )
    two = second_whole(
        plan, dict(small, route_all=route_rows, **weights), cotangent,
        one.next, one.joint_later, one.out_later,
    )
    saved = {key: getattr(one, "out_" + key) for key in forward_shapes(plan)}
    three = first_backward(
        plan, small, saved, two.grad, two.gfar, two.gown, two.out_packed, tokens.shape
    )
    return (
        two.result, three.grad, three.grad_gain, three.grad_bias[:, 0], three.grad_bias[:, 1],
        three.grad_qkv, three.grad_out, three.grad_router.transpose(0, 2, 1),
        three.grad_up[:, None], three.grad_down[:, None],
    )


def solution(mesh):
    in_specs = (
        P("expert", None),
        P(None, "expert", None),
        P(),
        P(),
        P(None, None, None, "tensor"),
        P(None, "tensor", None),
        P(),
        P(None, "expert", None, "tensor"),
        P(None, "expert", "tensor", None),
        P("expert", None),
    )
    out_specs = (
        P("expert", None),
        P("expert", None),
        P(),
        P(),
        P(),
        P(None, None, None, "tensor"),
        P(None, "tensor", None),
        P(),
        P(None, "expert", None, "tensor"),
        P(None, "expert", "tensor", None),
    )
    return jax.shard_map(body, mesh=mesh, in_specs=in_specs, out_specs=out_specs, check_vma=False)
```

```python
import types

import jax
import jax.numpy as jnp
from jax import lax
from jax.experimental import pallas as pl
from jax.experimental.pallas import tpu as pltpu
from jax.sharding import PartitionSpec as P

HEAD_DIM = 64
SEQ = 197
PAD = 208
EPS = 1e-06
MESH = pl.DeviceIdType.MESH
EXPERT, TENSOR = "expert", "tensor"
F32 = jnp.float32
BF16 = jnp.bfloat16
SCALE = HEAD_DIM ** (-0.5)
MIB = 1 << 20
VMEM = pltpu.VMEM
DMA = pltpu.SemaphoreType.DMA


def up_to(count, multiple):
    return -(-count // multiple) * multiple


def dot(left, right):
    return lax.dot_general(left, right, (((1,), (0,)), ((), ())), preferred_element_type=F32)


def dot_nt(left, right):
    return lax.dot_general(left, right, (((1,), (1,)), ((), ())), preferred_element_type=F32)


def dot_tn(left, right):
    return lax.dot_general(left, right, (((0,), (0,)), ((), ())), preferred_element_type=F32)


def norm_parts(rows):
    centered = rows - jnp.mean(rows, -1, keepdims=True)
    scaled = lax.rsqrt(jnp.mean(centered * centered, -1, keepdims=True) + EPS)
    return centered * scaled, scaled


def norm_pull(grad_in, normed, scaled, gain_row):
    grad_normed = grad_in * gain_row
    inner = (
        grad_normed
        - jnp.mean(grad_normed, -1, keepdims=True)
        - normed * jnp.mean(grad_normed * normed, -1, keepdims=True)
    )
    return inner * scaled


def gelu(pre):
    inner = pre * (0.7978845608028654 + 0.035677408136300125 * (pre * pre))
    return 0.5 * pre * (1.0 + jnp.tanh(inner))


def gelu_both(pre):
    square = pre * pre
    inner = pre * (0.7978845608028654 + 0.035677408136300125 * square)
    bent = jnp.tanh(inner)
    half = 0.5 + 0.5 * bent
    slope = half + half * (1.0 - bent) * pre * (
        0.7978845608028654 + 0.10703222440890037 * square
    )
    return half * pre, slope


class Plan:
    def __init__(self, tok_rows, experts):
        self.images = tok_rows // SEQ
        self.rows = self.images * PAD
        self.lanes = up_to(self.rows, 128)
        self.experts = experts
        self.per_rank = max(1, 10 * tok_rows // (4 * experts * 4))
        self.capacity = 4 * self.per_rank
        self.block = up_to(self.per_rank + 2, 16)
        self.slots = experts * self.block
        self.blocks = up_to(4 * experts, 128)
        self.stored = 4 * self.slots <= 2560
        most = 320
        self.group = max(
            size for size in range(1, experts)
            if experts % size == 0 and (size == 1 or size * self.block <= most)
        )
        main = up_to(512, 16 * experts)
        small = up_to(4 * (4 + experts), 16 * experts)
        self.panels = [(start, main) for start in range(0, 2048, main)] + [(2048, small)]
        self.packed = 2048 + small


def image_rows(image):
    if isinstance(image, int):
        return pl.ds(image * PAD, PAD)
    return pl.ds(pl.multiple_of(image * PAD, PAD), PAD)


def each(low, high, use):
    def one(index, carry):
        use(index)
        return carry

    lax.fori_loop(low, high, one, 0)


def few(low, high, use):
    if high - low > 8:
        each(low, high, use)
        return
    for index in range(low, high):
        use(index)


class Place:
    def __init__(self, experts):
        self.tensor = lax.axis_index(TENSOR)
        self.core = lax.rem(self.tensor, 2)
        self.chip = lax.div(self.tensor, 2)
        self.core_peer = self.tensor + 1 - 2 * self.core
        self.chip_peer = lax.rem(self.tensor + 2, 4)
        self.experts = experts
        self.expert = lax.axis_index(EXPERT)

    def ahead(self, step):
        return lax.rem(self.expert + step, self.experts)

    def behind(self, step):
        return lax.rem(self.expert + self.experts - step, self.experts)

    def greet(self):
        barrier = pltpu.get_barrier_semaphore()
        for peer in (self.core_peer, self.chip_peer):
            pl.semaphore_signal(barrier, inc=1, device_id={TENSOR: peer}, device_id_type=MESH)

        def one(step):
            pl.semaphore_signal(
                barrier, inc=1, device_id={EXPERT: self.ahead(step)}, device_id_type=MESH
            )

        each(1, self.experts, one)

    def met(self):
        pl.semaphore_wait(pltpu.get_barrier_semaphore(), 2 + self.experts - 1)

    def to_core(self, src, dst, send, recv):
        return pltpu.make_async_remote_copy(
            src_ref=src, dst_ref=dst, send_sem=send, recv_sem=recv,
            device_id={TENSOR: self.core_peer}, device_id_type=MESH,
        )

    def to_chip(self, src, dst, send, recv):
        return pltpu.make_async_remote_copy(
            src_ref=src, dst_ref=dst, send_sem=send, recv_sem=recv,
            device_id={TENSOR: self.chip_peer}, device_id_type=MESH,
        )

    def to_expert(self, expert, src, dst, send, recv):
        return pltpu.make_async_remote_copy(
            src_ref=src, dst_ref=dst, send_sem=send, recv_sem=recv,
            device_id={EXPERT: expert}, device_id_type=MESH,
        )


class CoreSum:
    def __init__(self, place, refs):
        self.place = place
        self.part, self.near, self.send, self.recv = refs

    @staticmethod
    def scratch(images):
        rows = (images * PAD, 512)
        return [VMEM(rows, BF16), VMEM(rows, BF16), DMA((images,)), DMA((images,))]

    def copy(self, image):
        rows = image_rows(image)
        return self.place.to_core(
            self.part.at[rows], self.near.at[rows], self.send.at[image], self.recv.at[image]
        )

    def put(self, image, value):
        self.part[image_rows(image), :] = value.astype(BF16)
        self.copy(image).start()

    def get(self, image):
        rows = image_rows(image)
        self.copy(image).wait()
        return self.part[rows, :].astype(F32) + self.near[rows, :].astype(F32)


class HeadSwap:
    def __init__(self, place, qkv, out, joint, out_all, refs):
        self.place, self.qkv, self.out = place, qkv, out
        self.joint, self.out_all = joint, out_all
        self.send, self.recv, self.local = refs

    @staticmethod
    def scratch():
        return [DMA((4,)), DMA((4,)), DMA((4,))]

    def ends(self, part):
        if part == 3:
            rows = pl.ds(pl.multiple_of(self.place.chip * 128, 128), 128)
            return self.out, self.out_all.at[rows]
        columns = pl.ds(part * 128, 128)
        return self.qkv.at[part], self.joint.at[self.place.chip, :, columns]

    def own(self, part):
        return pltpu.make_async_copy(*self.ends(part), self.local.at[part])

    def swap(self, part):
        return self.place.to_chip(*self.ends(part), self.send.at[part], self.recv.at[part])

    def start_own(self):
        for part in range(4):
            self.own(part).start()

    def start_swap(self):
        for part in range(4):
            self.swap(part).start()

    def wait_own(self):
        for part in range(4):
            self.own(part).wait()

    def wait_swap(self, parts=range(4)):
        for part in parts:
            self.swap(part).wait()


class Exchange:
    def __init__(self, place, block, src, dst, refs):
        self.place, self.block, self.src, self.dst = place, block, src, dst
        self.send, self.recv, self.local = refs

    @staticmethod
    def scratch(experts):
        return [DMA((2, experts)), DMA((2, experts)), DMA((2,))]

    def part(self, step, tail):
        base = pl.multiple_of(step * self.block, self.block)
        if tail is None:
            return pl.ds(base, self.block)
        if tail:
            return pl.ds(pl.multiple_of(base + self.block - 16, 16), 16)
        return pl.ds(base, self.block - 16)

    def own(self, tail=None):
        rows = self.part(0, tail)
        return pltpu.make_async_copy(
            self.src.at[rows], self.dst.at[rows], self.local.at[int(bool(tail))]
        )

    def copy(self, step, tail=None):
        rows, which = self.part(step, tail), int(bool(tail))
        return self.place.to_expert(
            self.place.ahead(step), self.src.at[rows], self.dst.at[rows],
            self.send.at[which, step], self.recv.at[which, step],
        )

    def start_all(self, tail=None):
        self.own(tail).start()
        each(1, self.place.experts, lambda step: self.copy(step, tail).start())

    def wait(self, low, high, tail=None):
        if low == 0:
            self.own(tail).wait()
        each(max(1, low), high, lambda step: self.copy(step, tail).wait())


class Return:
    def __init__(self, place, block, slots, src, dst, refs):
        self.place, self.block, self.slots, self.src, self.dst = place, block, slots, src, dst
        self.send, self.recv, self.local = refs

    @staticmethod
    def scratch(experts):
        return [DMA((4, experts)), DMA((4, experts)), DMA]

    def rows(self, quarter, step):
        return pl.ds(
            pl.multiple_of(quarter * self.slots + step * self.block, self.block), self.block
        )

    def own(self):
        return pltpu.make_async_copy(
            self.src.at[pl.ds(0, self.block)],
            self.dst.at[self.rows(self.place.tensor, 0)], self.local,
        )

    def home(self, step):
        rows = pl.ds(pl.multiple_of(step * self.block, self.block), self.block)
        return self.place.to_expert(
            self.place.behind(step), self.src.at[rows],
            self.dst.at[self.rows(self.place.tensor, step)],
            self.send.at[0, step], self.recv.at[0, step],
        )

    def to_chip(self, step):
        block = self.dst.at[self.rows(self.place.tensor, step)]
        return self.place.to_chip(block, block, self.send.at[1, step], self.recv.at[1, step])

    def to_core(self, step):
        block = self.dst.at[self.rows(self.place.tensor, step)]
        return self.place.to_core(block, block, self.send.at[2, step], self.recv.at[2, step])

    def on_to_core(self, step):
        block = self.dst.at[self.rows(self.place.chip_peer, step)]
        return self.place.to_core(block, block, self.send.at[3, step], self.recv.at[3, step])

    def start(self, low, high):
        if low == 0:
            self.own().start()
        each(max(1, low), high, lambda step: self.home(step).start())

    def pass_on(self, arrived=lambda quarter, step: None):
        place, last = self.place, self.place.experts

        def give(step):
            self.to_chip(step).start()
            self.to_core(step).start()
            arrived(place.tensor, step)

        def one(step):
            self.home(step).wait_recv()
            give(step)

        def two(step):
            one(step)
            self.on(step - self.LAG, arrived)

        self.own().wait()
        give(0)
        each(1, self.LAG, one)
        each(self.LAG, last, two)

    LAG = 4

    def on(self, step, arrived):
        self.to_chip(step).wait_recv()
        self.on_to_core(step).start()
        arrived(self.place.chip_peer, step)

    def near(self, arrived=lambda quarter, step: None):
        def one(step):
            self.to_core(step).wait_recv()
            arrived(self.place.core_peer, step)

        each(0, self.place.experts, one)

    def far(self, arrived=lambda quarter, step: None):
        place, last = self.place, self.place.experts
        each(last - self.LAG, last, lambda step: self.on(step, arrived))

        def one(step):
            self.on_to_core(step).wait_recv()
            arrived(3 - place.tensor, step)

        each(0, last, one)

    def finish(self):
        def one(step):
            self.to_chip(step).wait_send()
            self.to_core(step).wait_send()
            self.on_to_core(step).wait_send()

        each(0, self.place.experts, one)
        each(1, self.place.experts, lambda step: self.home(step).wait_send())


class WeightGather:
    def __init__(self, place, shards, wholes, refs):
        self.place, self.shards, self.wholes = place, shards, wholes
        self.send, self.recv, self.local = refs

    @staticmethod
    def scratch():
        return [DMA((2, 3)), DMA((2, 3)), DMA((2,))]

    def own(self, which):
        return pltpu.make_async_copy(
            self.shards[which], self.wholes[which].at[self.place.tensor], self.local.at[which]
        )

    def to_chip(self, which):
        return self.place.to_chip(
            self.shards[which], self.wholes[which].at[self.place.tensor],
            self.send.at[which, 0], self.recv.at[which, 0],
        )

    def to_core(self, which):
        return self.place.to_core(
            self.shards[which], self.wholes[which].at[self.place.tensor],
            self.send.at[which, 1], self.recv.at[which, 1],
        )

    def on_to_core(self, which):
        part = self.wholes[which].at[self.place.chip_peer]
        return self.place.to_core(
            part, part, self.send.at[which, 2], self.recv.at[which, 2]
        )

    def start(self):
        for which in range(2):
            self.own(which).start()
            self.to_chip(which).start()
            self.to_core(which).start()

    def pass_on(self):
        for which in range(2):
            self.to_chip(which).wait()
            self.on_to_core(which).start()

    def finish(self):
        for which in range(2):
            self.own(which).wait()
            self.to_core(which).wait()
            self.on_to_core(which).wait()


class ExpertSum:
    def __init__(self, place, panels, src, total, refs):
        self.place, self.panels, self.src, self.total = place, panels, src, total
        self.inbox, self.chunks, self.send, self.recv = refs
        self.side = lax.rem(place.expert, 2)
        self.pair = place.expert + 1 - 2 * self.side
        self.group = place.experts // 2
        self.index = lax.div(place.expert, 2)

    @staticmethod
    def scratch(plan):
        panels = len(plan.panels)
        half = plan.packed // 2
        return [
            VMEM((half, 128), BF16), VMEM((half, 128), BF16),
            DMA((2, panels, max(2, plan.experts // 2))), DMA((2, panels, max(2, plan.experts // 2))),
        ]

    def half(self, panel, side):
        start, rows = self.panels[panel]
        return pl.ds(pl.multiple_of(start + side * (rows // 2), 16), rows // 2)

    def local(self, panel):
        start, rows = self.panels[panel]
        return pl.ds(start // 2, rows // 2)

    def chunk(self, panel, index):
        start, rows = self.panels[panel]
        size = rows // self.place.experts
        return pl.ds(pl.multiple_of(start // 2 + index * size, 16), size)

    def chunk_whole(self, panel, index):
        start, rows = self.panels[panel]
        size = rows // self.place.experts
        return pl.ds(pl.multiple_of(start + self.side * (rows // 2) + index * size, 16), size)

    def member(self, step):
        return lax.rem(self.place.expert + 2 * step, self.place.experts)

    def pair_in(self, panel):
        return self.place.to_expert(
            self.pair, self.src.at[self.half(panel, 1 - self.side)],
            self.inbox.at[self.local(panel)],
            self.send.at[0, panel, 0], self.recv.at[0, panel, 0],
        )

    def scatter(self, panel, step):
        peer = lax.rem(self.index + step, self.group)
        return self.place.to_expert(
            self.member(step), self.src.at[self.chunk_whole(panel, peer)],
            self.chunks.at[self.chunk(panel, step)],
            self.send.at[0, panel, step], self.recv.at[0, panel, step],
        )

    def share(self, panel, step):
        mine = self.total.at[self.chunk_whole(panel, self.index)]
        return self.place.to_expert(
            self.member(step), mine, mine,
            self.send.at[1, panel, step], self.recv.at[1, panel, step],
        )

    def pair_out(self, panel):
        half = self.total.at[self.half(panel, self.side)]
        return self.place.to_expert(
            self.pair, half, half, self.send.at[1, panel, 0], self.recv.at[1, panel, 0]
        )

    def step_pair(self, panel):
        self.pair_in(panel).start()

    def step_scatter(self, panel):
        self.pair_in(panel).wait()
        mine = self.half(panel, self.side)
        self.src[mine, :] = (
            self.src[mine, :].astype(F32) + self.inbox[self.local(panel), :].astype(F32)
        ).astype(BF16)
        each(1, self.group, lambda step: self.scatter(panel, step).start())

    def step_share(self, panel):
        mine = self.chunk_whole(panel, self.index)

        def one(step, total):
            self.scatter(panel, step).wait()
            return total + self.chunks[self.chunk(panel, step), :].astype(F32)

        total = lax.fori_loop(1, self.group, one, self.src[mine, :].astype(F32))
        self.total[mine, :] = total.astype(BF16)
        each(1, self.group, lambda step: self.share(panel, step).start())

    def step_out(self, panel):
        each(1, self.group, lambda step: self.share(panel, step).wait())
        self.pair_out(panel).start()

    def step_end(self, panel):
        self.pair_out(panel).wait()

    def every(self, step):
        for panel in range(len(self.panels)):
            step(panel)


class PairSum:
    @staticmethod
    def scratch_near():
        return [VMEM((2, 2, 512, 512), BF16), DMA((2, 2)), DMA((2, 2))]

    @staticmethod
    def scratch_far():
        return [VMEM((2, 512, 512), BF16), DMA((2,)), DMA((2,))]

    @staticmethod
    def near(place, part, refs, which, chip):
        inbox, send, recv = refs
        quarter = 2 * chip + 1 - place.core
        return place.to_core(
            part.at[which, quarter], inbox.at[which, chip],
            send.at[which, chip], recv.at[which, chip],
        )

    @staticmethod
    def far(place, out, refs, which):
        inbox, send, recv = refs
        return place.to_chip(out, inbox.at[which], send.at[which], recv.at[which])


def route_places(plan, place, r):
    shape = (plan.experts, plan.lanes)
    expert_id = lax.broadcasted_iota(jnp.int32, shape, 0)
    lane = lax.broadcasted_iota(jnp.int32, shape, 1)
    first, second = r.route[0:1, :], r.route[1:2, :]
    is_first, is_second = expert_id == first, expert_id == second
    named = is_first | is_second
    count = jnp.where(named, 1.0, 0.0)
    running = count
    step = 1
    while step < plan.lanes:
        running = running + jnp.where(lane >= step, pltpu.roll(running, step, 1), 0.0)
        step *= 2
    before = running - count
    mine = before - (place.tensor * plan.per_rank).astype(F32)
    valid = named & (mine >= 0.0) & (mine < float(plan.per_rank))
    r.place[...] = jnp.where(valid, mine, -1.0)
    quarter = jnp.zeros(shape, F32)
    for bound in range(1, 4):
        quarter = quarter + jnp.where(before >= float(bound * plan.per_rank), 1.0, 0.0)
    step_of = expert_id - place.expert
    step_of = jnp.where(step_of < 0, step_of + plan.experts, step_of).astype(F32)
    code = (
        quarter * float(plan.slots - plan.per_rank) + step_of * float(plan.block) + before
    )
    kept = before < float(plan.capacity)
    nowhere = -1.0
    code_first = jnp.max(jnp.where(is_first & kept, code, nowhere), 0, keepdims=True)
    code_second = jnp.max(jnp.where(is_second & kept, code, nowhere), 0, keepdims=True)
    r.codes[...] = jnp.concatenate(
        [code_first, code_second, first.astype(F32), second.astype(F32)], axis=0
    )


def build_members(plan, place, r):
    slot = lax.broadcasted_iota(jnp.int32, (plan.block, plan.lanes), 0).astype(F32)

    def one(step):
        rows = pl.ds(pl.multiple_of(step * plan.block, plan.block), plan.block)
        hit = r.place[pl.ds(place.ahead(step), 1), :] == slot
        r.member[rows, :] = jnp.where(hit, 1.0, 0.0).astype(BF16)

    each(0, plan.experts, one)


def picks_part(plan, r, image, quarter):
    slot = lax.broadcasted_iota(jnp.int32, (PAD, plan.slots), 1) + quarter * plan.slots
    slot = slot.astype(F32)
    rows = image_rows(image)
    hit = (r.table[rows, 0:1] == slot) | (r.table[rows, 1:2] == slot)
    return jnp.where(hit, 1.0, 0.0).astype(BF16)


def build_picks(plan, r):
    if not plan.stored:
        return
    for quarter in range(4):
        columns = slice(quarter % 2 * plan.slots, (quarter % 2 + 1) * plan.slots)

        def one(image):
            r.picks[quarter // 2, image_rows(image), columns] = picks_part(
                plan, r, image, quarter
            )

        each(0, plan.images, one)


def picks_scratch(plan):
    return VMEM((2, plan.rows, 2 * plan.slots) if plan.stored else (2, 16, 128), BF16)


def diagonal(plan):
    shape = (plan.block, 128)
    return lax.broadcasted_iota(jnp.int32, shape, 0) == lax.broadcasted_iota(jnp.int32, shape, 1)


def tail_rows(plan, base):
    return pl.ds(pl.multiple_of(base + plan.block - 16, 16), 16)


def write_spare(plan, ref, base, column):
    row = jnp.sum(jnp.where(diagonal(plan), column, 0.0), 0, keepdims=True)
    high = row.astype(BF16).astype(F32)
    rest = jnp.zeros((1, 512 - 128), F32)
    high_row = jnp.concatenate([high, rest], axis=1)
    low_row = jnp.concatenate([row - high, rest], axis=1)
    rows = tail_rows(plan, base)
    index = lax.broadcasted_iota(jnp.int32, (16, 512), 0)
    old = ref[rows, :].astype(F32)
    ref[rows, :] = jnp.where(index == 14, high_row, jnp.where(index == 15, low_row, old)).astype(
        BF16
    )


def read_spare(plan, ref, base):
    index = lax.broadcasted_iota(jnp.int32, (16, 128), 0)
    tail = ref[tail_rows(plan, base), 0:128].astype(F32)
    row = jnp.sum(jnp.where(index >= 14, tail, 0.0), 0, keepdims=True)
    return jnp.sum(jnp.where(diagonal(plan), row, 0.0), 1, keepdims=True)


def head_split(value):
    first_head = lax.broadcasted_iota(jnp.int32, value.shape, 1) < HEAD_DIM
    nothing = jnp.zeros(value.shape, value.dtype)
    return jnp.concatenate(
        [jnp.where(first_head, value, nothing), jnp.where(first_head, nothing, value)], axis=0
    )


def head_join(value):
    rows = value.shape[0] // 2
    first_head = lax.broadcasted_iota(jnp.int32, (rows, 128), 1) < HEAD_DIM
    return jnp.where(first_head, value[:rows], value[rows:])


def first_norm(r, image):
    rows = image_rows(image)
    normed, _ = norm_parts(r.x[rows, :])
    r.h[rows, :] = (normed * r.gain[0:1, :] + r.bias[0:1, :]).astype(BF16)


def attend_forward(r, image, side):
    key_real = lax.broadcasted_iota(jnp.int32, (2 * PAD, PAD), 1) < SEQ
    rows = image_rows(image)
    proj = dot(r.h[rows, :], r.joint[side]).astype(BF16)
    r.qkv[side, rows, :] = proj
    query, keyed, valued = proj[:, :128], proj[:, 128:256], proj[:, 256:]
    scores = jnp.where(key_real, dot_nt(head_split(query * SCALE), keyed), -1e30)
    expd = jnp.exp(scores - jnp.max(scores, -1, keepdims=True))
    prob = (expd * (1.0 / jnp.sum(expd, -1, keepdims=True))).astype(BF16)
    r.prob[side, image] = prob
    r.mixed[side, rows, :] = head_join(dot(prob, valued)).astype(BF16)


def attend_out(r, total, image):
    rows = image_rows(image)
    mixed = jnp.concatenate([r.mixed[0, rows, :], r.mixed[1, rows, :]], axis=1)
    total.put(image, dot(mixed, r.out_all[...]))


def attend_backward(r, total, image):
    rows = image_rows(image)
    mixed_grads = dot_nt(r.gin[rows, :].astype(BF16), r.out_all[...])
    back = jnp.zeros((PAD, 512), F32)
    for side in range(2):
        proj = r.qkv[side, rows, :]
        query, keyed, valued = proj[:, :128], proj[:, 128:256], proj[:, 256:]
        grad = mixed_grads[:, side * 128 : (side + 1) * 128]
        mixed_grad = head_split(grad.astype(BF16))
        inner = jnp.sum(head_split(grad * r.mixed[side, rows, :].astype(F32)), -1, keepdims=True)
        prob = r.prob[side, image]
        prob_grad = dot_nt(mixed_grad, valued)
        score_grad = (prob.astype(F32) * (prob_grad - inner)).astype(BF16)
        query_grad = head_join(dot(score_grad, keyed)) * SCALE
        key_grad = dot_tn(score_grad, head_split(query * SCALE))
        value_grad = dot_tn(prob, mixed_grad)
        proj_grad = jnp.concatenate([query_grad, key_grad, value_grad], axis=1).astype(BF16)
        r.dproj[side, rows, :] = proj_grad
        back = back + dot_nt(proj_grad, r.joint[side])
    total.put(image, back)


def pack_out(plan, place, r):
    r.packed[0:512, :] = dot_tn(r.gin[...].astype(BF16), r.mixed[place.chip]).astype(BF16)


def pack_qkv(plan, place, r):
    grads = dot_tn(r.h[...], r.dproj[place.chip]).astype(BF16)
    for part in range(3):
        r.packed[(part + 1) * 512 : (part + 2) * 512, :] = grads[:, part * 128 : (part + 1) * 128]


def pack_small(plan, r):
    router = dot_tn(r.dz[...], r.h2[: plan.rows, :])[: plan.experts]
    rows = jnp.concatenate([r.vec[0:4, :], router], axis=0)
    rows = jnp.concatenate([rows[:, part * 128 : (part + 1) * 128] for part in range(4)], axis=0)
    spare = plan.packed - 2048 - rows.shape[0]
    r.packed[2048:, :] = jnp.concatenate([rows, jnp.zeros((spare, 128), F32)], axis=0).astype(BF16)


def second_norm(plan, r, total):
    def one(image):
        rows = image_rows(image)
        after = r.x[rows, :] + total.get(image)
        r.y[rows, :] = after
        normed, _ = norm_parts(after)
        r.h2[rows, :] = (normed * r.gain[1:2, :] + r.bias[1:2, :]).astype(BF16)

    if plan.lanes > plan.rows:
        r.h2[plan.rows :, :] = jnp.zeros((plan.lanes - plan.rows, 512), BF16)
    few(0, plan.images, one)


def send_slots(plan, place, r, move):
    r.send[...] = dot(r.member[...], r.h2[...]).astype(BF16)
    move.start_all(False)
    logits = dot_nt(r.router[: plan.experts, :], r.h2[...])
    expert_id = lax.broadcasted_iota(jnp.int32, (plan.experts, plan.lanes), 0)
    is_first, is_second = expert_id == r.route[0:1, :], expert_id == r.route[1:2, :]
    named = is_first | is_second
    shifted = jnp.where(named, logits, -1e30)
    top = jnp.max(shifted, 0, keepdims=True)
    expd = jnp.where(named, jnp.exp(shifted - top), 0.0)
    share = expd / jnp.maximum(jnp.sum(expd, 0, keepdims=True), 1e-30)
    r.gate[...] = share
    gate_first = jnp.sum(jnp.where(is_first, share, 0.0), 0, keepdims=True)
    gate_second = jnp.sum(jnp.where(is_second, share, 0.0), 0, keepdims=True)
    r.table[...] = jnp.concatenate(
        [r.codes[...], gate_first, gate_second, jnp.zeros((10, plan.lanes), F32)], axis=0
    ).T
    slot = lax.broadcasted_iota(jnp.int32, (plan.block, plan.lanes), 0).astype(F32)

    def one(step):
        expert = place.ahead(step)
        hit = r.place[pl.ds(expert, 1), :] == slot
        column = jnp.sum(jnp.where(hit, r.gate[pl.ds(expert, 1), :], 0.0), 1, keepdims=True)
        write_spare(plan, r.send, step * plan.block, column)

    few(0, plan.experts, one)
    move.start_all(True)


def read_gates(plan, r, low, high):
    def one(step):
        base = step * plan.block
        rows = pl.ds(pl.multiple_of(base, plan.block), plan.block)
        r.slot_gate[rows, :] = read_spare(plan, r.recv, base)

    few(low, high, one)


def groups(plan):
    return [(low, low + plan.group) for low in range(0, plan.experts, plan.group)]


def return_gradient(plan, r, low, high, value, column):
    r.gret[low * plan.block : high * plan.block, :] = value.astype(BF16)
    r.column[low * plan.block : high * plan.block, :] = column

    def one(step):
        base = step * plan.block
        rows = pl.ds(pl.multiple_of(base, plan.block), plan.block)
        write_spare(plan, r.gret, base, r.column[rows, :])

    few(low, high, one)


def expert_grads(plan, place, r, near):
    drecv, recv = r.dr[...], r.recv[...]
    for part in range(4):
        r.gpart[0, part] = dot_tn(recv, r.dpre[part]).astype(BF16)
        r.gpart[1, part] = dot_tn(r.act[part], drecv).astype(BF16)
    for which in range(2):
        for chip in range(2):
            PairSum.near(place, r.gpart, near, which, chip).start()


def near_sums(place, r, near):
    chip = place.tensor // 2
    inbox = near[0]
    for which in range(2):
        for side in range(2):
            PairSum.near(place, r.gpart, near, which, side).wait()
        for quarter, side in ((place.chip_peer, 1 - chip), (place.tensor, chip)):
            r.gpart[which, quarter] = (
                r.gpart[which, quarter].astype(F32) + inbox[which, side].astype(F32)
            ).astype(BF16)


def near_outs(place, r):
    return [
        pltpu.make_async_copy(r.gpart.at[which, quarter], out.at[which], r.out_sems.at[which, side])
        for which in range(2)
        for side, (quarter, out) in enumerate(((place.chip_peer, r.gfar), (place.tensor, r.gown)))
    ]


def combined(plan, r, chip, rows_in, out, add):
    rows = pl.ds(pl.multiple_of(chip * 2 * plan.slots, plan.slots), 2 * plan.slots)
    if plan.stored:
        value = dot(r.picks[chip], rows_in[rows, :])
        out[...] = out[...] + value if add else value
        return

    def one(image):
        picks = [picks_part(plan, r, image, 2 * chip + quarter) for quarter in range(2)]
        value = dot(jnp.concatenate(picks, axis=1), rows_in[rows, :])
        tokens = image_rows(image)
        out[tokens, :] = out[tokens, :] + value if add else value

    each(0, plan.images, one)


def norm_table(plan, r):
    def one(image):
        rows = image_rows(image)
        for source, column in ((r.y, 6), (r.x, 8)):
            value = source[rows, :]
            mean = jnp.mean(value, -1, keepdims=True)
            centered = value - mean
            r.table[rows, column : column + 1] = mean
            r.table[rows, column + 1 : column + 2] = lax.rsqrt(
                jnp.mean(centered * centered, -1, keepdims=True) + EPS
            )

    few(0, plan.images, one)


def norm_again(r, source, rows, column):
    scaled = r.table[rows, column + 1 : column + 2]
    return (source[rows, :] - r.table[rows, column : column + 1]) * scaled, scaled


def keep_gates(plan, r):
    def arrived(quarter, step):
        tail = tail_rows(plan, quarter * plan.slots + step * plan.block)
        rows = r.gback[tail, 0:128].astype(F32)
        index = quarter * plan.experts + step
        r.high[pl.ds(index, 1), :] = rows[14:15]
        r.low[pl.ds(index, 1), :] = rows[15:16]

    return arrived


def pick_gates(plan, r, rows, column):
    code = r.table[rows, column : column + 1]
    block = jnp.floor((code + 0.5) * (1.0 / plan.block))
    inside = code - block * float(plan.block)
    lane = lax.broadcasted_iota(jnp.int32, (PAD, plan.blocks), 1).astype(F32)
    chosen = jnp.where(lane == block, 1.0, 0.0).astype(BF16)
    values = dot(chosen, r.high[...].astype(BF16)) + dot(chosen, r.low[...].astype(BF16))
    lane = lax.broadcasted_iota(jnp.int32, (PAD, 128), 1).astype(F32)
    return jnp.sum(jnp.where(lane == inside, values, 0.0), -1, keepdims=True)


def back_to_attention(plan, place, r, gback, between):
    arrived = keep_gates(plan, r)
    r.high[...] = jnp.zeros_like(r.high)
    r.low[...] = jnp.zeros_like(r.low)
    gback.pass_on(arrived)
    gback.near(arrived)
    combined(plan, r, place.chip, r.gback, r.gin, False)
    between()
    gback.far(arrived)
    combined(plan, r, 1 - place.chip, r.gback, r.gin, True)
    r.vec[...] = jnp.zeros_like(r.vec)

    def one(image):
        rows = image_rows(image)
        lane = lax.broadcasted_iota(jnp.int32, (PAD, 128), 1).astype(F32)
        first, second = pick_gates(plan, r, rows, 0), pick_gates(plan, r, rows, 1)
        both = first + second
        logit_grad = jnp.where(
            lane == r.table[rows, 2:3], first - r.table[rows, 4:5] * both,
            jnp.where(lane == r.table[rows, 3:4], second - r.table[rows, 5:6] * both, 0.0),
        ).astype(BF16)
        r.dz[rows, :] = logit_grad
        value = r.gin[rows, :] + dot(logit_grad, r.router[...])
        normed, scaled = norm_again(r, r.y, rows, 6)
        r.gin[rows, :] = r.g[rows, :].astype(F32) + norm_pull(
            value, normed, scaled, r.gain[1:2, :]
        )
        r.vec[1:2, :] += jnp.sum(value * normed, 0, keepdims=True)
        r.vec[3:4, :] += jnp.sum(value, 0, keepdims=True)

    few(0, plan.images, one)


def first_norm_back(plan, r, total, image):
    rows = image_rows(image)
    value = total.get(image)
    normed, scaled = norm_again(r, r.x, rows, 8)
    r.vec[0:1, :] += jnp.sum(value * normed, 0, keepdims=True)
    r.vec[2:3, :] += jnp.sum(value, 0, keepdims=True)
    return r.gin[rows, :] + norm_pull(value, normed, scaled, r.gain[0:1, :])


class Copies:
    def __init__(self, pairs, sems):
        self.copies = {
            key: pltpu.make_async_copy(src, dst, sems.at[index])
            for index, (key, (src, dst)) in enumerate(pairs.items())
        }

    def start(self, *keys):
        for key in keys:
            self.copies[key].start()

    def wait(self, *keys):
        for key in keys:
            self.copies[key].wait()


def run_kernel(name, body, inputs, outputs, scratch, collective_id, vmem, in_vmem=()):
    flat, layout = [], []
    for key, value in scratch.items():
        group = value if isinstance(value, list) else [value]
        layout.append((key, len(group), isinstance(value, list)))
        flat.extend(group)
    plain = list(inputs) + list(outputs)

    def kernel(*refs):
        named = dict(zip(plain, refs))
        at = len(plain)
        for key, size, grouped in layout:
            named[key] = refs[at : at + size] if grouped else refs[at]
            at += size
        body(types.SimpleNamespace(**named))

    def spec(key):
        return pl.BlockSpec(memory_space=VMEM if key in in_vmem else pl.ANY)

    results = pl.pallas_call(
        kernel,
        name=name,
        in_specs=[spec(key) for key in inputs],
        out_specs=tuple(spec(key) for key in outputs),
        out_shape=tuple(jax.ShapeDtypeStruct(*value) for value in outputs.values()),
        scratch_shapes=flat,
        compiler_params=pltpu.CompilerParams(
            collective_id=collective_id, has_side_effects=True, vmem_limit_bytes=int(vmem * MIB)
        ),
    )(*inputs.values())
    return types.SimpleNamespace(**dict(zip(outputs, results)))


ATTENDED = ("joint", "out_all", "h", "qkv", "prob", "mixed")
SMALL = ("route_all", "gain_all", "bias_all", "router_all")
KEPT = ("routes",) + SMALL[1:]


def layer_views(r, layer):
    r.gain, r.bias = r.gain_all.at[layer], r.bias_all.at[layer]
    r.router = r.router_all.at[layer]
    if hasattr(r, "route_all"):
        r.route = r.route_all.at[layer]


def forward_shapes(plan):
    rows, lanes, slots = plan.rows, plan.lanes, plan.slots
    return dict(
        joint=((2, 512, 384), BF16),
        out_all=((256, 512), BF16),
        x=((rows, 512), F32),
        y=((rows, 512), F32),
        h=((rows, 512), BF16),
        qkv=((2, rows, 384), BF16),
        prob=((2, plan.images, 2 * PAD, PAD), BF16),
        mixed=((2, rows, 128), BF16),
        h2=((lanes, 512), BF16),
        place=((plan.experts, lanes), F32),
        table=((lanes, 16), F32),
        recv=((slots, 512), BF16),
        ret=((slots, 512), BF16),
        slot_gate=((slots, 1), F32),
        up=((4, 512, 512), BF16),
        down=((4, 512, 512), BF16),
    )


def as_scratch(shapes):
    return {key: VMEM(*value) for key, value in shapes.items()}


def as_saved(shapes):
    return {"out_" + key: value for key, value in shapes.items()}


def pad_images(plan, source, target, staging):
    tokens = plan.images * SEQ
    staging[0:tokens, :] = source[...].astype(F32)
    target[...] = jnp.zeros_like(target)
    for image in range(plan.images):
        target[image * PAD : image * PAD + SEQ, :] = staging[
            image * SEQ : (image + 1) * SEQ, :
        ].astype(target.dtype)


def first_forward(plan, inputs, tokens):
    saved = forward_shapes(plan)

    def body(r):
        place = Place(plan.experts)
        place.greet()
        layer_views(r, 0)
        swap = HeadSwap(
            place, r.w_qkv.at[0], r.w_out.at[0], r.joint, r.out_all, r.swap
        )
        later = HeadSwap(
            place, r.w_qkv.at[1], r.w_out.at[1], r.joint_later, r.out_later, r.swap_later
        )
        saves = Copies({k: (getattr(r, k), getattr(r, "out_" + k)) for k in saved}, r.saves)
        total = CoreSum(place, r.total)
        weights = WeightGather(
            place, (r.w_up.at[0, 0], r.w_down.at[0, 0]), (r.up, r.down), r.weights
        )
        move = Exchange(place, plan.block, r.send, r.recv, r.move)
        back = Return(place, plan.block, plan.slots, r.ret, r.back, r.back_sems)
        swap.start_own()
        pad_images(plan, r.tokens, r.x, r.y)
        saves.start("x")
        place.met()
        swap.start_swap()
        weights.start()
        later.start_own()
        later.start_swap()
        swap.wait_own()

        def own_heads(image):
            first_norm(r, image)
            attend_forward(r, image, place.chip)

        each(0, plan.images, own_heads)
        route_places(plan, place, r)
        build_members(plan, place, r)
        swap.wait_swap(range(3))
        each(0, plan.images, lambda image: attend_forward(r, image, 1 - place.chip))
        swap.wait_swap((3,))
        each(0, plan.images, lambda image: attend_out(r, total, image))
        saves.start(*ATTENDED, "place")
        second_norm(plan, r, total)
        send_slots(plan, place, r, move)
        saves.start("y", "h2")
        norm_table(plan, r)
        saves.start("table")
        build_picks(plan, r)
        weights.pass_on()
        weights.finish()
        saves.start("up", "down")
        for low, high in groups(plan):
            move.wait(low, high, False)
            move.wait(low, high, True)
            read_gates(plan, r, low, high)
            rows = slice(low * plan.block, high * plan.block)
            rows_in = r.recv[rows, :]
            result = jnp.zeros((rows.stop - rows.start, 512), F32)
            for part in range(4):
                act = gelu(dot(rows_in, r.up[part])).astype(BF16)
                result = result + dot(act, r.down[part])
            r.ret[rows, :] = (result * r.slot_gate[rows, :]).astype(BF16)
            back.start(low, high)
        saves.start("recv", "ret", "slot_gate")
        saves.wait("x")
        back.pass_on()
        back.near()
        combined(plan, r, place.chip, r.back, r.x, False)
        back.far()
        combined(plan, r, 1 - place.chip, r.back, r.x, True)
        r.x[...] += r.y[...]
        back.finish()
        out = pltpu.make_async_copy(r.x, r.next, r.out_sem)
        out.start()
        saves.wait(*(k for k in saved if k != "x"))
        later.wait_own()
        later.wait_swap()
        out.wait()

    outputs = dict(
        as_saved(saved),
        next=((plan.rows, 512), F32),
        joint_later=saved["joint"],
        out_later=saved["out_all"],
    )
    scratch = dict(
        as_scratch(saved),
        codes=VMEM((4, plan.lanes), F32),
        member=VMEM((plan.slots, plan.lanes), BF16),
        gate=VMEM((plan.experts, plan.lanes), F32),
        picks=picks_scratch(plan),
        send=VMEM((plan.slots, 512), BF16),
        back=VMEM((4 * plan.slots, 512), BF16),
        total=CoreSum.scratch(plan.images),
        weights=WeightGather.scratch(),
        swap=HeadSwap.scratch(),
        swap_later=HeadSwap.scratch(),
        move=Exchange.scratch(plan.experts),
        back_sems=Return.scratch(plan.experts),
        saves=DMA((len(saved),)),
        out_sem=DMA,
    )
    return run_kernel(
        "first_forward", body, dict(inputs, tokens=tokens), outputs, scratch, 0, 62,
        SMALL + ("tokens",),
    )


def second_whole(plan, inputs, cotangent, start, joint, out_all):
    def body(r):
        place = Place(plan.experts)
        place.greet()
        layer_views(r, 1)
        r.gret, r.ret, r.dr, r.column = r.send, r.gsend, r.grecv, r.slot_gate
        loads = Copies(
            {k: (getattr(r, "in_" + k), getattr(r, k)) for k in ("x", "joint", "out_all")}, r.loads
        )
        total = CoreSum(place, r.total)
        total_back = CoreSum(place, r.total)
        weights = WeightGather(
            place, (r.w_up.at[1, 0], r.w_down.at[1, 0]), (r.up, r.down), r.weights
        )
        move = Exchange(place, plan.block, r.send, r.recv, r.move)
        gmove = Exchange(place, plan.block, r.gsend, r.grecv, r.gmove)
        back = Return(place, plan.block, plan.slots, r.ret, r.back, r.back_sems)
        gback = Return(place, plan.block, plan.slots, r.gret, r.gback, r.gback_sems)
        loads.start("x", "joint", "out_all")
        pad_images(plan, r.cotangent, r.g, r.y)
        route_places(plan, place, r)
        build_members(plan, place, r)
        r.gsend[...] = dot(r.member[:, : plan.rows], r.g[...]).astype(BF16)
        place.met()
        weights.start()
        gmove.start_all()
        loads.wait("x", "joint", "out_all")

        def heads(image):
            first_norm(r, image)
            for side in range(2):
                attend_forward(r, image, side)
            attend_out(r, total, image)

        each(0, plan.images, heads)
        second_norm(plan, r, total)
        send_slots(plan, place, r, move)
        norm_table(plan, r)
        build_picks(plan, r)
        weights.pass_on()
        weights.finish()
        gmove.wait(0, plan.experts)
        for low, high in groups(plan):
            move.wait(low, high, False)
            move.wait(low, high, True)
            read_gates(plan, r, low, high)
            rows = slice(low * plan.block, high * plan.block)
            rows_in = r.recv[rows, :]
            gate = r.slot_gate[rows, :]
            raw = r.grecv[rows, :].astype(F32)
            scaled = (raw * gate).astype(BF16)
            r.dr[rows, :] = scaled
            result = jnp.zeros((rows.stop - rows.start, 512), F32)
            slots_grad = jnp.zeros((rows.stop - rows.start, 512), F32)
            for part in range(4):
                act, slope = gelu_both(dot(rows_in, r.up[part]))
                act = act.astype(BF16)
                r.act[part, rows, :] = act
                result = result + dot(act, r.down[part])
                pre_grad = (dot_nt(scaled, r.down[part]) * slope).astype(BF16)
                r.dpre[part, rows, :] = pre_grad
                slots_grad = slots_grad + dot_nt(pre_grad, r.up[part])
            result = result * gate
            r.ret[rows, :] = result.astype(BF16)
            column = jnp.sum(result * raw, -1, keepdims=True)
            return_gradient(plan, r, low, high, slots_grad, column)
            gback.start(low, high)
        back.start(0, plan.experts)
        expert_grads(plan, place, r, r.near)
        outs = near_outs(place, r)

        def between():
            near_sums(place, r, r.near)
            for copy in outs:
                copy.start()

        back_to_attention(plan, place, r, gback, between)
        back.pass_on()
        each(0, plan.images, lambda image: attend_backward(r, total_back, image))
        pack_out(plan, place, r)
        pack_qkv(plan, place, r)

        def input_grad(image):
            rows = image_rows(image)
            r.gin[rows, :] = first_norm_back(plan, r, total_back, image)

        each(0, plan.images, input_grad)
        out = pltpu.make_async_copy(r.gin, r.grad, r.late_sems.at[0])
        out.start()
        pack_small(plan, r)
        out_packed = pltpu.make_async_copy(r.packed, r.out_packed, r.late_sems.at[1])
        out_packed.start()
        back.near()
        combined(plan, r, place.chip, r.back, r.x, False)
        back.far()
        combined(plan, r, 1 - place.chip, r.back, r.x, True)
        for image in range(plan.images):
            rows = slice(image * PAD, image * PAD + SEQ)
            r.y[image * SEQ : (image + 1) * SEQ, :] = r.y[rows, :] + r.x[rows, :]
        r.result[...] = r.y[0 : plan.images * SEQ, :].astype(BF16)
        back.finish()
        gback.finish()
        for copy in outs + [out, out_packed]:
            copy.wait()

    outputs = {
        "result": (cotangent.shape, BF16),
        "grad": ((plan.rows, 512), F32),
        "out_packed": ((plan.packed, 128), BF16),
        "gfar": ((2, 512, 512), BF16),
        "gown": ((2, 512, 512), BF16),
    }
    scratch = dict(
        as_scratch({k: v for k, v in forward_shapes(plan).items() if k != "ret"}),
        codes=VMEM((4, plan.lanes), F32),
        member=VMEM((plan.slots, plan.lanes), BF16),
        gate=VMEM((plan.experts, plan.lanes), F32),
        picks=picks_scratch(plan),
        send=VMEM((plan.slots, 512), BF16),
        back=VMEM((4 * plan.slots, 512), BF16),
        total=CoreSum.scratch(plan.images),
        weights=WeightGather.scratch(),
        move=Exchange.scratch(plan.experts),
        back_sems=Return.scratch(plan.experts),
        gmove=Exchange.scratch(plan.experts),
        gback_sems=Return.scratch(plan.experts),
        gsend=VMEM((plan.slots, 512), BF16),
        grecv=VMEM((plan.slots, 512), BF16),
        g=VMEM((plan.rows, 512), BF16),
        out_sems=DMA((2, 2)),
        late_sems=DMA((2,)),
        loads=DMA((3,)),
        **backward_scratch(plan),
    )
    return run_kernel(
        "second_whole", body,
        dict(inputs, cotangent=cotangent, in_x=start, in_joint=joint, in_out_all=out_all),
        outputs, scratch, 1, 63, SMALL + ("cotangent", "result"),
    )


def backward_scratch(plan):
    return dict(
        gback=VMEM((4 * plan.slots, 512), BF16),
        act=VMEM((4, plan.slots, 512), BF16),
        dpre=VMEM((4, plan.slots, 512), BF16),
        gpart=VMEM((2, 4, 512, 512), BF16),
        high=VMEM((plan.blocks, 128), F32),
        low=VMEM((plan.blocks, 128), F32),
        dz=VMEM((plan.rows, 128), BF16),
        gin=VMEM((plan.rows, 512), F32),
        dproj=VMEM((2, plan.rows, 384), BF16),
        packed=VMEM((plan.packed, 128), BF16),
        vec=VMEM((8, 512), F32),
        near=PairSum.scratch_near(),
    )


def expert_out(place, r, layer, which):
    out = (r.grad_up, r.grad_down)[which]
    return pltpu.make_async_copy(
        r.y.at[pl.ds(which * 512, 512)], out.at[layer], r.expert_sems.at[layer, which]
    )


class Finals:
    def __init__(self, plan, r):
        self.plan, self.r = plan, r

    def write(self, layer, total):
        r, experts = self.r, self.plan.experts
        r.grad_out[layer] = total[0:512, :].astype(F32).T
        for part in range(3):
            r.grad_qkv[layer, part] = total[(part + 1) * 512 : (part + 2) * 512, :].astype(F32)
        count = 4 + experts
        small = total[2048 : 2048 + up_to(4 * count, 16), :].astype(F32)
        rows = jnp.concatenate(
            [small[part * count : (part + 1) * count] for part in range(4)], axis=1
        )
        r.grad_gain[layer] = rows[0:2]
        if self.plan.stored:
            r.grad_bias_one[layer : layer + 1, :] = rows[2:3]
            r.grad_bias_two[layer : layer + 1, :] = rows[3:4]
        else:
            r.grad_bias[layer] = rows[2:4]
        r.grad_router[layer] = rows[4:]


def first_backward(plan, inputs, saved, grad, gfar, gown, packed, out_shape):
    def body(r):
        place = Place(plan.experts)
        place.greet()
        layer_views(r, 0)
        r.gret, r.dr, r.column = r.gsend, r.grecv, r.slot_gate
        r.x = r.g
        loads = Copies(
            {k: (getattr(r, "in_" + k), getattr(r, k)) for k in list(saved) + ["g", "later"]},
            r.loads,
        )
        total = CoreSum(place, r.total)
        gmove = Exchange(place, plan.block, r.gsend, r.grecv, r.gmove)
        gback = Return(place, plan.block, plan.slots, r.gret, r.gback, r.gback_sems)
        later = ExpertSum(place, plan.panels, r.later, r.sum_later, r.later_sum)
        sooner = ExpertSum(place, plan.panels, r.packed, r.sum_first, r.sooner_sum)
        first_loads = ("g", "place", "recv", "up", "down", "ret", "slot_gate", "table")
        loads.start(*first_loads)
        loads.start(*(k for k in loads.copies if k not in first_loads + ("x",)))
        loads.wait("place")
        build_members(plan, place, r)
        loads.wait("g")
        r.gsend[...] = dot(r.member[:, : plan.rows], r.g[...].astype(BF16)).astype(BF16)
        place.met()
        gmove.start_all()
        for which in range(2):
            PairSum.far(place, r.gfar_later.at[which], r.far_later, which).start()
        own_copy = pltpu.make_async_copy(r.gown_later, r.own_later, r.own_sem)
        own_copy.start()
        loads.wait("recv", "up", "down")
        for low, high in groups(plan):
            rows = slice(low * plan.block, high * plan.block)
            for part in range(4):
                act, slope = gelu_both(dot(r.recv[rows, :], r.up[part]))
                r.act[part, rows, :] = act.astype(BF16)
                r.dpre[part, rows, :] = slope.astype(BF16)
        loads.wait("table")
        build_picks(plan, r)
        loads.wait("ret", "slot_gate", "later")
        for low, high in groups(plan):
            gmove.wait(low, high)
            rows = slice(low * plan.block, high * plan.block)
            raw = r.grecv[rows, :].astype(F32)
            scaled = (raw * r.slot_gate[rows, :]).astype(BF16)
            r.dr[rows, :] = scaled
            slots_grad = jnp.zeros((rows.stop - rows.start, 512), F32)
            for part in range(4):
                pre_grad = (
                    dot_nt(scaled, r.down[part]) * r.dpre[part, rows, :].astype(F32)
                ).astype(BF16)
                r.dpre[part, rows, :] = pre_grad
                slots_grad = slots_grad + dot_nt(pre_grad, r.up[part])
            column = jnp.sum(r.ret[rows, :].astype(F32) * raw, -1, keepdims=True)
            return_gradient(plan, r, low, high, slots_grad, column)
            gback.start(low, high)
        expert_grads(plan, place, r, r.near)

        def between():
            later.every(later.step_pair)
            near_sums(place, r, r.near)
            for which in range(2):
                PairSum.far(place, r.gpart.at[which, place.chip_peer], r.far, which).start()

        loads.wait(*(k for k in loads.copies if k not in first_loads + ("later", "x")))
        back_to_attention(plan, place, r, gback, between)
        loads.start("x")
        later.every(later.step_scatter)
        pack_out(plan, place, r)
        sooner.step_pair(0)
        own_copy.wait()
        outs = [expert_out(place, r, layer, which) for layer in range(2) for which in range(2)]
        for which in range(2):
            PairSum.far(place, r.gfar_later.at[which], r.far_later, which).wait()
            r.y[which * 512 : (which + 1) * 512, :] = (
                r.own_later[which].astype(F32) + r.far_later[0][which].astype(F32)
            )
            outs[2 + which].start()
        half = plan.images // 2
        each(0, half, lambda image: attend_backward(r, total, image))
        later.every(later.step_share)
        sooner.step_scatter(0)
        each(half, plan.images, lambda image: attend_backward(r, total, image))
        pack_qkv(plan, place, r)
        panels = len(plan.panels)
        for panel in range(1, panels - 1):
            sooner.step_pair(panel)
        later.every(later.step_out)
        loads.wait("x")
        for image in range(plan.images):
            out = first_norm_back(plan, r, total, image)
            r.grad[image * SEQ : (image + 1) * SEQ, :] = out[:SEQ]
        pack_small(plan, r)
        sooner.step_pair(panels - 1)
        for panel in range(1, panels):
            sooner.step_scatter(panel)
        later.every(later.step_end)
        finals = Finals(plan, r)
        finals.write(1, r.sum_later)
        sooner.every(sooner.step_share)
        for which in range(2):
            outs[2 + which].wait()
            PairSum.far(place, r.gpart.at[which, place.chip_peer], r.far, which).wait()
            r.y[which * 512 : (which + 1) * 512, :] = (
                r.gpart[which, place.tensor].astype(F32) + r.far[0][which].astype(F32)
            )
            outs[which].start()
        gback.finish()
        sooner.every(sooner.step_out)
        sooner.every(sooner.step_end)
        finals.write(0, r.sum_first)
        for which in range(2):
            outs[which].wait()

    outputs = {
        "grad": (out_shape, F32),
        "grad_up": ((2, 512, 512), F32),
        "grad_down": ((2, 512, 512), F32),
        "grad_qkv": ((2, 3, 512, 128), F32),
        "grad_out": ((2, 128, 512), F32),
        "grad_gain": ((2, 2, 512), F32),
        "grad_bias": ((2, 2, 512), F32),
        "grad_router": ((2, plan.experts, 512), F32),
    }
    scratch = dict(
        as_scratch({k: v for k, v in forward_shapes(plan).items() if k != "x"}),
        member=VMEM((plan.slots, plan.lanes), BF16),
        picks=picks_scratch(plan),
        total=CoreSum.scratch(plan.images),
        gmove=Exchange.scratch(plan.experts),
        gback_sems=Return.scratch(plan.experts),
        gsend=VMEM((plan.slots, 512), BF16),
        grecv=VMEM((plan.slots, 512), BF16),
        g=VMEM((plan.rows, 512), F32),
        later=VMEM((plan.packed, 128), BF16),
        own_later=VMEM((2, 512, 512), BF16),
        sum_first=VMEM((plan.packed, 128), BF16),
        sum_later=VMEM((plan.packed, 128), BF16),
        expert_sems=DMA((2, 2)),
        own_sem=DMA,
        far=PairSum.scratch_far(),
        far_later=PairSum.scratch_far(),
        later_sum=ExpertSum.scratch(plan),
        sooner_sum=ExpertSum.scratch(plan),
        loads=DMA((len(saved) + 2,)),
        **backward_scratch(plan),
    )
    arrays = dict({"in_" + k: v for k, v in saved.items()}, in_g=grad, in_later=packed)
    return run_kernel(
        "first_backward", body,
        dict(inputs, gfar_later=gfar, gown_later=gown, **arrays),
        outputs, scratch, 2, 63,
        SMALL + tuple(k for k in outputs if k not in ("grad_up", "grad_down")),
    )


def expert_forward_backward(plan, r, low, high):
    rows = slice(low * plan.block, high * plan.block)
    rows_in = r.recv[rows, :]
    gate = r.slot_gate[rows, :]
    raw = r.grecv[rows, :].astype(F32)
    scaled = (raw * gate).astype(BF16)
    r.dr[rows, :] = scaled
    result = jnp.zeros((rows.stop - rows.start, 512), F32)
    slots_grad = jnp.zeros((rows.stop - rows.start, 512), F32)
    for part in range(4):
        act, slope = gelu_both(dot(rows_in, r.up[part]))
        act = act.astype(BF16)
        r.act[part, rows, :] = act
        result = result + dot(act, r.down[part])
        pre_grad = (dot_nt(scaled, r.down[part]) * slope).astype(BF16)
        r.dpre[part, rows, :] = pre_grad
        slots_grad = slots_grad + dot_nt(pre_grad, r.up[part])
    result = result * gate
    r.ret[rows, :] = result.astype(BF16)
    column = jnp.sum(result * raw, -1, keepdims=True)
    return_gradient(plan, r, low, high, slots_grad, column)


def expert_forward(plan, r, low, high):
    rows = slice(low * plan.block, high * plan.block)
    rows_in = r.recv[rows, :]
    result = jnp.zeros((rows.stop - rows.start, 512), F32)
    for part in range(4):
        act = gelu(dot(rows_in, r.up[part])).astype(BF16)
        result = result + dot(act, r.down[part])
    r.ret[rows, :] = (result * r.slot_gate[rows, :]).astype(BF16)


def expert_again(plan, r, low, high):
    rows = slice(low * plan.block, high * plan.block)
    for part in range(4):
        act, slope = gelu_both(dot(r.recv[rows, :], r.up[part]))
        r.act[part, rows, :] = act.astype(BF16)
        r.dpre[part, rows, :] = slope.astype(BF16)


def expert_backward(plan, r, low, high):
    rows = slice(low * plan.block, high * plan.block)
    raw = r.grecv[rows, :].astype(F32)
    scaled = (raw * r.slot_gate[rows, :]).astype(BF16)
    r.dr[rows, :] = scaled
    slots_grad = jnp.zeros((rows.stop - rows.start, 512), F32)
    for part in range(4):
        pre_grad = (dot_nt(scaled, r.down[part]) * r.dpre[part, rows, :].astype(F32)).astype(BF16)
        r.dpre[part, rows, :] = pre_grad
        slots_grad = slots_grad + dot_nt(pre_grad, r.up[part])
    column = jnp.sum(r.ret[rows, :].astype(F32) * raw, -1, keepdims=True)
    return_gradient(plan, r, low, high, slots_grad, column)


def prepare(plan, r):
    lane = lax.broadcasted_iota(jnp.int32, (2, plan.lanes), 1)
    for layer in range(2):
        raw = r.routes[layer]
        spread = jnp.full((2, plan.lanes), -1, jnp.int32)
        for image in range(plan.images):
            moved = pltpu.roll(raw, image * (PAD - SEQ), 1) if image else raw
            inside = (lane >= image * PAD) & (lane < image * PAD + SEQ)
            spread = jnp.where(inside, moved, spread)
        r.route_all[layer] = spread


SAVED = ATTENDED + ("x", "y", "h2", "up", "down")


def one_kernel(plan, inputs):
    shapes = forward_shapes(plan)
    shape_of_edge = inputs["tokens"].shape

    def body(r):
        place = Place(plan.experts)
        place.greet()
        first = types.SimpleNamespace(**vars(r))
        second = types.SimpleNamespace(**vars(r))
        for layer, view in ((0, first), (1, second)):
            layer_views(view, layer)
            for key in ("place", "codes", "table", "recv", "slot_gate", "packed"):
                setattr(view, key, getattr(r, f"{key}_{layer}"))
            view.column = view.slot_gate
            view.gret, view.dr = r.send, r.grecv
        first.ret, second.ret = r.ret_0, r.gsend
        saves = Copies({k: (getattr(r, k), getattr(r, "out_" + k)) for k in SAVED}, r.saves)
        loads = Copies({k: (getattr(r, "out_" + k), getattr(r, k)) for k in SAVED}, r.loads)
        edges = Copies(
            {"tokens": (r.tokens, r.edge), "cotangent": (r.cotangent, r.edge),
             "result": (r.edge, r.result)}, r.edges,
        )
        total = CoreSum(place, r.total)
        swaps = [
            HeadSwap(place, r.w_qkv.at[k], r.w_out.at[k], r.joint, r.out_all, sems)
            for k, sems in enumerate((r.swap_0, r.swap_1))
        ]
        gathers = [
            WeightGather(place, (r.w_up.at[k, 0], r.w_down.at[k, 0]), (r.up, r.down), sems)
            for k, sems in enumerate((r.weights_0, r.weights_1))
        ]
        moves = [
            Exchange(place, plan.block, r.send, dst, sems)
            for dst, sems in ((r.recv_0, r.move_0), (r.recv_1, r.move_1))
        ]
        gmoves = [
            Exchange(place, plan.block, src, r.grecv, sems)
            for src, sems in ((r.send, r.gmove_0), (r.gsend, r.gmove_1))
        ]
        backs = [
            Return(place, plan.block, plan.slots, src, r.back, sems)
            for src, sems in ((r.ret_0, r.back_0), (r.gsend, r.back_1))
        ]
        gbacks = [
            Return(place, plan.block, plan.slots, r.send, r.gback, sems)
            for sems in (r.gback_0, r.gback_1)
        ]
        sums = [
            ExpertSum(place, plan.panels, src, out, refs)
            for src, out, refs in (
                (r.packed_0, r.sum_0, r.sums_0), (r.packed_1, r.sum_1, r.sums_1)
            )
        ]
        experts = plan.experts

        edges.start("tokens")
        swaps[0].start_own()
        place.met()
        swaps[0].start_swap()
        gathers[0].start()
        prepare(plan, r)
        edges.wait("tokens")
        pad_images(plan, r.edge, r.x, r.y)
        edges.start("cotangent")
        saves.start("x")
        edges.wait("cotangent")
        pad_images(plan, r.edge, r.g, r.y)
        route_places(plan, place, second)
        build_members(plan, place, second)
        r.gsend[...] = dot(r.member[:, : plan.rows], r.g[...].astype(BF16)).astype(BF16)
        gmoves[1].start_all()
        swaps[0].wait_own()

        def own_heads(view):
            def one(image):
                first_norm(view, image)
                attend_forward(view, image, place.chip)

            each(0, plan.images, one)

        def other_heads(view, swap):
            swap.wait_swap(range(3))
            each(0, plan.images, lambda image: attend_forward(view, image, 1 - place.chip))
            swap.wait_swap((3,))
            each(0, plan.images, lambda image: attend_out(view, total, image))

        own_heads(first)
        route_places(plan, place, first)
        build_members(plan, place, first)
        other_heads(first, swaps[0])
        saves.start(*ATTENDED)
        second_norm(plan, first, total)
        send_slots(plan, place, first, moves[0])
        saves.start("y", "h2")
        norm_table(plan, first)
        build_picks(plan, first)
        gathers[0].pass_on()
        gathers[0].finish()
        saves.start("up", "down")
        gmoves[1].wait(0, experts)
        for low, high in groups(plan):
            moves[0].wait(low, high, False)
            moves[0].wait(low, high, True)
            read_gates(plan, first, low, high)
            expert_forward(plan, first, low, high)
            backs[0].start(low, high)
        build_members(plan, place, second)
        saves.wait(*SAVED)
        backs[0].pass_on()
        backs[0].near()
        swaps[1].start_own()
        swaps[1].start_swap()
        gathers[1].start()
        combined(plan, r, place.chip, r.back, r.x, False)
        backs[0].far()
        combined(plan, r, 1 - place.chip, r.back, r.x, True)
        r.x[...] += r.y[...]
        backs[0].finish()

        swaps[1].wait_own()
        own_heads(second)
        other_heads(second, swaps[1])
        second_norm(plan, second, total)
        send_slots(plan, place, second, moves[1])
        build_members(plan, place, first)
        norm_table(plan, second)
        build_picks(plan, second)
        gathers[1].pass_on()
        gathers[1].finish()
        for low, high in groups(plan):
            moves[1].wait(low, high, False)
            moves[1].wait(low, high, True)
            read_gates(plan, second, low, high)
            expert_forward_backward(plan, second, low, high)
            gbacks[1].start(low, high)
        expert_grads(plan, place, second, r.near)
        backs[1].start(0, experts)
        loads.start("up", "down")

        def inbox(layer, which):
            if layer:
                return r.recv_1.at[pl.ds(0, 512)] if which else r.far_in
            return r.back.at[pl.ds(which * 512, 512)]

        def far(layer, which):
            return place.to_chip(
                r.gpart.at[which, place.chip_peer], inbox(layer, which),
                r.far_sems.at[0, layer, which], r.far_sems.at[1, layer, which],
            )

        def between_second():
            near_sums(place, second, r.near)
            far(1, 0).start()

        back_to_attention(plan, place, second, gbacks[1], between_second)
        gbacks[1].finish()
        backs[1].pass_on()
        far(1, 1).start()
        each(0, plan.images, lambda image: attend_backward(second, total, image))

        def input_grad(image):
            r.g[image_rows(image), :] = first_norm_back(plan, second, total, image)

        few(0, plan.images, input_grad)

        r.send[...] = dot(r.member[:, : plan.rows], r.g[...].astype(BF16)).astype(BF16)
        gmoves[0].start_all()
        pack_out(plan, place, second)
        pack_qkv(plan, place, second)
        pack_small(plan, second)
        loads.start(*ATTENDED, "h2")
        sums[1].every(sums[1].step_pair)
        loads.wait("up", "down")
        for low, high in groups(plan):
            expert_again(plan, first, low, high)
        backs[1].near()
        combined(plan, r, place.chip, r.back, r.x, False)
        backs[1].far()
        combined(plan, r, 1 - place.chip, r.back, r.x, True)
        for image in range(plan.images):
            rows = slice(image * PAD, image * PAD + SEQ)
            r.y[image * SEQ : (image + 1) * SEQ, :] = r.y[rows, :] + r.x[rows, :]
        r.edge[...] = r.y[0 : plan.images * SEQ, :].astype(BF16)
        edges.start("result")
        backs[1].finish()
        loads.start("y", "x")
        build_picks(plan, first)
        for low, high in groups(plan):
            gmoves[0].wait(low, high)
            expert_backward(plan, first, low, high)
            gbacks[0].start(low, high)
        sums[1].every(sums[1].step_scatter)
        loads.wait(*ATTENDED, "h2", "y", "x")

        def weights_out(layer, which):
            return pltpu.make_async_copy(
                r.gpart.at[which, place.tensor], r.grad_experts.at[layer, which],
                r.expert_sems.at[layer, which],
            )

        def add_far(layer):
            for which in range(2):
                far(layer, which).wait()
                r.gpart[which, place.tensor] = (
                    r.gpart[which, place.tensor].astype(F32)
                    + inbox(layer, which)[...].astype(F32)
                ).astype(BF16)
                weights_out(layer, which).start()

        def between_first():
            add_far(1)
            for which in range(2):
                weights_out(1, which).wait()
            expert_grads(plan, place, first, r.near)
            near_sums(place, first, r.near)
            for which in range(2):
                far(0, which).start()

        back_to_attention(plan, place, first, gbacks[0], between_first)
        sums[1].every(sums[1].step_share)
        pack_out(plan, place, first)
        sums[0].step_pair(0)
        half = plan.images // 2
        each(0, half, lambda image: attend_backward(first, total, image))
        sums[1].every(sums[1].step_out)
        sums[0].step_scatter(0)
        each(half, plan.images, lambda image: attend_backward(first, total, image))
        pack_qkv(plan, place, first)
        panels = len(plan.panels)
        for panel in range(1, panels - 1):
            sums[0].step_pair(panel)
        for image in range(plan.images):
            value = first_norm_back(plan, first, total, image)
            r.g[image * SEQ : (image + 1) * SEQ, :] = value[:SEQ]
        rows_out = pl.ds(0, up_to(plan.images * SEQ, 16))
        out = pltpu.make_async_copy(r.g.at[rows_out], r.grad, r.out_sems.at[0])
        out.start()
        pack_small(plan, first)
        sums[0].step_pair(panels - 1)
        for panel in range(1, panels):
            sums[0].step_scatter(panel)
        sums[1].every(sums[1].step_end)
        sum_out = [
            pltpu.make_async_copy(src, dst, r.out_sems.at[1 + k])
            for k, (src, dst) in enumerate(((r.sum_0, r.total_0), (r.sum_1, r.total_1)))
        ]
        sum_out[1].start()
        sums[0].every(sums[0].step_share)
        add_far(0)
        gbacks[0].finish()
        sums[0].every(sums[0].step_out)
        sums[0].every(sums[0].step_end)
        sum_out[0].start()
        edges.wait("result")
        for which in range(2):
            weights_out(0, which).wait()
        for copy in [out] + sum_out:
            copy.wait()

    rows, slots = plan.rows, plan.slots
    outputs = {"out_" + key: shapes[key] for key in SAVED}
    outputs.update(
        result=(shape_of_edge, BF16),
        grad=((up_to(plan.images * SEQ, 16), 512), F32),
        grad_experts=((2, 2, 512, 512), BF16),
        total_0=((plan.packed, 128), BF16),
        total_1=((plan.packed, 128), BF16),
    )
    scratch = {key: VMEM(*shapes[key]) for key in SAVED}
    for layer in range(2):
        for key in ("place", "table", "recv", "slot_gate"):
            scratch[f"{key}_{layer}"] = VMEM(*shapes[key])
        scratch[f"codes_{layer}"] = VMEM((4, plan.lanes), F32)
        scratch[f"packed_{layer}"] = VMEM((plan.packed, 128), BF16)
        scratch[f"sum_{layer}"] = VMEM((plan.packed, 128), BF16)
        scratch[f"sums_{layer}"] = ExpertSum.scratch(plan)
        scratch[f"swap_{layer}"] = HeadSwap.scratch()
        scratch[f"weights_{layer}"] = WeightGather.scratch()
        scratch[f"move_{layer}"] = Exchange.scratch(plan.experts)
        scratch[f"gmove_{layer}"] = Exchange.scratch(plan.experts)
        scratch[f"back_{layer}"] = Return.scratch(plan.experts)
        scratch[f"gback_{layer}"] = Return.scratch(plan.experts)
    scratch.update(backward_scratch(plan))
    scratch.pop("packed")
    scratch.update(
        edge=VMEM(shape_of_edge, BF16),
        route_all=VMEM((2, 2, plan.lanes), jnp.int32),
        g=VMEM((rows, 512), F32),
        ret_0=VMEM((slots, 512), BF16),
        member=VMEM((slots, plan.lanes), BF16),
        gate=VMEM((plan.experts, plan.lanes), F32),
        picks=picks_scratch(plan),
        send=VMEM((slots, 512), BF16),
        gsend=VMEM((slots, 512), BF16),
        grecv=VMEM((slots, 512), BF16),
        back=VMEM((4 * slots, 512), BF16),
        total=CoreSum.scratch(plan.images),
        far_in=VMEM((512, 512), BF16),
        far_sems=DMA((2, 2, 2)),
        saves=DMA((len(SAVED),)),
        loads=DMA((len(SAVED),)),
        edges=DMA((3,)),
        expert_sems=DMA((2, 2)),
        out_sems=DMA((3,)),
    )
    return run_kernel("two_blocks", body, inputs, outputs, scratch, 3, 63.75, KEPT)


def final_form(plan, raw):
    experts = plan.experts
    tokens = plan.images * SEQ
    names = (
        "result", "grad", "grad_up", "grad_down", "grad_qkv", "grad_out", "grad_gain",
        "grad_bias_one", "grad_bias_two", "grad_router",
    )

    def kernel(*refs):
        result, grad, weights, total_0, total_1 = refs[:5]
        r = types.SimpleNamespace(**dict(zip(names, refs[5:15])))
        rows_buf, grad_buf, low, full, packs, sems, sems_out = refs[15:]
        loads = [
            pltpu.make_async_copy(src, dst, sems.at[k])
            for k, (src, dst) in enumerate(
                [(total_0, packs.at[0]), (total_1, packs.at[1]), (result, rows_buf)]
                + [(weights.at[k], low.at[k]) for k in range(2)] + [(grad, grad_buf)]
            )
        ]
        for copy in loads:
            copy.start()
        loads[2].wait()
        outs = [pltpu.make_async_copy(rows_buf, r.result, sems_out.at[0])]
        outs[0].start()
        for layer in range(2):
            loads[3 + layer].wait()
            for which, out in enumerate((r.grad_up, r.grad_down)):
                full[layer, which] = low[layer, which].astype(F32)
                outs.append(
                    pltpu.make_async_copy(
                        full.at[layer, which], out.at[layer], sems_out.at[1 + 2 * layer + which]
                    )
                )
                outs[-1].start()
        for layer in range(2):
            loads[layer].wait()
            Finals(plan, r).write(layer, packs[layer])
        loads[5].wait()
        r.grad[...] = grad_buf[0:tokens, :]
        for copy in outs:
            copy.wait()

    shapes = (
        ((tokens, 512), BF16), ((tokens, 512), F32), ((2, 512, 512), F32), ((2, 512, 512), F32),
        ((2, 3, 512, 128), F32), ((2, 128, 512), F32), ((2, 2, 512), F32), ((2, 512), F32),
        ((2, 512), F32), ((2, experts, 512), F32),
    )
    far_away = ("result", "grad_up", "grad_down")
    outs = pl.pallas_call(
        kernel,
        name="final_form",
        in_specs=[pl.BlockSpec(memory_space=pl.ANY)] * 5,
        out_specs=tuple(
            pl.BlockSpec(memory_space=pl.ANY if key in far_away else VMEM) for key in names
        ),
        out_shape=tuple(jax.ShapeDtypeStruct(*shape) for shape in shapes),
        scratch_shapes=[
            VMEM((tokens, 512), BF16), VMEM((up_to(tokens, 16), 512), F32),
            VMEM((2, 2, 512, 512), BF16), VMEM((2, 2, 512, 512), F32),
            VMEM((2, plan.packed, 128), BF16), DMA((6,)), DMA((5,)),
        ],
        compiler_params=pltpu.CompilerParams(vmem_limit_bytes=63 * MIB),
    )(raw.result, raw.grad, raw.grad_experts, raw.total_0, raw.total_1)
    return types.SimpleNamespace(**dict(zip(names, outs)))


def body(tokens, routes, ln_gain, ln_bias, w_qkv, w_out, w_router, w_up, w_down, cotangent):
    tok_rows = tokens.shape[0]
    experts = w_router.shape[2]
    plan = Plan(tok_rows, experts)
    router_rows = jnp.pad(w_router.transpose(0, 2, 1), ((0, 0), (0, 128 - experts), (0, 0)))
    if plan.stored:
        raw = one_kernel(
            plan,
            dict(
                gain_all=ln_gain, bias_all=ln_bias, router_all=router_rows, w_qkv=w_qkv, w_out=w_out,
                w_up=w_up, w_down=w_down, tokens=tokens, cotangent=cotangent,
                routes=jnp.pad(
                    routes.transpose(0, 2, 1), ((0, 0), (0, 0), (0, plan.lanes - tok_rows)),
                    constant_values=-1,
                ),
            ),
        )
        ends = final_form(plan, raw)
        return (
            ends.result, ends.grad, ends.grad_gain, ends.grad_bias_one, ends.grad_bias_two,
            ends.grad_qkv, ends.grad_out, ends.grad_router.transpose(0, 2, 1),
            ends.grad_up[:, None], ends.grad_down[:, None],
        )
    route_rows = routes.reshape(2, plan.images, SEQ, 2)
    route_rows = jnp.pad(
        route_rows, ((0, 0), (0, 0), (0, PAD - SEQ), (0, 0)), constant_values=-1
    ).reshape(2, plan.rows, 2)
    route_rows = jnp.pad(
        route_rows, ((0, 0), (0, plan.lanes - plan.rows), (0, 0)), constant_values=-1
    ).transpose(0, 2, 1)
    small = {"gain_all": ln_gain, "bias_all": ln_bias, "router_all": router_rows}
    weights = {"w_up": w_up, "w_down": w_down}
    one = first_forward(
        plan, dict(small, route_all=route_rows, w_qkv=w_qkv, w_out=w_out, **weights), tokens
    )
    two = second_whole(
        plan, dict(small, route_all=route_rows, **weights), cotangent,
        one.next, one.joint_later, one.out_later,
    )
    saved = {key: getattr(one, "out_" + key) for key in forward_shapes(plan)}
    three = first_backward(
        plan, small, saved, two.grad, two.gfar, two.gown, two.out_packed, tokens.shape
    )
    return (
        two.result, three.grad, three.grad_gain, three.grad_bias[:, 0], three.grad_bias[:, 1],
        three.grad_qkv, three.grad_out, three.grad_router.transpose(0, 2, 1),
        three.grad_up[:, None], three.grad_down[:, None],
    )


def solution(mesh):
    in_specs = (
        P(EXPERT, None),
        P(None, EXPERT, None),
        P(),
        P(),
        P(None, None, None, TENSOR),
        P(None, TENSOR, None),
        P(),
        P(None, EXPERT, None, TENSOR),
        P(None, EXPERT, TENSOR, None),
        P(EXPERT, None),
    )
    out_specs = (
        P(EXPERT, None),
        P(EXPERT, None),
        P(),
        P(),
        P(),
        P(None, None, None, TENSOR),
        P(None, TENSOR, None),
        P(),
        P(None, EXPERT, None, TENSOR),
        P(None, EXPERT, TENSOR, None),
    )
    return jax.shard_map(body, mesh=mesh, in_specs=in_specs, out_specs=out_specs, check_vma=False)
```

```python
import types

import jax
import jax.numpy as jnp
from jax import lax
from jax.experimental import pallas as pl
from jax.experimental.pallas import tpu as pltpu
from jax.sharding import PartitionSpec as P

HEAD_DIM = 64
SEQ = 197
PAD = 208
EPS = 1e-06
MESH = pl.DeviceIdType.MESH
EXPERT, TENSOR = "expert", "tensor"
F32 = jnp.float32
BF16 = jnp.bfloat16
SCALE = HEAD_DIM ** (-0.5)
MIB = 1 << 20
VMEM = pltpu.VMEM
DMA = pltpu.SemaphoreType.DMA


def up_to(count, multiple):
    return -(-count // multiple) * multiple


def dot(left, right):
    return lax.dot_general(left, right, (((1,), (0,)), ((), ())), preferred_element_type=F32)


def dot_nt(left, right):
    return lax.dot_general(left, right, (((1,), (1,)), ((), ())), preferred_element_type=F32)


def dot_tn(left, right):
    return lax.dot_general(left, right, (((0,), (0,)), ((), ())), preferred_element_type=F32)


def norm_parts(rows):
    centered = rows - jnp.mean(rows, -1, keepdims=True)
    scaled = lax.rsqrt(jnp.mean(centered * centered, -1, keepdims=True) + EPS)
    return centered * scaled, scaled


def norm_pull(grad_in, normed, scaled, gain_row):
    grad_normed = grad_in * gain_row
    inner = (
        grad_normed
        - jnp.mean(grad_normed, -1, keepdims=True)
        - normed * jnp.mean(grad_normed * normed, -1, keepdims=True)
    )
    return inner * scaled


def gelu(pre):
    inner = pre * (0.7978845608028654 + 0.035677408136300125 * (pre * pre))
    return 0.5 * pre * (1.0 + jnp.tanh(inner))


def gelu_both(pre):
    square = pre * pre
    inner = pre * (0.7978845608028654 + 0.035677408136300125 * square)
    bent = jnp.tanh(inner)
    half = 0.5 + 0.5 * bent
    slope = half + half * (1.0 - bent) * pre * (
        0.7978845608028654 + 0.10703222440890037 * square
    )
    return half * pre, slope


class Plan:
    def __init__(self, tok_rows, experts):
        self.images = tok_rows // SEQ
        self.rows = self.images * PAD
        self.lanes = up_to(self.rows, 128)
        self.experts = experts
        self.per_rank = max(1, 10 * tok_rows // (4 * experts * 4))
        self.capacity = 4 * self.per_rank
        self.block = up_to(self.per_rank + 2, 16)
        self.slots = experts * self.block
        self.blocks = up_to(4 * experts, 128)
        self.stored = 4 * self.slots <= 2560
        most = 320
        self.group = max(
            size for size in range(1, experts)
            if experts % size == 0 and (size == 1 or size * self.block <= most)
        )
        main = up_to(512, 16 * experts)
        small = up_to(4 * (4 + experts), 16 * experts)
        self.panels = [(start, main) for start in range(0, 2048, main)] + [(2048, small)]
        self.packed = 2048 + small


def image_rows(image):
    if isinstance(image, int):
        return pl.ds(image * PAD, PAD)
    return pl.ds(pl.multiple_of(image * PAD, PAD), PAD)


def each(low, high, use):
    def one(index, carry):
        use(index)
        return carry

    lax.fori_loop(low, high, one, 0)


def few(low, high, use):
    if high - low > 8:
        each(low, high, use)
        return
    for index in range(low, high):
        use(index)


class Place:
    def __init__(self, experts):
        self.tensor = lax.axis_index(TENSOR)
        self.core = lax.rem(self.tensor, 2)
        self.chip = lax.div(self.tensor, 2)
        self.core_peer = self.tensor + 1 - 2 * self.core
        self.chip_peer = lax.rem(self.tensor + 2, 4)
        self.experts = experts
        self.expert = lax.axis_index(EXPERT)

    def ahead(self, step):
        return lax.rem(self.expert + step, self.experts)

    def behind(self, step):
        return lax.rem(self.expert + self.experts - step, self.experts)

    def greet(self):
        barrier = pltpu.get_barrier_semaphore()
        for peer in (self.core_peer, self.chip_peer):
            pl.semaphore_signal(barrier, inc=1, device_id={TENSOR: peer}, device_id_type=MESH)

        def one(step):
            pl.semaphore_signal(
                barrier, inc=1, device_id={EXPERT: self.ahead(step)}, device_id_type=MESH
            )

        each(1, self.experts, one)

    def met(self):
        pl.semaphore_wait(pltpu.get_barrier_semaphore(), 2 + self.experts - 1)

    def to_core(self, src, dst, send, recv):
        return pltpu.make_async_remote_copy(
            src_ref=src, dst_ref=dst, send_sem=send, recv_sem=recv,
            device_id={TENSOR: self.core_peer}, device_id_type=MESH,
        )

    def to_chip(self, src, dst, send, recv):
        return pltpu.make_async_remote_copy(
            src_ref=src, dst_ref=dst, send_sem=send, recv_sem=recv,
            device_id={TENSOR: self.chip_peer}, device_id_type=MESH,
        )

    def to_expert(self, expert, src, dst, send, recv):
        return pltpu.make_async_remote_copy(
            src_ref=src, dst_ref=dst, send_sem=send, recv_sem=recv,
            device_id={EXPERT: expert}, device_id_type=MESH,
        )


class CoreSum:
    def __init__(self, place, refs):
        self.place = place
        self.part, self.near, self.send, self.recv = refs

    @staticmethod
    def scratch(images):
        rows = (images * PAD, 512)
        return [VMEM(rows, BF16), VMEM(rows, BF16), DMA((images,)), DMA((images,))]

    def copy(self, image):
        rows = image_rows(image)
        return self.place.to_core(
            self.part.at[rows], self.near.at[rows], self.send.at[image], self.recv.at[image]
        )

    def put(self, image, value):
        self.part[image_rows(image), :] = value.astype(BF16)
        self.copy(image).start()

    def get(self, image):
        rows = image_rows(image)
        self.copy(image).wait()
        return self.part[rows, :].astype(F32) + self.near[rows, :].astype(F32)


class HeadSwap:
    def __init__(self, place, qkv, out, joint, out_all, refs):
        self.place, self.qkv, self.out = place, qkv, out
        self.joint, self.out_all = joint, out_all
        self.send, self.recv, self.local = refs

    @staticmethod
    def scratch():
        return [DMA((4,)), DMA((4,)), DMA((4,))]

    def ends(self, part):
        if part == 3:
            rows = pl.ds(pl.multiple_of(self.place.chip * 128, 128), 128)
            return self.out, self.out_all.at[rows]
        columns = pl.ds(part * 128, 128)
        return self.qkv.at[part], self.joint.at[self.place.chip, :, columns]

    def own(self, part):
        return pltpu.make_async_copy(*self.ends(part), self.local.at[part])

    def swap(self, part):
        return self.place.to_chip(*self.ends(part), self.send.at[part], self.recv.at[part])

    def start_own(self):
        for part in range(4):
            self.own(part).start()

    def start_swap(self):
        for part in range(4):
            self.swap(part).start()

    def wait_own(self):
        for part in range(4):
            self.own(part).wait()

    def wait_swap(self, parts=range(4)):
        for part in parts:
            self.swap(part).wait()


class Exchange:
    def __init__(self, place, block, src, dst, refs):
        self.place, self.block, self.src, self.dst = place, block, src, dst
        self.send, self.recv, self.local = refs

    @staticmethod
    def scratch(experts):
        return [DMA((2, experts)), DMA((2, experts)), DMA((2,))]

    def part(self, step, tail):
        base = pl.multiple_of(step * self.block, self.block)
        if tail is None:
            return pl.ds(base, self.block)
        if tail:
            return pl.ds(pl.multiple_of(base + self.block - 16, 16), 16)
        return pl.ds(base, self.block - 16)

    def own(self, tail=None):
        rows = self.part(0, tail)
        return pltpu.make_async_copy(
            self.src.at[rows], self.dst.at[rows], self.local.at[int(bool(tail))]
        )

    def copy(self, step, tail=None):
        rows, which = self.part(step, tail), int(bool(tail))
        return self.place.to_expert(
            self.place.ahead(step), self.src.at[rows], self.dst.at[rows],
            self.send.at[which, step], self.recv.at[which, step],
        )

    def start_all(self, tail=None):
        self.own(tail).start()
        each(1, self.place.experts, lambda step: self.copy(step, tail).start())

    def wait(self, low, high, tail=None):
        if low == 0:
            self.own(tail).wait()
        each(max(1, low), high, lambda step: self.copy(step, tail).wait())


class Return:
    def __init__(self, place, block, slots, src, dst, refs):
        self.place, self.block, self.slots, self.src, self.dst = place, block, slots, src, dst
        self.send, self.recv, self.local = refs

    @staticmethod
    def scratch(experts):
        return [DMA((4, experts)), DMA((4, experts)), DMA]

    def rows(self, quarter, step):
        return pl.ds(
            pl.multiple_of(quarter * self.slots + step * self.block, self.block), self.block
        )

    def own(self):
        return pltpu.make_async_copy(
            self.src.at[pl.ds(0, self.block)],
            self.dst.at[self.rows(self.place.tensor, 0)], self.local,
        )

    def home(self, step):
        rows = pl.ds(pl.multiple_of(step * self.block, self.block), self.block)
        return self.place.to_expert(
            self.place.behind(step), self.src.at[rows],
            self.dst.at[self.rows(self.place.tensor, step)],
            self.send.at[0, step], self.recv.at[0, step],
        )

    def to_chip(self, step):
        block = self.dst.at[self.rows(self.place.tensor, step)]
        return self.place.to_chip(block, block, self.send.at[1, step], self.recv.at[1, step])

    def to_core(self, step):
        block = self.dst.at[self.rows(self.place.tensor, step)]
        return self.place.to_core(block, block, self.send.at[2, step], self.recv.at[2, step])

    def on_to_core(self, step):
        block = self.dst.at[self.rows(self.place.chip_peer, step)]
        return self.place.to_core(block, block, self.send.at[3, step], self.recv.at[3, step])

    def start(self, low, high):
        if low == 0:
            self.own().start()
        each(max(1, low), high, lambda step: self.home(step).start())

    def pass_on(self, arrived=lambda quarter, step: None):
        place, last = self.place, self.place.experts

        def give(step):
            self.to_chip(step).start()
            self.to_core(step).start()
            arrived(place.tensor, step)

        def one(step):
            self.home(step).wait_recv()
            give(step)

        def two(step):
            one(step)
            self.on(step - self.LAG, arrived)

        self.own().wait()
        give(0)
        each(1, self.LAG, one)
        each(self.LAG, last, two)

    LAG = 4

    def on(self, step, arrived):
        self.to_chip(step).wait_recv()
        self.on_to_core(step).start()
        arrived(self.place.chip_peer, step)

    def near(self, arrived=lambda quarter, step: None):
        def one(step):
            self.to_core(step).wait_recv()
            arrived(self.place.core_peer, step)

        each(0, self.place.experts, one)

    def far(self, arrived=lambda quarter, step: None):
        place, last = self.place, self.place.experts
        each(last - self.LAG, last, lambda step: self.on(step, arrived))

        def one(step):
            self.on_to_core(step).wait_recv()
            arrived(3 - place.tensor, step)

        each(0, last, one)

    def finish(self):
        def one(step):
            self.to_chip(step).wait_send()
            self.to_core(step).wait_send()
            self.on_to_core(step).wait_send()

        each(0, self.place.experts, one)
        each(1, self.place.experts, lambda step: self.home(step).wait_send())


class WeightGather:
    def __init__(self, place, shards, wholes, refs):
        self.place, self.shards, self.wholes = place, shards, wholes
        self.send, self.recv, self.local = refs

    @staticmethod
    def scratch():
        return [DMA((2, 3)), DMA((2, 3)), DMA((2,))]

    def own(self, which):
        return pltpu.make_async_copy(
            self.shards[which], self.wholes[which].at[self.place.tensor], self.local.at[which]
        )

    def to_chip(self, which):
        return self.place.to_chip(
            self.shards[which], self.wholes[which].at[self.place.tensor],
            self.send.at[which, 0], self.recv.at[which, 0],
        )

    def to_core(self, which):
        return self.place.to_core(
            self.shards[which], self.wholes[which].at[self.place.tensor],
            self.send.at[which, 1], self.recv.at[which, 1],
        )

    def on_to_core(self, which):
        part = self.wholes[which].at[self.place.chip_peer]
        return self.place.to_core(
            part, part, self.send.at[which, 2], self.recv.at[which, 2]
        )

    def start(self):
        for which in range(2):
            self.own(which).start()
            self.to_chip(which).start()
            self.to_core(which).start()

    def pass_on(self):
        for which in range(2):
            self.to_chip(which).wait()
            self.on_to_core(which).start()

    def finish(self):
        for which in range(2):
            self.own(which).wait()
            self.to_core(which).wait()
            self.on_to_core(which).wait()


class ExpertSum:
    def __init__(self, place, panels, src, total, refs):
        self.place, self.panels, self.src, self.total = place, panels, src, total
        self.inbox, self.chunks, self.send, self.recv = refs
        self.side = lax.rem(place.expert, 2)
        self.pair = place.expert + 1 - 2 * self.side
        self.group = place.experts // 2
        self.index = lax.div(place.expert, 2)

    @staticmethod
    def scratch(plan):
        panels = len(plan.panels)
        half = plan.packed // 2
        return [
            VMEM((half, 128), BF16), VMEM((half, 128), BF16),
            DMA((2, panels, max(2, plan.experts // 2))), DMA((2, panels, max(2, plan.experts // 2))),
        ]

    def half(self, panel, side):
        start, rows = self.panels[panel]
        return pl.ds(pl.multiple_of(start + side * (rows // 2), 16), rows // 2)

    def local(self, panel):
        start, rows = self.panels[panel]
        return pl.ds(start // 2, rows // 2)

    def chunk(self, panel, index):
        start, rows = self.panels[panel]
        size = rows // self.place.experts
        return pl.ds(pl.multiple_of(start // 2 + index * size, 16), size)

    def chunk_whole(self, panel, index):
        start, rows = self.panels[panel]
        size = rows // self.place.experts
        return pl.ds(pl.multiple_of(start + self.side * (rows // 2) + index * size, 16), size)

    def member(self, step):
        return lax.rem(self.place.expert + 2 * step, self.place.experts)

    def pair_in(self, panel):
        return self.place.to_expert(
            self.pair, self.src.at[self.half(panel, 1 - self.side)],
            self.inbox.at[self.local(panel)],
            self.send.at[0, panel, 0], self.recv.at[0, panel, 0],
        )

    def scatter(self, panel, step):
        peer = lax.rem(self.index + step, self.group)
        return self.place.to_expert(
            self.member(step), self.src.at[self.chunk_whole(panel, peer)],
            self.chunks.at[self.chunk(panel, step)],
            self.send.at[0, panel, step], self.recv.at[0, panel, step],
        )

    def share(self, panel, step):
        mine = self.total.at[self.chunk_whole(panel, self.index)]
        return self.place.to_expert(
            self.member(step), mine, mine,
            self.send.at[1, panel, step], self.recv.at[1, panel, step],
        )

    def pair_out(self, panel):
        half = self.total.at[self.half(panel, self.side)]
        return self.place.to_expert(
            self.pair, half, half, self.send.at[1, panel, 0], self.recv.at[1, panel, 0]
        )

    def step_pair(self, panel):
        self.pair_in(panel).start()

    def step_scatter(self, panel):
        self.pair_in(panel).wait()
        mine = self.half(panel, self.side)
        self.src[mine, :] = (
            self.src[mine, :].astype(F32) + self.inbox[self.local(panel), :].astype(F32)
        ).astype(BF16)
        each(1, self.group, lambda step: self.scatter(panel, step).start())

    def step_share(self, panel):
        mine = self.chunk_whole(panel, self.index)

        def one(step, total):
            self.scatter(panel, step).wait()
            return total + self.chunks[self.chunk(panel, step), :].astype(F32)

        total = lax.fori_loop(1, self.group, one, self.src[mine, :].astype(F32))
        self.total[mine, :] = total.astype(BF16)
        each(1, self.group, lambda step: self.share(panel, step).start())

    def step_out(self, panel):
        each(1, self.group, lambda step: self.share(panel, step).wait())
        self.pair_out(panel).start()

    def step_end(self, panel):
        self.pair_out(panel).wait()

    def every(self, step):
        for panel in range(len(self.panels)):
            step(panel)


class PairSum:
    @staticmethod
    def scratch_near():
        return [VMEM((2, 2, 512, 512), BF16), DMA((2, 2)), DMA((2, 2))]

    @staticmethod
    def scratch_far():
        return [VMEM((2, 512, 512), BF16), DMA((2,)), DMA((2,))]

    @staticmethod
    def near(place, part, refs, which, chip):
        inbox, send, recv = refs
        quarter = 2 * chip + 1 - place.core
        return place.to_core(
            part.at[which, quarter], inbox.at[which, chip],
            send.at[which, chip], recv.at[which, chip],
        )

    @staticmethod
    def far(place, out, refs, which):
        inbox, send, recv = refs
        return place.to_chip(out, inbox.at[which], send.at[which], recv.at[which])


def route_places(plan, place, r):
    shape = (plan.experts, plan.lanes)
    expert_id = lax.broadcasted_iota(jnp.int32, shape, 0)
    lane = lax.broadcasted_iota(jnp.int32, shape, 1)
    first, second = r.route[0:1, :], r.route[1:2, :]
    is_first, is_second = expert_id == first, expert_id == second
    named = is_first | is_second
    count = jnp.where(named, 1.0, 0.0)
    running = count
    step = 1
    while step < plan.lanes:
        running = running + jnp.where(lane >= step, pltpu.roll(running, step, 1), 0.0)
        step *= 2
    before = running - count
    mine = before - (place.tensor * plan.per_rank).astype(F32)
    valid = named & (mine >= 0.0) & (mine < float(plan.per_rank))
    r.place[...] = jnp.where(valid, mine, -1.0)
    quarter = jnp.zeros(shape, F32)
    for bound in range(1, 4):
        quarter = quarter + jnp.where(before >= float(bound * plan.per_rank), 1.0, 0.0)
    step_of = expert_id - place.expert
    step_of = jnp.where(step_of < 0, step_of + plan.experts, step_of).astype(F32)
    code = (
        quarter * float(plan.slots - plan.per_rank) + step_of * float(plan.block) + before
    )
    kept = before < float(plan.capacity)
    nowhere = -1.0
    code_first = jnp.max(jnp.where(is_first & kept, code, nowhere), 0, keepdims=True)
    code_second = jnp.max(jnp.where(is_second & kept, code, nowhere), 0, keepdims=True)
    r.codes[...] = jnp.concatenate(
        [code_first, code_second, first.astype(F32), second.astype(F32)], axis=0
    )


def build_members(plan, place, r):
    slot = lax.broadcasted_iota(jnp.int32, (plan.block, plan.lanes), 0).astype(F32)

    def one(step):
        rows = pl.ds(pl.multiple_of(step * plan.block, plan.block), plan.block)
        hit = r.place[pl.ds(place.ahead(step), 1), :] == slot
        r.member[rows, :] = jnp.where(hit, 1.0, 0.0).astype(BF16)

    each(0, plan.experts, one)


def picks_part(plan, r, image, quarter):
    slot = lax.broadcasted_iota(jnp.int32, (PAD, plan.slots), 1) + quarter * plan.slots
    slot = slot.astype(F32)
    rows = image_rows(image)
    hit = (r.table[rows, 0:1] == slot) | (r.table[rows, 1:2] == slot)
    return jnp.where(hit, 1.0, 0.0).astype(BF16)


def build_picks(plan, r):
    if not plan.stored:
        return
    for quarter in range(4):
        columns = slice(quarter % 2 * plan.slots, (quarter % 2 + 1) * plan.slots)

        def one(image):
            r.picks[quarter // 2, image_rows(image), columns] = picks_part(
                plan, r, image, quarter
            )

        each(0, plan.images, one)


def picks_scratch(plan):
    return VMEM((2, plan.rows, 2 * plan.slots) if plan.stored else (2, 16, 128), BF16)


def diagonal(plan):
    shape = (plan.block, 128)
    return lax.broadcasted_iota(jnp.int32, shape, 0) == lax.broadcasted_iota(jnp.int32, shape, 1)


def tail_rows(plan, base):
    return pl.ds(pl.multiple_of(base + plan.block - 16, 16), 16)


def write_spare(plan, ref, base, column):
    row = jnp.sum(jnp.where(diagonal(plan), column, 0.0), 0, keepdims=True)
    high = row.astype(BF16).astype(F32)
    rest = jnp.zeros((1, 512 - 128), F32)
    high_row = jnp.concatenate([high, rest], axis=1)
    low_row = jnp.concatenate([row - high, rest], axis=1)
    rows = tail_rows(plan, base)
    index = lax.broadcasted_iota(jnp.int32, (16, 512), 0)
    old = ref[rows, :].astype(F32)
    ref[rows, :] = jnp.where(index == 14, high_row, jnp.where(index == 15, low_row, old)).astype(
        BF16
    )


def read_spare(plan, ref, base):
    index = lax.broadcasted_iota(jnp.int32, (16, 128), 0)
    tail = ref[tail_rows(plan, base), 0:128].astype(F32)
    row = jnp.sum(jnp.where(index >= 14, tail, 0.0), 0, keepdims=True)
    return jnp.sum(jnp.where(diagonal(plan), row, 0.0), 1, keepdims=True)


def head_split(value):
    first_head = lax.broadcasted_iota(jnp.int32, value.shape, 1) < HEAD_DIM
    nothing = jnp.zeros(value.shape, value.dtype)
    return jnp.concatenate(
        [jnp.where(first_head, value, nothing), jnp.where(first_head, nothing, value)], axis=0
    )


def head_join(value):
    rows = value.shape[0] // 2
    first_head = lax.broadcasted_iota(jnp.int32, (rows, 128), 1) < HEAD_DIM
    return jnp.where(first_head, value[:rows], value[rows:])


def first_norm(r, image):
    rows = image_rows(image)
    normed, _ = norm_parts(r.x[rows, :])
    r.h[rows, :] = (normed * r.gain[0:1, :] + r.bias[0:1, :]).astype(BF16)


def attend_forward(r, image, side):
    key_real = lax.broadcasted_iota(jnp.int32, (2 * PAD, PAD), 1) < SEQ
    rows = image_rows(image)
    proj = dot(r.h[rows, :], r.joint[side]).astype(BF16)
    r.qkv[side, rows, :] = proj
    query, keyed, valued = proj[:, :128], proj[:, 128:256], proj[:, 256:]
    scores = jnp.where(key_real, dot_nt(head_split(query * SCALE), keyed), -1e30)
    expd = jnp.exp(scores - jnp.max(scores, -1, keepdims=True))
    prob = (expd * (1.0 / jnp.sum(expd, -1, keepdims=True))).astype(BF16)
    r.prob[side, image] = prob
    r.mixed[side, rows, :] = head_join(dot(prob, valued)).astype(BF16)


def attend_out(r, total, image):
    rows = image_rows(image)
    mixed = jnp.concatenate([r.mixed[0, rows, :], r.mixed[1, rows, :]], axis=1)
    total.put(image, dot(mixed, r.out_all[...]))


def attend_backward(r, total, image):
    rows = image_rows(image)
    mixed_grads = dot_nt(r.gin[rows, :].astype(BF16), r.out_all[...])
    back = jnp.zeros((PAD, 512), F32)
    for side in range(2):
        proj = r.qkv[side, rows, :]
        query, keyed, valued = proj[:, :128], proj[:, 128:256], proj[:, 256:]
        grad = mixed_grads[:, side * 128 : (side + 1) * 128]
        mixed_grad = head_split(grad.astype(BF16))
        inner = jnp.sum(head_split(grad * r.mixed[side, rows, :].astype(F32)), -1, keepdims=True)
        prob = r.prob[side, image]
        prob_grad = dot_nt(mixed_grad, valued)
        score_grad = (prob.astype(F32) * (prob_grad - inner)).astype(BF16)
        query_grad = head_join(dot(score_grad, keyed)) * SCALE
        key_grad = dot_tn(score_grad, head_split(query * SCALE))
        value_grad = dot_tn(prob, mixed_grad)
        proj_grad = jnp.concatenate([query_grad, key_grad, value_grad], axis=1).astype(BF16)
        r.dproj[side, rows, :] = proj_grad
        back = back + dot_nt(proj_grad, r.joint[side])
    total.put(image, back)


def pack_out(plan, place, r):
    r.packed[0:512, :] = dot_tn(r.gin[...].astype(BF16), r.mixed[place.chip]).astype(BF16)


def pack_qkv(plan, place, r):
    grads = dot_tn(r.h[...], r.dproj[place.chip]).astype(BF16)
    for part in range(3):
        r.packed[(part + 1) * 512 : (part + 2) * 512, :] = grads[:, part * 128 : (part + 1) * 128]


def pack_small(plan, r):
    router = dot_tn(r.dz[...], r.h2[: plan.rows, :])[: plan.experts]
    rows = jnp.concatenate([r.vec[0:4, :], router], axis=0)
    rows = jnp.concatenate([rows[:, part * 128 : (part + 1) * 128] for part in range(4)], axis=0)
    spare = plan.packed - 2048 - rows.shape[0]
    r.packed[2048:, :] = jnp.concatenate([rows, jnp.zeros((spare, 128), F32)], axis=0).astype(BF16)


def second_norm(plan, r, total):
    def one(image):
        rows = image_rows(image)
        after = r.x[rows, :] + total.get(image)
        r.y[rows, :] = after
        normed, _ = norm_parts(after)
        r.h2[rows, :] = (normed * r.gain[1:2, :] + r.bias[1:2, :]).astype(BF16)

    if plan.lanes > plan.rows:
        r.h2[plan.rows :, :] = jnp.zeros((plan.lanes - plan.rows, 512), BF16)
    few(0, plan.images, one)


def send_slots(plan, place, r, move):
    r.send[...] = dot(r.member[...], r.h2[...]).astype(BF16)
    move.start_all(False)
    logits = dot_nt(r.router[: plan.experts, :], r.h2[...])
    expert_id = lax.broadcasted_iota(jnp.int32, (plan.experts, plan.lanes), 0)
    is_first, is_second = expert_id == r.route[0:1, :], expert_id == r.route[1:2, :]
    named = is_first | is_second
    shifted = jnp.where(named, logits, -1e30)
    top = jnp.max(shifted, 0, keepdims=True)
    expd = jnp.where(named, jnp.exp(shifted - top), 0.0)
    share = expd / jnp.maximum(jnp.sum(expd, 0, keepdims=True), 1e-30)
    r.gate[...] = share
    gate_first = jnp.sum(jnp.where(is_first, share, 0.0), 0, keepdims=True)
    gate_second = jnp.sum(jnp.where(is_second, share, 0.0), 0, keepdims=True)
    r.table[...] = jnp.concatenate(
        [r.codes[...], gate_first, gate_second, jnp.zeros((10, plan.lanes), F32)], axis=0
    ).T
    slot = lax.broadcasted_iota(jnp.int32, (plan.block, plan.lanes), 0).astype(F32)

    def one(step):
        expert = place.ahead(step)
        hit = r.place[pl.ds(expert, 1), :] == slot
        column = jnp.sum(jnp.where(hit, r.gate[pl.ds(expert, 1), :], 0.0), 1, keepdims=True)
        write_spare(plan, r.send, step * plan.block, column)

    few(0, plan.experts, one)
    move.start_all(True)


def read_gates(plan, r, low, high):
    def one(step):
        base = step * plan.block
        rows = pl.ds(pl.multiple_of(base, plan.block), plan.block)
        r.slot_gate[rows, :] = read_spare(plan, r.recv, base)

    few(low, high, one)


def groups(plan):
    return [(low, low + plan.group) for low in range(0, plan.experts, plan.group)]


def return_gradient(plan, r, low, high, value, column):
    r.gret[low * plan.block : high * plan.block, :] = value.astype(BF16)
    r.column[low * plan.block : high * plan.block, :] = column

    def one(step):
        base = step * plan.block
        rows = pl.ds(pl.multiple_of(base, plan.block), plan.block)
        write_spare(plan, r.gret, base, r.column[rows, :])

    few(low, high, one)


def expert_grads(plan, place, r, near):
    drecv, recv = r.dr[...], r.recv[...]
    for part in range(4):
        r.gpart[0, part] = dot_tn(recv, r.dpre[part]).astype(BF16)
        r.gpart[1, part] = dot_tn(r.act[part], drecv).astype(BF16)
    for which in range(2):
        for chip in range(2):
            PairSum.near(place, r.gpart, near, which, chip).start()


def near_sums(place, r, near):
    chip = place.tensor // 2
    inbox = near[0]
    for which in range(2):
        for side in range(2):
            PairSum.near(place, r.gpart, near, which, side).wait()
        for quarter, side in ((place.chip_peer, 1 - chip), (place.tensor, chip)):
            r.gpart[which, quarter] = (
                r.gpart[which, quarter].astype(F32) + inbox[which, side].astype(F32)
            ).astype(BF16)


def near_outs(place, r):
    return [
        pltpu.make_async_copy(r.gpart.at[which, quarter], out.at[which], r.out_sems.at[which, side])
        for which in range(2)
        for side, (quarter, out) in enumerate(((place.chip_peer, r.gfar), (place.tensor, r.gown)))
    ]


def combined(plan, r, chip, rows_in, out, add):
    rows = pl.ds(pl.multiple_of(chip * 2 * plan.slots, plan.slots), 2 * plan.slots)
    if plan.stored:
        value = dot(r.picks[chip], rows_in[rows, :])
        out[...] = out[...] + value if add else value
        return

    def one(image):
        picks = [picks_part(plan, r, image, 2 * chip + quarter) for quarter in range(2)]
        value = dot(jnp.concatenate(picks, axis=1), rows_in[rows, :])
        tokens = image_rows(image)
        out[tokens, :] = out[tokens, :] + value if add else value

    each(0, plan.images, one)


def norm_table(plan, r):
    def one(image):
        rows = image_rows(image)
        for source, column in ((r.y, 6), (r.x, 8)):
            value = source[rows, :]
            mean = jnp.mean(value, -1, keepdims=True)
            centered = value - mean
            r.table[rows, column : column + 1] = mean
            r.table[rows, column + 1 : column + 2] = lax.rsqrt(
                jnp.mean(centered * centered, -1, keepdims=True) + EPS
            )

    few(0, plan.images, one)


def norm_again(r, source, rows, column):
    scaled = r.table[rows, column + 1 : column + 2]
    return (source[rows, :] - r.table[rows, column : column + 1]) * scaled, scaled


def keep_gates(plan, r):
    def arrived(quarter, step):
        tail = tail_rows(plan, quarter * plan.slots + step * plan.block)
        rows = r.gback[tail, 0:128].astype(F32)
        index = quarter * plan.experts + step
        r.high[pl.ds(index, 1), :] = rows[14:15]
        r.low[pl.ds(index, 1), :] = rows[15:16]

    return arrived


def pick_gates(plan, r, rows, column):
    code = r.table[rows, column : column + 1]
    block = jnp.floor((code + 0.5) * (1.0 / plan.block))
    inside = code - block * float(plan.block)
    lane = lax.broadcasted_iota(jnp.int32, (PAD, plan.blocks), 1).astype(F32)
    chosen = jnp.where(lane == block, 1.0, 0.0).astype(BF16)
    values = dot(chosen, r.high[...].astype(BF16)) + dot(chosen, r.low[...].astype(BF16))
    lane = lax.broadcasted_iota(jnp.int32, (PAD, 128), 1).astype(F32)
    return jnp.sum(jnp.where(lane == inside, values, 0.0), -1, keepdims=True)


def back_to_attention(plan, place, r, gback, between):
    arrived = keep_gates(plan, r)
    r.high[...] = jnp.zeros_like(r.high)
    r.low[...] = jnp.zeros_like(r.low)
    gback.pass_on(arrived)
    gback.near(arrived)
    combined(plan, r, place.chip, r.gback, r.gin, False)
    between()
    gback.far(arrived)
    combined(plan, r, 1 - place.chip, r.gback, r.gin, True)
    r.vec[...] = jnp.zeros_like(r.vec)

    def one(image):
        rows = image_rows(image)
        lane = lax.broadcasted_iota(jnp.int32, (PAD, 128), 1).astype(F32)
        first, second = pick_gates(plan, r, rows, 0), pick_gates(plan, r, rows, 1)
        both = first + second
        logit_grad = jnp.where(
            lane == r.table[rows, 2:3], first - r.table[rows, 4:5] * both,
            jnp.where(lane == r.table[rows, 3:4], second - r.table[rows, 5:6] * both, 0.0),
        ).astype(BF16)
        r.dz[rows, :] = logit_grad
        value = r.gin[rows, :] + dot(logit_grad, r.router[...])
        normed, scaled = norm_again(r, r.y, rows, 6)
        r.gin[rows, :] = r.g[rows, :].astype(F32) + norm_pull(
            value, normed, scaled, r.gain[1:2, :]
        )
        r.vec[1:2, :] += jnp.sum(value * normed, 0, keepdims=True)
        r.vec[3:4, :] += jnp.sum(value, 0, keepdims=True)

    few(0, plan.images, one)


def first_norm_back(plan, r, total, image):
    rows = image_rows(image)
    value = total.get(image)
    normed, scaled = norm_again(r, r.x, rows, 8)
    r.vec[0:1, :] += jnp.sum(value * normed, 0, keepdims=True)
    r.vec[2:3, :] += jnp.sum(value, 0, keepdims=True)
    return r.gin[rows, :] + norm_pull(value, normed, scaled, r.gain[0:1, :])


class Copies:
    def __init__(self, pairs, sems):
        self.copies = {
            key: pltpu.make_async_copy(src, dst, sems.at[index])
            for index, (key, (src, dst)) in enumerate(pairs.items())
        }

    def start(self, *keys):
        for key in keys:
            self.copies[key].start()

    def wait(self, *keys):
        for key in keys:
            self.copies[key].wait()


def run_kernel(name, body, inputs, outputs, scratch, collective_id, vmem, in_vmem=()):
    flat, layout = [], []
    for key, value in scratch.items():
        group = value if isinstance(value, list) else [value]
        layout.append((key, len(group), isinstance(value, list)))
        flat.extend(group)
    plain = list(inputs) + list(outputs)

    def kernel(*refs):
        named = dict(zip(plain, refs))
        at = len(plain)
        for key, size, grouped in layout:
            named[key] = refs[at : at + size] if grouped else refs[at]
            at += size
        body(types.SimpleNamespace(**named))

    def spec(key):
        return pl.BlockSpec(memory_space=VMEM if key in in_vmem else pl.ANY)

    results = pl.pallas_call(
        kernel,
        name=name,
        in_specs=[spec(key) for key in inputs],
        out_specs=tuple(spec(key) for key in outputs),
        out_shape=tuple(jax.ShapeDtypeStruct(*value) for value in outputs.values()),
        scratch_shapes=flat,
        compiler_params=pltpu.CompilerParams(
            collective_id=collective_id, has_side_effects=True, vmem_limit_bytes=int(vmem * MIB)
        ),
    )(*inputs.values())
    return types.SimpleNamespace(**dict(zip(outputs, results)))


ATTENDED = ("joint", "out_all", "h", "qkv", "prob", "mixed")
SMALL = ("route_all", "gain_all", "bias_all", "router_all")
KEPT = ("routes", "router_in") + SMALL[1:3]


def layer_views(r, layer):
    r.gain, r.bias = r.gain_all.at[layer], r.bias_all.at[layer]
    r.router = r.router_all.at[layer]
    if hasattr(r, "route_all"):
        r.route = r.route_all.at[layer]


def forward_shapes(plan):
    rows, lanes, slots = plan.rows, plan.lanes, plan.slots
    return dict(
        joint=((2, 512, 384), BF16),
        out_all=((256, 512), BF16),
        x=((rows, 512), F32),
        y=((rows, 512), F32),
        h=((rows, 512), BF16),
        qkv=((2, rows, 384), BF16),
        prob=((2, plan.images, 2 * PAD, PAD), BF16),
        mixed=((2, rows, 128), BF16),
        h2=((lanes, 512), BF16),
        place=((plan.experts, lanes), F32),
        table=((lanes, 16), F32),
        recv=((slots, 512), BF16),
        ret=((slots, 512), BF16),
        slot_gate=((slots, 1), F32),
        up=((4, 512, 512), BF16),
        down=((4, 512, 512), BF16),
    )


def as_scratch(shapes):
    return {key: VMEM(*value) for key, value in shapes.items()}


def as_saved(shapes):
    return {"out_" + key: value for key, value in shapes.items()}


def pad_images(plan, source, target, staging):
    tokens = plan.images * SEQ
    staging[0:tokens, :] = source[...].astype(F32)
    target[...] = jnp.zeros_like(target)
    for image in range(plan.images):
        target[image * PAD : image * PAD + SEQ, :] = staging[
            image * SEQ : (image + 1) * SEQ, :
        ].astype(target.dtype)


def first_forward(plan, inputs, tokens):
    saved = forward_shapes(plan)

    def body(r):
        place = Place(plan.experts)
        place.greet()
        layer_views(r, 0)
        swap = HeadSwap(
            place, r.w_qkv.at[0], r.w_out.at[0], r.joint, r.out_all, r.swap
        )
        later = HeadSwap(
            place, r.w_qkv.at[1], r.w_out.at[1], r.joint_later, r.out_later, r.swap_later
        )
        saves = Copies({k: (getattr(r, k), getattr(r, "out_" + k)) for k in saved}, r.saves)
        total = CoreSum(place, r.total)
        weights = WeightGather(
            place, (r.w_up.at[0, 0], r.w_down.at[0, 0]), (r.up, r.down), r.weights
        )
        move = Exchange(place, plan.block, r.send, r.recv, r.move)
        back = Return(place, plan.block, plan.slots, r.ret, r.back, r.back_sems)
        swap.start_own()
        pad_images(plan, r.tokens, r.x, r.y)
        saves.start("x")
        place.met()
        swap.start_swap()
        weights.start()
        later.start_own()
        later.start_swap()
        swap.wait_own()

        def own_heads(image):
            first_norm(r, image)
            attend_forward(r, image, place.chip)

        each(0, plan.images, own_heads)
        route_places(plan, place, r)
        build_members(plan, place, r)
        swap.wait_swap(range(3))
        each(0, plan.images, lambda image: attend_forward(r, image, 1 - place.chip))
        swap.wait_swap((3,))
        each(0, plan.images, lambda image: attend_out(r, total, image))
        saves.start(*ATTENDED, "place")
        second_norm(plan, r, total)
        send_slots(plan, place, r, move)
        saves.start("y", "h2")
        norm_table(plan, r)
        saves.start("table")
        build_picks(plan, r)
        weights.pass_on()
        weights.finish()
        saves.start("up", "down")
        for low, high in groups(plan):
            move.wait(low, high, False)
            move.wait(low, high, True)
            read_gates(plan, r, low, high)
            rows = slice(low * plan.block, high * plan.block)
            rows_in = r.recv[rows, :]
            result = jnp.zeros((rows.stop - rows.start, 512), F32)
            for part in range(4):
                act = gelu(dot(rows_in, r.up[part])).astype(BF16)
                result = result + dot(act, r.down[part])
            r.ret[rows, :] = (result * r.slot_gate[rows, :]).astype(BF16)
            back.start(low, high)
        saves.start("recv", "ret", "slot_gate")
        saves.wait("x")
        back.pass_on()
        back.near()
        combined(plan, r, place.chip, r.back, r.x, False)
        back.far()
        combined(plan, r, 1 - place.chip, r.back, r.x, True)
        r.x[...] += r.y[...]
        back.finish()
        out = pltpu.make_async_copy(r.x, r.next, r.out_sem)
        out.start()
        saves.wait(*(k for k in saved if k != "x"))
        later.wait_own()
        later.wait_swap()
        out.wait()

    outputs = dict(
        as_saved(saved),
        next=((plan.rows, 512), F32),
        joint_later=saved["joint"],
        out_later=saved["out_all"],
    )
    scratch = dict(
        as_scratch(saved),
        codes=VMEM((4, plan.lanes), F32),
        member=VMEM((plan.slots, plan.lanes), BF16),
        gate=VMEM((plan.experts, plan.lanes), F32),
        picks=picks_scratch(plan),
        send=VMEM((plan.slots, 512), BF16),
        back=VMEM((4 * plan.slots, 512), BF16),
        total=CoreSum.scratch(plan.images),
        weights=WeightGather.scratch(),
        swap=HeadSwap.scratch(),
        swap_later=HeadSwap.scratch(),
        move=Exchange.scratch(plan.experts),
        back_sems=Return.scratch(plan.experts),
        saves=DMA((len(saved),)),
        out_sem=DMA,
    )
    return run_kernel(
        "first_forward", body, dict(inputs, tokens=tokens), outputs, scratch, 0, 62,
        SMALL + ("tokens",),
    )


def second_whole(plan, inputs, cotangent, start, joint, out_all):
    def body(r):
        place = Place(plan.experts)
        place.greet()
        layer_views(r, 1)
        r.gret, r.ret, r.dr, r.column = r.send, r.gsend, r.grecv, r.slot_gate
        loads = Copies(
            {k: (getattr(r, "in_" + k), getattr(r, k)) for k in ("x", "joint", "out_all")}, r.loads
        )
        total = CoreSum(place, r.total)
        total_back = CoreSum(place, r.total)
        weights = WeightGather(
            place, (r.w_up.at[1, 0], r.w_down.at[1, 0]), (r.up, r.down), r.weights
        )
        move = Exchange(place, plan.block, r.send, r.recv, r.move)
        gmove = Exchange(place, plan.block, r.gsend, r.grecv, r.gmove)
        back = Return(place, plan.block, plan.slots, r.ret, r.back, r.back_sems)
        gback = Return(place, plan.block, plan.slots, r.gret, r.gback, r.gback_sems)
        loads.start("x", "joint", "out_all")
        pad_images(plan, r.cotangent, r.g, r.y)
        route_places(plan, place, r)
        build_members(plan, place, r)
        r.gsend[...] = dot(r.member[:, : plan.rows], r.g[...]).astype(BF16)
        place.met()
        weights.start()
        gmove.start_all()
        loads.wait("x", "joint", "out_all")

        def heads(image):
            first_norm(r, image)
            for side in range(2):
                attend_forward(r, image, side)
            attend_out(r, total, image)

        each(0, plan.images, heads)
        second_norm(plan, r, total)
        send_slots(plan, place, r, move)
        norm_table(plan, r)
        build_picks(plan, r)
        weights.pass_on()
        weights.finish()
        gmove.wait(0, plan.experts)
        for low, high in groups(plan):
            move.wait(low, high, False)
            move.wait(low, high, True)
            read_gates(plan, r, low, high)
            rows = slice(low * plan.block, high * plan.block)
            rows_in = r.recv[rows, :]
            gate = r.slot_gate[rows, :]
            raw = r.grecv[rows, :].astype(F32)
            scaled = (raw * gate).astype(BF16)
            r.dr[rows, :] = scaled
            result = jnp.zeros((rows.stop - rows.start, 512), F32)
            slots_grad = jnp.zeros((rows.stop - rows.start, 512), F32)
            for part in range(4):
                act, slope = gelu_both(dot(rows_in, r.up[part]))
                act = act.astype(BF16)
                r.act[part, rows, :] = act
                result = result + dot(act, r.down[part])
                pre_grad = (dot_nt(scaled, r.down[part]) * slope).astype(BF16)
                r.dpre[part, rows, :] = pre_grad
                slots_grad = slots_grad + dot_nt(pre_grad, r.up[part])
            result = result * gate
            r.ret[rows, :] = result.astype(BF16)
            column = jnp.sum(result * raw, -1, keepdims=True)
            return_gradient(plan, r, low, high, slots_grad, column)
            gback.start(low, high)
        back.start(0, plan.experts)
        expert_grads(plan, place, r, r.near)
        outs = near_outs(place, r)

        def between():
            near_sums(place, r, r.near)
            for copy in outs:
                copy.start()

        back_to_attention(plan, place, r, gback, between)
        back.pass_on()
        each(0, plan.images, lambda image: attend_backward(r, total_back, image))
        pack_out(plan, place, r)
        pack_qkv(plan, place, r)

        def input_grad(image):
            rows = image_rows(image)
            r.gin[rows, :] = first_norm_back(plan, r, total_back, image)

        each(0, plan.images, input_grad)
        out = pltpu.make_async_copy(r.gin, r.grad, r.late_sems.at[0])
        out.start()
        pack_small(plan, r)
        out_packed = pltpu.make_async_copy(r.packed, r.out_packed, r.late_sems.at[1])
        out_packed.start()
        back.near()
        combined(plan, r, place.chip, r.back, r.x, False)
        back.far()
        combined(plan, r, 1 - place.chip, r.back, r.x, True)
        for image in range(plan.images):
            rows = slice(image * PAD, image * PAD + SEQ)
            r.y[image * SEQ : (image + 1) * SEQ, :] = r.y[rows, :] + r.x[rows, :]
        r.result[...] = r.y[0 : plan.images * SEQ, :].astype(BF16)
        back.finish()
        gback.finish()
        for copy in outs + [out, out_packed]:
            copy.wait()

    outputs = {
        "result": (cotangent.shape, BF16),
        "grad": ((plan.rows, 512), F32),
        "out_packed": ((plan.packed, 128), BF16),
        "gfar": ((2, 512, 512), BF16),
        "gown": ((2, 512, 512), BF16),
    }
    scratch = dict(
        as_scratch({k: v for k, v in forward_shapes(plan).items() if k != "ret"}),
        codes=VMEM((4, plan.lanes), F32),
        member=VMEM((plan.slots, plan.lanes), BF16),
        gate=VMEM((plan.experts, plan.lanes), F32),
        picks=picks_scratch(plan),
        send=VMEM((plan.slots, 512), BF16),
        back=VMEM((4 * plan.slots, 512), BF16),
        total=CoreSum.scratch(plan.images),
        weights=WeightGather.scratch(),
        move=Exchange.scratch(plan.experts),
        back_sems=Return.scratch(plan.experts),
        gmove=Exchange.scratch(plan.experts),
        gback_sems=Return.scratch(plan.experts),
        gsend=VMEM((plan.slots, 512), BF16),
        grecv=VMEM((plan.slots, 512), BF16),
        g=VMEM((plan.rows, 512), BF16),
        out_sems=DMA((2, 2)),
        late_sems=DMA((2,)),
        loads=DMA((3,)),
        **backward_scratch(plan),
    )
    return run_kernel(
        "second_whole", body,
        dict(inputs, cotangent=cotangent, in_x=start, in_joint=joint, in_out_all=out_all),
        outputs, scratch, 1, 63, SMALL + ("cotangent", "result"),
    )


def backward_scratch(plan):
    return dict(
        gback=VMEM((4 * plan.slots, 512), BF16),
        act=VMEM((4, plan.slots, 512), BF16),
        dpre=VMEM((4, plan.slots, 512), BF16),
        gpart=VMEM((2, 4, 512, 512), BF16),
        high=VMEM((plan.blocks, 128), F32),
        low=VMEM((plan.blocks, 128), F32),
        dz=VMEM((plan.rows, 128), BF16),
        gin=VMEM((plan.rows, 512), F32),
        dproj=VMEM((2, plan.rows, 384), BF16),
        packed=VMEM((plan.packed, 128), BF16),
        vec=VMEM((8, 512), F32),
        near=PairSum.scratch_near(),
    )


def expert_out(place, r, layer, which):
    out = (r.grad_up, r.grad_down)[which]
    return pltpu.make_async_copy(
        r.y.at[pl.ds(which * 512, 512)], out.at[layer], r.expert_sems.at[layer, which]
    )


class Finals:
    def __init__(self, plan, r):
        self.plan, self.r = plan, r

    def write(self, layer, total):
        r, experts = self.r, self.plan.experts
        r.grad_out[layer] = total[0:512, :].astype(F32).T
        for part in range(3):
            r.grad_qkv[layer, part] = total[(part + 1) * 512 : (part + 2) * 512, :].astype(F32)
        count = 4 + experts
        small = total[2048 : 2048 + up_to(4 * count, 16), :].astype(F32)
        rows = jnp.concatenate(
            [small[part * count : (part + 1) * count] for part in range(4)], axis=1
        )
        r.grad_gain[layer] = rows[0:2]
        if self.plan.stored:
            r.grad_bias_one[layer : layer + 1, :] = rows[2:3]
            r.grad_bias_two[layer : layer + 1, :] = rows[3:4]
        else:
            r.grad_bias[layer] = rows[2:4]
        r.grad_router[layer] = rows[4:]


def first_backward(plan, inputs, saved, grad, gfar, gown, packed, out_shape):
    def body(r):
        place = Place(plan.experts)
        place.greet()
        layer_views(r, 0)
        r.gret, r.dr, r.column = r.gsend, r.grecv, r.slot_gate
        r.x = r.g
        loads = Copies(
            {k: (getattr(r, "in_" + k), getattr(r, k)) for k in list(saved) + ["g", "later"]},
            r.loads,
        )
        total = CoreSum(place, r.total)
        gmove = Exchange(place, plan.block, r.gsend, r.grecv, r.gmove)
        gback = Return(place, plan.block, plan.slots, r.gret, r.gback, r.gback_sems)
        later = ExpertSum(place, plan.panels, r.later, r.sum_later, r.later_sum)
        sooner = ExpertSum(place, plan.panels, r.packed, r.sum_first, r.sooner_sum)
        first_loads = ("g", "place", "recv", "up", "down", "ret", "slot_gate", "table")
        loads.start(*first_loads)
        loads.start(*(k for k in loads.copies if k not in first_loads + ("x",)))
        loads.wait("place")
        build_members(plan, place, r)
        loads.wait("g")
        r.gsend[...] = dot(r.member[:, : plan.rows], r.g[...].astype(BF16)).astype(BF16)
        place.met()
        gmove.start_all()
        for which in range(2):
            PairSum.far(place, r.gfar_later.at[which], r.far_later, which).start()
        own_copy = pltpu.make_async_copy(r.gown_later, r.own_later, r.own_sem)
        own_copy.start()
        loads.wait("recv", "up", "down")
        for low, high in groups(plan):
            rows = slice(low * plan.block, high * plan.block)
            for part in range(4):
                act, slope = gelu_both(dot(r.recv[rows, :], r.up[part]))
                r.act[part, rows, :] = act.astype(BF16)
                r.dpre[part, rows, :] = slope.astype(BF16)
        loads.wait("table")
        build_picks(plan, r)
        loads.wait("ret", "slot_gate", "later")
        for low, high in groups(plan):
            gmove.wait(low, high)
            rows = slice(low * plan.block, high * plan.block)
            raw = r.grecv[rows, :].astype(F32)
            scaled = (raw * r.slot_gate[rows, :]).astype(BF16)
            r.dr[rows, :] = scaled
            slots_grad = jnp.zeros((rows.stop - rows.start, 512), F32)
            for part in range(4):
                pre_grad = (
                    dot_nt(scaled, r.down[part]) * r.dpre[part, rows, :].astype(F32)
                ).astype(BF16)
                r.dpre[part, rows, :] = pre_grad
                slots_grad = slots_grad + dot_nt(pre_grad, r.up[part])
            column = jnp.sum(r.ret[rows, :].astype(F32) * raw, -1, keepdims=True)
            return_gradient(plan, r, low, high, slots_grad, column)
            gback.start(low, high)
        expert_grads(plan, place, r, r.near)

        def between():
            later.every(later.step_pair)
            near_sums(place, r, r.near)
            for which in range(2):
                PairSum.far(place, r.gpart.at[which, place.chip_peer], r.far, which).start()

        loads.wait(*(k for k in loads.copies if k not in first_loads + ("later", "x")))
        back_to_attention(plan, place, r, gback, between)
        loads.start("x")
        later.every(later.step_scatter)
        pack_out(plan, place, r)
        sooner.step_pair(0)
        own_copy.wait()
        outs = [expert_out(place, r, layer, which) for layer in range(2) for which in range(2)]
        for which in range(2):
            PairSum.far(place, r.gfar_later.at[which], r.far_later, which).wait()
            r.y[which * 512 : (which + 1) * 512, :] = (
                r.own_later[which].astype(F32) + r.far_later[0][which].astype(F32)
            )
            outs[2 + which].start()
        half = plan.images // 2
        each(0, half, lambda image: attend_backward(r, total, image))
        later.every(later.step_share)
        sooner.step_scatter(0)
        each(half, plan.images, lambda image: attend_backward(r, total, image))
        pack_qkv(plan, place, r)
        panels = len(plan.panels)
        for panel in range(1, panels - 1):
            sooner.step_pair(panel)
        later.every(later.step_out)
        loads.wait("x")
        for image in range(plan.images):
            out = first_norm_back(plan, r, total, image)
            r.grad[image * SEQ : (image + 1) * SEQ, :] = out[:SEQ]
        pack_small(plan, r)
        sooner.step_pair(panels - 1)
        for panel in range(1, panels):
            sooner.step_scatter(panel)
        later.every(later.step_end)
        finals = Finals(plan, r)
        finals.write(1, r.sum_later)
        sooner.every(sooner.step_share)
        for which in range(2):
            outs[2 + which].wait()
            PairSum.far(place, r.gpart.at[which, place.chip_peer], r.far, which).wait()
            r.y[which * 512 : (which + 1) * 512, :] = (
                r.gpart[which, place.tensor].astype(F32) + r.far[0][which].astype(F32)
            )
            outs[which].start()
        gback.finish()
        sooner.every(sooner.step_out)
        sooner.every(sooner.step_end)
        finals.write(0, r.sum_first)
        for which in range(2):
            outs[which].wait()

    outputs = {
        "grad": (out_shape, F32),
        "grad_up": ((2, 512, 512), F32),
        "grad_down": ((2, 512, 512), F32),
        "grad_qkv": ((2, 3, 512, 128), F32),
        "grad_out": ((2, 128, 512), F32),
        "grad_gain": ((2, 2, 512), F32),
        "grad_bias": ((2, 2, 512), F32),
        "grad_router": ((2, plan.experts, 512), F32),
    }
    scratch = dict(
        as_scratch({k: v for k, v in forward_shapes(plan).items() if k != "x"}),
        member=VMEM((plan.slots, plan.lanes), BF16),
        picks=picks_scratch(plan),
        total=CoreSum.scratch(plan.images),
        gmove=Exchange.scratch(plan.experts),
        gback_sems=Return.scratch(plan.experts),
        gsend=VMEM((plan.slots, 512), BF16),
        grecv=VMEM((plan.slots, 512), BF16),
        g=VMEM((plan.rows, 512), F32),
        later=VMEM((plan.packed, 128), BF16),
        own_later=VMEM((2, 512, 512), BF16),
        sum_first=VMEM((plan.packed, 128), BF16),
        sum_later=VMEM((plan.packed, 128), BF16),
        expert_sems=DMA((2, 2)),
        own_sem=DMA,
        far=PairSum.scratch_far(),
        far_later=PairSum.scratch_far(),
        later_sum=ExpertSum.scratch(plan),
        sooner_sum=ExpertSum.scratch(plan),
        loads=DMA((len(saved) + 2,)),
        **backward_scratch(plan),
    )
    arrays = dict({"in_" + k: v for k, v in saved.items()}, in_g=grad, in_later=packed)
    return run_kernel(
        "first_backward", body,
        dict(inputs, gfar_later=gfar, gown_later=gown, **arrays),
        outputs, scratch, 2, 63,
        SMALL + tuple(k for k in outputs if k not in ("grad_up", "grad_down")),
    )


def expert_forward_backward(plan, r, low, high):
    rows = slice(low * plan.block, high * plan.block)
    rows_in = r.recv[rows, :]
    gate = r.slot_gate[rows, :]
    raw = r.grecv[rows, :].astype(F32)
    scaled = (raw * gate).astype(BF16)
    r.dr[rows, :] = scaled
    result = jnp.zeros((rows.stop - rows.start, 512), F32)
    slots_grad = jnp.zeros((rows.stop - rows.start, 512), F32)
    for part in range(4):
        act, slope = gelu_both(dot(rows_in, r.up[part]))
        act = act.astype(BF16)
        r.act[part, rows, :] = act
        result = result + dot(act, r.down[part])
        pre_grad = (dot_nt(scaled, r.down[part]) * slope).astype(BF16)
        r.dpre[part, rows, :] = pre_grad
        slots_grad = slots_grad + dot_nt(pre_grad, r.up[part])
    result = result * gate
    r.ret[rows, :] = result.astype(BF16)
    column = jnp.sum(result * raw, -1, keepdims=True)
    return_gradient(plan, r, low, high, slots_grad, column)


def expert_forward(plan, r, low, high):
    rows = slice(low * plan.block, high * plan.block)
    rows_in = r.recv[rows, :]
    result = jnp.zeros((rows.stop - rows.start, 512), F32)
    for part in range(4):
        act = gelu(dot(rows_in, r.up[part])).astype(BF16)
        result = result + dot(act, r.down[part])
    r.ret[rows, :] = (result * r.slot_gate[rows, :]).astype(BF16)


def expert_again(plan, r, low, high):
    rows = slice(low * plan.block, high * plan.block)
    for part in range(4):
        act, slope = gelu_both(dot(r.recv[rows, :], r.up[part]))
        r.act[part, rows, :] = act.astype(BF16)
        r.dpre[part, rows, :] = slope.astype(BF16)


def expert_backward(plan, r, low, high):
    rows = slice(low * plan.block, high * plan.block)
    raw = r.grecv[rows, :].astype(F32)
    scaled = (raw * r.slot_gate[rows, :]).astype(BF16)
    r.dr[rows, :] = scaled
    slots_grad = jnp.zeros((rows.stop - rows.start, 512), F32)
    for part in range(4):
        pre_grad = (dot_nt(scaled, r.down[part]) * r.dpre[part, rows, :].astype(F32)).astype(BF16)
        r.dpre[part, rows, :] = pre_grad
        slots_grad = slots_grad + dot_nt(pre_grad, r.up[part])
    column = jnp.sum(r.ret[rows, :].astype(F32) * raw, -1, keepdims=True)
    return_gradient(plan, r, low, high, slots_grad, column)


def prepare(plan, r):
    lane = lax.broadcasted_iota(jnp.int32, (2, plan.lanes), 1)
    tokens = plan.images * SEQ
    empty = jnp.zeros((128 - plan.experts, 512), F32)
    for layer in range(2):
        router = r.router_in[layer].astype(F32)
        r.router_all[layer] = jnp.concatenate([router, empty], axis=0).astype(BF16)
        r.route_all[layer] = jnp.zeros((2, plan.lanes), jnp.int32)
        r.route_all[layer, :, 0:tokens] = r.routes[layer]
        raw = r.route_all[layer]
        spread = jnp.full((2, plan.lanes), -1, jnp.int32)
        for image in range(plan.images):
            moved = pltpu.roll(raw, image * (PAD - SEQ), 1) if image else raw
            inside = (lane >= image * PAD) & (lane < image * PAD + SEQ)
            spread = jnp.where(inside, moved, spread)
        r.route_all[layer] = spread


SAVED = ATTENDED + ("x", "y", "h2", "up", "down")


def one_kernel(plan, inputs):
    shapes = forward_shapes(plan)
    shape_of_edge = inputs["tokens"].shape

    def body(r):
        place = Place(plan.experts)
        place.greet()
        first = types.SimpleNamespace(**vars(r))
        second = types.SimpleNamespace(**vars(r))
        for layer, view in ((0, first), (1, second)):
            layer_views(view, layer)
            for key in ("place", "codes", "table", "recv", "slot_gate", "packed"):
                setattr(view, key, getattr(r, f"{key}_{layer}"))
            view.column = view.slot_gate
            view.gret, view.dr = r.send, r.grecv
        first.ret, second.ret = r.ret_0, r.gsend
        saves = Copies({k: (getattr(r, k), getattr(r, "out_" + k)) for k in SAVED}, r.saves)
        loads = Copies({k: (getattr(r, "out_" + k), getattr(r, k)) for k in SAVED}, r.loads)
        edges = Copies(
            {"tokens": (r.tokens, r.edge), "cotangent": (r.cotangent, r.edge),
             "result": (r.edge, r.result)}, r.edges,
        )
        total = CoreSum(place, r.total)
        swaps = [
            HeadSwap(place, r.w_qkv.at[k], r.w_out.at[k], r.joint, r.out_all, sems)
            for k, sems in enumerate((r.swap_0, r.swap_1))
        ]
        gathers = [
            WeightGather(place, (r.w_up.at[k, 0], r.w_down.at[k, 0]), (r.up, r.down), sems)
            for k, sems in enumerate((r.weights_0, r.weights_1))
        ]
        moves = [
            Exchange(place, plan.block, r.send, dst, sems)
            for dst, sems in ((r.recv_0, r.move_0), (r.recv_1, r.move_1))
        ]
        gmoves = [
            Exchange(place, plan.block, src, r.grecv, sems)
            for src, sems in ((r.send, r.gmove_0), (r.gsend, r.gmove_1))
        ]
        backs = [
            Return(place, plan.block, plan.slots, src, r.back, sems)
            for src, sems in ((r.ret_0, r.back_0), (r.gsend, r.back_1))
        ]
        gbacks = [
            Return(place, plan.block, plan.slots, r.send, r.gback, sems)
            for sems in (r.gback_0, r.gback_1)
        ]
        sums = [
            ExpertSum(place, plan.panels, src, out, refs)
            for src, out, refs in (
                (r.packed_0, r.sum_0, r.sums_0), (r.packed_1, r.sum_1, r.sums_1)
            )
        ]
        experts = plan.experts

        edges.start("tokens")
        swaps[0].start_own()
        place.met()
        swaps[0].start_swap()
        gathers[0].start()
        prepare(plan, r)
        edges.wait("tokens")
        pad_images(plan, r.edge, r.x, r.y)
        edges.start("cotangent")
        saves.start("x")
        edges.wait("cotangent")
        pad_images(plan, r.edge, r.g, r.y)
        route_places(plan, place, second)
        build_members(plan, place, second)
        r.gsend[...] = dot(r.member[:, : plan.rows], r.g[...].astype(BF16)).astype(BF16)
        gmoves[1].start_all()
        swaps[0].wait_own()

        def own_heads(view):
            def one(image):
                first_norm(view, image)
                attend_forward(view, image, place.chip)

            each(0, plan.images, one)

        def other_heads(view, swap):
            swap.wait_swap(range(3))
            each(0, plan.images, lambda image: attend_forward(view, image, 1 - place.chip))
            swap.wait_swap((3,))
            each(0, plan.images, lambda image: attend_out(view, total, image))

        own_heads(first)
        route_places(plan, place, first)
        build_members(plan, place, first)
        other_heads(first, swaps[0])
        saves.start(*ATTENDED)
        second_norm(plan, first, total)
        send_slots(plan, place, first, moves[0])
        saves.start("y", "h2")
        norm_table(plan, first)
        build_picks(plan, first)
        gathers[0].pass_on()
        gathers[0].finish()
        saves.start("up", "down")
        gmoves[1].wait(0, experts)
        for low, high in groups(plan):
            moves[0].wait(low, high, False)
            moves[0].wait(low, high, True)
            read_gates(plan, first, low, high)
            expert_forward(plan, first, low, high)
            backs[0].start(low, high)
        build_members(plan, place, second)
        saves.wait(*SAVED)
        backs[0].pass_on()
        backs[0].near()
        swaps[1].start_own()
        swaps[1].start_swap()
        gathers[1].start()
        combined(plan, r, place.chip, r.back, r.x, False)
        backs[0].far()
        combined(plan, r, 1 - place.chip, r.back, r.x, True)
        r.x[...] += r.y[...]
        backs[0].finish()

        swaps[1].wait_own()
        own_heads(second)
        other_heads(second, swaps[1])
        second_norm(plan, second, total)
        send_slots(plan, place, second, moves[1])
        build_members(plan, place, first)
        norm_table(plan, second)
        build_picks(plan, second)
        gathers[1].pass_on()
        gathers[1].finish()
        for low, high in groups(plan):
            moves[1].wait(low, high, False)
            moves[1].wait(low, high, True)
            read_gates(plan, second, low, high)
            expert_forward_backward(plan, second, low, high)
            gbacks[1].start(low, high)
        expert_grads(plan, place, second, r.near)
        backs[1].start(0, experts)
        loads.start("up", "down")

        def inbox(layer, which):
            if layer:
                return r.recv_1.at[pl.ds(0, 512)] if which else r.far_in
            return r.back.at[pl.ds(which * 512, 512)]

        def far(layer, which):
            return place.to_chip(
                r.gpart.at[which, place.chip_peer], inbox(layer, which),
                r.far_sems.at[0, layer, which], r.far_sems.at[1, layer, which],
            )

        def between_second():
            near_sums(place, second, r.near)
            far(1, 0).start()

        back_to_attention(plan, place, second, gbacks[1], between_second)
        gbacks[1].finish()
        backs[1].pass_on()
        far(1, 1).start()
        each(0, plan.images, lambda image: attend_backward(second, total, image))

        def input_grad(image):
            r.g[image_rows(image), :] = first_norm_back(plan, second, total, image)

        few(0, plan.images, input_grad)

        r.send[...] = dot(r.member[:, : plan.rows], r.g[...].astype(BF16)).astype(BF16)
        gmoves[0].start_all()
        pack_out(plan, place, second)
        pack_qkv(plan, place, second)
        pack_small(plan, second)
        loads.start(*ATTENDED, "h2")
        sums[1].every(sums[1].step_pair)
        loads.wait("up", "down")
        for low, high in groups(plan):
            expert_again(plan, first, low, high)
        for low, high in groups(plan):
            gmoves[0].wait(low, high)
            expert_backward(plan, first, low, high)
            gbacks[0].start(low, high)
        backs[1].near()
        combined(plan, r, place.chip, r.back, r.x, False)
        backs[1].far()
        combined(plan, r, 1 - place.chip, r.back, r.x, True)
        for image in range(plan.images):
            rows = slice(image * PAD, image * PAD + SEQ)
            r.y[image * SEQ : (image + 1) * SEQ, :] = r.y[rows, :] + r.x[rows, :]
        r.edge[...] = r.y[0 : plan.images * SEQ, :].astype(BF16)
        edges.start("result")
        backs[1].finish()
        loads.start("y", "x")
        build_picks(plan, first)
        sums[1].every(sums[1].step_scatter)
        loads.wait(*ATTENDED, "h2", "y", "x")

        def weights_out(layer, which):
            return pltpu.make_async_copy(
                r.gpart.at[which, place.tensor], r.grad_experts.at[layer, which],
                r.expert_sems.at[layer, which],
            )

        def add_far(layer):
            for which in range(2):
                far(layer, which).wait()
                r.gpart[which, place.tensor] = (
                    r.gpart[which, place.tensor].astype(F32)
                    + inbox(layer, which)[...].astype(F32)
                ).astype(BF16)
                weights_out(layer, which).start()

        def between_first():
            add_far(1)
            for which in range(2):
                weights_out(1, which).wait()
            expert_grads(plan, place, first, r.near)
            near_sums(place, first, r.near)
            for which in range(2):
                far(0, which).start()

        back_to_attention(plan, place, first, gbacks[0], between_first)
        sums[1].every(sums[1].step_share)
        pack_out(plan, place, first)
        sums[0].step_pair(0)
        half = plan.images // 2
        each(0, half, lambda image: attend_backward(first, total, image))
        sums[1].every(sums[1].step_out)
        sums[0].step_scatter(0)
        each(half, plan.images, lambda image: attend_backward(first, total, image))
        pack_qkv(plan, place, first)
        panels = len(plan.panels)
        for panel in range(1, panels - 1):
            sums[0].step_pair(panel)
        for image in range(plan.images):
            value = first_norm_back(plan, first, total, image)
            r.g[image * SEQ : (image + 1) * SEQ, :] = value[:SEQ]
        rows_out = pl.ds(0, up_to(plan.images * SEQ, 16))
        out = pltpu.make_async_copy(r.g.at[rows_out], r.grad, r.out_sems.at[0])
        out.start()
        pack_small(plan, first)
        sums[0].step_pair(panels - 1)
        for panel in range(1, panels):
            sums[0].step_scatter(panel)
        sums[1].every(sums[1].step_end)
        sum_out = [
            pltpu.make_async_copy(src, dst, r.out_sems.at[1 + k])
            for k, (src, dst) in enumerate(((r.sum_0, r.total_0), (r.sum_1, r.total_1)))
        ]
        sum_out[1].start()
        add_far(0)
        sums[0].every(sums[0].step_share)
        gbacks[0].finish()
        sums[0].every(sums[0].step_out)
        sums[0].every(sums[0].step_end)
        sum_out[0].start()
        edges.wait("result")
        for which in range(2):
            weights_out(0, which).wait()
        for copy in [out] + sum_out:
            copy.wait()

    rows, slots = plan.rows, plan.slots
    outputs = {"out_" + key: shapes[key] for key in SAVED}
    outputs.update(
        result=(shape_of_edge, BF16),
        grad=((up_to(plan.images * SEQ, 16), 512), F32),
        grad_experts=((2, 2, 512, 512), BF16),
        total_0=((plan.packed, 128), BF16),
        total_1=((plan.packed, 128), BF16),
    )
    scratch = {key: VMEM(*shapes[key]) for key in SAVED}
    for layer in range(2):
        for key in ("place", "table", "recv", "slot_gate"):
            scratch[f"{key}_{layer}"] = VMEM(*shapes[key])
        scratch[f"codes_{layer}"] = VMEM((4, plan.lanes), F32)
        scratch[f"packed_{layer}"] = VMEM((plan.packed, 128), BF16)
        scratch[f"sum_{layer}"] = VMEM((plan.packed, 128), BF16)
        scratch[f"sums_{layer}"] = ExpertSum.scratch(plan)
        scratch[f"swap_{layer}"] = HeadSwap.scratch()
        scratch[f"weights_{layer}"] = WeightGather.scratch()
        scratch[f"move_{layer}"] = Exchange.scratch(plan.experts)
        scratch[f"gmove_{layer}"] = Exchange.scratch(plan.experts)
        scratch[f"back_{layer}"] = Return.scratch(plan.experts)
        scratch[f"gback_{layer}"] = Return.scratch(plan.experts)
    scratch.update(backward_scratch(plan))
    scratch.pop("packed")
    scratch.update(
        edge=VMEM(shape_of_edge, BF16),
        route_all=VMEM((2, 2, plan.lanes), jnp.int32),
        router_all=VMEM((2, 128, 512), BF16),
        g=VMEM((rows, 512), F32),
        ret_0=VMEM((slots, 512), BF16),
        member=VMEM((slots, plan.lanes), BF16),
        gate=VMEM((plan.experts, plan.lanes), F32),
        picks=picks_scratch(plan),
        send=VMEM((slots, 512), BF16),
        gsend=VMEM((slots, 512), BF16),
        grecv=VMEM((slots, 512), BF16),
        back=VMEM((4 * slots, 512), BF16),
        total=CoreSum.scratch(plan.images),
        far_in=VMEM((512, 512), BF16),
        far_sems=DMA((2, 2, 2)),
        saves=DMA((len(SAVED),)),
        loads=DMA((len(SAVED),)),
        edges=DMA((3,)),
        expert_sems=DMA((2, 2)),
        out_sems=DMA((3,)),
    )
    return run_kernel("two_blocks", body, inputs, outputs, scratch, 3, 63.75, KEPT)


def final_form(plan, raw):
    experts = plan.experts
    tokens = plan.images * SEQ
    names = (
        "result", "grad", "grad_up", "grad_down", "grad_qkv", "grad_out", "grad_gain",
        "grad_bias_one", "grad_bias_two", "grad_router",
    )

    def kernel(*refs):
        result, grad, weights, total_0, total_1 = refs[:5]
        r = types.SimpleNamespace(**dict(zip(names, refs[5:15])))
        rows_buf, grad_buf, low, full, packs, sems, sems_out = refs[15:]
        loads = [
            pltpu.make_async_copy(src, dst, sems.at[k])
            for k, (src, dst) in enumerate(
                [(total_0, packs.at[0]), (total_1, packs.at[1]), (result, rows_buf)]
                + [(weights.at[k], low.at[k]) for k in range(2)] + [(grad, grad_buf)]
            )
        ]
        for copy in loads:
            copy.start()
        loads[2].wait()
        outs = [pltpu.make_async_copy(rows_buf, r.result, sems_out.at[0])]
        outs[0].start()
        for layer in range(2):
            loads[3 + layer].wait()
            for which, out in enumerate((r.grad_up, r.grad_down)):
                full[layer, which] = low[layer, which].astype(F32)
                outs.append(
                    pltpu.make_async_copy(
                        full.at[layer, which], out.at[layer], sems_out.at[1 + 2 * layer + which]
                    )
                )
                outs[-1].start()
        for layer in range(2):
            loads[layer].wait()
            Finals(plan, r).write(layer, packs[layer])
        loads[5].wait()
        r.grad[...] = grad_buf[0:tokens, :]
        for copy in outs:
            copy.wait()

    shapes = (
        ((tokens, 512), BF16), ((tokens, 512), F32), ((2, 512, 512), F32), ((2, 512, 512), F32),
        ((2, 3, 512, 128), F32), ((2, 128, 512), F32), ((2, 2, 512), F32), ((2, 512), F32),
        ((2, 512), F32), ((2, experts, 512), F32),
    )
    far_away = ("result", "grad_up", "grad_down")
    outs = pl.pallas_call(
        kernel,
        name="final_form",
        in_specs=[pl.BlockSpec(memory_space=pl.ANY)] * 5,
        out_specs=tuple(
            pl.BlockSpec(memory_space=pl.ANY if key in far_away else VMEM) for key in names
        ),
        out_shape=tuple(jax.ShapeDtypeStruct(*shape) for shape in shapes),
        scratch_shapes=[
            VMEM((tokens, 512), BF16), VMEM((up_to(tokens, 16), 512), F32),
            VMEM((2, 2, 512, 512), BF16), VMEM((2, 2, 512, 512), F32),
            VMEM((2, plan.packed, 128), BF16), DMA((6,)), DMA((5,)),
        ],
        compiler_params=pltpu.CompilerParams(vmem_limit_bytes=63 * MIB),
    )(raw.result, raw.grad, raw.grad_experts, raw.total_0, raw.total_1)
    return types.SimpleNamespace(**dict(zip(names, outs)))


def body(tokens, routes, ln_gain, ln_bias, w_qkv, w_out, w_router, w_up, w_down, cotangent):
    tok_rows = tokens.shape[0]
    experts = w_router.shape[2]
    plan = Plan(tok_rows, experts)
    if plan.stored:
        raw = one_kernel(
            plan,
            dict(
                gain_all=ln_gain, bias_all=ln_bias, w_qkv=w_qkv, w_out=w_out,
                w_up=w_up, w_down=w_down, tokens=tokens, cotangent=cotangent,
                routes=routes.transpose(0, 2, 1), router_in=w_router.transpose(0, 2, 1),
            ),
        )
        ends = final_form(plan, raw)
        return (
            ends.result, ends.grad, ends.grad_gain, ends.grad_bias_one, ends.grad_bias_two,
            ends.grad_qkv, ends.grad_out, ends.grad_router.transpose(0, 2, 1),
            ends.grad_up[:, None], ends.grad_down[:, None],
        )
    router_rows = jnp.pad(w_router.transpose(0, 2, 1), ((0, 0), (0, 128 - experts), (0, 0)))
    route_rows = routes.reshape(2, plan.images, SEQ, 2)
    route_rows = jnp.pad(
        route_rows, ((0, 0), (0, 0), (0, PAD - SEQ), (0, 0)), constant_values=-1
    ).reshape(2, plan.rows, 2)
    route_rows = jnp.pad(
        route_rows, ((0, 0), (0, plan.lanes - plan.rows), (0, 0)), constant_values=-1
    ).transpose(0, 2, 1)
    small = {"gain_all": ln_gain, "bias_all": ln_bias, "router_all": router_rows}
    weights = {"w_up": w_up, "w_down": w_down}
    one = first_forward(
        plan, dict(small, route_all=route_rows, w_qkv=w_qkv, w_out=w_out, **weights), tokens
    )
    two = second_whole(
        plan, dict(small, route_all=route_rows, **weights), cotangent,
        one.next, one.joint_later, one.out_later,
    )
    saved = {key: getattr(one, "out_" + key) for key in forward_shapes(plan)}
    three = first_backward(
        plan, small, saved, two.grad, two.gfar, two.gown, two.out_packed, tokens.shape
    )
    return (
        two.result, three.grad, three.grad_gain, three.grad_bias[:, 0], three.grad_bias[:, 1],
        three.grad_qkv, three.grad_out, three.grad_router.transpose(0, 2, 1),
        three.grad_up[:, None], three.grad_down[:, None],
    )


def solution(mesh):
    in_specs = (
        P(EXPERT, None),
        P(None, EXPERT, None),
        P(),
        P(),
        P(None, None, None, TENSOR),
        P(None, TENSOR, None),
        P(),
        P(None, EXPERT, None, TENSOR),
        P(None, EXPERT, TENSOR, None),
        P(EXPERT, None),
    )
    out_specs = (
        P(EXPERT, None),
        P(EXPERT, None),
        P(),
        P(),
        P(),
        P(None, None, None, TENSOR),
        P(None, TENSOR, None),
        P(),
        P(None, EXPERT, None, TENSOR),
        P(None, EXPERT, TENSOR, None),
    )
    return jax.shard_map(body, mesh=mesh, in_specs=in_specs, out_specs=out_specs, check_vma=False)
```

```python
import types

import jax
import jax.numpy as jnp
from jax import lax
from jax.experimental import pallas as pl
from jax.experimental.pallas import tpu as pltpu
from jax.sharding import PartitionSpec as P

HEAD_DIM = 64
SEQ = 197
PAD = 208
EPS = 1e-06
MESH = pl.DeviceIdType.MESH
EXPERT, TENSOR = "expert", "tensor"
F32 = jnp.float32
BF16 = jnp.bfloat16
SCALE = HEAD_DIM ** (-0.5)
MIB = 1 << 20
VMEM = pltpu.VMEM
DMA = pltpu.SemaphoreType.DMA


def up_to(count, multiple):
    return -(-count // multiple) * multiple


def dot(left, right):
    return lax.dot_general(left, right, (((1,), (0,)), ((), ())), preferred_element_type=F32)


def dot_nt(left, right):
    return lax.dot_general(left, right, (((1,), (1,)), ((), ())), preferred_element_type=F32)


def dot_tn(left, right):
    return lax.dot_general(left, right, (((0,), (0,)), ((), ())), preferred_element_type=F32)


def norm_parts(rows):
    centered = rows - jnp.mean(rows, -1, keepdims=True)
    scaled = lax.rsqrt(jnp.mean(centered * centered, -1, keepdims=True) + EPS)
    return centered * scaled, scaled


def norm_pull(grad_in, normed, scaled, gain_row):
    grad_normed = grad_in * gain_row
    inner = (
        grad_normed
        - jnp.mean(grad_normed, -1, keepdims=True)
        - normed * jnp.mean(grad_normed * normed, -1, keepdims=True)
    )
    return inner * scaled


def gelu(pre):
    inner = pre * (0.7978845608028654 + 0.035677408136300125 * (pre * pre))
    return 0.5 * pre * (1.0 + jnp.tanh(inner))


def gelu_both(pre):
    square = pre * pre
    inner = pre * (0.7978845608028654 + 0.035677408136300125 * square)
    bent = jnp.tanh(inner)
    half = 0.5 + 0.5 * bent
    slope = half + half * (1.0 - bent) * pre * (
        0.7978845608028654 + 0.10703222440890037 * square
    )
    return half * pre, slope


class Plan:
    def __init__(self, tok_rows, experts):
        self.images = tok_rows // SEQ
        self.rows = self.images * PAD
        self.lanes = up_to(self.rows, 128)
        self.experts = experts
        self.per_rank = max(1, 10 * tok_rows // (4 * experts * 4))
        self.capacity = 4 * self.per_rank
        self.block = up_to(self.per_rank + 2, 16)
        self.slots = experts * self.block
        self.blocks = up_to(4 * experts, 128)
        self.stored = 4 * self.slots <= 2560
        most = 320
        self.group = max(
            size for size in range(1, experts)
            if experts % size == 0 and (size == 1 or size * self.block <= most)
        )
        main = up_to(512, 16 * experts)
        small = up_to(4 * (4 + experts), 16 * experts)
        self.panels = [(start, main) for start in range(0, 2048, main)] + [(2048, small)]
        self.packed = 2048 + small


def image_rows(image):
    if isinstance(image, int):
        return pl.ds(image * PAD, PAD)
    return pl.ds(pl.multiple_of(image * PAD, PAD), PAD)


def each(low, high, use):
    def one(index, carry):
        use(index)
        return carry

    lax.fori_loop(low, high, one, 0)


def few(low, high, use):
    if high - low > 8:
        each(low, high, use)
        return
    for index in range(low, high):
        use(index)


class Place:
    def __init__(self, experts):
        self.tensor = lax.axis_index(TENSOR)
        self.core = lax.rem(self.tensor, 2)
        self.chip = lax.div(self.tensor, 2)
        self.core_peer = self.tensor + 1 - 2 * self.core
        self.chip_peer = lax.rem(self.tensor + 2, 4)
        self.experts = experts
        self.expert = lax.axis_index(EXPERT)

    def ahead(self, step):
        return lax.rem(self.expert + step, self.experts)

    def behind(self, step):
        return lax.rem(self.expert + self.experts - step, self.experts)

    def greet(self):
        barrier = pltpu.get_barrier_semaphore()
        for peer in (self.core_peer, self.chip_peer):
            pl.semaphore_signal(barrier, inc=1, device_id={TENSOR: peer}, device_id_type=MESH)

        def one(step):
            pl.semaphore_signal(
                barrier, inc=1, device_id={EXPERT: self.ahead(step)}, device_id_type=MESH
            )

        each(1, self.experts, one)

    def met(self):
        pl.semaphore_wait(pltpu.get_barrier_semaphore(), 2 + self.experts - 1)

    def to_core(self, src, dst, send, recv):
        return pltpu.make_async_remote_copy(
            src_ref=src, dst_ref=dst, send_sem=send, recv_sem=recv,
            device_id={TENSOR: self.core_peer}, device_id_type=MESH,
        )

    def to_chip(self, src, dst, send, recv):
        return pltpu.make_async_remote_copy(
            src_ref=src, dst_ref=dst, send_sem=send, recv_sem=recv,
            device_id={TENSOR: self.chip_peer}, device_id_type=MESH,
        )

    def to_expert(self, expert, src, dst, send, recv):
        return pltpu.make_async_remote_copy(
            src_ref=src, dst_ref=dst, send_sem=send, recv_sem=recv,
            device_id={EXPERT: expert}, device_id_type=MESH,
        )


class CoreSum:
    def __init__(self, place, refs):
        self.place = place
        self.part, self.near, self.send, self.recv = refs

    @staticmethod
    def scratch(images):
        rows = (images * PAD, 512)
        return [VMEM(rows, BF16), VMEM(rows, BF16), DMA((images,)), DMA((images,))]

    def copy(self, image):
        rows = image_rows(image)
        return self.place.to_core(
            self.part.at[rows], self.near.at[rows], self.send.at[image], self.recv.at[image]
        )

    def put(self, image, value):
        self.part[image_rows(image), :] = value.astype(BF16)
        self.copy(image).start()

    def get(self, image):
        rows = image_rows(image)
        self.copy(image).wait()
        return self.part[rows, :].astype(F32) + self.near[rows, :].astype(F32)


class HeadSwap:
    def __init__(self, place, qkv, out, joint, out_all, refs):
        self.place, self.qkv, self.out = place, qkv, out
        self.joint, self.out_all = joint, out_all
        self.send, self.recv, self.local = refs

    @staticmethod
    def scratch():
        return [DMA((4,)), DMA((4,)), DMA((4,))]

    def ends(self, part):
        if part == 3:
            rows = pl.ds(pl.multiple_of(self.place.chip * 128, 128), 128)
            return self.out, self.out_all.at[rows]
        columns = pl.ds(part * 128, 128)
        return self.qkv.at[part], self.joint.at[self.place.chip, :, columns]

    def own(self, part):
        return pltpu.make_async_copy(*self.ends(part), self.local.at[part])

    def swap(self, part):
        return self.place.to_chip(*self.ends(part), self.send.at[part], self.recv.at[part])

    def start_own(self):
        for part in range(4):
            self.own(part).start()

    def start_swap(self):
        for part in range(4):
            self.swap(part).start()

    def wait_own(self):
        for part in range(4):
            self.own(part).wait()

    def wait_swap(self, parts=range(4)):
        for part in parts:
            self.swap(part).wait()


class Exchange:
    def __init__(self, place, block, src, dst, refs):
        self.place, self.block, self.src, self.dst = place, block, src, dst
        self.send, self.recv, self.local = refs

    @staticmethod
    def scratch(experts):
        return [DMA((2, experts)), DMA((2, experts)), DMA((2,))]

    def part(self, step, tail):
        base = pl.multiple_of(step * self.block, self.block)
        if tail is None:
            return pl.ds(base, self.block)
        if tail:
            return pl.ds(pl.multiple_of(base + self.block - 16, 16), 16)
        return pl.ds(base, self.block - 16)

    def own(self, tail=None):
        rows = self.part(0, tail)
        return pltpu.make_async_copy(
            self.src.at[rows], self.dst.at[rows], self.local.at[int(bool(tail))]
        )

    def copy(self, step, tail=None):
        rows, which = self.part(step, tail), int(bool(tail))
        return self.place.to_expert(
            self.place.ahead(step), self.src.at[rows], self.dst.at[rows],
            self.send.at[which, step], self.recv.at[which, step],
        )

    def start_all(self, tail=None):
        self.own(tail).start()
        each(1, self.place.experts, lambda step: self.copy(step, tail).start())

    def wait(self, low, high, tail=None):
        if low == 0:
            self.own(tail).wait()
        each(max(1, low), high, lambda step: self.copy(step, tail).wait())


class Return:
    def __init__(self, place, block, slots, src, dst, refs):
        self.place, self.block, self.slots, self.src, self.dst = place, block, slots, src, dst
        self.send, self.recv, self.local = refs

    @staticmethod
    def scratch(experts):
        return [DMA((4, experts)), DMA((4, experts)), DMA]

    def rows(self, quarter, step):
        return pl.ds(
            pl.multiple_of(quarter * self.slots + step * self.block, self.block), self.block
        )

    def own(self):
        return pltpu.make_async_copy(
            self.src.at[pl.ds(0, self.block)],
            self.dst.at[self.rows(self.place.tensor, 0)], self.local,
        )

    def home(self, step):
        rows = pl.ds(pl.multiple_of(step * self.block, self.block), self.block)
        return self.place.to_expert(
            self.place.behind(step), self.src.at[rows],
            self.dst.at[self.rows(self.place.tensor, step)],
            self.send.at[0, step], self.recv.at[0, step],
        )

    def to_chip(self, step):
        block = self.dst.at[self.rows(self.place.tensor, step)]
        return self.place.to_chip(block, block, self.send.at[1, step], self.recv.at[1, step])

    def to_core(self, step):
        block = self.dst.at[self.rows(self.place.tensor, step)]
        return self.place.to_core(block, block, self.send.at[2, step], self.recv.at[2, step])

    def on_to_core(self, step):
        block = self.dst.at[self.rows(self.place.chip_peer, step)]
        return self.place.to_core(block, block, self.send.at[3, step], self.recv.at[3, step])

    def start(self, low, high):
        if low == 0:
            self.own().start()
        each(max(1, low), high, lambda step: self.home(step).start())

    def pass_on(self, arrived=lambda quarter, step: None):
        place, last = self.place, self.place.experts

        def give(step):
            self.to_chip(step).start()
            self.to_core(step).start()
            arrived(place.tensor, step)

        def one(step):
            self.home(step).wait_recv()
            give(step)

        def two(step):
            one(step)
            self.on(step - self.LAG, arrived)

        self.own().wait()
        give(0)
        each(1, self.LAG, one)
        each(self.LAG, last, two)

    LAG = 2

    def on(self, step, arrived):
        self.to_chip(step).wait_recv()
        self.on_to_core(step).start()
        arrived(self.place.chip_peer, step)

    def near(self, arrived=lambda quarter, step: None):
        def one(step):
            self.to_core(step).wait_recv()
            arrived(self.place.core_peer, step)

        each(0, self.place.experts, one)

    def far(self, arrived=lambda quarter, step: None):
        place, last = self.place, self.place.experts
        each(last - self.LAG, last, lambda step: self.on(step, arrived))

        def one(step):
            self.on_to_core(step).wait_recv()
            arrived(3 - place.tensor, step)

        each(0, last, one)

    def finish(self):
        def one(step):
            self.to_chip(step).wait_send()
            self.to_core(step).wait_send()
            self.on_to_core(step).wait_send()

        each(0, self.place.experts, one)
        each(1, self.place.experts, lambda step: self.home(step).wait_send())


class WeightGather:
    def __init__(self, place, shards, wholes, refs):
        self.place, self.shards, self.wholes = place, shards, wholes
        self.send, self.recv, self.local = refs

    @staticmethod
    def scratch():
        return [DMA((2, 3)), DMA((2, 3)), DMA((2,))]

    def own(self, which):
        return pltpu.make_async_copy(
            self.shards[which], self.wholes[which].at[self.place.tensor], self.local.at[which]
        )

    def to_chip(self, which):
        return self.place.to_chip(
            self.shards[which], self.wholes[which].at[self.place.tensor],
            self.send.at[which, 0], self.recv.at[which, 0],
        )

    def to_core(self, which):
        return self.place.to_core(
            self.shards[which], self.wholes[which].at[self.place.tensor],
            self.send.at[which, 1], self.recv.at[which, 1],
        )

    def on_to_core(self, which):
        part = self.wholes[which].at[self.place.chip_peer]
        return self.place.to_core(
            part, part, self.send.at[which, 2], self.recv.at[which, 2]
        )

    def start(self):
        for which in range(2):
            self.own(which).start()
            self.to_chip(which).start()
            self.to_core(which).start()

    def pass_on(self):
        for which in range(2):
            self.to_chip(which).wait()
            self.on_to_core(which).start()

    def finish(self):
        for which in range(2):
            self.own(which).wait()
            self.to_core(which).wait()
            self.on_to_core(which).wait()


class ExpertSum:
    def __init__(self, place, panels, src, total, refs):
        self.place, self.panels, self.src, self.total = place, panels, src, total
        self.inbox, self.chunks, self.send, self.recv = refs
        self.side = lax.rem(place.expert, 2)
        self.pair = place.expert + 1 - 2 * self.side
        self.group = place.experts // 2
        self.index = lax.div(place.expert, 2)

    @staticmethod
    def scratch(plan):
        panels = len(plan.panels)
        half = plan.packed // 2
        return [
            VMEM((half, 128), BF16), VMEM((half, 128), BF16),
            DMA((2, panels, max(2, plan.experts // 2))), DMA((2, panels, max(2, plan.experts // 2))),
        ]

    def half(self, panel, side):
        start, rows = self.panels[panel]
        return pl.ds(pl.multiple_of(start + side * (rows // 2), 16), rows // 2)

    def local(self, panel):
        start, rows = self.panels[panel]
        return pl.ds(start // 2, rows // 2)

    def chunk(self, panel, index):
        start, rows = self.panels[panel]
        size = rows // self.place.experts
        return pl.ds(pl.multiple_of(start // 2 + index * size, 16), size)

    def chunk_whole(self, panel, index):
        start, rows = self.panels[panel]
        size = rows // self.place.experts
        return pl.ds(pl.multiple_of(start + self.side * (rows // 2) + index * size, 16), size)

    def member(self, step):
        return lax.rem(self.place.expert + 2 * step, self.place.experts)

    def pair_in(self, panel):
        return self.place.to_expert(
            self.pair, self.src.at[self.half(panel, 1 - self.side)],
            self.inbox.at[self.local(panel)],
            self.send.at[0, panel, 0], self.recv.at[0, panel, 0],
        )

    def scatter(self, panel, step):
        peer = lax.rem(self.index + step, self.group)
        return self.place.to_expert(
            self.member(step), self.src.at[self.chunk_whole(panel, peer)],
            self.chunks.at[self.chunk(panel, step)],
            self.send.at[0, panel, step], self.recv.at[0, panel, step],
        )

    def share(self, panel, step):
        mine = self.total.at[self.chunk_whole(panel, self.index)]
        return self.place.to_expert(
            self.member(step), mine, mine,
            self.send.at[1, panel, step], self.recv.at[1, panel, step],
        )

    def pair_out(self, panel):
        half = self.total.at[self.half(panel, self.side)]
        return self.place.to_expert(
            self.pair, half, half, self.send.at[1, panel, 0], self.recv.at[1, panel, 0]
        )

    def step_pair(self, panel):
        self.pair_in(panel).start()

    def step_scatter(self, panel):
        self.pair_in(panel).wait()
        mine = self.half(panel, self.side)
        self.src[mine, :] = (
            self.src[mine, :].astype(F32) + self.inbox[self.local(panel), :].astype(F32)
        ).astype(BF16)
        each(1, self.group, lambda step: self.scatter(panel, step).start())

    def step_share(self, panel):
        mine = self.chunk_whole(panel, self.index)

        def one(step, total):
            self.scatter(panel, step).wait()
            return total + self.chunks[self.chunk(panel, step), :].astype(F32)

        total = lax.fori_loop(1, self.group, one, self.src[mine, :].astype(F32))
        self.total[mine, :] = total.astype(BF16)
        each(1, self.group, lambda step: self.share(panel, step).start())

    def step_out(self, panel):
        each(1, self.group, lambda step: self.share(panel, step).wait())
        self.pair_out(panel).start()

    def step_end(self, panel):
        self.pair_out(panel).wait()

    def every(self, step):
        for panel in range(len(self.panels)):
            step(panel)


class PairSum:
    @staticmethod
    def scratch_near():
        return [VMEM((2, 2, 512, 512), BF16), DMA((2, 2)), DMA((2, 2))]

    @staticmethod
    def scratch_far():
        return [VMEM((2, 512, 512), BF16), DMA((2,)), DMA((2,))]

    @staticmethod
    def near(place, part, refs, which, chip):
        inbox, send, recv = refs
        quarter = 2 * chip + 1 - place.core
        return place.to_core(
            part.at[which, quarter], inbox.at[which, chip],
            send.at[which, chip], recv.at[which, chip],
        )

    @staticmethod
    def far(place, out, refs, which):
        inbox, send, recv = refs
        return place.to_chip(out, inbox.at[which], send.at[which], recv.at[which])


def route_places(plan, place, r):
    shape = (plan.experts, plan.lanes)
    expert_id = lax.broadcasted_iota(jnp.int32, shape, 0)
    lane = lax.broadcasted_iota(jnp.int32, shape, 1)
    first, second = r.route[0:1, :], r.route[1:2, :]
    is_first, is_second = expert_id == first, expert_id == second
    named = is_first | is_second
    count = jnp.where(named, 1.0, 0.0)
    running = count
    step = 1
    while step < plan.lanes:
        running = running + jnp.where(lane >= step, pltpu.roll(running, step, 1), 0.0)
        step *= 2
    before = running - count
    mine = before - (place.tensor * plan.per_rank).astype(F32)
    valid = named & (mine >= 0.0) & (mine < float(plan.per_rank))
    r.place[...] = jnp.where(valid, mine, -1.0)
    quarter = jnp.zeros(shape, F32)
    for bound in range(1, 4):
        quarter = quarter + jnp.where(before >= float(bound * plan.per_rank), 1.0, 0.0)
    step_of = expert_id - place.expert
    step_of = jnp.where(step_of < 0, step_of + plan.experts, step_of).astype(F32)
    code = (
        quarter * float(plan.slots - plan.per_rank) + step_of * float(plan.block) + before
    )
    kept = before < float(plan.capacity)
    nowhere = -1.0
    code_first = jnp.max(jnp.where(is_first & kept, code, nowhere), 0, keepdims=True)
    code_second = jnp.max(jnp.where(is_second & kept, code, nowhere), 0, keepdims=True)
    r.codes[...] = jnp.concatenate(
        [code_first, code_second, first.astype(F32), second.astype(F32)], axis=0
    )


def build_members(plan, place, r):
    slot = lax.broadcasted_iota(jnp.int32, (plan.block, plan.lanes), 0).astype(F32)

    def one(step):
        rows = pl.ds(pl.multiple_of(step * plan.block, plan.block), plan.block)
        hit = r.place[pl.ds(place.ahead(step), 1), :] == slot
        r.member[rows, :] = jnp.where(hit, 1.0, 0.0).astype(BF16)

    each(0, plan.experts, one)


def picks_part(plan, r, image, quarter):
    slot = lax.broadcasted_iota(jnp.int32, (PAD, plan.slots), 1) + quarter * plan.slots
    slot = slot.astype(F32)
    rows = image_rows(image)
    hit = (r.table[rows, 0:1] == slot) | (r.table[rows, 1:2] == slot)
    return jnp.where(hit, 1.0, 0.0).astype(BF16)


def build_picks(plan, r):
    if not plan.stored:
        return
    for quarter in range(4):
        columns = slice(quarter % 2 * plan.slots, (quarter % 2 + 1) * plan.slots)

        def one(image):
            r.picks[quarter // 2, image_rows(image), columns] = picks_part(
                plan, r, image, quarter
            )

        each(0, plan.images, one)


def picks_scratch(plan):
    return VMEM((2, plan.rows, 2 * plan.slots) if plan.stored else (2, 16, 128), BF16)


def diagonal(plan):
    shape = (plan.block, 128)
    return lax.broadcasted_iota(jnp.int32, shape, 0) == lax.broadcasted_iota(jnp.int32, shape, 1)


def tail_rows(plan, base):
    return pl.ds(pl.multiple_of(base + plan.block - 16, 16), 16)


def write_spare(plan, ref, base, column):
    row = jnp.sum(jnp.where(diagonal(plan), column, 0.0), 0, keepdims=True)
    high = row.astype(BF16).astype(F32)
    rest = jnp.zeros((1, 512 - 128), F32)
    high_row = jnp.concatenate([high, rest], axis=1)
    low_row = jnp.concatenate([row - high, rest], axis=1)
    rows = tail_rows(plan, base)
    index = lax.broadcasted_iota(jnp.int32, (16, 512), 0)
    old = ref[rows, :].astype(F32)
    ref[rows, :] = jnp.where(index == 14, high_row, jnp.where(index == 15, low_row, old)).astype(
        BF16
    )


def read_spare(plan, ref, base):
    index = lax.broadcasted_iota(jnp.int32, (16, 128), 0)
    tail = ref[tail_rows(plan, base), 0:128].astype(F32)
    row = jnp.sum(jnp.where(index >= 14, tail, 0.0), 0, keepdims=True)
    return jnp.sum(jnp.where(diagonal(plan), row, 0.0), 1, keepdims=True)


def head_split(value):
    first_head = lax.broadcasted_iota(jnp.int32, value.shape, 1) < HEAD_DIM
    nothing = jnp.zeros(value.shape, value.dtype)
    return jnp.concatenate(
        [jnp.where(first_head, value, nothing), jnp.where(first_head, nothing, value)], axis=0
    )


def head_join(value):
    rows = value.shape[0] // 2
    first_head = lax.broadcasted_iota(jnp.int32, (rows, 128), 1) < HEAD_DIM
    return jnp.where(first_head, value[:rows], value[rows:])


def first_norm(r, image):
    rows = image_rows(image)
    normed, _ = norm_parts(r.x[rows, :])
    r.h[rows, :] = (normed * r.gain[0:1, :] + r.bias[0:1, :]).astype(BF16)


def attend_forward(r, image, side):
    key_real = lax.broadcasted_iota(jnp.int32, (2 * PAD, PAD), 1) < SEQ
    rows = image_rows(image)
    proj = dot(r.h[rows, :], r.joint[side]).astype(BF16)
    r.qkv[side, rows, :] = proj
    query, keyed, valued = proj[:, :128], proj[:, 128:256], proj[:, 256:]
    scores = jnp.where(key_real, dot_nt(head_split(query * SCALE), keyed), -1e30)
    expd = jnp.exp(scores - jnp.max(scores, -1, keepdims=True))
    prob = (expd * (1.0 / jnp.sum(expd, -1, keepdims=True))).astype(BF16)
    r.prob[side, image] = prob
    r.mixed[side, rows, :] = head_join(dot(prob, valued)).astype(BF16)


def attend_out(r, total, image):
    rows = image_rows(image)
    mixed = jnp.concatenate([r.mixed[0, rows, :], r.mixed[1, rows, :]], axis=1)
    total.put(image, dot(mixed, r.out_all[...]))


def attend_backward(r, total, image):
    rows = image_rows(image)
    mixed_grads = dot_nt(r.gin[rows, :].astype(BF16), r.out_all[...])
    back = jnp.zeros((PAD, 512), F32)
    for side in range(2):
        proj = r.qkv[side, rows, :]
        query, keyed, valued = proj[:, :128], proj[:, 128:256], proj[:, 256:]
        grad = mixed_grads[:, side * 128 : (side + 1) * 128]
        mixed_grad = head_split(grad.astype(BF16))
        inner = jnp.sum(head_split(grad * r.mixed[side, rows, :].astype(F32)), -1, keepdims=True)
        prob = r.prob[side, image]
        prob_grad = dot_nt(mixed_grad, valued)
        score_grad = (prob.astype(F32) * (prob_grad - inner)).astype(BF16)
        query_grad = head_join(dot(score_grad, keyed)) * SCALE
        key_grad = dot_tn(score_grad, head_split(query * SCALE))
        value_grad = dot_tn(prob, mixed_grad)
        proj_grad = jnp.concatenate([query_grad, key_grad, value_grad], axis=1).astype(BF16)
        r.dproj[side, rows, :] = proj_grad
        back = back + dot_nt(proj_grad, r.joint[side])
    total.put(image, back)


def pack_out(plan, place, r):
    r.packed[0:512, :] = dot_tn(r.gin[...].astype(BF16), r.mixed[place.chip]).astype(BF16)


def pack_qkv(plan, place, r):
    grads = dot_tn(r.h[...], r.dproj[place.chip]).astype(BF16)
    for part in range(3):
        r.packed[(part + 1) * 512 : (part + 2) * 512, :] = grads[:, part * 128 : (part + 1) * 128]


def pack_small(plan, r):
    router = dot_tn(r.dz[...], r.h2[: plan.rows, :])[: plan.experts]
    rows = jnp.concatenate([r.vec[0:4, :], router], axis=0)
    rows = jnp.concatenate([rows[:, part * 128 : (part + 1) * 128] for part in range(4)], axis=0)
    spare = plan.packed - 2048 - rows.shape[0]
    r.packed[2048:, :] = jnp.concatenate([rows, jnp.zeros((spare, 128), F32)], axis=0).astype(BF16)


def second_norm(plan, r, total):
    def one(image):
        rows = image_rows(image)
        after = r.x[rows, :] + total.get(image)
        r.y[rows, :] = after
        normed, _ = norm_parts(after)
        r.h2[rows, :] = (normed * r.gain[1:2, :] + r.bias[1:2, :]).astype(BF16)

    if plan.lanes > plan.rows:
        r.h2[plan.rows :, :] = jnp.zeros((plan.lanes - plan.rows, 512), BF16)
    few(0, plan.images, one)


def send_slots(plan, place, r, move):
    r.send[...] = dot(r.member[...], r.h2[...]).astype(BF16)
    move.start_all(False)
    logits = dot_nt(r.router[: plan.experts, :], r.h2[...])
    expert_id = lax.broadcasted_iota(jnp.int32, (plan.experts, plan.lanes), 0)
    is_first, is_second = expert_id == r.route[0:1, :], expert_id == r.route[1:2, :]
    named = is_first | is_second
    shifted = jnp.where(named, logits, -1e30)
    top = jnp.max(shifted, 0, keepdims=True)
    expd = jnp.where(named, jnp.exp(shifted - top), 0.0)
    share = expd / jnp.maximum(jnp.sum(expd, 0, keepdims=True), 1e-30)
    r.gate[...] = share
    gate_first = jnp.sum(jnp.where(is_first, share, 0.0), 0, keepdims=True)
    gate_second = jnp.sum(jnp.where(is_second, share, 0.0), 0, keepdims=True)
    r.table[...] = jnp.concatenate(
        [r.codes[...], gate_first, gate_second, jnp.zeros((10, plan.lanes), F32)], axis=0
    ).T
    slot = lax.broadcasted_iota(jnp.int32, (plan.block, plan.lanes), 0).astype(F32)

    def one(step):
        expert = place.ahead(step)
        hit = r.place[pl.ds(expert, 1), :] == slot
        column = jnp.sum(jnp.where(hit, r.gate[pl.ds(expert, 1), :], 0.0), 1, keepdims=True)
        write_spare(plan, r.send, step * plan.block, column)

    few(0, plan.experts, one)
    move.start_all(True)


def read_gates(plan, r, low, high):
    def one(step):
        base = step * plan.block
        rows = pl.ds(pl.multiple_of(base, plan.block), plan.block)
        r.slot_gate[rows, :] = read_spare(plan, r.recv, base)

    few(low, high, one)


def groups(plan):
    return [(low, low + plan.group) for low in range(0, plan.experts, plan.group)]


def return_gradient(plan, r, low, high, value, column):
    r.gret[low * plan.block : high * plan.block, :] = value.astype(BF16)
    r.column[low * plan.block : high * plan.block, :] = column

    def one(step):
        base = step * plan.block
        rows = pl.ds(pl.multiple_of(base, plan.block), plan.block)
        write_spare(plan, r.gret, base, r.column[rows, :])

    few(low, high, one)


def expert_grads(plan, place, r, near):
    drecv, recv = r.dr[...], r.recv[...]
    for part in range(4):
        r.gpart[0, part] = dot_tn(recv, r.dpre[part]).astype(BF16)
        r.gpart[1, part] = dot_tn(r.act[part], drecv).astype(BF16)
    for which in range(2):
        for chip in range(2):
            PairSum.near(place, r.gpart, near, which, chip).start()


def near_sums(place, r, near):
    chip = place.tensor // 2
    inbox = near[0]
    for which in range(2):
        for side in range(2):
            PairSum.near(place, r.gpart, near, which, side).wait()
        for quarter, side in ((place.chip_peer, 1 - chip), (place.tensor, chip)):
            r.gpart[which, quarter] = (
                r.gpart[which, quarter].astype(F32) + inbox[which, side].astype(F32)
            ).astype(BF16)


def near_outs(place, r):
    return [
        pltpu.make_async_copy(r.gpart.at[which, quarter], out.at[which], r.out_sems.at[which, side])
        for which in range(2)
        for side, (quarter, out) in enumerate(((place.chip_peer, r.gfar), (place.tensor, r.gown)))
    ]


def combined(plan, r, chip, rows_in, out, add):
    rows = pl.ds(pl.multiple_of(chip * 2 * plan.slots, plan.slots), 2 * plan.slots)
    if plan.stored:
        value = dot(r.picks[chip], rows_in[rows, :])
        out[...] = out[...] + value if add else value
        return

    def one(image):
        picks = [picks_part(plan, r, image, 2 * chip + quarter) for quarter in range(2)]
        value = dot(jnp.concatenate(picks, axis=1), rows_in[rows, :])
        tokens = image_rows(image)
        out[tokens, :] = out[tokens, :] + value if add else value

    each(0, plan.images, one)


def norm_table(plan, r):
    def one(image):
        rows = image_rows(image)
        for source, column in ((r.y, 6), (r.x, 8)):
            value = source[rows, :]
            mean = jnp.mean(value, -1, keepdims=True)
            centered = value - mean
            r.table[rows, column : column + 1] = mean
            r.table[rows, column + 1 : column + 2] = lax.rsqrt(
                jnp.mean(centered * centered, -1, keepdims=True) + EPS
            )

    few(0, plan.images, one)


def norm_again(r, source, rows, column):
    scaled = r.table[rows, column + 1 : column + 2]
    return (source[rows, :] - r.table[rows, column : column + 1]) * scaled, scaled


def keep_gates(plan, r):
    def arrived(quarter, step):
        tail = tail_rows(plan, quarter * plan.slots + step * plan.block)
        rows = r.gback[tail, 0:128].astype(F32)
        index = quarter * plan.experts + step
        r.high[pl.ds(index, 1), :] = rows[14:15]
        r.low[pl.ds(index, 1), :] = rows[15:16]

    return arrived


def pick_gates(plan, r, rows, column):
    code = r.table[rows, column : column + 1]
    block = jnp.floor((code + 0.5) * (1.0 / plan.block))
    inside = code - block * float(plan.block)
    lane = lax.broadcasted_iota(jnp.int32, (PAD, plan.blocks), 1).astype(F32)
    chosen = jnp.where(lane == block, 1.0, 0.0).astype(BF16)
    values = dot(chosen, r.high[...].astype(BF16)) + dot(chosen, r.low[...].astype(BF16))
    lane = lax.broadcasted_iota(jnp.int32, (PAD, 128), 1).astype(F32)
    return jnp.sum(jnp.where(lane == inside, values, 0.0), -1, keepdims=True)


def back_to_attention(plan, place, r, gback, between):
    arrived = keep_gates(plan, r)
    r.high[...] = jnp.zeros_like(r.high)
    r.low[...] = jnp.zeros_like(r.low)
    gback.pass_on(arrived)
    gback.near(arrived)
    combined(plan, r, place.chip, r.gback, r.gin, False)
    between()
    gback.far(arrived)
    combined(plan, r, 1 - place.chip, r.gback, r.gin, True)
    r.vec[...] = jnp.zeros_like(r.vec)

    def one(image):
        rows = image_rows(image)
        lane = lax.broadcasted_iota(jnp.int32, (PAD, 128), 1).astype(F32)
        first, second = pick_gates(plan, r, rows, 0), pick_gates(plan, r, rows, 1)
        both = first + second
        logit_grad = jnp.where(
            lane == r.table[rows, 2:3], first - r.table[rows, 4:5] * both,
            jnp.where(lane == r.table[rows, 3:4], second - r.table[rows, 5:6] * both, 0.0),
        ).astype(BF16)
        r.dz[rows, :] = logit_grad
        value = r.gin[rows, :] + dot(logit_grad, r.router[...])
        normed, scaled = norm_again(r, r.y, rows, 6)
        r.gin[rows, :] = r.g[rows, :].astype(F32) + norm_pull(
            value, normed, scaled, r.gain[1:2, :]
        )
        r.vec[1:2, :] += jnp.sum(value * normed, 0, keepdims=True)
        r.vec[3:4, :] += jnp.sum(value, 0, keepdims=True)

    few(0, plan.images, one)


def first_norm_back(plan, r, total, image):
    rows = image_rows(image)
    value = total.get(image)
    normed, scaled = norm_again(r, r.x, rows, 8)
    r.vec[0:1, :] += jnp.sum(value * normed, 0, keepdims=True)
    r.vec[2:3, :] += jnp.sum(value, 0, keepdims=True)
    return r.gin[rows, :] + norm_pull(value, normed, scaled, r.gain[0:1, :])


class Copies:
    def __init__(self, pairs, sems):
        self.copies = {
            key: pltpu.make_async_copy(src, dst, sems.at[index])
            for index, (key, (src, dst)) in enumerate(pairs.items())
        }

    def start(self, *keys):
        for key in keys:
            self.copies[key].start()

    def wait(self, *keys):
        for key in keys:
            self.copies[key].wait()


def run_kernel(name, body, inputs, outputs, scratch, collective_id, vmem, in_vmem=()):
    flat, layout = [], []
    for key, value in scratch.items():
        group = value if isinstance(value, list) else [value]
        layout.append((key, len(group), isinstance(value, list)))
        flat.extend(group)
    plain = list(inputs) + list(outputs)

    def kernel(*refs):
        named = dict(zip(plain, refs))
        at = len(plain)
        for key, size, grouped in layout:
            named[key] = refs[at : at + size] if grouped else refs[at]
            at += size
        body(types.SimpleNamespace(**named))

    def spec(key):
        return pl.BlockSpec(memory_space=VMEM if key in in_vmem else pl.ANY)

    results = pl.pallas_call(
        kernel,
        name=name,
        in_specs=[spec(key) for key in inputs],
        out_specs=tuple(spec(key) for key in outputs),
        out_shape=tuple(jax.ShapeDtypeStruct(*value) for value in outputs.values()),
        scratch_shapes=flat,
        compiler_params=pltpu.CompilerParams(
            collective_id=collective_id, has_side_effects=True, vmem_limit_bytes=int(vmem * MIB)
        ),
    )(*inputs.values())
    return types.SimpleNamespace(**dict(zip(outputs, results)))


ATTENDED = ("joint", "out_all", "h", "qkv", "prob", "mixed")
SMALL = ("route_all", "gain_all", "bias_all", "router_all")
KEPT = ("routes", "router_in") + SMALL[1:3]


def layer_views(r, layer):
    r.gain, r.bias = r.gain_all.at[layer], r.bias_all.at[layer]
    r.router = r.router_all.at[layer]
    if hasattr(r, "route_all"):
        r.route = r.route_all.at[layer]


def forward_shapes(plan):
    rows, lanes, slots = plan.rows, plan.lanes, plan.slots
    return dict(
        joint=((2, 512, 384), BF16),
        out_all=((256, 512), BF16),
        x=((rows, 512), F32),
        y=((rows, 512), F32),
        h=((rows, 512), BF16),
        qkv=((2, rows, 384), BF16),
        prob=((2, plan.images, 2 * PAD, PAD), BF16),
        mixed=((2, rows, 128), BF16),
        h2=((lanes, 512), BF16),
        place=((plan.experts, lanes), F32),
        table=((lanes, 16), F32),
        recv=((slots, 512), BF16),
        ret=((slots, 512), BF16),
        slot_gate=((slots, 1), F32),
        up=((4, 512, 512), BF16),
        down=((4, 512, 512), BF16),
    )


def as_scratch(shapes):
    return {key: VMEM(*value) for key, value in shapes.items()}


def as_saved(shapes):
    return {"out_" + key: value for key, value in shapes.items()}


def pad_images(plan, source, target, staging):
    tokens = plan.images * SEQ
    staging[0:tokens, :] = source[...].astype(F32)
    target[...] = jnp.zeros_like(target)
    for image in range(plan.images):
        target[image * PAD : image * PAD + SEQ, :] = staging[
            image * SEQ : (image + 1) * SEQ, :
        ].astype(target.dtype)


def first_forward(plan, inputs, tokens):
    saved = forward_shapes(plan)

    def body(r):
        place = Place(plan.experts)
        place.greet()
        layer_views(r, 0)
        swap = HeadSwap(
            place, r.w_qkv.at[0], r.w_out.at[0], r.joint, r.out_all, r.swap
        )
        later = HeadSwap(
            place, r.w_qkv.at[1], r.w_out.at[1], r.joint_later, r.out_later, r.swap_later
        )
        saves = Copies({k: (getattr(r, k), getattr(r, "out_" + k)) for k in saved}, r.saves)
        total = CoreSum(place, r.total)
        weights = WeightGather(
            place, (r.w_up.at[0, 0], r.w_down.at[0, 0]), (r.up, r.down), r.weights
        )
        move = Exchange(place, plan.block, r.send, r.recv, r.move)
        back = Return(place, plan.block, plan.slots, r.ret, r.back, r.back_sems)
        swap.start_own()
        pad_images(plan, r.tokens, r.x, r.y)
        saves.start("x")
        place.met()
        swap.start_swap()
        weights.start()
        later.start_own()
        later.start_swap()
        swap.wait_own()

        def own_heads(image):
            first_norm(r, image)
            attend_forward(r, image, place.chip)

        each(0, plan.images, own_heads)
        route_places(plan, place, r)
        build_members(plan, place, r)
        swap.wait_swap(range(3))
        each(0, plan.images, lambda image: attend_forward(r, image, 1 - place.chip))
        swap.wait_swap((3,))
        each(0, plan.images, lambda image: attend_out(r, total, image))
        saves.start(*ATTENDED, "place")
        second_norm(plan, r, total)
        send_slots(plan, place, r, move)
        saves.start("y", "h2")
        norm_table(plan, r)
        saves.start("table")
        build_picks(plan, r)
        weights.pass_on()
        weights.finish()
        saves.start("up", "down")
        for low, high in groups(plan):
            move.wait(low, high, False)
            move.wait(low, high, True)
            read_gates(plan, r, low, high)
            rows = slice(low * plan.block, high * plan.block)
            rows_in = r.recv[rows, :]
            result = jnp.zeros((rows.stop - rows.start, 512), F32)
            for part in range(4):
                act = gelu(dot(rows_in, r.up[part])).astype(BF16)
                result = result + dot(act, r.down[part])
            r.ret[rows, :] = (result * r.slot_gate[rows, :]).astype(BF16)
            back.start(low, high)
        saves.start("recv", "ret", "slot_gate")
        saves.wait("x")
        back.pass_on()
        back.near()
        combined(plan, r, place.chip, r.back, r.x, False)
        back.far()
        combined(plan, r, 1 - place.chip, r.back, r.x, True)
        r.x[...] += r.y[...]
        back.finish()
        out = pltpu.make_async_copy(r.x, r.next, r.out_sem)
        out.start()
        saves.wait(*(k for k in saved if k != "x"))
        later.wait_own()
        later.wait_swap()
        out.wait()

    outputs = dict(
        as_saved(saved),
        next=((plan.rows, 512), F32),
        joint_later=saved["joint"],
        out_later=saved["out_all"],
    )
    scratch = dict(
        as_scratch(saved),
        codes=VMEM((4, plan.lanes), F32),
        member=VMEM((plan.slots, plan.lanes), BF16),
        gate=VMEM((plan.experts, plan.lanes), F32),
        picks=picks_scratch(plan),
        send=VMEM((plan.slots, 512), BF16),
        back=VMEM((4 * plan.slots, 512), BF16),
        total=CoreSum.scratch(plan.images),
        weights=WeightGather.scratch(),
        swap=HeadSwap.scratch(),
        swap_later=HeadSwap.scratch(),
        move=Exchange.scratch(plan.experts),
        back_sems=Return.scratch(plan.experts),
        saves=DMA((len(saved),)),
        out_sem=DMA,
    )
    return run_kernel(
        "first_forward", body, dict(inputs, tokens=tokens), outputs, scratch, 0, 62,
        SMALL + ("tokens",),
    )


def second_whole(plan, inputs, cotangent, start, joint, out_all):
    def body(r):
        place = Place(plan.experts)
        place.greet()
        layer_views(r, 1)
        r.gret, r.ret, r.dr, r.column = r.send, r.gsend, r.grecv, r.slot_gate
        loads = Copies(
            {k: (getattr(r, "in_" + k), getattr(r, k)) for k in ("x", "joint", "out_all")}, r.loads
        )
        total = CoreSum(place, r.total)
        total_back = CoreSum(place, r.total)
        weights = WeightGather(
            place, (r.w_up.at[1, 0], r.w_down.at[1, 0]), (r.up, r.down), r.weights
        )
        move = Exchange(place, plan.block, r.send, r.recv, r.move)
        gmove = Exchange(place, plan.block, r.gsend, r.grecv, r.gmove)
        back = Return(place, plan.block, plan.slots, r.ret, r.back, r.back_sems)
        gback = Return(place, plan.block, plan.slots, r.gret, r.gback, r.gback_sems)
        loads.start("x", "joint", "out_all")
        pad_images(plan, r.cotangent, r.g, r.y)
        route_places(plan, place, r)
        build_members(plan, place, r)
        r.gsend[...] = dot(r.member[:, : plan.rows], r.g[...]).astype(BF16)
        place.met()
        weights.start()
        gmove.start_all()
        loads.wait("x", "joint", "out_all")

        def heads(image):
            first_norm(r, image)
            for side in range(2):
                attend_forward(r, image, side)
            attend_out(r, total, image)

        each(0, plan.images, heads)
        second_norm(plan, r, total)
        send_slots(plan, place, r, move)
        norm_table(plan, r)
        build_picks(plan, r)
        weights.pass_on()
        weights.finish()
        gmove.wait(0, plan.experts)
        for low, high in groups(plan):
            move.wait(low, high, False)
            move.wait(low, high, True)
            read_gates(plan, r, low, high)
            rows = slice(low * plan.block, high * plan.block)
            rows_in = r.recv[rows, :]
            gate = r.slot_gate[rows, :]
            raw = r.grecv[rows, :].astype(F32)
            scaled = (raw * gate).astype(BF16)
            r.dr[rows, :] = scaled
            result = jnp.zeros((rows.stop - rows.start, 512), F32)
            slots_grad = jnp.zeros((rows.stop - rows.start, 512), F32)
            for part in range(4):
                act, slope = gelu_both(dot(rows_in, r.up[part]))
                act = act.astype(BF16)
                r.act[part, rows, :] = act
                result = result + dot(act, r.down[part])
                pre_grad = (dot_nt(scaled, r.down[part]) * slope).astype(BF16)
                r.dpre[part, rows, :] = pre_grad
                slots_grad = slots_grad + dot_nt(pre_grad, r.up[part])
            result = result * gate
            r.ret[rows, :] = result.astype(BF16)
            column = jnp.sum(result * raw, -1, keepdims=True)
            return_gradient(plan, r, low, high, slots_grad, column)
            gback.start(low, high)
        back.start(0, plan.experts)
        expert_grads(plan, place, r, r.near)
        outs = near_outs(place, r)

        def between():
            near_sums(place, r, r.near)
            for copy in outs:
                copy.start()

        back_to_attention(plan, place, r, gback, between)
        back.pass_on()
        each(0, plan.images, lambda image: attend_backward(r, total_back, image))
        pack_out(plan, place, r)
        pack_qkv(plan, place, r)

        def input_grad(image):
            rows = image_rows(image)
            r.gin[rows, :] = first_norm_back(plan, r, total_back, image)

        each(0, plan.images, input_grad)
        out = pltpu.make_async_copy(r.gin, r.grad, r.late_sems.at[0])
        out.start()
        pack_small(plan, r)
        out_packed = pltpu.make_async_copy(r.packed, r.out_packed, r.late_sems.at[1])
        out_packed.start()
        back.near()
        combined(plan, r, place.chip, r.back, r.x, False)
        back.far()
        combined(plan, r, 1 - place.chip, r.back, r.x, True)
        for image in range(plan.images):
            rows = slice(image * PAD, image * PAD + SEQ)
            r.y[image * SEQ : (image + 1) * SEQ, :] = r.y[rows, :] + r.x[rows, :]
        r.result[...] = r.y[0 : plan.images * SEQ, :].astype(BF16)
        back.finish()
        gback.finish()
        for copy in outs + [out, out_packed]:
            copy.wait()

    outputs = {
        "result": (cotangent.shape, BF16),
        "grad": ((plan.rows, 512), F32),
        "out_packed": ((plan.packed, 128), BF16),
        "gfar": ((2, 512, 512), BF16),
        "gown": ((2, 512, 512), BF16),
    }
    scratch = dict(
        as_scratch({k: v for k, v in forward_shapes(plan).items() if k != "ret"}),
        codes=VMEM((4, plan.lanes), F32),
        member=VMEM((plan.slots, plan.lanes), BF16),
        gate=VMEM((plan.experts, plan.lanes), F32),
        picks=picks_scratch(plan),
        send=VMEM((plan.slots, 512), BF16),
        back=VMEM((4 * plan.slots, 512), BF16),
        total=CoreSum.scratch(plan.images),
        weights=WeightGather.scratch(),
        move=Exchange.scratch(plan.experts),
        back_sems=Return.scratch(plan.experts),
        gmove=Exchange.scratch(plan.experts),
        gback_sems=Return.scratch(plan.experts),
        gsend=VMEM((plan.slots, 512), BF16),
        grecv=VMEM((plan.slots, 512), BF16),
        g=VMEM((plan.rows, 512), BF16),
        out_sems=DMA((2, 2)),
        late_sems=DMA((2,)),
        loads=DMA((3,)),
        **backward_scratch(plan),
    )
    return run_kernel(
        "second_whole", body,
        dict(inputs, cotangent=cotangent, in_x=start, in_joint=joint, in_out_all=out_all),
        outputs, scratch, 1, 63, SMALL + ("cotangent", "result"),
    )


def backward_scratch(plan):
    return dict(
        gback=VMEM((4 * plan.slots, 512), BF16),
        act=VMEM((4, plan.slots, 512), BF16),
        dpre=VMEM((4, plan.slots, 512), BF16),
        gpart=VMEM((2, 4, 512, 512), BF16),
        high=VMEM((plan.blocks, 128), F32),
        low=VMEM((plan.blocks, 128), F32),
        dz=VMEM((plan.rows, 128), BF16),
        gin=VMEM((plan.rows, 512), F32),
        dproj=VMEM((2, plan.rows, 384), BF16),
        packed=VMEM((plan.packed, 128), BF16),
        vec=VMEM((8, 512), F32),
        near=PairSum.scratch_near(),
    )


def expert_out(place, r, layer, which):
    out = (r.grad_up, r.grad_down)[which]
    return pltpu.make_async_copy(
        r.y.at[pl.ds(which * 512, 512)], out.at[layer], r.expert_sems.at[layer, which]
    )


class Finals:
    def __init__(self, plan, r):
        self.plan, self.r = plan, r

    def write(self, layer, total):
        r, experts = self.r, self.plan.experts
        r.grad_out[layer] = total[0:512, :].astype(F32).T
        for part in range(3):
            r.grad_qkv[layer, part] = total[(part + 1) * 512 : (part + 2) * 512, :].astype(F32)
        count = 4 + experts
        small = total[2048 : 2048 + up_to(4 * count, 16), :].astype(F32)
        rows = jnp.concatenate(
            [small[part * count : (part + 1) * count] for part in range(4)], axis=1
        )
        r.grad_gain[layer] = rows[0:2]
        if self.plan.stored:
            r.grad_bias_one[layer : layer + 1, :] = rows[2:3]
            r.grad_bias_two[layer : layer + 1, :] = rows[3:4]
        else:
            r.grad_bias[layer] = rows[2:4]
        r.grad_router[layer] = rows[4:]


def first_backward(plan, inputs, saved, grad, gfar, gown, packed, out_shape):
    def body(r):
        place = Place(plan.experts)
        place.greet()
        layer_views(r, 0)
        r.gret, r.dr, r.column = r.gsend, r.grecv, r.slot_gate
        r.x = r.g
        loads = Copies(
            {k: (getattr(r, "in_" + k), getattr(r, k)) for k in list(saved) + ["g", "later"]},
            r.loads,
        )
        total = CoreSum(place, r.total)
        gmove = Exchange(place, plan.block, r.gsend, r.grecv, r.gmove)
        gback = Return(place, plan.block, plan.slots, r.gret, r.gback, r.gback_sems)
        later = ExpertSum(place, plan.panels, r.later, r.sum_later, r.later_sum)
        sooner = ExpertSum(place, plan.panels, r.packed, r.sum_first, r.sooner_sum)
        first_loads = ("g", "place", "recv", "up", "down", "ret", "slot_gate", "table")
        loads.start(*first_loads)
        loads.start(*(k for k in loads.copies if k not in first_loads + ("x",)))
        loads.wait("place")
        build_members(plan, place, r)
        loads.wait("g")
        r.gsend[...] = dot(r.member[:, : plan.rows], r.g[...].astype(BF16)).astype(BF16)
        place.met()
        gmove.start_all()
        for which in range(2):
            PairSum.far(place, r.gfar_later.at[which], r.far_later, which).start()
        own_copy = pltpu.make_async_copy(r.gown_later, r.own_later, r.own_sem)
        own_copy.start()
        loads.wait("recv", "up", "down")
        for low, high in groups(plan):
            rows = slice(low * plan.block, high * plan.block)
            for part in range(4):
                act, slope = gelu_both(dot(r.recv[rows, :], r.up[part]))
                r.act[part, rows, :] = act.astype(BF16)
                r.dpre[part, rows, :] = slope.astype(BF16)
        loads.wait("table")
        build_picks(plan, r)
        loads.wait("ret", "slot_gate", "later")
        for low, high in groups(plan):
            gmove.wait(low, high)
            rows = slice(low * plan.block, high * plan.block)
            raw = r.grecv[rows, :].astype(F32)
            scaled = (raw * r.slot_gate[rows, :]).astype(BF16)
            r.dr[rows, :] = scaled
            slots_grad = jnp.zeros((rows.stop - rows.start, 512), F32)
            for part in range(4):
                pre_grad = (
                    dot_nt(scaled, r.down[part]) * r.dpre[part, rows, :].astype(F32)
                ).astype(BF16)
                r.dpre[part, rows, :] = pre_grad
                slots_grad = slots_grad + dot_nt(pre_grad, r.up[part])
            column = jnp.sum(r.ret[rows, :].astype(F32) * raw, -1, keepdims=True)
            return_gradient(plan, r, low, high, slots_grad, column)
            gback.start(low, high)
        expert_grads(plan, place, r, r.near)

        def between():
            later.every(later.step_pair)
            near_sums(place, r, r.near)
            for which in range(2):
                PairSum.far(place, r.gpart.at[which, place.chip_peer], r.far, which).start()

        loads.wait(*(k for k in loads.copies if k not in first_loads + ("later", "x")))
        back_to_attention(plan, place, r, gback, between)
        loads.start("x")
        later.every(later.step_scatter)
        pack_out(plan, place, r)
        sooner.step_pair(0)
        own_copy.wait()
        outs = [expert_out(place, r, layer, which) for layer in range(2) for which in range(2)]
        for which in range(2):
            PairSum.far(place, r.gfar_later.at[which], r.far_later, which).wait()
            r.y[which * 512 : (which + 1) * 512, :] = (
                r.own_later[which].astype(F32) + r.far_later[0][which].astype(F32)
            )
            outs[2 + which].start()
        half = plan.images // 2
        each(0, half, lambda image: attend_backward(r, total, image))
        later.every(later.step_share)
        sooner.step_scatter(0)
        each(half, plan.images, lambda image: attend_backward(r, total, image))
        pack_qkv(plan, place, r)
        panels = len(plan.panels)
        for panel in range(1, panels - 1):
            sooner.step_pair(panel)
        later.every(later.step_out)
        loads.wait("x")
        for image in range(plan.images):
            out = first_norm_back(plan, r, total, image)
            r.grad[image * SEQ : (image + 1) * SEQ, :] = out[:SEQ]
        pack_small(plan, r)
        sooner.step_pair(panels - 1)
        for panel in range(1, panels):
            sooner.step_scatter(panel)
        later.every(later.step_end)
        finals = Finals(plan, r)
        finals.write(1, r.sum_later)
        sooner.every(sooner.step_share)
        for which in range(2):
            outs[2 + which].wait()
            PairSum.far(place, r.gpart.at[which, place.chip_peer], r.far, which).wait()
            r.y[which * 512 : (which + 1) * 512, :] = (
                r.gpart[which, place.tensor].astype(F32) + r.far[0][which].astype(F32)
            )
            outs[which].start()
        gback.finish()
        sooner.every(sooner.step_out)
        sooner.every(sooner.step_end)
        finals.write(0, r.sum_first)
        for which in range(2):
            outs[which].wait()

    outputs = {
        "grad": (out_shape, F32),
        "grad_up": ((2, 512, 512), F32),
        "grad_down": ((2, 512, 512), F32),
        "grad_qkv": ((2, 3, 512, 128), F32),
        "grad_out": ((2, 128, 512), F32),
        "grad_gain": ((2, 2, 512), F32),
        "grad_bias": ((2, 2, 512), F32),
        "grad_router": ((2, plan.experts, 512), F32),
    }
    scratch = dict(
        as_scratch({k: v for k, v in forward_shapes(plan).items() if k != "x"}),
        member=VMEM((plan.slots, plan.lanes), BF16),
        picks=picks_scratch(plan),
        total=CoreSum.scratch(plan.images),
        gmove=Exchange.scratch(plan.experts),
        gback_sems=Return.scratch(plan.experts),
        gsend=VMEM((plan.slots, 512), BF16),
        grecv=VMEM((plan.slots, 512), BF16),
        g=VMEM((plan.rows, 512), F32),
        later=VMEM((plan.packed, 128), BF16),
        own_later=VMEM((2, 512, 512), BF16),
        sum_first=VMEM((plan.packed, 128), BF16),
        sum_later=VMEM((plan.packed, 128), BF16),
        expert_sems=DMA((2, 2)),
        own_sem=DMA,
        far=PairSum.scratch_far(),
        far_later=PairSum.scratch_far(),
        later_sum=ExpertSum.scratch(plan),
        sooner_sum=ExpertSum.scratch(plan),
        loads=DMA((len(saved) + 2,)),
        **backward_scratch(plan),
    )
    arrays = dict({"in_" + k: v for k, v in saved.items()}, in_g=grad, in_later=packed)
    return run_kernel(
        "first_backward", body,
        dict(inputs, gfar_later=gfar, gown_later=gown, **arrays),
        outputs, scratch, 2, 63,
        SMALL + tuple(k for k in outputs if k not in ("grad_up", "grad_down")),
    )


def expert_forward_backward(plan, r, low, high):
    rows = slice(low * plan.block, high * plan.block)
    rows_in = r.recv[rows, :]
    gate = r.slot_gate[rows, :]
    raw = r.grecv[rows, :].astype(F32)
    scaled = (raw * gate).astype(BF16)
    r.dr[rows, :] = scaled
    result = jnp.zeros((rows.stop - rows.start, 512), F32)
    slots_grad = jnp.zeros((rows.stop - rows.start, 512), F32)
    for part in range(4):
        act, slope = gelu_both(dot(rows_in, r.up[part]))
        act = act.astype(BF16)
        r.act[part, rows, :] = act
        result = result + dot(act, r.down[part])
        pre_grad = (dot_nt(scaled, r.down[part]) * slope).astype(BF16)
        r.dpre[part, rows, :] = pre_grad
        slots_grad = slots_grad + dot_nt(pre_grad, r.up[part])
    result = result * gate
    r.ret[rows, :] = result.astype(BF16)
    column = jnp.sum(result * raw, -1, keepdims=True)
    return_gradient(plan, r, low, high, slots_grad, column)


def expert_forward(plan, r, low, high):
    rows = slice(low * plan.block, high * plan.block)
    rows_in = r.recv[rows, :]
    result = jnp.zeros((rows.stop - rows.start, 512), F32)
    for part in range(4):
        act = gelu(dot(rows_in, r.up[part])).astype(BF16)
        result = result + dot(act, r.down[part])
    r.ret[rows, :] = (result * r.slot_gate[rows, :]).astype(BF16)


def expert_again(plan, r, low, high):
    rows = slice(low * plan.block, high * plan.block)
    for part in range(4):
        act, slope = gelu_both(dot(r.recv[rows, :], r.up[part]))
        r.act[part, rows, :] = act.astype(BF16)
        r.dpre[part, rows, :] = slope.astype(BF16)


def expert_backward(plan, r, low, high):
    rows = slice(low * plan.block, high * plan.block)
    raw = r.grecv[rows, :].astype(F32)
    scaled = (raw * r.slot_gate[rows, :]).astype(BF16)
    r.dr[rows, :] = scaled
    slots_grad = jnp.zeros((rows.stop - rows.start, 512), F32)
    for part in range(4):
        pre_grad = (dot_nt(scaled, r.down[part]) * r.dpre[part, rows, :].astype(F32)).astype(BF16)
        r.dpre[part, rows, :] = pre_grad
        slots_grad = slots_grad + dot_nt(pre_grad, r.up[part])
    column = jnp.sum(r.ret[rows, :].astype(F32) * raw, -1, keepdims=True)
    return_gradient(plan, r, low, high, slots_grad, column)


def prepare(plan, r):
    lane = lax.broadcasted_iota(jnp.int32, (2, plan.lanes), 1)
    tokens = plan.images * SEQ
    empty = jnp.zeros((128 - plan.experts, 512), F32)
    for layer in range(2):
        router = r.router_in[layer].astype(F32)
        r.router_all[layer] = jnp.concatenate([router, empty], axis=0).astype(BF16)
        r.route_all[layer] = jnp.zeros((2, plan.lanes), jnp.int32)
        r.route_all[layer, :, 0:tokens] = r.routes[layer]
        raw = r.route_all[layer]
        spread = jnp.full((2, plan.lanes), -1, jnp.int32)
        for image in range(plan.images):
            moved = pltpu.roll(raw, image * (PAD - SEQ), 1) if image else raw
            inside = (lane >= image * PAD) & (lane < image * PAD + SEQ)
            spread = jnp.where(inside, moved, spread)
        r.route_all[layer] = spread


SAVED = ATTENDED + ("x", "y", "h2", "up", "down")


def one_kernel(plan, inputs):
    shapes = forward_shapes(plan)
    shape_of_edge = inputs["tokens"].shape

    def body(r):
        place = Place(plan.experts)
        place.greet()
        first = types.SimpleNamespace(**vars(r))
        second = types.SimpleNamespace(**vars(r))
        for layer, view in ((0, first), (1, second)):
            layer_views(view, layer)
            for key in ("place", "codes", "table", "recv", "slot_gate", "packed"):
                setattr(view, key, getattr(r, f"{key}_{layer}"))
            view.column = view.slot_gate
            view.gret, view.dr = r.send, r.grecv
        first.ret, second.ret = r.ret_0, r.gsend
        saves = Copies({k: (getattr(r, k), getattr(r, "out_" + k)) for k in SAVED}, r.saves)
        loads = Copies({k: (getattr(r, "out_" + k), getattr(r, k)) for k in SAVED}, r.loads)
        edges = Copies(
            {"tokens": (r.tokens, r.edge), "cotangent": (r.cotangent, r.edge),
             "result": (r.edge, r.result)}, r.edges,
        )
        total = CoreSum(place, r.total)
        swaps = [
            HeadSwap(place, r.w_qkv.at[k], r.w_out.at[k], r.joint, r.out_all, sems)
            for k, sems in enumerate((r.swap_0, r.swap_1))
        ]
        gathers = [
            WeightGather(place, (r.w_up.at[k, 0], r.w_down.at[k, 0]), (r.up, r.down), sems)
            for k, sems in enumerate((r.weights_0, r.weights_1))
        ]
        moves = [
            Exchange(place, plan.block, r.send, dst, sems)
            for dst, sems in ((r.recv_0, r.move_0), (r.recv_1, r.move_1))
        ]
        gmoves = [
            Exchange(place, plan.block, src, r.grecv, sems)
            for src, sems in ((r.send, r.gmove_0), (r.gsend, r.gmove_1))
        ]
        backs = [
            Return(place, plan.block, plan.slots, src, r.back, sems)
            for src, sems in ((r.ret_0, r.back_0), (r.gsend, r.back_1))
        ]
        gbacks = [
            Return(place, plan.block, plan.slots, r.send, r.gback, sems)
            for sems in (r.gback_0, r.gback_1)
        ]
        sums = [
            ExpertSum(place, plan.panels, src, out, refs)
            for src, out, refs in (
                (r.packed_0, r.sum_0, r.sums_0), (r.packed_1, r.sum_1, r.sums_1)
            )
        ]
        experts = plan.experts

        edges.start("tokens")
        swaps[0].start_own()
        place.met()
        swaps[0].start_swap()
        gathers[0].start()
        prepare(plan, r)
        edges.wait("tokens")
        pad_images(plan, r.edge, r.x, r.y)
        edges.start("cotangent")
        saves.start("x")
        edges.wait("cotangent")
        pad_images(plan, r.edge, r.g, r.y)
        route_places(plan, place, second)
        build_members(plan, place, second)
        r.gsend[...] = dot(r.member[:, : plan.rows], r.g[...].astype(BF16)).astype(BF16)
        gmoves[1].start_all()
        swaps[0].wait_own()

        def own_heads(view):
            def one(image):
                first_norm(view, image)
                attend_forward(view, image, place.chip)

            each(0, plan.images, one)

        def other_heads(view, swap):
            swap.wait_swap(range(3))
            each(0, plan.images, lambda image: attend_forward(view, image, 1 - place.chip))
            swap.wait_swap((3,))
            each(0, plan.images, lambda image: attend_out(view, total, image))

        own_heads(first)
        route_places(plan, place, first)
        build_members(plan, place, first)
        other_heads(first, swaps[0])
        saves.start(*ATTENDED)
        second_norm(plan, first, total)
        send_slots(plan, place, first, moves[0])
        saves.start("y", "h2")
        norm_table(plan, first)
        build_picks(plan, first)
        gathers[0].pass_on()
        gathers[0].finish()
        saves.start("up", "down")
        gmoves[1].wait(0, experts)
        for low, high in groups(plan):
            moves[0].wait(low, high, False)
            moves[0].wait(low, high, True)
            read_gates(plan, first, low, high)
            expert_forward(plan, first, low, high)
            backs[0].start(low, high)
        build_members(plan, place, second)
        saves.wait(*SAVED)
        backs[0].pass_on()
        backs[0].near()
        swaps[1].start_own()
        swaps[1].start_swap()
        gathers[1].start()
        combined(plan, r, place.chip, r.back, r.x, False)
        backs[0].far()
        combined(plan, r, 1 - place.chip, r.back, r.x, True)
        r.x[...] += r.y[...]
        backs[0].finish()

        swaps[1].wait_own()
        own_heads(second)
        other_heads(second, swaps[1])
        second_norm(plan, second, total)
        send_slots(plan, place, second, moves[1])
        build_members(plan, place, first)
        norm_table(plan, second)
        build_picks(plan, second)
        gathers[1].pass_on()
        gathers[1].finish()
        for low, high in groups(plan):
            moves[1].wait(low, high, False)
            moves[1].wait(low, high, True)
            read_gates(plan, second, low, high)
            expert_forward_backward(plan, second, low, high)
            gbacks[1].start(low, high)
        expert_grads(plan, place, second, r.near)
        backs[1].start(0, experts)
        loads.start("up", "down")

        def inbox(layer, which):
            if layer:
                return r.recv_1.at[pl.ds(0, 512)] if which else r.far_in
            return r.back.at[pl.ds(which * 512, 512)]

        def far(layer, which):
            return place.to_chip(
                r.gpart.at[which, place.chip_peer], inbox(layer, which),
                r.far_sems.at[0, layer, which], r.far_sems.at[1, layer, which],
            )

        def between_second():
            near_sums(place, second, r.near)
            far(1, 0).start()

        back_to_attention(plan, place, second, gbacks[1], between_second)
        gbacks[1].finish()
        backs[1].pass_on()
        far(1, 1).start()
        each(0, plan.images, lambda image: attend_backward(second, total, image))

        def input_grad(image):
            r.g[image_rows(image), :] = first_norm_back(plan, second, total, image)

        few(0, plan.images, input_grad)

        r.send[...] = dot(r.member[:, : plan.rows], r.g[...].astype(BF16)).astype(BF16)
        gmoves[0].start_all()
        pack_out(plan, place, second)
        pack_qkv(plan, place, second)
        pack_small(plan, second)
        loads.start(*ATTENDED, "h2")
        sums[1].every(sums[1].step_pair)
        loads.wait("up", "down")
        for low, high in groups(plan):
            expert_again(plan, first, low, high)
        for low, high in groups(plan):
            gmoves[0].wait(low, high)
            expert_backward(plan, first, low, high)
            gbacks[0].start(low, high)
        backs[1].near()
        combined(plan, r, place.chip, r.back, r.x, False)
        backs[1].far()
        combined(plan, r, 1 - place.chip, r.back, r.x, True)
        for image in range(plan.images):
            rows = slice(image * PAD, image * PAD + SEQ)
            r.y[image * SEQ : (image + 1) * SEQ, :] = r.y[rows, :] + r.x[rows, :]
        r.edge[...] = r.y[0 : plan.images * SEQ, :].astype(BF16)
        edges.start("result")
        backs[1].finish()
        loads.start("y", "x")
        build_picks(plan, first)
        sums[1].every(sums[1].step_scatter)
        loads.wait(*ATTENDED, "h2", "y", "x")

        def weights_out(layer, which):
            return pltpu.make_async_copy(
                r.gpart.at[which, place.tensor], r.grad_experts.at[layer, which],
                r.expert_sems.at[layer, which],
            )

        def add_far(layer):
            for which in range(2):
                far(layer, which).wait()
                r.gpart[which, place.tensor] = (
                    r.gpart[which, place.tensor].astype(F32)
                    + inbox(layer, which)[...].astype(F32)
                ).astype(BF16)
                weights_out(layer, which).start()

        def between_first():
            add_far(1)
            for which in range(2):
                weights_out(1, which).wait()
            expert_grads(plan, place, first, r.near)
            near_sums(place, first, r.near)
            for which in range(2):
                far(0, which).start()

        back_to_attention(plan, place, first, gbacks[0], between_first)
        sums[1].every(sums[1].step_share)
        pack_out(plan, place, first)
        sums[0].step_pair(0)
        half = plan.images // 2
        each(0, half, lambda image: attend_backward(first, total, image))
        sums[1].every(sums[1].step_out)
        sums[0].step_scatter(0)
        each(half, plan.images, lambda image: attend_backward(first, total, image))
        pack_qkv(plan, place, first)
        panels = len(plan.panels)
        for panel in range(1, panels - 1):
            sums[0].step_pair(panel)
        for image in range(plan.images):
            value = first_norm_back(plan, first, total, image)
            r.g[image * SEQ : (image + 1) * SEQ, :] = value[:SEQ]
        rows_out = pl.ds(0, up_to(plan.images * SEQ, 16))
        out = pltpu.make_async_copy(r.g.at[rows_out], r.grad, r.out_sems.at[0])
        out.start()
        pack_small(plan, first)
        sums[0].step_pair(panels - 1)
        for panel in range(1, panels):
            sums[0].step_scatter(panel)
        sums[1].every(sums[1].step_end)
        sum_out = [
            pltpu.make_async_copy(src, dst, r.out_sems.at[1 + k])
            for k, (src, dst) in enumerate(((r.sum_0, r.total_0), (r.sum_1, r.total_1)))
        ]
        sum_out[1].start()
        add_far(0)
        sums[0].every(sums[0].step_share)
        gbacks[0].finish()
        sums[0].every(sums[0].step_out)
        sums[0].every(sums[0].step_end)
        sum_out[0].start()
        edges.wait("result")
        for which in range(2):
            weights_out(0, which).wait()
        for copy in [out] + sum_out:
            copy.wait()

    rows, slots = plan.rows, plan.slots
    outputs = {"out_" + key: shapes[key] for key in SAVED}
    outputs.update(
        result=(shape_of_edge, BF16),
        grad=((up_to(plan.images * SEQ, 16), 512), F32),
        grad_experts=((2, 2, 512, 512), BF16),
        total_0=((plan.packed, 128), BF16),
        total_1=((plan.packed, 128), BF16),
    )
    scratch = {key: VMEM(*shapes[key]) for key in SAVED}
    for layer in range(2):
        for key in ("place", "table", "recv", "slot_gate"):
            scratch[f"{key}_{layer}"] = VMEM(*shapes[key])
        scratch[f"codes_{layer}"] = VMEM((4, plan.lanes), F32)
        scratch[f"packed_{layer}"] = VMEM((plan.packed, 128), BF16)
        scratch[f"sum_{layer}"] = VMEM((plan.packed, 128), BF16)
        scratch[f"sums_{layer}"] = ExpertSum.scratch(plan)
        scratch[f"swap_{layer}"] = HeadSwap.scratch()
        scratch[f"weights_{layer}"] = WeightGather.scratch()
        scratch[f"move_{layer}"] = Exchange.scratch(plan.experts)
        scratch[f"gmove_{layer}"] = Exchange.scratch(plan.experts)
        scratch[f"back_{layer}"] = Return.scratch(plan.experts)
        scratch[f"gback_{layer}"] = Return.scratch(plan.experts)
    scratch.update(backward_scratch(plan))
    scratch.pop("packed")
    scratch.update(
        edge=VMEM(shape_of_edge, BF16),
        route_all=VMEM((2, 2, plan.lanes), jnp.int32),
        router_all=VMEM((2, 128, 512), BF16),
        g=VMEM((rows, 512), F32),
        ret_0=VMEM((slots, 512), BF16),
        member=VMEM((slots, plan.lanes), BF16),
        gate=VMEM((plan.experts, plan.lanes), F32),
        picks=picks_scratch(plan),
        send=VMEM((slots, 512), BF16),
        gsend=VMEM((slots, 512), BF16),
        grecv=VMEM((slots, 512), BF16),
        back=VMEM((4 * slots, 512), BF16),
        total=CoreSum.scratch(plan.images),
        far_in=VMEM((512, 512), BF16),
        far_sems=DMA((2, 2, 2)),
        saves=DMA((len(SAVED),)),
        loads=DMA((len(SAVED),)),
        edges=DMA((3,)),
        expert_sems=DMA((2, 2)),
        out_sems=DMA((3,)),
    )
    return run_kernel("two_blocks", body, inputs, outputs, scratch, 3, 63.75, KEPT)


def final_form(plan, raw):
    experts = plan.experts
    tokens = plan.images * SEQ
    names = (
        "result", "grad", "grad_up", "grad_down", "grad_qkv", "grad_out", "grad_gain",
        "grad_bias_one", "grad_bias_two", "grad_router",
    )

    def kernel(*refs):
        result, grad, weights, total_0, total_1 = refs[:5]
        r = types.SimpleNamespace(**dict(zip(names, refs[5:15])))
        rows_buf, grad_buf, low, full, packs, sems, sems_out = refs[15:]
        loads = [
            pltpu.make_async_copy(src, dst, sems.at[k])
            for k, (src, dst) in enumerate(
                [(total_0, packs.at[0]), (total_1, packs.at[1]), (result, rows_buf)]
                + [(weights.at[k], low.at[k]) for k in range(2)] + [(grad, grad_buf)]
            )
        ]
        for copy in loads:
            copy.start()
        loads[2].wait()
        outs = [pltpu.make_async_copy(rows_buf, r.result, sems_out.at[0])]
        outs[0].start()
        for layer in range(2):
            loads[3 + layer].wait()
            for which, out in enumerate((r.grad_up, r.grad_down)):
                full[layer, which] = low[layer, which].astype(F32)
                outs.append(
                    pltpu.make_async_copy(
                        full.at[layer, which], out.at[layer], sems_out.at[1 + 2 * layer + which]
                    )
                )
                outs[-1].start()
        for layer in range(2):
            loads[layer].wait()
            Finals(plan, r).write(layer, packs[layer])
        loads[5].wait()
        r.grad[...] = grad_buf[0:tokens, :]
        for copy in outs:
            copy.wait()

    shapes = (
        ((tokens, 512), BF16), ((tokens, 512), F32), ((2, 512, 512), F32), ((2, 512, 512), F32),
        ((2, 3, 512, 128), F32), ((2, 128, 512), F32), ((2, 2, 512), F32), ((2, 512), F32),
        ((2, 512), F32), ((2, experts, 512), F32),
    )
    far_away = ("result", "grad_up", "grad_down")
    outs = pl.pallas_call(
        kernel,
        name="final_form",
        in_specs=[pl.BlockSpec(memory_space=pl.ANY)] * 5,
        out_specs=tuple(
            pl.BlockSpec(memory_space=pl.ANY if key in far_away else VMEM) for key in names
        ),
        out_shape=tuple(jax.ShapeDtypeStruct(*shape) for shape in shapes),
        scratch_shapes=[
            VMEM((tokens, 512), BF16), VMEM((up_to(tokens, 16), 512), F32),
            VMEM((2, 2, 512, 512), BF16), VMEM((2, 2, 512, 512), F32),
            VMEM((2, plan.packed, 128), BF16), DMA((6,)), DMA((5,)),
        ],
        compiler_params=pltpu.CompilerParams(vmem_limit_bytes=63 * MIB),
    )(raw.result, raw.grad, raw.grad_experts, raw.total_0, raw.total_1)
    return types.SimpleNamespace(**dict(zip(names, outs)))


def body(tokens, routes, ln_gain, ln_bias, w_qkv, w_out, w_router, w_up, w_down, cotangent):
    tok_rows = tokens.shape[0]
    experts = w_router.shape[2]
    plan = Plan(tok_rows, experts)
    if plan.stored:
        raw = one_kernel(
            plan,
            dict(
                gain_all=ln_gain, bias_all=ln_bias, w_qkv=w_qkv, w_out=w_out,
                w_up=w_up, w_down=w_down, tokens=tokens, cotangent=cotangent,
                routes=routes.transpose(0, 2, 1), router_in=w_router.transpose(0, 2, 1),
            ),
        )
        ends = final_form(plan, raw)
        return (
            ends.result, ends.grad, ends.grad_gain, ends.grad_bias_one, ends.grad_bias_two,
            ends.grad_qkv, ends.grad_out, ends.grad_router.transpose(0, 2, 1),
            ends.grad_up[:, None], ends.grad_down[:, None],
        )
    router_rows = jnp.pad(w_router.transpose(0, 2, 1), ((0, 0), (0, 128 - experts), (0, 0)))
    route_rows = routes.reshape(2, plan.images, SEQ, 2)
    route_rows = jnp.pad(
        route_rows, ((0, 0), (0, 0), (0, PAD - SEQ), (0, 0)), constant_values=-1
    ).reshape(2, plan.rows, 2)
    route_rows = jnp.pad(
        route_rows, ((0, 0), (0, plan.lanes - plan.rows), (0, 0)), constant_values=-1
    ).transpose(0, 2, 1)
    small = {"gain_all": ln_gain, "bias_all": ln_bias, "router_all": router_rows}
    weights = {"w_up": w_up, "w_down": w_down}
    one = first_forward(
        plan, dict(small, route_all=route_rows, w_qkv=w_qkv, w_out=w_out, **weights), tokens
    )
    two = second_whole(
        plan, dict(small, route_all=route_rows, **weights), cotangent,
        one.next, one.joint_later, one.out_later,
    )
    saved = {key: getattr(one, "out_" + key) for key in forward_shapes(plan)}
    three = first_backward(
        plan, small, saved, two.grad, two.gfar, two.gown, two.out_packed, tokens.shape
    )
    return (
        two.result, three.grad, three.grad_gain, three.grad_bias[:, 0], three.grad_bias[:, 1],
        three.grad_qkv, three.grad_out, three.grad_router.transpose(0, 2, 1),
        three.grad_up[:, None], three.grad_down[:, None],
    )


def solution(mesh):
    in_specs = (
        P(EXPERT, None),
        P(None, EXPERT, None),
        P(),
        P(),
        P(None, None, None, TENSOR),
        P(None, TENSOR, None),
        P(),
        P(None, EXPERT, None, TENSOR),
        P(None, EXPERT, TENSOR, None),
        P(EXPERT, None),
    )
    out_specs = (
        P(EXPERT, None),
        P(EXPERT, None),
        P(),
        P(),
        P(),
        P(None, None, None, TENSOR),
        P(None, TENSOR, None),
        P(),
        P(None, EXPERT, None, TENSOR),
        P(None, EXPERT, TENSOR, None),
    )
    return jax.shard_map(body, mesh=mesh, in_specs=in_specs, out_specs=out_specs, check_vma=False)
```
